32 devices in a mesh: rcv: 8 (over z, core), tm: 4 (over y, x).
Axes of the slice: x: 2, y: 2, z: 4, core: 2. Of those that a mesh axis runs over, the one named last changes fastest.
Arguments:
- spectra: bfloat16 [1024, 4, 3072], P('rcv', 'tm'), may hold values from -6 to 6
- valid: int32 [1024, 4], P('rcv', 'tm'), may hold values 0 or 1
- sources: int32 [2, 8], replicated, may hold values from 0 to 1023
Outputs:
- stack: float32 [2, 8, 1024, 301], P(None, None, ('rcv', 'tm'))
The draws below stay inside these ranges and needn't reach their ends.
All inputs are finite; a program needn't handle non-finite values. No bound on the sum of `valid` on one device may be relied on, other than what follows from the above.
Results may differ from the reference program's by a relative error of at most 0.004.
Values may be sent and summed in bfloat16 or wider, within the bound.
No kernel may reach another device: no remote copies, remote signals or barrier semaphores. Data moves between devices by JAX's collectives and lax.ppermute only.
A program may use at most 64 MiB of HBM per device.

```python
import math
import jax
import jax.numpy as jnp
from jax import lax

NF = 1536
NT = 4096
LAG = 150
HALF_WIN = 64
NSRC = 8
ROUNDS = 2
CHANNELS = 1024
SEGMENTS = 4


def place_ends(entries, stream_key, low, high):
    dims = entries.shape
    place = [jax.random.randint(jax.random.fold_in(stream_key, axis), (), 0, dims[axis]) for axis in range(len(dims))]
    entries = entries.at[tuple(place)].set(low)
    longest = dims.index(max(dims))
    place[longest] = (place[longest] + 1) % dims[longest]
    return entries.at[tuple(place)].set(high)


def level_of(own_key, extent, shards, least, high):
    def one(dim, parts):
        heights = jax.random.uniform(jax.random.fold_in(jax.random.fold_in(own_key, 6), dim), (parts,), jnp.float32, least / len(shards), high / len(shards))
        return jnp.repeat(jnp.exp(heights), extent[dim] // parts).reshape((-1,) + (1,) * (len(extent) - dim - 1))

    level = one(*shards[0])
    for cut in shards[1:]:
        level = level * one(*cut)
    return level


def scatter_about(stream_key, shape, deviation, reach, cuts=(), kind=jnp.bfloat16):
    values = jax.random.normal(stream_key, shape, jnp.float32) * deviation
    if len(cuts) > 0:
        values = level_of(stream_key, shape, cuts, -0.22, 0.18) * values
    return jnp.clip(values, min=-reach, max=reach).astype(kind)


def setup_inputs(seed: int = 0) -> dict:
    key_list = jax.random.split(jax.random.key(seed), 4)
    spectra = scatter_about(key_list[0], (CHANNELS, SEGMENTS, 2 * NF), 1.0, 6.0, ((0, 8), (1, 4)))
    valid = place_ends((jax.random.randint(key_list[1], (CHANNELS, SEGMENTS), 0, 2) < 1).astype(jnp.int32), jax.random.fold_in(key_list[1], 1), 0, 1)
    sources = place_ends(jax.random.randint(key_list[2], (ROUNDS, NSRC), 0, CHANNELS), jax.random.fold_in(key_list[2], 1), 0, CHANNELS - 1).astype(jnp.int32)
    return {"spectra": spectra, "valid": valid, "sources": sources}


epsilon = 1e-06

def window_counts(nbins, half_width):
    index = jnp.arange(nbins, dtype=jnp.int32)
    counted = jnp.minimum(index, half_width) + jnp.minimum(nbins - 1 - index, half_width) + 1
    return counted.astype(jnp.float32)

def smooth_mean(values, half_width):
    nbins = values.shape[-1]
    padding = [(0, 0)] * (values.ndim - 1) + [(half_width + 1, half_width)]
    padded = jnp.pad(values, padding)
    summed = jnp.cumsum(padded, axis=-1)
    window_sum = summed[..., 2 * half_width + 1:] - summed[..., :nbins]
    return window_sum / window_counts(nbins, half_width)

def whiten(spectra, validity):
    nbins = spectra.shape[-1] // 2
    real_part = spectra[..., :nbins].astype(jnp.float32)
    imag_part = spectra[..., nbins:].astype(jnp.float32)
    amplitude = jnp.sqrt(real_part * real_part + imag_part * imag_part)
    smooth = smooth_mean(amplitude, HALF_WIN)
    factor = validity / (smooth + epsilon)
    return jnp.concatenate([real_part * factor, imag_part * factor], axis=-1).astype(jnp.bfloat16)

def lag_tables(block_start, block_width):
    freq_bins = (block_start + 1 + jnp.arange(block_width, dtype=jnp.int32))[:, None]
    lag_steps = jnp.arange(-LAG, LAG + 1, dtype=jnp.int32)[None, :]
    windings = jnp.mod(freq_bins * lag_steps, NT).astype(jnp.float32)
    phases = windings * (2.0 * math.pi / NT)
    return (jnp.cos(phases), jnp.sin(phases))

def reference(spectra, valid, sources):
    validity = valid.astype(jnp.float32)
    whitened = whiten(spectra, validity[:, :, None])
    rcv_real = whitened[:, :, :NF].astype(jnp.float32)
    rcv_imag = whitened[:, :, NF:].astype(jnp.float32)
    cos_table, sin_table = lag_tables(0, NF)
    lag_scale = 2.0 / math.sqrt(NF)
    highest = lax.Precision.HIGHEST

    def one_source(source):
        chosen = whitened[source].astype(jnp.float32)
        src_real = chosen[:, :NF]
        src_imag = chosen[:, NF:]
        real_cross = jnp.einsum('tk,rtk->rk', src_real, rcv_real, precision=highest) + jnp.einsum('tk,rtk->rk', src_imag, rcv_imag, precision=highest)
        imag_cross = jnp.einsum('tk,rtk->rk', src_imag, rcv_real, precision=highest) - jnp.einsum('tk,rtk->rk', src_real, rcv_imag, precision=highest)
        lagged = (jnp.dot(real_cross, cos_table, precision=highest) - jnp.dot(imag_cross, sin_table, precision=highest)) * lag_scale
        intersection = jnp.dot(validity, validity[source], precision=highest)
        return lagged / jnp.maximum(intersection, 1.0)[:, None]
    stacked = lax.map(one_source, sources.reshape(-1))
    return stacked.reshape(ROUNDS, NSRC, CHANNELS, 2 * LAG + 1)
```

```python
import functools
import math

import jax
import jax.numpy as jnp
import numpy as np
from jax import lax
from jax.experimental import pallas as pl
from jax.experimental.pallas import tpu as pltpu
from jax.sharding import PartitionSpec as P

NT = 4096
LAG = 150
HALF_WIN = 64
EPSILON = 1e-06

UNUSABLE = 64.0
USABLE_BELOW = 32.0

LANES = 128
BLOCK = 256
MEBI = 1 << 20


def band_matrix():
    row = np.arange(BLOCK + 2 * LANES)[:, None] - LANES
    col = np.arange(BLOCK)[None, :]
    return (np.abs(row - col) <= HALF_WIN).astype(jnp.bfloat16)


def lag_table(nbins):
    winding = np.mod(
        np.arange(1, nbins + 1, dtype=np.int64)[:, None]
        * np.arange(-LAG, LAG + 1, dtype=np.int64)[None, :],
        NT,
    )
    theta = winding * (2.0 * math.pi / NT)
    table = np.concatenate([np.cos(theta), -np.sin(theta)], axis=0)
    columns = table.shape[1]
    padded = -(-columns // LANES) * LANES
    return np.pad(table, ((0, 0), (0, padded - columns))).astype(jnp.bfloat16)


def whiten_rows(rows, nbins, band_ref, high, low, store):
    count = rows.shape[0]
    real = rows[:, :nbins].astype(jnp.float32)
    imag = rows[:, nbins:].astype(jnp.float32)
    amplitude = jnp.sqrt(real * real + imag * imag)
    rounded = amplitude.astype(jnp.bfloat16)
    edge = jnp.zeros((count, LANES), jnp.bfloat16)
    for part, value in (
        (high, rounded),
        (low, (amplitude - rounded.astype(jnp.float32)).astype(jnp.bfloat16)),
    ):
        part[:count, :LANES] = edge
        part[:count, LANES : LANES + nbins] = value
        part[:count, LANES + nbins :] = edge
    band = band_ref[...]
    for first in range(0, nbins, BLOCK):
        span = slice(first, first + BLOCK + 2 * LANES)
        window = jnp.dot(high[:count, span], band, preferred_element_type=jnp.float32)
        window += jnp.dot(low[:count, span], band, preferred_element_type=jnp.float32)
        index = first + lax.broadcasted_iota(jnp.int32, (1, BLOCK), 1)
        counted = jnp.minimum(index, HALF_WIN) + jnp.minimum(nbins - 1 - index, HALF_WIN) + 1
        smooth = window / counted.astype(jnp.float32)
        factor = 1.0 / (smooth + EPSILON)
        re = real[:, first : first + BLOCK]
        im = imag[:, first : first + BLOCK]
        usable = re < USABLE_BELOW
        store(
            first,
            jnp.where(usable, re * factor, 0.0).astype(jnp.bfloat16),
            jnp.where(usable, im * factor, 0.0).astype(jnp.bfloat16),
        )


def whiten_kernel(segments, *refs):
    blocks, (band_ref, out_ref, valid_ref, high, low) = refs[:segments], refs[segments:]
    rows = jnp.concatenate([ref[...] for ref in blocks], axis=0)
    nbins = rows.shape[1] // 2

    def store(first, re, im):
        out_ref[:, first : first + BLOCK] = re
        out_ref[:, nbins + first : nbins + first + BLOCK] = im

    whiten_rows(rows, nbins, band_ref, high, low, store)
    valid_ref[...] = jnp.where(rows[:, :LANES].astype(jnp.float32) < USABLE_BELOW, 1.0, 0.0)


def stack_kernel(segments, keep, *refs):
    blocks = refs[:segments]
    rcv_ref, rcv_valid, band_ref, table_ref, out_ref, src, src_valid, high, low, cross = refs[
        segments:
    ]
    nsrc = blocks[0].shape[0]
    nbins = rcv_ref.shape[1] // 2
    rows = jnp.concatenate([ref[...] for ref in blocks], axis=0)

    def store(first, re, im):
        src[:, first : first + BLOCK] = re.astype(jnp.float32)
        src[:, nbins + first : nbins + first + BLOCK] = im.astype(jnp.float32)

    whiten_rows(rows, nbins, band_ref, high, low, store)
    src_valid[...] = jnp.where(rows[:, :LANES].astype(jnp.float32) < USABLE_BELOW, 1.0, 0.0)

    def one_block(block, carry):
        re_at = pl.ds(pl.multiple_of(block * LANES, LANES), LANES)
        im_at = pl.ds(pl.multiple_of(nbins + block * LANES, LANES), LANES)
        rcv_re = rcv_ref[:, re_at].astype(jnp.float32)
        rcv_im = rcv_ref[:, im_at].astype(jnp.float32)
        for source in range(nsrc):
            real, imag = 0.0, 0.0
            for segment in range(segments):
                row = segment * nsrc + source
                s_re, s_im = src[row : row + 1, re_at], src[row : row + 1, im_at]
                r_re = rcv_re[segment * keep : (segment + 1) * keep]
                r_im = rcv_im[segment * keep : (segment + 1) * keep]
                real = real + (s_re * r_re + s_im * r_im)
                imag = imag + (s_im * r_re - s_re * r_im)
            at = slice(source * keep, (source + 1) * keep)
            cross[at, re_at] = real.astype(cross.dtype)
            cross[at, im_at] = imag.astype(cross.dtype)
        return carry

    lax.fori_loop(0, nbins // LANES, one_block, 0)

    lags = out_ref.shape[1]
    scale = 2.0 / math.sqrt(nbins)
    lagged = jnp.dot(
        cross[...].astype(jnp.bfloat16), table_ref[...], preferred_element_type=jnp.float32
    )
    for source in range(nsrc):
        pairs = 0.0
        for segment in range(segments):
            row = segment * nsrc + source
            pairs = pairs + src_valid[row : row + 1, :] * rcv_valid[
                segment * keep : (segment + 1) * keep, :
            ]
        weight = scale / jnp.maximum(pairs, 1.0)
        for first in range(0, lags, LANES):
            last = min(first + LANES, lags)
            value = lagged[source * keep : (source + 1) * keep, first : first + LANES] * weight
            out_ref[source * keep : (source + 1) * keep, first:last] = value[:, : last - first]


def whiten_blocks(blocks, band):
    segments, (keep, width) = len(blocks), blocks[0].shape
    count, nbins = segments * keep, width // 2
    padded = pltpu.VMEM((count, nbins + 2 * LANES), jnp.bfloat16)
    vmem = pl.BlockSpec(memory_space=pltpu.VMEM)
    return pl.pallas_call(
        functools.partial(whiten_kernel, segments),
        out_shape=(
            jax.ShapeDtypeStruct((count, width), jnp.bfloat16),
            jax.ShapeDtypeStruct((count, LANES), jnp.float32),
        ),
        in_specs=[vmem] * (segments + 1),
        out_specs=(vmem, vmem),
        scratch_shapes=[padded, padded],
        compiler_params=pltpu.CompilerParams(vmem_limit_bytes=32 * MEBI),
        cost_estimate=pl.CostEstimate(
            flops=count * width * 1024, bytes_accessed=count * width * 4, transcendentals=0
        ),
        name="whiten_receivers",
    )(*blocks, band)


def stack_blocks(sources, receivers, receivers_valid, band, table):
    segments, (nsrc, width) = len(sources), sources[0].shape
    keep = receivers.shape[0] // segments
    nbins, count = width // 2, segments * nsrc
    padded = pltpu.VMEM((count, nbins + 2 * LANES), jnp.bfloat16)
    cross_type = jnp.bfloat16 if keep % 16 == 0 else jnp.float32
    vmem = pl.BlockSpec(memory_space=pltpu.VMEM)
    return pl.pallas_call(
        functools.partial(stack_kernel, segments, keep),
        out_shape=jax.ShapeDtypeStruct((nsrc * keep, 2 * LAG + 1), jnp.float32),
        in_specs=[vmem] * (segments + 4),
        out_specs=vmem,
        scratch_shapes=[
            pltpu.VMEM((count, width), jnp.float32),
            pltpu.VMEM((count, LANES), jnp.float32),
            padded,
            padded,
            pltpu.VMEM((nsrc * keep, width), cross_type),
        ],
        compiler_params=pltpu.CompilerParams(vmem_limit_bytes=40 * MEBI),
        cost_estimate=pl.CostEstimate(
            flops=2 * nsrc * keep * width * 2 * LAG,
            bytes_accessed=width * 1024,
            transcendentals=0,
        ),
        name="stack_sources",
    )(*sources, receivers, receivers_valid, band, table)


def swapped(value, axis, size, step):
    return lax.ppermute(value, axis, [(i, i ^ step) for i in range(size)])


def shards(rcv_size, tm_size, spectra, valid, sources):
    channels, _, width = spectra.shape
    keep = channels // tm_size
    rounds, per_round = sources.shape
    mine = lax.axis_index("tm")
    encoded = jnp.where(valid != 0, spectra[:, 0, :], jnp.bfloat16(UNUSABLE))

    onehot = (
        sources.reshape(-1)[:, None] - lax.axis_index("rcv") * channels
        == jnp.arange(channels, dtype=jnp.int32)[None, :]
    )
    picked = jnp.dot(
        onehot.astype(jnp.bfloat16), encoded, preferred_element_type=jnp.float32
    ).astype(jnp.bfloat16)

    def block_for(step):
        return lax.dynamic_slice_in_dim(encoded, (mine ^ step) * keep, keep, 0)

    receivers = [block_for(0)] + [
        swapped(block_for(step), "tm", tm_size, step) for step in range(1, tm_size)
    ]
    step = 1
    while step < rcv_size:
        picked = picked + swapped(picked, "rcv", rcv_size, step)
        step *= 2
    chosen = [picked] + [swapped(picked, "tm", tm_size, step) for step in range(1, tm_size)]

    band = jnp.asarray(band_matrix())
    whitened, usable = whiten_blocks(receivers, band)
    stack = stack_blocks(chosen, whitened, usable, band, jnp.asarray(lag_table(width // 2)))
    return stack.reshape(rounds, per_round, keep, 2 * LAG + 1)


def solution(mesh):
    body = functools.partial(shards, mesh.shape["rcv"], mesh.shape["tm"])
    in_specs = (P("rcv", "tm", None), P("rcv", "tm"), P())
    out_specs = P(None, None, ("rcv", "tm"), None)
    return jax.shard_map(body, mesh=mesh, in_specs=in_specs, out_specs=out_specs, check_vma=False)
```

```python
import functools
import math

import jax
import jax.numpy as jnp
import numpy as np
from jax import lax
from jax.experimental import pallas as pl
from jax.experimental.pallas import tpu as pltpu
from jax.sharding import PartitionSpec as P

NT = 4096
LAG = 150
HALF_WIN = 64
EPSILON = 1e-06

UNUSABLE = 64.0
USABLE_BELOW = 32.0

LANES = 128
BLOCK = 256
MEBI = 1 << 20
VMEM = pl.BlockSpec(memory_space=pltpu.VMEM)
HBM = pl.BlockSpec(memory_space=pltpu.HBM)
ANY = pl.BlockSpec(memory_space=pl.ANY)


def lag_table(nbins):
    winding = np.mod(
        np.arange(1, nbins + 1, dtype=np.int64)[:, None]
        * np.arange(-LAG, LAG + 1, dtype=np.int64)[None, :],
        NT,
    )
    theta = winding * (2.0 * math.pi / NT)
    table = np.concatenate([np.cos(theta), -np.sin(theta)], axis=0)
    columns = table.shape[1]
    padded = -(-columns // LANES) * LANES
    return np.pad(table, ((0, 0), (0, padded - columns))).astype(jnp.bfloat16)


def iota(shape, dim):
    return lax.broadcasted_iota(jnp.int32, shape, dim)


def whitening(real, imag, high, low):
    count, nbins = real.shape
    blocks = nbins // BLOCK
    span = BLOCK + 2 * LANES
    amplitude = jnp.sqrt(real * real + imag * imag)
    rounded = amplitude.astype(jnp.bfloat16)
    edge = jnp.zeros((count, LANES), jnp.bfloat16)
    for part, value in (
        (high, rounded),
        (low, (amplitude - rounded.astype(jnp.float32)).astype(jnp.bfloat16)),
    ):
        part[:, :LANES] = edge
        part[:, LANES : LANES + nbins] = value
        part[:, LANES + nbins :] = edge
    near = jnp.abs(iota((span, BLOCK), 0) - LANES - iota((span, BLOCK), 1)) <= HALF_WIN
    band = jnp.where(near, 1.0, 0.0).astype(jnp.bfloat16)
    pieces = [
        part[:, block * BLOCK : block * BLOCK + span] for block in range(blocks) for part in (high, low)
    ]
    windows = jnp.dot(
        jnp.concatenate(pieces, axis=0), band, preferred_element_type=jnp.float32
    )
    for block in range(blocks):
        first = block * BLOCK
        at = 2 * block * count
        window = windows[at : at + count] + windows[at + count : at + 2 * count]
        index = first + iota((1, BLOCK), 1)
        counted = jnp.minimum(index, HALF_WIN) + jnp.minimum(nbins - 1 - index, HALF_WIN) + 1
        factor = 1.0 / (window / counted.astype(jnp.float32) + EPSILON)
        re = real[:, first : first + BLOCK]
        im = imag[:, first : first + BLOCK]
        usable = re < USABLE_BELOW
        re = jnp.where(usable, re * factor, 0.0).astype(jnp.bfloat16).astype(jnp.float32)
        im = jnp.where(usable, im * factor, 0.0).astype(jnp.bfloat16).astype(jnp.float32)
        yield slice(first, first + BLOCK), re, im


def usable_rows(real):
    return jnp.where(real[:, :LANES] < USABLE_BELOW, 1.0, 0.0)


def encode_kernel(
    spectra_ref, valid_ref, sources_ref, encoded_ref, own_ref, other_ref,
    spectra, valid, sources, arrived
):
    copies = [
        pltpu.make_async_copy(sources_ref, sources, arrived.at[0]),
        pltpu.make_async_copy(valid_ref, valid, arrived.at[1]),
        pltpu.make_async_copy(spectra_ref, spectra, arrived.at[2]),
    ]
    for copy in copies:
        copy.start()
    channels, width = spectra_ref.shape
    nbins = width // 2
    per_round = sources.shape[1]
    half = sources.shape[0] * per_round // 2
    index = lax.axis_index("rcv")
    copies[0].wait()
    copies[1].wait()
    diagonal = iota((channels, channels), 0) == iota((channels, channels), 1)
    usable = jnp.sum(jnp.where(diagonal, valid[...], 0), axis=1, keepdims=True) != 0
    onehots = []
    for part in (index % 2, 1 - index % 2):
        onehot = jnp.zeros((half, channels), jnp.float32)
        for source in range(half):
            number = part * half + source
            local = sources[number // per_round, number % per_round] - index * channels
            hit = (iota((half, channels), 0) == source) & (iota((half, channels), 1) == local)
            onehot = jnp.where(hit, 1.0, onehot)
        onehots.append(onehot)
    onehot = jnp.concatenate(onehots, axis=0).astype(jnp.bfloat16)
    copies[2].wait()
    encoded = jnp.where(usable, spectra[...].astype(jnp.float32), UNUSABLE).astype(jnp.bfloat16)
    encoded_ref[...] = encoded
    picked = jnp.dot(onehot, encoded, preferred_element_type=jnp.float32)
    for part, ref in enumerate((own_ref, other_ref)):
        rows = picked[part * half : (part + 1) * half]
        ref[...] = jnp.concatenate([rows[:, :nbins], rows[:, nbins:]], axis=0).astype(ref.dtype)


def whiten_kernel(segments, *refs):
    blocks, (real_ref, imag_ref, both_ref, valid_ref, high, low) = refs[:segments], refs[segments:]
    rows = jnp.concatenate([ref[...].astype(jnp.float32) for ref in blocks], axis=0)
    nbins = rows.shape[1] // 2
    real, imag = rows[:, :nbins], rows[:, nbins:]
    for at, re, im in whitening(real, imag, high, low):
        real_ref[:, at] = re
        imag_ref[:, at] = im
        both_ref[:, at] = re + im
    valid_ref[...] = usable_rows(real)


def stack_kernel(segments, swap, *refs):
    (
        slabs_ref, rcv_re, rcv_im, rcv_both, rcv_valid, table_ref, *_, out_ref,
        src_re, src_diff, src_sum, high, low, cross_a, cross_b, total, result, written
    ) = refs
    half = slabs_ref.shape[0] // (2 * segments)
    nbins = slabs_ref.shape[1]
    keep = rcv_re.shape[0] // segments
    chunk = min(keep, 16)
    slabs = slabs_ref[...].astype(jnp.float32)
    real = jnp.concatenate(
        [slabs[2 * half * t : 2 * half * t + half] for t in range(segments)], axis=0
    )
    imag = jnp.concatenate(
        [slabs[2 * half * t + half : 2 * half * (t + 1)] for t in range(segments)], axis=0
    )
    for at, re, im in whitening(real, imag, high, low):
        src_re[:, at] = re
        src_diff[:, at] = im - re
        src_sum[:, at] = im + re
    src_valid = usable_rows(real)
    total[...] = jnp.zeros_like(total)
    cross_b[...] = jnp.zeros_like(cross_b)

    def multiply(block, cross):
        for sub in range(BLOCK // LANES):
            at = pl.ds(pl.multiple_of(block * BLOCK + sub * LANES, LANES), LANES)
            for first in range(0, keep, chunk):
                rows = [slice(t * keep + first, t * keep + first + chunk) for t in range(segments)]
                r_re = [rcv_re[row, at] for row in rows]
                r_im = [rcv_im[row, at] for row in rows]
                r_both = [rcv_both[row, at] for row in rows]
                for source in range(half):
                    p, q, w = 0.0, 0.0, 0.0
                    for t in range(segments):
                        row = slice(t * half + source, t * half + source + 1)
                        p = p + src_re[row, at] * r_both[t]
                        q = q + src_diff[row, at] * r_im[t]
                        w = w + src_sum[row, at] * r_re[t]
                    to = slice(source * keep + first, source * keep + first + chunk)
                    cross[to, sub * LANES : (sub + 1) * LANES] = (p + q).astype(cross.dtype)
                    cross[to, BLOCK + sub * LANES : BLOCK + (sub + 1) * LANES] = (w - p).astype(
                        cross.dtype
                    )

    def project(block, cross):
        value = cross[...].astype(jnp.bfloat16)
        re_at = pl.ds(pl.multiple_of(block * BLOCK, BLOCK), BLOCK)
        im_at = pl.ds(pl.multiple_of(nbins + block * BLOCK, BLOCK), BLOCK)
        total[...] += jnp.dot(
            value[:, :BLOCK], table_ref[re_at, :], preferred_element_type=jnp.float32
        ) + jnp.dot(value[:, BLOCK:], table_ref[im_at, :], preferred_element_type=jnp.float32)

    def two_blocks(pair, carry):
        multiply(2 * pair, cross_a)
        project(jnp.maximum(2 * pair - 1, 0), cross_b)
        multiply(2 * pair + 1, cross_b)
        project(2 * pair, cross_a)
        return carry

    pairs = nbins // (2 * BLOCK)
    lax.fori_loop(0, pairs, two_blocks, 0)
    project(2 * pairs - 1, cross_b)

    lags = result.shape[1]
    scale = 2.0 / math.sqrt(nbins)
    for source in range(half):
        common = 0.0
        for t in range(segments):
            row = t * half + source
            common = common + src_valid[row : row + 1] * rcv_valid[t * keep : (t + 1) * keep, :]
        weight = scale / jnp.maximum(common, 1.0)
        to = slice(source * keep, (source + 1) * keep)
        for first in range(0, lags, LANES):
            last = min(first + LANES, lags)
            value = total[to, first : first + LANES] * weight
            result[to, first:last] = value[:, : last - first]
    part = (lax.axis_index("rcv") + swap) % 2
    count = half * keep
    copy = pltpu.make_async_copy(
        result, out_ref.at[pl.ds(pl.multiple_of(part * count, count), count)], written
    )
    copy.start()
    copy.wait()


def encode(spectra, valid, sources):
    channels, width = spectra.shape
    count = sources.size
    slab = jax.ShapeDtypeStruct((count, width // 2), jnp.bfloat16)
    return pl.pallas_call(
        encode_kernel,
        out_shape=(jax.ShapeDtypeStruct((channels, width), jnp.bfloat16), slab, slab),
        in_specs=[HBM] * 3,
        out_specs=(VMEM,) * 3,
        scratch_shapes=[
            pltpu.VMEM((channels, width), jnp.bfloat16),
            pltpu.VMEM((1, channels), jnp.int32),
            pltpu.SMEM(sources.shape, jnp.int32),
            pltpu.SemaphoreType.DMA((3,)),
        ],
        compiler_params=pltpu.CompilerParams(vmem_limit_bytes=60 * MEBI),
        name="encode_and_pick",
    )(spectra, valid, sources)


def whiten_blocks(blocks):
    segments, (keep, width) = len(blocks), blocks[0].shape
    count, nbins = segments * keep, width // 2
    padded = pltpu.VMEM((count, nbins + 2 * LANES), jnp.bfloat16)
    part = jax.ShapeDtypeStruct((count, nbins), jnp.float32)
    return pl.pallas_call(
        functools.partial(whiten_kernel, segments),
        out_shape=(part, part, part, jax.ShapeDtypeStruct((count, LANES), jnp.float32)),
        in_specs=[VMEM] * segments,
        out_specs=(VMEM,) * 4,
        scratch_shapes=[padded, padded],
        compiler_params=pltpu.CompilerParams(vmem_limit_bytes=24 * MEBI),
        cost_estimate=pl.CostEstimate(
            flops=count * width * 1024, bytes_accessed=count * width * 4, transcendentals=0
        ),
        name="whiten_receivers",
    )(*blocks)


def stack_half(segments, swap, slabs, receivers, table, rest=()):
    half, nbins = slabs.shape[0] // (2 * segments), slabs.shape[1]
    keep = receivers[0].shape[0] // segments
    count, rows = segments * half, half * keep
    padded = pltpu.VMEM((count, nbins + 2 * LANES), jnp.bfloat16)
    part = pltpu.VMEM((count, nbins), jnp.float32)
    cross = pltpu.VMEM((rows, 2 * BLOCK), jnp.bfloat16 if keep % 16 == 0 else jnp.float32)
    return pl.pallas_call(
        functools.partial(stack_kernel, segments, swap),
        out_shape=jax.ShapeDtypeStruct((2 * rows, 2 * LAG + 1), jnp.float32),
        in_specs=[VMEM] * 6 + [ANY] * len(rest),
        out_specs=ANY,
        input_output_aliases={6: 0} if rest else {},
        scratch_shapes=[
            part,
            part,
            part,
            padded,
            padded,
            cross,
            cross,
            pltpu.VMEM((rows, table.shape[1]), jnp.float32),
            pltpu.VMEM((rows, 2 * LAG + 1), jnp.float32),
            pltpu.SemaphoreType.DMA,
        ],
        compiler_params=pltpu.CompilerParams(vmem_limit_bytes=32 * MEBI),
        cost_estimate=pl.CostEstimate(
            flops=4 * rows * nbins * 2 * LAG, bytes_accessed=nbins * 2048, transcendentals=0
        ),
        name="stack_other_half" if swap else "stack_own_half",
    )(slabs, *receivers, table, *rest)


def swapped(value, axis, size, step):
    return lax.ppermute(value, axis, [(i, i ^ step) for i in range(size)])


def shards(rcv_size, tm_size, spectra, valid, sources):
    channels, _, width = spectra.shape
    keep = channels // tm_size
    rounds, per_round = sources.shape
    mine = lax.axis_index("tm")
    encoded, own, other = encode(spectra[:, 0, :], valid.reshape(1, channels), sources)

    def block_for(step, block):
        return lax.dynamic_slice_in_dim(block, (mine ^ step) * keep, keep, 0)

    own = own + swapped(other, "rcv", rcv_size, 1)
    receivers = [block_for(0, encoded)]
    step, later = 2, tm_size - 1
    while step < rcv_size:
        now, later = later - later // 2, later // 2
        own, encoded = lax.optimization_barrier((own, encoded))
        for swap in range(len(receivers), len(receivers) + now):
            receivers.append(swapped(block_for(swap, encoded), "tm", tm_size, swap))
        own = own + swapped(own, "rcv", rcv_size, step)
        step *= 2
    for swap in range(len(receivers), tm_size):
        receivers.append(swapped(block_for(swap, encoded), "tm", tm_size, swap))
    own, receivers = lax.optimization_barrier((own, receivers))
    own = [own] + [swapped(own, "tm", tm_size, step) for step in range(1, tm_size)]
    whitened = whiten_blocks(receivers)
    own, whitened = lax.optimization_barrier((own, whitened))
    own = jnp.concatenate(own, axis=0)
    other = swapped(own, "rcv", rcv_size, 1)

    table = jnp.asarray(lag_table(width // 2))
    stack = stack_half(tm_size, 0, own, whitened, table)
    stack = stack_half(tm_size, 1, other, whitened, table, (stack,))
    return stack.reshape(rounds, per_round, keep, 2 * LAG + 1)


def solution(mesh):
    body = functools.partial(shards, mesh.shape["rcv"], mesh.shape["tm"])
    in_specs = (P("rcv", "tm", None), P("rcv", "tm"), P())
    out_specs = P(None, None, ("rcv", "tm"), None)
    return jax.shard_map(body, mesh=mesh, in_specs=in_specs, out_specs=out_specs, check_vma=False)
```

```python
import functools
import math

import jax
import jax.numpy as jnp
import numpy as np
from jax import lax
from jax.experimental import pallas as pl
from jax.experimental.pallas import tpu as pltpu
from jax.sharding import PartitionSpec as P

NT = 4096
LAG = 150
HALF_WIN = 64
EPSILON = 1e-06

UNUSABLE = 64.0
USABLE_BELOW = 32.0

LANES = 128
BLOCK = 256
MEBI = 1 << 20
FIRST_LAG = LANES - LAG
VMEM = pl.BlockSpec(memory_space=pltpu.VMEM)
HBM = pl.BlockSpec(memory_space=pltpu.HBM)


def lag_table(nbins):
    winding = np.mod(
        np.arange(1, nbins + 1, dtype=np.int64)[:, None]
        * np.arange(FIRST_LAG, FIRST_LAG + BLOCK, dtype=np.int64)[None, :],
        NT,
    )
    theta = winding * (2.0 * math.pi / NT)
    return np.concatenate([np.cos(theta), -np.sin(theta)], axis=0).astype(jnp.bfloat16)


def iota(shape, dim):
    return lax.broadcasted_iota(jnp.int32, shape, dim)


def whitening(real, imag, high, low):
    count, nbins = real.shape
    blocks = nbins // BLOCK
    span = BLOCK + 2 * LANES
    amplitude = jnp.sqrt(real * real + imag * imag)
    rounded = amplitude.astype(jnp.bfloat16)
    edge = jnp.zeros((count, LANES), jnp.bfloat16)
    for part, value in (
        (high, rounded),
        (low, (amplitude - rounded.astype(jnp.float32)).astype(jnp.bfloat16)),
    ):
        part[:, :LANES] = edge
        part[:, LANES : LANES + nbins] = value
        part[:, LANES + nbins :] = edge
    near = jnp.abs(iota((span, BLOCK), 0) - LANES - iota((span, BLOCK), 1)) <= HALF_WIN
    band = jnp.where(near, 1.0, 0.0).astype(jnp.bfloat16)
    pieces = [
        part[:, block * BLOCK : block * BLOCK + span] for block in range(blocks) for part in (high, low)
    ]
    windows = jnp.dot(
        jnp.concatenate(pieces, axis=0), band, preferred_element_type=jnp.float32
    )
    for block in range(blocks):
        first = block * BLOCK
        at = 2 * block * count
        window = windows[at : at + count] + windows[at + count : at + 2 * count]
        index = first + iota((1, BLOCK), 1)
        counted = jnp.minimum(index, HALF_WIN) + jnp.minimum(nbins - 1 - index, HALF_WIN) + 1
        factor = 1.0 / (window / counted.astype(jnp.float32) + EPSILON)
        re = real[:, first : first + BLOCK]
        im = imag[:, first : first + BLOCK]
        usable = re < USABLE_BELOW
        re = jnp.where(usable, re * factor, 0.0).astype(jnp.bfloat16).astype(jnp.float32)
        im = jnp.where(usable, im * factor, 0.0).astype(jnp.bfloat16).astype(jnp.float32)
        yield slice(first, first + BLOCK), re, im


def usable_rows(real):
    return jnp.where(real[:, :LANES] < USABLE_BELOW, 1.0, 0.0)


def encode_kernel(
    segments, spectra_ref, valid_ref, sources_ref, picked_ref, *refs
):
    blocks, (encoded_ref, spectra, valid, sources, arrived) = refs[:segments], refs[segments:]
    copies = [
        pltpu.make_async_copy(sources_ref, sources, arrived.at[0]),
        pltpu.make_async_copy(valid_ref, valid, arrived.at[1]),
        pltpu.make_async_copy(spectra_ref, spectra, arrived.at[2]),
    ]
    for copy in copies:
        copy.start()
    channels, width = spectra_ref.shape
    rounds, per_round = sources.shape
    count = rounds * per_round
    first_channel = lax.axis_index("rcv") * channels
    copies[0].wait()
    copies[1].wait()
    diagonal = iota((channels, channels), 0) == iota((channels, channels), 1)
    usable = jnp.sum(jnp.where(diagonal, valid[...], 0), axis=1, keepdims=True) != 0
    local = jnp.zeros((count, channels), jnp.int32)
    for source in range(count):
        here = sources[source // per_round, source % per_round] - first_channel
        local = jnp.where(iota((count, channels), 0) == source, here, local)
    onehot = jnp.where(local == iota((count, channels), 1), 1.0, 0.0).astype(jnp.bfloat16)
    copies[2].wait()
    encoded = jnp.where(usable, spectra[...].astype(jnp.float32), UNUSABLE)
    encoded_ref[...] = encoded
    picked = jnp.dot(onehot, encoded.astype(jnp.bfloat16), preferred_element_type=jnp.float32)
    parts = picked_ref.shape[0]
    for part in range(parts):
        at = slice(part * width // parts, (part + 1) * width // parts)
        picked_ref[part] = picked[:, at].astype(jnp.bfloat16)
    keep = channels // segments
    for step, block in enumerate(blocks):
        at = pl.multiple_of((lax.axis_index("tm") ^ step) * keep, keep)
        block[...] = encoded_ref[pl.ds(at, keep), :].astype(jnp.bfloat16)


def whiten_kernel(segments, *refs):
    blocks, (real_ref, imag_ref, both_ref, valid_ref, high, low) = refs[:segments], refs[segments:]
    rows = jnp.concatenate([ref[...].astype(jnp.float32) for ref in blocks], axis=0)
    nbins = rows.shape[1] // 2
    real, imag = rows[:, :nbins], rows[:, nbins:]
    for at, re, im in whitening(real, imag, high, low):
        real_ref[:, at] = re
        imag_ref[:, at] = im
        both_ref[:, at] = re + im
    valid_ref[...] = usable_rows(real)


def stack_kernel(
    segments, slabs_ref, rcv_re, rcv_im, rcv_both, rcv_valid, table_ref, out_ref,
    src_re, src_diff, src_sum, high, low, cross_a, cross_b, total_re, total_im
):
    parts, count, share = slabs_ref.shape[1:]
    nbins = parts * share // 2
    keep = rcv_re.shape[0] // segments
    chunk = min(keep, 16)
    slabs = []
    for step in range(segments):
        slab = slabs_ref[lax.axis_index("tm") ^ step].astype(jnp.float32)
        slabs.append(jnp.concatenate([slab[part] for part in range(parts)], axis=1))
    slabs = jnp.concatenate(slabs, axis=0)
    real, imag = slabs[:, :nbins], slabs[:, nbins:]
    for at, re, im in whitening(real, imag, high, low):
        src_re[:, at] = re
        src_diff[:, at] = im - re
        src_sum[:, at] = im + re
    src_valid = usable_rows(real)
    total_re[...] = jnp.zeros_like(total_re)
    total_im[...] = jnp.zeros_like(total_im)
    cross_b[...] = jnp.zeros_like(cross_b)

    def multiply(block, cross):
        for sub in range(BLOCK // LANES):
            at = pl.ds(pl.multiple_of(block * BLOCK + sub * LANES, LANES), LANES)
            for first in range(0, keep, chunk):
                rows = [slice(t * keep + first, t * keep + first + chunk) for t in range(segments)]
                r_re = [rcv_re[row, at] for row in rows]
                r_im = [rcv_im[row, at] for row in rows]
                r_both = [rcv_both[row, at] for row in rows]
                for source in range(count):
                    p, q, w = 0.0, 0.0, 0.0
                    for t in range(segments):
                        row = slice(t * count + source, t * count + source + 1)
                        p = p + src_re[row, at] * r_both[t]
                        q = q + src_diff[row, at] * r_im[t]
                        w = w + src_sum[row, at] * r_re[t]
                    to = slice(source * keep + first, source * keep + first + chunk)
                    cross[to, sub * LANES : (sub + 1) * LANES] = (p + q).astype(cross.dtype)
                    cross[to, BLOCK + sub * LANES : BLOCK + (sub + 1) * LANES] = (w - p).astype(
                        cross.dtype
                    )

    def project(block, cross):
        value = cross[...].astype(jnp.bfloat16)
        re_at = pl.ds(pl.multiple_of(block * BLOCK, BLOCK), BLOCK)
        im_at = pl.ds(pl.multiple_of(nbins + block * BLOCK, BLOCK), BLOCK)
        total_re[...] += jnp.dot(
            value[:, :BLOCK], table_ref[re_at, :], preferred_element_type=jnp.float32
        )
        total_im[...] += jnp.dot(
            value[:, BLOCK:], table_ref[im_at, :], preferred_element_type=jnp.float32
        )

    def two_blocks(pair, carry):
        multiply(2 * pair, cross_a)
        project(jnp.maximum(2 * pair - 1, 0), cross_b)
        multiply(2 * pair + 1, cross_b)
        project(2 * pair, cross_a)
        return carry

    pairs = nbins // (2 * BLOCK)
    lax.fori_loop(0, pairs, two_blocks, 0)
    project(2 * pairs - 1, cross_b)

    lags = out_ref.shape[1]
    scale = 2.0 / math.sqrt(nbins)
    mirror = LAG - FIRST_LAG - iota((keep, LANES), 1)
    for source in range(count):
        common = 0.0
        for t in range(segments):
            row = t * count + source
            common = common + src_valid[row : row + 1] * rcv_valid[t * keep : (t + 1) * keep, :]
        weight = scale / jnp.maximum(common, 1.0)
        to = slice(source * keep, (source + 1) * keep)
        even, odd = total_re[to], total_im[to]
        ahead = even + odd
        behind = even - odd
        low_part = jnp.take_along_axis(
            behind[:, :LANES], jnp.clip(mirror, 0, LANES - 1), axis=1
        )
        high_part = jnp.take_along_axis(
            behind[:, LANES:], jnp.clip(mirror - LANES, 0, LANES - 1), axis=1
        )
        out_ref[to, :LANES] = jnp.where(mirror < LANES, low_part, high_part) * weight
        for first in range(0, lags - LANES, LANES):
            last = min(first + LANES, lags - LANES)
            value = ahead[:, first : first + LANES] * weight
            out_ref[to, LANES + first : LANES + last] = value[:, : last - first]


def encode(rcv_size, tm_size, spectra, valid, sources):
    channels, width = spectra.shape
    keep, count = channels // tm_size, sources.size
    picked = jax.ShapeDtypeStruct((rcv_size, count, width // rcv_size), jnp.bfloat16)
    block = jax.ShapeDtypeStruct((keep, width), jnp.bfloat16)
    return pl.pallas_call(
        functools.partial(encode_kernel, tm_size),
        out_shape=(picked,) + (block,) * tm_size,
        in_specs=[HBM] * 3,
        out_specs=(VMEM,) * (1 + tm_size),
        scratch_shapes=[
            pltpu.VMEM((channels, width), jnp.float32),
            pltpu.VMEM((channels, width), jnp.bfloat16),
            pltpu.VMEM((1, channels), jnp.int32),
            pltpu.SMEM(sources.shape, jnp.int32),
            pltpu.SemaphoreType.DMA((3,)),
        ],
        compiler_params=pltpu.CompilerParams(vmem_limit_bytes=60 * MEBI),
        name="encode_and_pick",
    )(spectra, valid, sources)


def whiten_blocks(blocks):
    segments, (keep, width) = len(blocks), blocks[0].shape
    count, nbins = segments * keep, width // 2
    padded = pltpu.VMEM((count, nbins + 2 * LANES), jnp.bfloat16)
    part = jax.ShapeDtypeStruct((count, nbins), jnp.float32)
    return pl.pallas_call(
        functools.partial(whiten_kernel, segments),
        out_shape=(part, part, part, jax.ShapeDtypeStruct((count, LANES), jnp.float32)),
        in_specs=[VMEM] * segments,
        out_specs=(VMEM,) * 4,
        scratch_shapes=[padded, padded],
        compiler_params=pltpu.CompilerParams(vmem_limit_bytes=24 * MEBI),
        cost_estimate=pl.CostEstimate(
            flops=count * width * 1024, bytes_accessed=count * width * 4, transcendentals=0
        ),
        name="whiten_receivers",
    )(*blocks)


def stack_all(slabs, receivers, table):
    segments, parts, nsrc, share = slabs.shape
    nbins = parts * share // 2
    keep = receivers[0].shape[0] // segments
    count, rows = segments * nsrc, nsrc * keep
    padded = pltpu.VMEM((count, nbins + 2 * LANES), jnp.bfloat16)
    part = pltpu.VMEM((count, nbins), jnp.float32)
    cross = pltpu.VMEM((rows, 2 * BLOCK), jnp.bfloat16 if keep % 16 == 0 else jnp.float32)
    total = pltpu.VMEM((rows, BLOCK), jnp.float32)
    return pl.pallas_call(
        functools.partial(stack_kernel, segments),
        out_shape=jax.ShapeDtypeStruct((rows, 2 * LAG + 1), jnp.float32),
        in_specs=[VMEM] * 6,
        out_specs=VMEM,
        scratch_shapes=[part, part, part, padded, padded, cross, cross, total, total],
        compiler_params=pltpu.CompilerParams(vmem_limit_bytes=40 * MEBI),
        cost_estimate=pl.CostEstimate(
            flops=4 * rows * nbins * 2 * LAG, bytes_accessed=nbins * 2048, transcendentals=0
        ),
        name="stack_sources",
    )(slabs, *receivers, table)


def swapped(value, axis, size, step):
    return lax.ppermute(value, axis, [(i, i ^ step) for i in range(size)])


def exchanged(value, axis):
    return lax.all_to_all(value, axis, 0, 0, tiled=True)


def shards(rcv_size, tm_size, spectra, valid, sources):
    channels, _, width = spectra.shape
    keep = channels // tm_size
    rounds, per_round = sources.shape
    picked, *receivers = encode(
        rcv_size, tm_size, spectra[:, 0, :], valid.reshape(1, channels), sources
    )
    receivers = receivers[:1] + [
        swapped(receivers[step], "tm", tm_size, step) for step in range(1, tm_size)
    ]
    mine = jnp.sum(exchanged(picked, "rcv"), axis=0, dtype=jnp.float32).astype(picked.dtype)
    chosen = exchanged(jnp.broadcast_to(mine[None], picked.shape), "rcv")
    chosen, receivers = lax.optimization_barrier((chosen, receivers))
    chosen = exchanged(jnp.broadcast_to(chosen[None], (tm_size,) + chosen.shape), "tm")
    if chosen.shape[-1] % LANES:
        chosen = jnp.swapaxes(chosen, 1, 2).reshape(tm_size, 1, rounds * per_round, width)
    whitened = whiten_blocks(receivers)
    stack = stack_all(chosen, whitened, jnp.asarray(lag_table(width // 2)))
    return stack.reshape(rounds, per_round, keep, 2 * LAG + 1)


def solution(mesh):
    body = functools.partial(shards, mesh.shape["rcv"], mesh.shape["tm"])
    in_specs = (P("rcv", "tm", None), P("rcv", "tm"), P())
    out_specs = P(None, None, ("rcv", "tm"), None)
    return jax.shard_map(body, mesh=mesh, in_specs=in_specs, out_specs=out_specs, check_vma=False)
```

```python
import functools
import math

import jax
import jax.numpy as jnp
import numpy as np
from jax import lax
from jax.experimental import pallas as pl
from jax.experimental.pallas import tpu as pltpu
from jax.sharding import PartitionSpec as P

NT = 4096
LAG = 150
HALF_WIN = 64
EPSILON = 1e-06

UNUSABLE = 64.0
USABLE_BELOW = 32.0

LANES = 128
BLOCK = 256
MEBI = 1 << 20
FIRST_LAG = LANES - LAG
VMEM = pl.BlockSpec(memory_space=pltpu.VMEM)
HBM = pl.BlockSpec(memory_space=pltpu.HBM)


def lag_table(nbins):
    winding = np.mod(
        np.arange(1, nbins + 1, dtype=np.int64)[:, None]
        * np.arange(FIRST_LAG, FIRST_LAG + BLOCK, dtype=np.int64)[None, :],
        NT,
    )
    theta = winding * (2.0 * math.pi / NT)
    return np.concatenate([np.cos(theta), -np.sin(theta)], axis=0).astype(jnp.bfloat16)


def iota(shape, dim):
    return lax.broadcasted_iota(jnp.int32, shape, dim)


def whitening(real, imag, high, low):
    count, nbins = real.shape
    blocks = nbins // BLOCK
    span = BLOCK + 2 * LANES
    amplitude = jnp.sqrt(real * real + imag * imag)
    rounded = amplitude.astype(jnp.bfloat16)
    edge = jnp.zeros((count, LANES), jnp.bfloat16)
    for part, value in (
        (high, rounded),
        (low, (amplitude - rounded.astype(jnp.float32)).astype(jnp.bfloat16)),
    ):
        part[:, :LANES] = edge
        part[:, LANES : LANES + nbins] = value
        part[:, LANES + nbins :] = edge
    near = jnp.abs(iota((span, BLOCK), 0) - LANES - iota((span, BLOCK), 1)) <= HALF_WIN
    band = jnp.where(near, 1.0, 0.0).astype(jnp.bfloat16)
    pieces = [
        part[:, block * BLOCK : block * BLOCK + span] for block in range(blocks) for part in (high, low)
    ]
    windows = jnp.dot(
        jnp.concatenate(pieces, axis=0), band, preferred_element_type=jnp.float32
    )
    for block in range(blocks):
        first = block * BLOCK
        at = 2 * block * count
        window = windows[at : at + count] + windows[at + count : at + 2 * count]
        index = first + iota((1, BLOCK), 1)
        counted = jnp.minimum(index, HALF_WIN) + jnp.minimum(nbins - 1 - index, HALF_WIN) + 1
        factor = 1.0 / (window / counted.astype(jnp.float32) + EPSILON)
        re = real[:, first : first + BLOCK]
        im = imag[:, first : first + BLOCK]
        usable = re < USABLE_BELOW
        re = jnp.where(usable, re * factor, 0.0).astype(jnp.bfloat16).astype(jnp.float32)
        im = jnp.where(usable, im * factor, 0.0).astype(jnp.bfloat16).astype(jnp.float32)
        yield slice(first, first + BLOCK), re, im


def usable_rows(real):
    return jnp.where(real[:, :LANES] < USABLE_BELOW, 1.0, 0.0)


def encode_kernel(
    segments, spectra_ref, valid_ref, sources_ref, own_ref, other_ref, *refs
):
    blocks, (encoded_ref, spectra, valid, sources, arrived) = refs[:segments], refs[segments:]
    copies = [
        pltpu.make_async_copy(spectra_ref, spectra, arrived.at[0]),
        pltpu.make_async_copy(sources_ref, sources, arrived.at[1]),
        pltpu.make_async_copy(valid_ref, valid, arrived.at[2]),
    ]
    for copy in copies:
        copy.start()
    channels, width = spectra_ref.shape
    nbins = width // 2
    rounds, per_round = sources.shape
    half = rounds * per_round // 2
    index = lax.axis_index("rcv")
    copies[1].wait()
    copies[2].wait()
    diagonal = iota((channels, channels), 0) == iota((channels, channels), 1)
    usable = jnp.sum(jnp.where(diagonal, valid[...], 0), axis=1, keepdims=True) != 0
    row = iota((2 * half, channels), 0)
    local = jnp.zeros((2 * half, channels), jnp.int32)
    for place in range(2 * half):
        number = (index % 2 if place < half else 1 - index % 2) * half + place % half
        here = sources[number // per_round, number % per_round] - index * channels
        local = jnp.where(row == place, here, local)
    onehot = jnp.where(local == iota((2 * half, channels), 1), 1.0, 0.0).astype(jnp.bfloat16)
    copies[0].wait()
    encoded = jnp.where(usable, spectra[...].astype(jnp.float32), UNUSABLE).astype(jnp.bfloat16)
    picked = jnp.dot(onehot, encoded, preferred_element_type=jnp.float32)
    for first, ref in ((0, own_ref), (half, other_ref)):
        rows = picked[first : first + half]
        ref[...] = jnp.concatenate([rows[:, :nbins], rows[:, nbins:]], axis=0).astype(ref.dtype)
    encoded_ref[...] = encoded.astype(encoded_ref.dtype)
    keep = channels // segments
    for step, block in enumerate(blocks):
        at = pl.multiple_of((lax.axis_index("tm") ^ step) * keep, keep)
        block[...] = encoded_ref[pl.ds(at, keep), :].astype(block.dtype)


def whiten_kernel(segments, *refs):
    blocks, (real_ref, imag_ref, valid_ref, high, low) = refs[:segments], refs[segments:]
    rows = jnp.concatenate([ref[...].astype(jnp.float32) for ref in blocks], axis=0)
    nbins = rows.shape[1] // 2
    real, imag = rows[:, :nbins], rows[:, nbins:]
    for at, re, im in whitening(real, imag, high, low):
        real_ref[:, at] = re
        imag_ref[:, at] = im
    valid_ref[...] = usable_rows(real)


def stack_kernel(
    segments, slabs_ref, rcv_re, rcv_im, rcv_valid, table_ref, *refs
):
    *rest, out_ref, src_re, src_im, high, low, cross_a, cross_b, total_re, total_im = refs[
        : 10 if len(refs) == 12 else 9
    ]
    half = slabs_ref.shape[0] // (2 * segments)
    nbins = slabs_ref.shape[1]
    keep = rcv_re.shape[0] // segments
    rows = half * keep
    if rest:
        result, written = refs[10:]
        part = lax.axis_index("rcv") % 2
        first_copy = pltpu.make_async_copy(
            rest[0], out_ref.at[pl.ds(pl.multiple_of(part * rows, rows), rows)], written.at[0]
        )
        first_copy.start()
    else:
        result = out_ref
    slabs = slabs_ref[...].astype(jnp.float32)
    real = jnp.concatenate(
        [slabs[2 * half * t : 2 * half * t + half] for t in range(segments)], axis=0
    )
    imag = jnp.concatenate(
        [slabs[2 * half * t + half : 2 * half * (t + 1)] for t in range(segments)], axis=0
    )
    for at, re, im in whitening(real, imag, high, low):
        src_re[:, at] = re
        src_im[:, at] = im
    src_valid = usable_rows(real)
    total_re[...] = jnp.zeros_like(total_re)
    total_im[...] = jnp.zeros_like(total_im)
    cross_b[...] = jnp.zeros_like(cross_b)

    def multiply(block, cross):
        for sub in range(BLOCK // LANES):
            at = pl.ds(pl.multiple_of(block * BLOCK + sub * LANES, LANES), LANES)
            r_re = [rcv_re[t * keep : (t + 1) * keep, at] for t in range(segments)]
            r_im = [rcv_im[t * keep : (t + 1) * keep, at] for t in range(segments)]
            for source in range(half):
                real, imag = 0.0, 0.0
                for t in range(segments):
                    row = slice(t * half + source, t * half + source + 1)
                    s_re, s_im = src_re[row, at], src_im[row, at]
                    real = real + s_re * r_re[t] + s_im * r_im[t]
                    imag = imag + s_im * r_re[t] - s_re * r_im[t]
                to = slice(source * keep, (source + 1) * keep)
                cross[to, sub * LANES : (sub + 1) * LANES] = real.astype(cross.dtype)
                cross[to, BLOCK + sub * LANES : BLOCK + (sub + 1) * LANES] = imag.astype(
                    cross.dtype
                )

    def project(block, cross):
        value = cross[...].astype(jnp.bfloat16)
        re_at = pl.ds(pl.multiple_of(block * BLOCK, BLOCK), BLOCK)
        im_at = pl.ds(pl.multiple_of(nbins + block * BLOCK, BLOCK), BLOCK)
        total_re[...] += jnp.dot(
            value[:, :BLOCK], table_ref[re_at, :], preferred_element_type=jnp.float32
        )
        total_im[...] += jnp.dot(
            value[:, BLOCK:], table_ref[im_at, :], preferred_element_type=jnp.float32
        )

    def two_blocks(pair, carry):
        multiply(2 * pair, cross_a)
        project(jnp.maximum(2 * pair - 1, 0), cross_b)
        multiply(2 * pair + 1, cross_b)
        project(2 * pair, cross_a)
        return carry

    pairs = nbins // (2 * BLOCK)
    lax.fori_loop(0, pairs, two_blocks, 0)
    project(2 * pairs - 1, cross_b)

    lags = result.shape[1]
    scale = 2.0 / math.sqrt(nbins)
    mirror = LAG - FIRST_LAG - iota((keep, LANES), 1)
    for source in range(half):
        common = 0.0
        for t in range(segments):
            row = t * half + source
            common = common + src_valid[row : row + 1] * rcv_valid[t * keep : (t + 1) * keep, :]
        weight = scale / jnp.maximum(common, 1.0)
        to = slice(source * keep, (source + 1) * keep)
        even, odd = total_re[to], total_im[to]
        ahead = even + odd
        behind = even - odd
        low_part = jnp.take_along_axis(
            behind[:, :LANES], jnp.clip(mirror, 0, LANES - 1), axis=1
        )
        high_part = jnp.take_along_axis(
            behind[:, LANES:], jnp.clip(mirror - LANES, 0, LANES - 1), axis=1
        )
        result[to, :LANES] = jnp.where(mirror < LANES, low_part, high_part) * weight
        for first in range(0, lags - LANES, LANES):
            last = min(first + LANES, lags - LANES)
            value = ahead[:, first : first + LANES] * weight
            result[to, LANES + first : LANES + last] = value[:, : last - first]
    if rest:
        second_copy = pltpu.make_async_copy(
            result,
            out_ref.at[pl.ds(pl.multiple_of((1 - part) * rows, rows), rows)],
            written.at[1],
        )
        second_copy.start()
        first_copy.wait()
        second_copy.wait()


def encode(segments, spectra, valid, sources):
    channels, width = spectra.shape
    keep = channels // segments
    slab = jax.ShapeDtypeStruct((sources.size, width // 2), jnp.bfloat16)
    block = jax.ShapeDtypeStruct((keep, width), jnp.bfloat16)
    pinned = [pltpu.with_memory_space_constraint(x, pltpu.HBM) for x in (spectra, valid, sources)]
    return pl.pallas_call(
        functools.partial(encode_kernel, segments),
        out_shape=(slab, slab) + (block,) * segments,
        in_specs=[HBM] * 3,
        out_specs=(VMEM,) * (2 + segments),
        scratch_shapes=[
            pltpu.VMEM((channels, width), jnp.bfloat16 if keep % 16 == 0 else jnp.float32),
            pltpu.VMEM((channels, width), jnp.bfloat16),
            pltpu.VMEM((1, channels), jnp.int32),
            pltpu.SMEM(sources.shape, jnp.int32),
            pltpu.SemaphoreType.DMA((3,)),
        ],
        compiler_params=pltpu.CompilerParams(vmem_limit_bytes=12 * MEBI),
        name="encode_and_pick",
    )(*pinned)


def whiten_blocks(blocks):
    segments, (keep, width) = len(blocks), blocks[0].shape
    count, nbins = segments * keep, width // 2
    padded = pltpu.VMEM((count, nbins + 2 * LANES), jnp.bfloat16)
    part = jax.ShapeDtypeStruct((count, nbins), jnp.float32)
    return pl.pallas_call(
        functools.partial(whiten_kernel, segments),
        out_shape=(part, part, jax.ShapeDtypeStruct((count, LANES), jnp.float32)),
        in_specs=[VMEM] * segments,
        out_specs=(VMEM,) * 3,
        scratch_shapes=[padded, padded],
        compiler_params=pltpu.CompilerParams(vmem_limit_bytes=20 * MEBI),
        cost_estimate=pl.CostEstimate(
            flops=count * width * 1024, bytes_accessed=count * width * 4, transcendentals=0
        ),
        name="whiten_receivers",
    )(*blocks)


def stack_half(segments, slabs, receivers, table, rest=()):
    half, nbins = slabs.shape[0] // (2 * segments), slabs.shape[1]
    keep = receivers[0].shape[0] // segments
    count, rows, lags = segments * half, half * keep, 2 * LAG + 1
    padded = pltpu.VMEM((count, nbins + 2 * LANES), jnp.bfloat16)
    part = pltpu.VMEM((count, nbins), jnp.float32)
    cross = pltpu.VMEM((rows, 2 * BLOCK), jnp.bfloat16 if keep % 16 == 0 else jnp.float32)
    total = pltpu.VMEM((rows, BLOCK), jnp.float32)
    scratch = [part, part, padded, padded, cross, cross, total, total]
    if rest:
        scratch += [pltpu.VMEM((rows, lags), jnp.float32), pltpu.SemaphoreType.DMA((2,))]
    return pl.pallas_call(
        functools.partial(stack_kernel, segments),
        out_shape=jax.ShapeDtypeStruct((2 * rows if rest else rows, lags), jnp.float32),
        in_specs=[VMEM] * (5 + len(rest)),
        out_specs=HBM if rest else VMEM,
        scratch_shapes=scratch,
        compiler_params=pltpu.CompilerParams(vmem_limit_bytes=20 * MEBI),
        cost_estimate=pl.CostEstimate(
            flops=4 * rows * nbins * 2 * LAG, bytes_accessed=nbins * 2048, transcendentals=0
        ),
        name="stack_other_half" if rest else "stack_own_half",
    )(slabs, *receivers, table, *rest)


def swapped(value, axis, size, step):
    return lax.ppermute(value, axis, [(i, i ^ step) for i in range(size)])


def shards(rcv_size, tm_size, spectra, valid, sources):
    channels, _, width = spectra.shape
    keep = channels // tm_size
    rounds, per_round = sources.shape
    own, other, *receivers = encode(
        tm_size, spectra[:, 0, :], valid.reshape(1, channels), sources
    )
    own = own + swapped(other, "rcv", rcv_size, 1)
    receivers = receivers[:1] + [
        swapped(receivers[step], "tm", tm_size, step) for step in range(1, tm_size)
    ]
    step = 2
    while step < rcv_size:
        own = own + swapped(own, "rcv", rcv_size, step)
        step *= 2
    own, receivers = lax.optimization_barrier((own, receivers))
    own = [own] + [swapped(own, "tm", tm_size, step) for step in range(1, tm_size)]
    whitened = whiten_blocks(receivers)
    own, whitened = lax.optimization_barrier((own, whitened))
    own = jnp.concatenate(own, axis=0)
    other = swapped(own, "rcv", rcv_size, 1)

    table = jnp.asarray(lag_table(width // 2))
    first = stack_half(tm_size, own, whitened, table)
    stack = stack_half(tm_size, other, whitened, table, (first,))
    return stack.reshape(rounds, per_round, keep, 2 * LAG + 1)


def solution(mesh):
    body = functools.partial(shards, mesh.shape["rcv"], mesh.shape["tm"])
    in_specs = (P("rcv", "tm", None), P("rcv", "tm"), P())
    out_specs = P(None, None, ("rcv", "tm"), None)
    return jax.shard_map(body, mesh=mesh, in_specs=in_specs, out_specs=out_specs, check_vma=False)
```

```python
import functools
import math

import jax
import jax.numpy as jnp
import numpy as np
from jax import lax
from jax.experimental import pallas as pl
from jax.experimental.pallas import tpu as pltpu
from jax.sharding import PartitionSpec as P

NT = 4096
LAG = 150
HALF_WIN = 64
EPSILON = 1e-06

UNUSABLE = 1024.0
USABLE_BELOW = 512.0

LANES = 128
BLOCK = 256
MEBI = 1 << 20
FIRST_LAG = LANES - LAG
VMEM = pl.BlockSpec(memory_space=pltpu.VMEM)
HBM = pl.BlockSpec(memory_space=pltpu.HBM)


def lag_table(nbins):
    winding = np.mod(
        np.arange(1, nbins + 1, dtype=np.int64)[:, None]
        * np.arange(FIRST_LAG, FIRST_LAG + BLOCK, dtype=np.int64)[None, :],
        NT,
    )
    theta = winding * (2.0 * math.pi / NT)
    return np.concatenate([np.cos(theta), -np.sin(theta)], axis=0).astype(jnp.bfloat16)


def iota(shape, dim):
    return lax.broadcasted_iota(jnp.int32, shape, dim)


def whitening(real, imag, high, low, unusable=0.0):
    count, nbins = real.shape
    blocks = nbins // BLOCK
    span = BLOCK + 2 * LANES
    amplitude = jnp.sqrt(real * real + imag * imag)
    rounded = amplitude.astype(jnp.bfloat16)
    edge = jnp.zeros((count, LANES), jnp.bfloat16)
    for part, value in (
        (high, rounded),
        (low, (amplitude - rounded.astype(jnp.float32)).astype(jnp.bfloat16)),
    ):
        part[:, :LANES] = edge
        part[:, LANES : LANES + nbins] = value
        part[:, LANES + nbins :] = edge
    near = jnp.abs(iota((span, BLOCK), 0) - LANES - iota((span, BLOCK), 1)) <= HALF_WIN
    band = jnp.where(near, 1.0, 0.0).astype(jnp.bfloat16)
    pieces = [
        part[:, block * BLOCK : block * BLOCK + span] for block in range(blocks) for part in (high, low)
    ]
    windows = jnp.dot(
        jnp.concatenate(pieces, axis=0), band, preferred_element_type=jnp.float32
    )
    for block in range(blocks):
        first = block * BLOCK
        at = 2 * block * count
        window = windows[at : at + count] + windows[at + count : at + 2 * count]
        index = first + iota((1, BLOCK), 1)
        counted = jnp.minimum(index, HALF_WIN) + jnp.minimum(nbins - 1 - index, HALF_WIN) + 1
        factor = 1.0 / (window / counted.astype(jnp.float32) + EPSILON)
        re = real[:, first : first + BLOCK]
        im = imag[:, first : first + BLOCK]
        usable = re < USABLE_BELOW
        re = jnp.where(usable, re * factor, unusable).astype(jnp.bfloat16).astype(jnp.float32)
        im = jnp.where(usable, im * factor, unusable).astype(jnp.bfloat16).astype(jnp.float32)
        yield slice(first, first + BLOCK), re, im


def usable_rows(real):
    return jnp.where(real[:, :LANES] < USABLE_BELOW, 1.0, 0.0)


def encode_kernel(
    segments, spectra_ref, valid_ref, sources_ref, own_ref, other_ref, *refs
):
    blocks, refs = refs[:segments], refs[segments:]
    encoded_ref, spectra, valid, sources, high, low, arrived = refs
    copies = [
        pltpu.make_async_copy(spectra_ref, spectra, arrived.at[0]),
        pltpu.make_async_copy(sources_ref, sources, arrived.at[1]),
        pltpu.make_async_copy(valid_ref, valid, arrived.at[2]),
    ]
    for copy in copies:
        copy.start()
    channels, width = spectra_ref.shape
    nbins = width // 2
    rounds, per_round = sources.shape
    half = rounds * per_round // 2
    index = lax.axis_index("rcv")
    copies[1].wait()
    copies[2].wait()
    diagonal = iota((channels, channels), 0) == iota((channels, channels), 1)
    usable = jnp.sum(jnp.where(diagonal, valid[...], 0), axis=1, keepdims=True) != 0
    row = iota((2 * half, channels), 0)
    local = jnp.zeros((2 * half, channels), jnp.int32)
    for place in range(2 * half):
        number = (index % 2 if place < half else 1 - index % 2) * half + place % half
        here = sources[number // per_round, number % per_round] - index * channels
        local = jnp.where(row == place, here, local)
    onehot = jnp.where(local == iota((2 * half, channels), 1), 1.0, 0.0).astype(jnp.bfloat16)
    copies[0].wait()
    encoded = jnp.where(usable, spectra[...].astype(jnp.float32), UNUSABLE).astype(jnp.bfloat16)
    picked = jnp.dot(onehot, encoded, preferred_element_type=jnp.float32)
    for at, re, im in whitening(picked[:, :nbins], picked[:, nbins:], high, low, UNUSABLE):
        for first, ref in ((0, own_ref), (half, other_ref)):
            rows = slice(first, first + half)
            ref[:, at] = jnp.concatenate([re[rows], im[rows]], axis=0).astype(ref.dtype)
    encoded_ref[...] = encoded.astype(encoded_ref.dtype)
    keep = channels // segments
    for step, block in enumerate(blocks):
        at = pl.multiple_of((lax.axis_index("tm") ^ step) * keep, keep)
        block[...] = encoded_ref[pl.ds(at, keep), :].astype(block.dtype)


def whiten_kernel(segments, *refs):
    blocks, (real_ref, imag_ref, valid_ref, high, low) = refs[:segments], refs[segments:]
    rows = jnp.concatenate([ref[...].astype(jnp.float32) for ref in blocks], axis=0)
    nbins = rows.shape[1] // 2
    real, imag = rows[:, :nbins], rows[:, nbins:]
    for at, re, im in whitening(real, imag, high, low):
        real_ref[:, at] = re
        imag_ref[:, at] = im
    valid_ref[...] = usable_rows(real)


def stack_kernel(
    segments, slabs_ref, rcv_re, rcv_im, rcv_valid, table_ref, *refs
):
    *rest, out_ref, src_re, src_im, cross_a, cross_b, total_re, total_im = refs[
        : 8 if len(refs) == 10 else 7
    ]
    half = slabs_ref.shape[0] // (2 * segments)
    nbins = slabs_ref.shape[1]
    keep = rcv_re.shape[0] // segments
    rows = half * keep
    if rest:
        result, written = refs[8:]
        part = lax.axis_index("rcv") % 2
        pieces = max(1, half // 4)
        at = pl.multiple_of(part * rows, rows)
        copies = [
            pltpu.make_async_copy(rest[0], out_ref.at[pl.ds(at, rows)], written.at[0])
        ]
        copies[0].start()
    else:
        result = out_ref
    slabs = slabs_ref[...].astype(jnp.float32)
    real = jnp.concatenate(
        [slabs[2 * half * t : 2 * half * t + half] for t in range(segments)], axis=0
    )
    imag = jnp.concatenate(
        [slabs[2 * half * t + half : 2 * half * (t + 1)] for t in range(segments)], axis=0
    )
    usable = real < USABLE_BELOW
    src_re[...] = jnp.where(usable, real, 0.0)
    src_im[...] = jnp.where(usable, imag, 0.0)
    src_valid = usable_rows(real)
    total_re[...] = jnp.zeros_like(total_re)
    total_im[...] = jnp.zeros_like(total_im)
    cross_b[...] = jnp.zeros_like(cross_b)

    def multiply(block, cross):
        for sub in range(BLOCK // LANES):
            at = pl.ds(pl.multiple_of(block * BLOCK + sub * LANES, LANES), LANES)
            r_re = [rcv_re[t * keep : (t + 1) * keep, at] for t in range(segments)]
            r_im = [rcv_im[t * keep : (t + 1) * keep, at] for t in range(segments)]
            for source in range(half):
                real, imag = [], []
                for t in range(segments):
                    row = slice(t * half + source, t * half + source + 1)
                    s_re, s_im = src_re[row, at], src_im[row, at]
                    real.append(s_re * r_re[t] + s_im * r_im[t])
                    imag.append(s_im * r_re[t] - s_re * r_im[t])
                real, imag = functools.reduce(jnp.add, real), functools.reduce(jnp.add, imag)
                to = slice(source * keep, (source + 1) * keep)
                cross[to, sub * LANES : (sub + 1) * LANES] = real.astype(cross.dtype)
                cross[to, BLOCK + sub * LANES : BLOCK + (sub + 1) * LANES] = imag.astype(
                    cross.dtype
                )

    def project(block, cross):
        value = cross[...].astype(jnp.bfloat16)
        re_at = pl.ds(pl.multiple_of(block * BLOCK, BLOCK), BLOCK)
        im_at = pl.ds(pl.multiple_of(nbins + block * BLOCK, BLOCK), BLOCK)
        total_re[...] += jnp.dot(
            value[:, :BLOCK], table_ref[re_at, :], preferred_element_type=jnp.float32
        )
        total_im[...] += jnp.dot(
            value[:, BLOCK:], table_ref[im_at, :], preferred_element_type=jnp.float32
        )

    def two_blocks(pair, carry):
        multiply(2 * pair, cross_a)
        project(jnp.maximum(2 * pair - 1, 0), cross_b)
        multiply(2 * pair + 1, cross_b)
        project(2 * pair, cross_a)
        return carry

    pairs = nbins // (2 * BLOCK)
    lax.fori_loop(0, pairs, two_blocks, 0)
    project(2 * pairs - 1, cross_b)

    lags = result.shape[1]
    scale = 2.0 / math.sqrt(nbins)
    mirror = LAG - FIRST_LAG - iota((keep, LANES), 1)
    for source in range(half):
        common = 0.0
        for t in range(segments):
            row = t * half + source
            common = common + src_valid[row : row + 1] * rcv_valid[t * keep : (t + 1) * keep, :]
        weight = scale / jnp.maximum(common, 1.0)
        to = slice(source * keep, (source + 1) * keep)
        even, odd = total_re[to], total_im[to]
        ahead = even + odd
        behind = even - odd
        low_part = jnp.take_along_axis(
            behind[:, :LANES], jnp.clip(mirror, 0, LANES - 1), axis=1
        )
        high_part = jnp.take_along_axis(
            behind[:, LANES:], jnp.clip(mirror - LANES, 0, LANES - 1), axis=1
        )
        result[to, :LANES] = jnp.where(mirror < LANES, low_part, high_part) * weight
        for first in range(0, lags - LANES, LANES):
            last = min(first + LANES, lags - LANES)
            value = ahead[:, first : first + LANES] * weight
            result[to, LANES + first : LANES + last] = value[:, : last - first]
        if rest and (source + 1) % pieces == 0:
            first, count = (source + 1 - pieces) * keep, pieces * keep
            at = pl.multiple_of((1 - part) * rows + first, count)
            copies.append(
                pltpu.make_async_copy(
                    result.at[pl.ds(first, count)],
                    out_ref.at[pl.ds(at, count)],
                    written.at[1 + source // pieces],
                )
            )
            copies[-1].start()
    if rest:
        for copy in copies:
            copy.wait()


def encode(segments, spectra, valid, sources):
    channels, width = spectra.shape
    keep = channels // segments
    slab = jax.ShapeDtypeStruct((sources.size, width // 2), jnp.bfloat16)
    block = jax.ShapeDtypeStruct((keep, width), jnp.bfloat16)
    padded = pltpu.VMEM((sources.size, width // 2 + 2 * LANES), jnp.bfloat16)
    pinned = [pltpu.with_memory_space_constraint(x, pltpu.HBM) for x in (spectra, valid, sources)]
    return pl.pallas_call(
        functools.partial(encode_kernel, segments),
        out_shape=(slab, slab) + (block,) * segments,
        in_specs=[HBM] * 3,
        out_specs=(VMEM,) * (2 + segments),
        scratch_shapes=[
            pltpu.VMEM((channels, width), jnp.bfloat16 if keep % 16 == 0 else jnp.float32),
            pltpu.VMEM((channels, width), jnp.bfloat16),
            pltpu.VMEM((1, channels), jnp.int32),
            pltpu.SMEM(sources.shape, jnp.int32),
            padded,
            padded,
            pltpu.SemaphoreType.DMA((3,)),
        ],
        compiler_params=pltpu.CompilerParams(vmem_limit_bytes=12 * MEBI),
        name="encode_and_pick",
    )(*pinned)


def whiten_blocks(blocks):
    segments, (keep, width) = len(blocks), blocks[0].shape
    count, nbins = segments * keep, width // 2
    padded = pltpu.VMEM((count, nbins + 2 * LANES), jnp.bfloat16)
    part = jax.ShapeDtypeStruct((count, nbins), jnp.float32)
    return pl.pallas_call(
        functools.partial(whiten_kernel, segments),
        out_shape=(part, part, jax.ShapeDtypeStruct((count, LANES), jnp.float32)),
        in_specs=[VMEM] * segments,
        out_specs=(VMEM,) * 3,
        scratch_shapes=[padded, padded],
        compiler_params=pltpu.CompilerParams(vmem_limit_bytes=20 * MEBI),
        cost_estimate=pl.CostEstimate(
            flops=count * width * 1024, bytes_accessed=count * width * 4, transcendentals=0
        ),
        name="whiten_receivers",
    )(*blocks)


def stack_half(segments, slabs, receivers, table, rest=()):
    half, nbins = slabs.shape[0] // (2 * segments), slabs.shape[1]
    keep = receivers[0].shape[0] // segments
    count, rows, lags = segments * half, half * keep, 2 * LAG + 1
    part = pltpu.VMEM((count, nbins), jnp.float32)
    cross = pltpu.VMEM((rows, 2 * BLOCK), jnp.bfloat16 if keep % 16 == 0 else jnp.float32)
    total = pltpu.VMEM((rows, BLOCK), jnp.float32)
    scratch = [part, part, cross, cross, total, total]
    if rest:
        scratch += [pltpu.VMEM((rows, lags), jnp.float32), pltpu.SemaphoreType.DMA((1 + half,))]
    return pl.pallas_call(
        functools.partial(stack_kernel, segments),
        out_shape=jax.ShapeDtypeStruct((2 * rows if rest else rows, lags), jnp.float32),
        in_specs=[VMEM] * (5 + len(rest)),
        out_specs=HBM if rest else VMEM,
        scratch_shapes=scratch,
        compiler_params=pltpu.CompilerParams(vmem_limit_bytes=20 * MEBI),
        cost_estimate=pl.CostEstimate(
            flops=4 * rows * nbins * 2 * LAG, bytes_accessed=nbins * 2048, transcendentals=0
        ),
        name="stack_other_half" if rest else "stack_own_half",
    )(slabs, *receivers, table, *rest)


def swapped(value, axis, size, step):
    return lax.ppermute(value, axis, [(i, i ^ step) for i in range(size)])


def shards(rcv_size, tm_size, spectra, valid, sources):
    channels, _, width = spectra.shape
    keep = channels // tm_size
    rounds, per_round = sources.shape
    own, other, *receivers = encode(
        tm_size, spectra[:, 0, :], valid.reshape(1, channels), sources
    )
    moving, step, place = other, 1, tm_size - 1
    while step < rcv_size:
        now = 1 if 2 * step < rcv_size else place
        for place in range(place, place - now, -1):
            receivers[place] = swapped(receivers[place], "tm", tm_size, place)
        place -= 1
        own = own + swapped(moving, "rcv", rcv_size, step)
        own, receivers[1 : place + 1] = lax.optimization_barrier((own, receivers[1 : place + 1]))
        moving, step = own, 2 * step
    own = [own] + [swapped(own, "tm", tm_size, step) for step in range(tm_size - 1, 1, -1)] + [own]
    own[-1], receivers = lax.optimization_barrier((own[-1], receivers))
    own = own[:1] + [swapped(own[-1], "tm", tm_size, 1)] + own[-2:0:-1]
    whitened = whiten_blocks(receivers)
    own, whitened = lax.optimization_barrier((own, whitened))
    own = jnp.concatenate(own, axis=0)
    other = swapped(own, "rcv", rcv_size, 1)

    table = jnp.asarray(lag_table(width // 2))
    first = stack_half(tm_size, own, whitened, table)
    stack = stack_half(tm_size, other, whitened, table, (first,))
    return stack.reshape(rounds, per_round, keep, 2 * LAG + 1)


def solution(mesh):
    body = functools.partial(shards, mesh.shape["rcv"], mesh.shape["tm"])
    in_specs = (P("rcv", "tm", None), P("rcv", "tm"), P())
    out_specs = P(None, None, ("rcv", "tm"), None)
    return jax.shard_map(body, mesh=mesh, in_specs=in_specs, out_specs=out_specs, check_vma=False)
```

```python
import functools
import math

import jax
import jax.numpy as jnp
import numpy as np
from jax import lax
from jax.experimental import pallas as pl
from jax.experimental.pallas import tpu as pltpu
from jax.sharding import PartitionSpec as P

NT = 4096
LAG = 150
HALF_WIN = 64
EPSILON = 1e-06

UNUSABLE = 1024.0
USABLE_BELOW = 512.0

LANES = 128
BLOCK = 256
MEBI = 1 << 20
FIRST_LAG = LANES - LAG
VMEM = pl.BlockSpec(memory_space=pltpu.VMEM)
HBM = pl.BlockSpec(memory_space=pltpu.HBM)


def lag_table(nbins):
    winding = np.mod(
        np.arange(1, nbins + 1, dtype=np.int64)[:, None]
        * np.arange(FIRST_LAG, FIRST_LAG + BLOCK, dtype=np.int64)[None, :],
        NT,
    )
    theta = winding * (2.0 * math.pi / NT)
    return np.concatenate([np.cos(theta), -np.sin(theta)], axis=0).astype(jnp.bfloat16)


def iota(shape, dim):
    return lax.broadcasted_iota(jnp.int32, shape, dim)


def whitening(real, imag, high, low, unusable=0.0):
    count, nbins = real.shape
    blocks = nbins // BLOCK
    span = BLOCK + 2 * LANES
    amplitude = jnp.sqrt(real * real + imag * imag)
    rounded = amplitude.astype(jnp.bfloat16)
    edge = jnp.zeros((count, LANES), jnp.bfloat16)
    for part, value in (
        (high, rounded),
        (low, (amplitude - rounded.astype(jnp.float32)).astype(jnp.bfloat16)),
    ):
        part[:, :LANES] = edge
        part[:, LANES : LANES + nbins] = value
        part[:, LANES + nbins :] = edge
    near = jnp.abs(iota((span, BLOCK), 0) - LANES - iota((span, BLOCK), 1)) <= HALF_WIN
    band = jnp.where(near, 1.0, 0.0).astype(jnp.bfloat16)
    pieces = [
        part[:, block * BLOCK : block * BLOCK + span] for block in range(blocks) for part in (high, low)
    ]
    windows = jnp.dot(
        jnp.concatenate(pieces, axis=0), band, preferred_element_type=jnp.float32
    )
    for block in range(blocks):
        first = block * BLOCK
        at = 2 * block * count
        window = windows[at : at + count] + windows[at + count : at + 2 * count]
        index = first + iota((1, BLOCK), 1)
        counted = jnp.minimum(index, HALF_WIN) + jnp.minimum(nbins - 1 - index, HALF_WIN) + 1
        factor = 1.0 / (window / counted.astype(jnp.float32) + EPSILON)
        re = real[:, first : first + BLOCK]
        im = imag[:, first : first + BLOCK]
        usable = re < USABLE_BELOW
        re = jnp.where(usable, re * factor, unusable).astype(jnp.bfloat16).astype(jnp.float32)
        im = jnp.where(usable, im * factor, unusable).astype(jnp.bfloat16).astype(jnp.float32)
        yield slice(first, first + BLOCK), re, im


def usable_rows(real):
    return jnp.where(real[:, :LANES] < USABLE_BELOW, 1.0, 0.0)


def encode_kernel(
    segments, spectra_ref, valid_ref, sources_ref, own_ref, other_ref, *refs
):
    blocks, refs = refs[:segments], refs[segments:]
    encoded_ref, spectra, valid, sources, high, low, arrived = refs
    copies = [
        pltpu.make_async_copy(spectra_ref, spectra, arrived.at[0]),
        pltpu.make_async_copy(sources_ref, sources, arrived.at[1]),
        pltpu.make_async_copy(valid_ref, valid, arrived.at[2]),
    ]
    for copy in copies:
        copy.start()
    channels, width = spectra_ref.shape
    nbins = width // 2
    rounds, per_round = sources.shape
    half = rounds * per_round // 2
    index = lax.axis_index("rcv")
    copies[1].wait()
    copies[2].wait()
    diagonal = iota((channels, channels), 0) == iota((channels, channels), 1)
    usable = jnp.sum(jnp.where(diagonal, valid[...], 0), axis=1, keepdims=True) != 0
    row = iota((2 * half, channels), 0)
    local = jnp.zeros((2 * half, channels), jnp.int32)
    for place in range(2 * half):
        number = (index % 2 if place < half else 1 - index % 2) * half + place % half
        here = sources[number // per_round, number % per_round] - index * channels
        local = jnp.where(row == place, here, local)
    onehot = jnp.where(local == iota((2 * half, channels), 1), 1.0, 0.0).astype(jnp.bfloat16)
    copies[0].wait()
    encoded = jnp.where(usable, spectra[...].astype(jnp.float32), UNUSABLE).astype(jnp.bfloat16)
    picked = jnp.dot(onehot, encoded, preferred_element_type=jnp.float32)
    for at, re, im in whitening(picked[:, :nbins], picked[:, nbins:], high, low, UNUSABLE):
        for first, ref in ((0, own_ref), (half, other_ref)):
            rows = slice(first, first + half)
            ref[:, at] = jnp.concatenate([re[rows], im[rows]], axis=0).astype(ref.dtype)
    encoded_ref[...] = encoded.astype(encoded_ref.dtype)
    keep = channels // segments
    for step, block in enumerate(blocks):
        at = pl.multiple_of((lax.axis_index("tm") ^ step) * keep, keep)
        block[...] = encoded_ref[pl.ds(at, keep), :].astype(block.dtype)


def whiten_kernel(segments, *refs):
    blocks, (real_ref, imag_ref, valid_ref, high, low) = refs[:segments], refs[segments:]
    rows = jnp.concatenate([ref[...].astype(jnp.float32) for ref in blocks], axis=0)
    nbins = rows.shape[1] // 2
    real, imag = rows[:, :nbins], rows[:, nbins:]
    for at, re, im in whitening(real, imag, high, low):
        real_ref[:, at] = re
        imag_ref[:, at] = im
    valid_ref[...] = usable_rows(real)


def stack_kernel(
    segments, slabs_ref, rcv_re, rcv_im, rcv_valid, table_ref, *refs
):
    *rest, out_ref, src_re, src_im, cross_a, cross_b, total_re, total_im = refs[
        : 8 if len(refs) == 10 else 7
    ]
    half = slabs_ref.shape[0] // (2 * segments)
    nbins = slabs_ref.shape[1]
    keep = rcv_re.shape[0] // segments
    rows = half * keep
    if rest:
        result, written = refs[8:]
        part = lax.axis_index("rcv") % 2
        pieces = max(1, half // 4)
        at = pl.multiple_of(part * rows, rows)
        copies = [
            pltpu.make_async_copy(rest[0], out_ref.at[pl.ds(at, rows)], written.at[0])
        ]
        copies[0].start()
    else:
        result = out_ref
    slabs = slabs_ref[...].astype(jnp.float32)
    real = jnp.concatenate(
        [slabs[2 * half * t : 2 * half * t + half] for t in range(segments)], axis=0
    )
    imag = jnp.concatenate(
        [slabs[2 * half * t + half : 2 * half * (t + 1)] for t in range(segments)], axis=0
    )
    usable = real < USABLE_BELOW
    src_re[...] = jnp.where(usable, real, 0.0)
    src_im[...] = jnp.where(usable, imag, 0.0)
    src_valid = usable_rows(real)
    total_re[...] = jnp.zeros_like(total_re)
    total_im[...] = jnp.zeros_like(total_im)
    cross_b[...] = jnp.zeros_like(cross_b)

    def multiply(block, cross):
        for sub in range(BLOCK // LANES):
            at = pl.ds(pl.multiple_of(block * BLOCK + sub * LANES, LANES), LANES)
            r_re = [rcv_re[t * keep : (t + 1) * keep, at] for t in range(segments)]
            r_im = [rcv_im[t * keep : (t + 1) * keep, at] for t in range(segments)]
            for source in range(half):
                real, imag = [], []
                for t in range(segments):
                    row = slice(t * half + source, t * half + source + 1)
                    s_re, s_im = src_re[row, at], src_im[row, at]
                    real.append(s_re * r_re[t] + s_im * r_im[t])
                    imag.append(s_im * r_re[t] - s_re * r_im[t])
                real, imag = functools.reduce(jnp.add, real), functools.reduce(jnp.add, imag)
                to = slice(source * keep, (source + 1) * keep)
                cross[to, sub * LANES : (sub + 1) * LANES] = real.astype(cross.dtype)
                cross[to, BLOCK + sub * LANES : BLOCK + (sub + 1) * LANES] = imag.astype(
                    cross.dtype
                )

    def project(block, cross):
        value = cross[...].astype(jnp.bfloat16)
        re_at = pl.ds(pl.multiple_of(block * BLOCK, BLOCK), BLOCK)
        im_at = pl.ds(pl.multiple_of(nbins + block * BLOCK, BLOCK), BLOCK)
        total_re[...] += jnp.dot(
            value[:, :BLOCK], table_ref[re_at, :], preferred_element_type=jnp.float32
        )
        total_im[...] += jnp.dot(
            value[:, BLOCK:], table_ref[im_at, :], preferred_element_type=jnp.float32
        )

    def two_blocks(pair, carry):
        multiply(2 * pair, cross_a)
        project(jnp.maximum(2 * pair - 1, 0), cross_b)
        multiply(2 * pair + 1, cross_b)
        project(2 * pair, cross_a)
        return carry

    pairs = nbins // (2 * BLOCK)
    lax.fori_loop(0, pairs, two_blocks, 0)
    project(2 * pairs - 1, cross_b)

    lags = result.shape[1]
    scale = 2.0 / math.sqrt(nbins)
    mirror = LAG - FIRST_LAG - iota((keep, LANES), 1)
    for source in range(half):
        common = 0.0
        for t in range(segments):
            row = t * half + source
            common = common + src_valid[row : row + 1] * rcv_valid[t * keep : (t + 1) * keep, :]
        weight = scale / jnp.maximum(common, 1.0)
        to = slice(source * keep, (source + 1) * keep)
        even, odd = total_re[to], total_im[to]
        ahead = even + odd
        behind = even - odd
        low_part = jnp.take_along_axis(
            behind[:, :LANES], jnp.clip(mirror, 0, LANES - 1), axis=1
        )
        high_part = jnp.take_along_axis(
            behind[:, LANES:], jnp.clip(mirror - LANES, 0, LANES - 1), axis=1
        )
        result[to, :LANES] = jnp.where(mirror < LANES, low_part, high_part) * weight
        for first in range(0, lags - LANES, LANES):
            last = min(first + LANES, lags - LANES)
            value = ahead[:, first : first + LANES] * weight
            result[to, LANES + first : LANES + last] = value[:, : last - first]
        if rest and (source + 1) % pieces == 0:
            first, count = (source + 1 - pieces) * keep, pieces * keep
            at = pl.multiple_of((1 - part) * rows + first, count)
            copies.append(
                pltpu.make_async_copy(
                    result.at[pl.ds(first, count)],
                    out_ref.at[pl.ds(at, count)],
                    written.at[1 + source // pieces],
                )
            )
            copies[-1].start()
    if rest:
        for copy in copies:
            copy.wait()


def encode(segments, spectra, valid, sources):
    channels, width = spectra.shape
    keep = channels // segments
    slab = jax.ShapeDtypeStruct((sources.size, width // 2), jnp.bfloat16)
    block = jax.ShapeDtypeStruct((keep, width), jnp.bfloat16)
    padded = pltpu.VMEM((sources.size, width // 2 + 2 * LANES), jnp.bfloat16)
    pinned = [pltpu.with_memory_space_constraint(x, pltpu.HBM) for x in (spectra, valid, sources)]
    return pl.pallas_call(
        functools.partial(encode_kernel, segments),
        out_shape=(slab, slab) + (block,) * segments,
        in_specs=[HBM] * 3,
        out_specs=(VMEM,) * (2 + segments),
        scratch_shapes=[
            pltpu.VMEM((channels, width), jnp.bfloat16 if keep % 16 == 0 else jnp.float32),
            pltpu.VMEM((channels, width), jnp.bfloat16),
            pltpu.VMEM((1, channels), jnp.int32),
            pltpu.SMEM(sources.shape, jnp.int32),
            padded,
            padded,
            pltpu.SemaphoreType.DMA((3,)),
        ],
        compiler_params=pltpu.CompilerParams(vmem_limit_bytes=12 * MEBI),
        name="encode_and_pick",
    )(*pinned)


def whiten_blocks(blocks):
    segments, (keep, width) = len(blocks), blocks[0].shape
    count, nbins = segments * keep, width // 2
    padded = pltpu.VMEM((count, nbins + 2 * LANES), jnp.bfloat16)
    part = jax.ShapeDtypeStruct((count, nbins), jnp.float32)
    return pl.pallas_call(
        functools.partial(whiten_kernel, segments),
        out_shape=(part, part, jax.ShapeDtypeStruct((count, LANES), jnp.float32)),
        in_specs=[VMEM] * segments,
        out_specs=(VMEM,) * 3,
        scratch_shapes=[padded, padded],
        compiler_params=pltpu.CompilerParams(vmem_limit_bytes=20 * MEBI),
        cost_estimate=pl.CostEstimate(
            flops=count * width * 1024, bytes_accessed=count * width * 4, transcendentals=0
        ),
        name="whiten_receivers",
    )(*blocks)


def stack_half(segments, slabs, receivers, table, rest=()):
    half, nbins = slabs.shape[0] // (2 * segments), slabs.shape[1]
    keep = receivers[0].shape[0] // segments
    count, rows, lags = segments * half, half * keep, 2 * LAG + 1
    part = pltpu.VMEM((count, nbins), jnp.float32)
    cross = pltpu.VMEM((rows, 2 * BLOCK), jnp.bfloat16 if keep % 16 == 0 else jnp.float32)
    total = pltpu.VMEM((rows, BLOCK), jnp.float32)
    scratch = [part, part, cross, cross, total, total]
    if rest:
        scratch += [pltpu.VMEM((rows, lags), jnp.float32), pltpu.SemaphoreType.DMA((1 + half,))]
    return pl.pallas_call(
        functools.partial(stack_kernel, segments),
        out_shape=jax.ShapeDtypeStruct((2 * rows if rest else rows, lags), jnp.float32),
        in_specs=[VMEM] * (5 + len(rest)),
        out_specs=HBM if rest else VMEM,
        scratch_shapes=scratch,
        compiler_params=pltpu.CompilerParams(vmem_limit_bytes=20 * MEBI),
        cost_estimate=pl.CostEstimate(
            flops=4 * rows * nbins * 2 * LAG, bytes_accessed=nbins * 2048, transcendentals=0
        ),
        name="stack_other_half" if rest else "stack_own_half",
    )(slabs, *receivers, table, *rest)


def swapped(value, axis, size, step):
    return lax.ppermute(value, axis, [(i, i ^ step) for i in range(size)])


def shards(rcv_size, tm_size, spectra, valid, sources):
    channels, _, width = spectra.shape
    keep = channels // tm_size
    rounds, per_round = sources.shape
    own, other, *receivers = encode(
        tm_size, spectra[:, 0, :], valid.reshape(1, channels), sources
    )
    receivers[1:] = [
        swapped(receivers[place], "tm", tm_size, place) for place in range(1, tm_size)
    ]
    own = own + swapped(other, "rcv", rcv_size, 1)
    step = 2
    while step < rcv_size:
        wide = min(4, rcv_size // step)
        others = [swapped(own, "rcv", rcv_size, place * step) for place in range(wide - 1, 0, -1)]
        own = functools.reduce(jnp.add, others, own)
        step *= wide
    own = [own] + [swapped(own, "tm", tm_size, place) for place in range(1, tm_size)]
    whitened = whiten_blocks(receivers)
    own, whitened = lax.optimization_barrier((own, whitened))
    own = jnp.concatenate(own, axis=0)
    other = swapped(own, "rcv", rcv_size, 1)

    table = jnp.asarray(lag_table(width // 2))
    first = stack_half(tm_size, own, whitened, table)
    stack = stack_half(tm_size, other, whitened, table, (first,))
    return stack.reshape(rounds, per_round, keep, 2 * LAG + 1)


def solution(mesh):
    body = functools.partial(shards, mesh.shape["rcv"], mesh.shape["tm"])
    in_specs = (P("rcv", "tm", None), P("rcv", "tm"), P())
    out_specs = P(None, None, ("rcv", "tm"), None)
    return jax.shard_map(body, mesh=mesh, in_specs=in_specs, out_specs=out_specs, check_vma=False)
```

```python
import functools
import math

import jax
import jax.numpy as jnp
import numpy as np
from jax import lax
from jax.experimental import pallas as pl
from jax.experimental.pallas import tpu as pltpu
from jax.sharding import PartitionSpec as P

NT = 4096
LAG = 150
HALF_WIN = 64
EPSILON = 1e-06

UNUSABLE = 1024.0
USABLE_BELOW = 512.0

LANES = 128
BLOCK = 256
MEBI = 1 << 20
FIRST_LAG = LANES - LAG
VMEM = pl.BlockSpec(memory_space=pltpu.VMEM)
HBM = pl.BlockSpec(memory_space=pltpu.HBM)


def lag_table(nbins):
    winding = np.mod(
        np.arange(1, nbins + 1, dtype=np.int64)[:, None]
        * np.arange(FIRST_LAG, FIRST_LAG + BLOCK, dtype=np.int64)[None, :],
        NT,
    )
    theta = winding * (2.0 * math.pi / NT)
    return np.concatenate([np.cos(theta), -np.sin(theta)], axis=0).astype(jnp.bfloat16)


def iota(shape, dim):
    return lax.broadcasted_iota(jnp.int32, shape, dim)


def whitening(real, imag, high, low, unusable=0.0):
    count, nbins = real.shape
    blocks = nbins // BLOCK
    span = BLOCK + 2 * LANES
    amplitude = jnp.sqrt(real * real + imag * imag)
    rounded = amplitude.astype(jnp.bfloat16)
    edge = jnp.zeros((count, LANES), jnp.bfloat16)
    for part, value in (
        (high, rounded),
        (low, (amplitude - rounded.astype(jnp.float32)).astype(jnp.bfloat16)),
    ):
        part[:, :LANES] = edge
        part[:, LANES : LANES + nbins] = value
        part[:, LANES + nbins :] = edge
    near = jnp.abs(iota((span, BLOCK), 0) - LANES - iota((span, BLOCK), 1)) <= HALF_WIN
    band = jnp.where(near, 1.0, 0.0).astype(jnp.bfloat16)
    pieces = [
        part[:, block * BLOCK : block * BLOCK + span] for block in range(blocks) for part in (high, low)
    ]
    windows = jnp.dot(
        jnp.concatenate(pieces, axis=0), band, preferred_element_type=jnp.float32
    )
    for block in range(blocks):
        first = block * BLOCK
        at = 2 * block * count
        window = windows[at : at + count] + windows[at + count : at + 2 * count]
        index = first + iota((1, BLOCK), 1)
        counted = jnp.minimum(index, HALF_WIN) + jnp.minimum(nbins - 1 - index, HALF_WIN) + 1
        factor = 1.0 / (window / counted.astype(jnp.float32) + EPSILON)
        re = real[:, first : first + BLOCK]
        im = imag[:, first : first + BLOCK]
        usable = re < USABLE_BELOW
        re = jnp.where(usable, re * factor, unusable).astype(jnp.bfloat16).astype(jnp.float32)
        im = jnp.where(usable, im * factor, unusable).astype(jnp.bfloat16).astype(jnp.float32)
        yield slice(first, first + BLOCK), re, im


def usable_rows(real):
    return jnp.where(real[:, :LANES] < USABLE_BELOW, 1.0, 0.0)


def encode_kernel(
    segments, spectra_ref, valid_ref, sources_ref, own_ref, other_ref, *refs
):
    blocks, refs = refs[:segments], refs[segments:]
    encoded_ref, spectra, valid, sources, high, low, arrived = refs
    copies = [
        pltpu.make_async_copy(spectra_ref, spectra, arrived.at[0]),
        pltpu.make_async_copy(sources_ref, sources, arrived.at[1]),
        pltpu.make_async_copy(valid_ref, valid, arrived.at[2]),
    ]
    for copy in copies:
        copy.start()
    channels, width = spectra_ref.shape
    nbins = width // 2
    rounds, per_round = sources.shape
    half = rounds * per_round // 2
    index = lax.axis_index("rcv")
    copies[1].wait()
    copies[2].wait()
    diagonal = iota((channels, channels), 0) == iota((channels, channels), 1)
    usable = jnp.sum(jnp.where(diagonal, valid[...], 0), axis=1, keepdims=True) != 0
    row = iota((2 * half, channels), 0)
    local = jnp.zeros((2 * half, channels), jnp.int32)
    for place in range(2 * half):
        number = (index % 2 if place < half else 1 - index % 2) * half + place % half
        here = sources[number // per_round, number % per_round] - index * channels
        local = jnp.where(row == place, here, local)
    onehot = jnp.where(local == iota((2 * half, channels), 1), 1.0, 0.0).astype(jnp.bfloat16)
    copies[0].wait()
    encoded = jnp.where(usable, spectra[...].astype(jnp.float32), UNUSABLE).astype(jnp.bfloat16)
    picked = jnp.dot(onehot, encoded, preferred_element_type=jnp.float32)
    for at, re, im in whitening(picked[:, :nbins], picked[:, nbins:], high, low, UNUSABLE):
        for first, ref in ((0, own_ref), (half, other_ref)):
            rows = slice(first, first + half)
            ref[:, at] = jnp.concatenate([re[rows], im[rows]], axis=0).astype(ref.dtype)
    encoded_ref[...] = encoded.astype(encoded_ref.dtype)
    keep = channels // segments
    for step, block in enumerate(blocks):
        at = pl.multiple_of((lax.axis_index("tm") ^ step) * keep, keep)
        block[...] = encoded_ref[pl.ds(at, keep), :].astype(block.dtype)


def whiten_kernel(segments, *refs):
    blocks, (real_ref, imag_ref, valid_ref, high, low) = refs[:segments], refs[segments:]
    rows = jnp.concatenate([ref[...].astype(jnp.float32) for ref in blocks], axis=0)
    nbins = rows.shape[1] // 2
    real, imag = rows[:, :nbins], rows[:, nbins:]
    for at, re, im in whitening(real, imag, high, low):
        real_ref[:, at] = re
        imag_ref[:, at] = im
    valid_ref[...] = usable_rows(real)


def stack_kernel(
    segments, slabs_ref, rcv_re, rcv_im, rcv_valid, table_ref, *refs
):
    *rest, out_ref, src_re, src_im, cross_a, cross_b, total_re, total_im = refs[
        : 8 if len(refs) == 10 else 7
    ]
    half = slabs_ref.shape[0] // (2 * segments)
    nbins = slabs_ref.shape[1]
    keep = rcv_re.shape[0] // segments
    rows = half * keep
    if rest:
        result, written = refs[8:]
        part = lax.axis_index("rcv") % 2
        pieces = max(1, half // 4)
        at = pl.multiple_of(part * rows, rows)
        copies = [
            pltpu.make_async_copy(rest[0], out_ref.at[pl.ds(at, rows)], written.at[0])
        ]
        copies[0].start()
    else:
        result = out_ref
    slabs = slabs_ref[...].astype(jnp.float32)
    real = jnp.concatenate(
        [slabs[2 * half * t : 2 * half * t + half] for t in range(segments)], axis=0
    )
    imag = jnp.concatenate(
        [slabs[2 * half * t + half : 2 * half * (t + 1)] for t in range(segments)], axis=0
    )
    usable = real < USABLE_BELOW
    src_re[...] = jnp.where(usable, real, 0.0)
    src_im[...] = jnp.where(usable, imag, 0.0)
    src_valid = usable_rows(real)
    total_re[...] = jnp.zeros_like(total_re)
    total_im[...] = jnp.zeros_like(total_im)
    cross_b[...] = jnp.zeros_like(cross_b)

    def multiply(block, cross):
        for sub in range(BLOCK // LANES):
            at = pl.ds(pl.multiple_of(block * BLOCK + sub * LANES, LANES), LANES)
            r_re = [rcv_re[t * keep : (t + 1) * keep, at] for t in range(segments)]
            r_im = [rcv_im[t * keep : (t + 1) * keep, at] for t in range(segments)]
            for source in range(half):
                real, imag = [], []
                for t in range(segments):
                    row = slice(t * half + source, t * half + source + 1)
                    s_re, s_im = src_re[row, at], src_im[row, at]
                    real.append(s_re * r_re[t] + s_im * r_im[t])
                    imag.append(s_im * r_re[t] - s_re * r_im[t])
                real, imag = functools.reduce(jnp.add, real), functools.reduce(jnp.add, imag)
                to = slice(source * keep, (source + 1) * keep)
                cross[to, sub * LANES : (sub + 1) * LANES] = real.astype(cross.dtype)
                cross[to, BLOCK + sub * LANES : BLOCK + (sub + 1) * LANES] = imag.astype(
                    cross.dtype
                )

    def project(block, cross):
        value = cross[...].astype(jnp.bfloat16)
        re_at = pl.ds(pl.multiple_of(block * BLOCK, BLOCK), BLOCK)
        im_at = pl.ds(pl.multiple_of(nbins + block * BLOCK, BLOCK), BLOCK)
        total_re[...] += jnp.dot(
            value[:, :BLOCK], table_ref[re_at, :], preferred_element_type=jnp.float32
        )
        total_im[...] += jnp.dot(
            value[:, BLOCK:], table_ref[im_at, :], preferred_element_type=jnp.float32
        )

    def two_blocks(pair, carry):
        multiply(2 * pair, cross_a)
        project(jnp.maximum(2 * pair - 1, 0), cross_b)
        multiply(2 * pair + 1, cross_b)
        project(2 * pair, cross_a)
        return carry

    pairs = nbins // (2 * BLOCK)
    lax.fori_loop(0, pairs, two_blocks, 0)
    project(2 * pairs - 1, cross_b)

    lags = result.shape[1]
    scale = 2.0 / math.sqrt(nbins)
    mirror = LAG - FIRST_LAG - iota((keep, LANES), 1)
    for source in range(half):
        common = 0.0
        for t in range(segments):
            row = t * half + source
            common = common + src_valid[row : row + 1] * rcv_valid[t * keep : (t + 1) * keep, :]
        weight = scale / jnp.maximum(common, 1.0)
        to = slice(source * keep, (source + 1) * keep)
        even, odd = total_re[to], total_im[to]
        ahead = even + odd
        behind = even - odd
        low_part = jnp.take_along_axis(
            behind[:, :LANES], jnp.clip(mirror, 0, LANES - 1), axis=1
        )
        high_part = jnp.take_along_axis(
            behind[:, LANES:], jnp.clip(mirror - LANES, 0, LANES - 1), axis=1
        )
        result[to, :LANES] = jnp.where(mirror < LANES, low_part, high_part) * weight
        for first in range(0, lags - LANES, LANES):
            last = min(first + LANES, lags - LANES)
            value = ahead[:, first : first + LANES] * weight
            result[to, LANES + first : LANES + last] = value[:, : last - first]
        if rest and (source + 1) % pieces == 0:
            first, count = (source + 1 - pieces) * keep, pieces * keep
            at = pl.multiple_of((1 - part) * rows + first, count)
            copies.append(
                pltpu.make_async_copy(
                    result.at[pl.ds(first, count)],
                    out_ref.at[pl.ds(at, count)],
                    written.at[1 + source // pieces],
                )
            )
            copies[-1].start()
    if rest:
        for copy in copies:
            copy.wait()


def encode(segments, spectra, valid, sources):
    channels, width = spectra.shape
    keep = channels // segments
    slab = jax.ShapeDtypeStruct((sources.size, width // 2), jnp.bfloat16)
    block = jax.ShapeDtypeStruct((keep, width), jnp.bfloat16)
    padded = pltpu.VMEM((sources.size, width // 2 + 2 * LANES), jnp.bfloat16)
    pinned = [pltpu.with_memory_space_constraint(x, pltpu.HBM) for x in (spectra, valid, sources)]
    return pl.pallas_call(
        functools.partial(encode_kernel, segments),
        out_shape=(slab, slab) + (block,) * segments,
        in_specs=[HBM] * 3,
        out_specs=(VMEM,) * (2 + segments),
        scratch_shapes=[
            pltpu.VMEM((channels, width), jnp.bfloat16 if keep % 16 == 0 else jnp.float32),
            pltpu.VMEM((channels, width), jnp.bfloat16),
            pltpu.VMEM((1, channels), jnp.int32),
            pltpu.SMEM(sources.shape, jnp.int32),
            padded,
            padded,
            pltpu.SemaphoreType.DMA((3,)),
        ],
        compiler_params=pltpu.CompilerParams(vmem_limit_bytes=12 * MEBI),
        name="encode_and_pick",
    )(*pinned)


def whiten_blocks(blocks):
    segments, (keep, width) = len(blocks), blocks[0].shape
    count, nbins = segments * keep, width // 2
    padded = pltpu.VMEM((count, nbins + 2 * LANES), jnp.bfloat16)
    part = jax.ShapeDtypeStruct((count, nbins), jnp.float32)
    return pl.pallas_call(
        functools.partial(whiten_kernel, segments),
        out_shape=(part, part, jax.ShapeDtypeStruct((count, LANES), jnp.float32)),
        in_specs=[VMEM] * segments,
        out_specs=(VMEM,) * 3,
        scratch_shapes=[padded, padded],
        compiler_params=pltpu.CompilerParams(vmem_limit_bytes=20 * MEBI),
        cost_estimate=pl.CostEstimate(
            flops=count * width * 1024, bytes_accessed=count * width * 4, transcendentals=0
        ),
        name="whiten_receivers",
    )(*blocks)


def stack_half(segments, slabs, receivers, table, rest=()):
    half, nbins = slabs.shape[0] // (2 * segments), slabs.shape[1]
    keep = receivers[0].shape[0] // segments
    count, rows, lags = segments * half, half * keep, 2 * LAG + 1
    part = pltpu.VMEM((count, nbins), jnp.float32)
    cross = pltpu.VMEM((rows, 2 * BLOCK), jnp.bfloat16 if keep % 16 == 0 else jnp.float32)
    total = pltpu.VMEM((rows, BLOCK), jnp.float32)
    scratch = [part, part, cross, cross, total, total]
    if rest:
        scratch += [pltpu.VMEM((rows, lags), jnp.float32), pltpu.SemaphoreType.DMA((1 + half,))]
    return pl.pallas_call(
        functools.partial(stack_kernel, segments),
        out_shape=jax.ShapeDtypeStruct((2 * rows if rest else rows, lags), jnp.float32),
        in_specs=[VMEM] * (5 + len(rest)),
        out_specs=HBM if rest else VMEM,
        scratch_shapes=scratch,
        compiler_params=pltpu.CompilerParams(vmem_limit_bytes=20 * MEBI),
        cost_estimate=pl.CostEstimate(
            flops=4 * rows * nbins * 2 * LAG, bytes_accessed=nbins * 2048, transcendentals=0
        ),
        name="stack_other_half" if rest else "stack_own_half",
    )(slabs, *receivers, table, *rest)


def swapped(value, axis, size, step):
    return lax.ppermute(value, axis, [(i, i ^ step) for i in range(size)])


def shards(rcv_size, tm_size, spectra, valid, sources):
    channels, _, width = spectra.shape
    keep = channels // tm_size
    rounds, per_round = sources.shape
    own, other, *receivers = encode(
        tm_size, spectra[:, 0, :], valid.reshape(1, channels), sources
    )
    receivers[-1] = swapped(receivers[-1], "tm", tm_size, tm_size - 1)
    own = own + swapped(other, "rcv", rcv_size, 1)
    step = 2
    while step < rcv_size:
        wide = min(4, rcv_size // step)
        parts = [swapped(own, "rcv", rcv_size, place * step) for place in range(wide - 1, 0, -1)]
        if step == 2:
            parts[-1], later = lax.optimization_barrier((parts[-1], receivers[1:-1]))
            receivers[1:-1] = [
                swapped(block, "tm", tm_size, place) for place, block in enumerate(later, 1)
            ]
            parts[0], receivers[-1] = lax.optimization_barrier((parts[0], receivers[-1]))
        own = functools.reduce(jnp.add, parts[::-1], own)
        step *= wide
    own = [own] + [swapped(own, "tm", tm_size, place) for place in range(1, tm_size)]
    whitened = whiten_blocks(receivers)
    own, whitened = lax.optimization_barrier((own, whitened))
    own = jnp.concatenate(own, axis=0)
    other = swapped(own, "rcv", rcv_size, 1)

    table = jnp.asarray(lag_table(width // 2))
    first = stack_half(tm_size, own, whitened, table)
    stack = stack_half(tm_size, other, whitened, table, (first,))
    return stack.reshape(rounds, per_round, keep, 2 * LAG + 1)


def solution(mesh):
    body = functools.partial(shards, mesh.shape["rcv"], mesh.shape["tm"])
    in_specs = (P("rcv", "tm", None), P("rcv", "tm"), P())
    out_specs = P(None, None, ("rcv", "tm"), None)
    return jax.shard_map(body, mesh=mesh, in_specs=in_specs, out_specs=out_specs, check_vma=False)
```

```python
import functools
import math

import jax
import jax.numpy as jnp
import numpy as np
from jax import lax
from jax.experimental import pallas as pl
from jax.experimental.pallas import tpu as pltpu
from jax.sharding import PartitionSpec as P

NT = 4096
LAG = 150
HALF_WIN = 64
EPSILON = 1e-06

UNUSABLE = 1024.0
USABLE_BELOW = 512.0

LANES = 128
BLOCK = 256
MEBI = 1 << 20
FIRST_LAG = LANES - LAG
VMEM = pl.BlockSpec(memory_space=pltpu.VMEM)
HBM = pl.BlockSpec(memory_space=pltpu.HBM)


def lag_table(nbins):
    winding = np.mod(
        np.arange(1, nbins + 1, dtype=np.int64)[:, None]
        * np.arange(FIRST_LAG, FIRST_LAG + BLOCK, dtype=np.int64)[None, :],
        NT,
    )
    theta = winding * (2.0 * math.pi / NT)
    return np.concatenate([np.cos(theta), -np.sin(theta)], axis=0).astype(jnp.bfloat16)


def kind_for(rows):
    return jnp.bfloat16 if rows % 16 == 0 else jnp.float32


def iota(shape, dim):
    return lax.broadcasted_iota(jnp.int32, shape, dim)


def whitening(real, imag, high, low, unusable=0.0):
    count, nbins = real.shape
    blocks = nbins // BLOCK
    span = BLOCK + 2 * LANES
    amplitude = jnp.sqrt(real * real + imag * imag)
    rounded = amplitude.astype(jnp.bfloat16)
    edge = jnp.zeros((count, LANES), jnp.bfloat16)
    for part, value in (
        (high, rounded),
        (low, (amplitude - rounded.astype(jnp.float32)).astype(jnp.bfloat16)),
    ):
        part[:, :LANES] = edge
        part[:, LANES : LANES + nbins] = value
        part[:, LANES + nbins :] = edge
    near = jnp.abs(iota((span, BLOCK), 0) - LANES - iota((span, BLOCK), 1)) <= HALF_WIN
    band = jnp.where(near, 1.0, 0.0).astype(jnp.bfloat16)
    pieces = [
        part[:, block * BLOCK : block * BLOCK + span] for block in range(blocks) for part in (high, low)
    ]
    windows = jnp.dot(
        jnp.concatenate(pieces, axis=0), band, preferred_element_type=jnp.float32
    )
    for block in range(blocks):
        first = block * BLOCK
        at = 2 * block * count
        window = windows[at : at + count] + windows[at + count : at + 2 * count]
        index = first + iota((1, BLOCK), 1)
        counted = jnp.minimum(index, HALF_WIN) + jnp.minimum(nbins - 1 - index, HALF_WIN) + 1
        factor = 1.0 / (window / counted.astype(jnp.float32) + EPSILON)
        re = real[:, first : first + BLOCK]
        im = imag[:, first : first + BLOCK]
        usable = re < USABLE_BELOW
        re = jnp.where(usable, re * factor, unusable).astype(jnp.bfloat16).astype(jnp.float32)
        im = jnp.where(usable, im * factor, unusable).astype(jnp.bfloat16).astype(jnp.float32)
        yield slice(first, first + BLOCK), re, im


def usable_rows(real):
    return jnp.where(real[:, :LANES] < USABLE_BELOW, 1.0, 0.0)


def encode_kernel(
    segments, spectra_ref, valid_ref, sources_ref, own_ref, other_ref, *refs
):
    blocks, refs = refs[:segments], refs[segments:]
    encoded_ref, spectra, valid, sources, high, low, arrived = refs
    copies = [
        pltpu.make_async_copy(spectra_ref, spectra, arrived.at[0]),
        pltpu.make_async_copy(sources_ref, sources, arrived.at[1]),
        pltpu.make_async_copy(valid_ref, valid, arrived.at[2]),
    ]
    for copy in copies:
        copy.start()
    channels, width = spectra_ref.shape
    nbins = width // 2
    rounds, per_round = sources.shape
    half = rounds * per_round // 2
    index = lax.axis_index("rcv")
    copies[1].wait()
    copies[2].wait()
    diagonal = iota((channels, channels), 0) == iota((channels, channels), 1)
    usable = jnp.sum(jnp.where(diagonal, valid[...], 0), axis=1, keepdims=True) != 0
    row = iota((2 * half, channels), 0)
    local = jnp.zeros((2 * half, channels), jnp.int32)
    for place in range(2 * half):
        number = (index % 2 if place < half else 1 - index % 2) * half + place % half
        here = sources[number // per_round, number % per_round] - index * channels
        local = jnp.where(row == place, here, local)
    onehot = jnp.where(local == iota((2 * half, channels), 1), 1.0, 0.0).astype(jnp.bfloat16)
    copies[0].wait()
    encoded = jnp.where(usable, spectra[...].astype(jnp.float32), UNUSABLE).astype(jnp.bfloat16)
    picked = jnp.dot(onehot, encoded, preferred_element_type=jnp.float32)
    for at, re, im in whitening(picked[:, :nbins], picked[:, nbins:], high, low, UNUSABLE):
        for first, ref in ((0, own_ref), (half, other_ref)):
            rows = slice(first, first + half)
            ref[:, at] = jnp.concatenate([re[rows], im[rows]], axis=0).astype(ref.dtype)
    encoded_ref[...] = encoded.astype(encoded_ref.dtype)
    keep = channels // segments
    for step, block in enumerate(blocks):
        at = pl.multiple_of((lax.axis_index("tm") ^ step) * keep, keep)
        block[...] = encoded_ref[pl.ds(at, keep), :].astype(block.dtype)


def whiten_kernel(segments, *refs):
    blocks, (real_ref, imag_ref, valid_ref, high, low) = refs[:segments], refs[segments:]
    rows = jnp.concatenate([ref[...].astype(jnp.float32) for ref in blocks], axis=0)
    nbins = rows.shape[1] // 2
    real, imag = rows[:, :nbins], rows[:, nbins:]
    for at, re, im in whitening(real, imag, high, low):
        real_ref[:, at] = re.astype(real_ref.dtype)
        imag_ref[:, at] = im.astype(imag_ref.dtype)
    valid_ref[...] = usable_rows(real)


def total_groups(segments, kind):
    return -(-segments // 2) if kind == jnp.bfloat16 and segments % 2 == 0 else 1


def stack_kernel(
    segments, slabs_ref, rcv_re, rcv_im, rcv_valid, table_ref, *refs
):
    *rest, out_ref, src_re, src_im, cross_a, cross_b, total_re, total_im = refs[
        : 8 if len(refs) == 10 else 7
    ]
    half = slabs_ref.shape[0] // (2 * segments)
    nbins = slabs_ref.shape[1]
    keep = rcv_re.shape[0] // segments
    rows = half * keep
    if rest:
        result, written = refs[8:]
        part = lax.axis_index("rcv") % 2
        pieces = max(1, half // 4)
        at = pl.multiple_of(part * rows, rows)
        copies = [
            pltpu.make_async_copy(rest[0], out_ref.at[pl.ds(at, rows)], written.at[0])
        ]
        copies[0].start()
    else:
        result = out_ref
    slabs = slabs_ref[...].astype(jnp.float32)
    real = jnp.concatenate(
        [slabs[2 * half * t : 2 * half * t + half] for t in range(segments)], axis=0
    )
    imag = jnp.concatenate(
        [slabs[2 * half * t + half : 2 * half * (t + 1)] for t in range(segments)], axis=0
    )
    usable = real < USABLE_BELOW
    src_re[...] = jnp.where(usable, real, 0.0)
    src_im[...] = jnp.where(usable, imag, 0.0)
    src_valid = usable_rows(real)
    total_re[...] = jnp.zeros_like(total_re)
    total_im[...] = jnp.zeros_like(total_im)
    cross_b[...] = jnp.zeros_like(cross_b)

    kind = rcv_re.dtype
    groups = total_groups(segments, kind)

    def spread(row):
        tile = jnp.broadcast_to(row, (min(keep, 16), LANES)).astype(kind)
        return jnp.concatenate([tile] * (keep // tile.shape[0]), axis=0)

    def multiply(block, cross):
        for sub in range(BLOCK // LANES):
            at = pl.ds(pl.multiple_of(block * BLOCK + sub * LANES, LANES), LANES)
            r_re = [rcv_re[t * keep : (t + 1) * keep, at] for t in range(segments)]
            r_im = [rcv_im[t * keep : (t + 1) * keep, at] for t in range(segments)]
            for source in range(half):
                real, imag = [], []
                for t in range(segments):
                    row = slice(t * half + source, t * half + source + 1)
                    s_re, s_im = spread(src_re[row, at]), spread(src_im[row, at])
                    real.append(s_re * r_re[t] + s_im * r_im[t])
                    imag.append(s_im * r_re[t] - s_re * r_im[t])
                to = slice(source * keep, (source + 1) * keep)
                share = segments // groups
                for place, part in enumerate((real, imag)):
                    for group in range(groups):
                        value = functools.reduce(jnp.add, part[group * share : (group + 1) * share])
                        first = (place * groups + group) * BLOCK + sub * LANES
                        cross[to, first : first + LANES] = value

    def project(block, cross):
        value = cross[...].astype(jnp.bfloat16)
        re_at = pl.ds(pl.multiple_of(block * BLOCK, BLOCK), BLOCK)
        im_at = pl.ds(pl.multiple_of(nbins + block * BLOCK, BLOCK), BLOCK)
        for first, at, total in ((0, re_at, total_re), (groups * BLOCK, im_at, total_im)):
            total[...] += jnp.dot(
                value[:, first : first + groups * BLOCK],
                jnp.concatenate([table_ref[at, :]] * groups, axis=0),
                preferred_element_type=jnp.float32,
            )

    def two_blocks(pair, carry):
        multiply(2 * pair, cross_a)
        project(jnp.maximum(2 * pair - 1, 0), cross_b)
        multiply(2 * pair + 1, cross_b)
        project(2 * pair, cross_a)
        return carry

    pairs = nbins // (2 * BLOCK)
    lax.fori_loop(0, pairs, two_blocks, 0)
    project(2 * pairs - 1, cross_b)

    lags = result.shape[1]
    scale = 2.0 / math.sqrt(nbins)
    mirror = LAG - FIRST_LAG - iota((keep, LANES), 1)
    for source in range(half):
        common = 0.0
        for t in range(segments):
            row = t * half + source
            common = common + src_valid[row : row + 1] * rcv_valid[t * keep : (t + 1) * keep, :]
        weight = scale / jnp.maximum(common, 1.0)
        to = slice(source * keep, (source + 1) * keep)
        even, odd = total_re[to], total_im[to]
        ahead = even + odd
        behind = even - odd
        low_part = jnp.take_along_axis(
            behind[:, :LANES], jnp.clip(mirror, 0, LANES - 1), axis=1
        )
        high_part = jnp.take_along_axis(
            behind[:, LANES:], jnp.clip(mirror - LANES, 0, LANES - 1), axis=1
        )
        result[to, :LANES] = jnp.where(mirror < LANES, low_part, high_part) * weight
        for first in range(0, lags - LANES, LANES):
            last = min(first + LANES, lags - LANES)
            value = ahead[:, first : first + LANES] * weight
            result[to, LANES + first : LANES + last] = value[:, : last - first]
        if rest and (source + 1) % pieces == 0:
            first, count = (source + 1 - pieces) * keep, pieces * keep
            at = pl.multiple_of((1 - part) * rows + first, count)
            copies.append(
                pltpu.make_async_copy(
                    result.at[pl.ds(first, count)],
                    out_ref.at[pl.ds(at, count)],
                    written.at[1 + source // pieces],
                )
            )
            copies[-1].start()
    if rest:
        for copy in copies:
            copy.wait()


def encode(segments, spectra, valid, sources):
    channels, width = spectra.shape
    keep = channels // segments
    slab = jax.ShapeDtypeStruct((sources.size, width // 2), jnp.bfloat16)
    block = jax.ShapeDtypeStruct((keep, width), jnp.bfloat16)
    padded = pltpu.VMEM((sources.size, width // 2 + 2 * LANES), jnp.bfloat16)
    pinned = [pltpu.with_memory_space_constraint(x, pltpu.HBM) for x in (spectra, valid, sources)]
    return pl.pallas_call(
        functools.partial(encode_kernel, segments),
        out_shape=(slab, slab) + (block,) * segments,
        in_specs=[HBM] * 3,
        out_specs=(VMEM,) * (2 + segments),
        scratch_shapes=[
            pltpu.VMEM((channels, width), kind_for(keep)),
            pltpu.VMEM((channels, width), jnp.bfloat16),
            pltpu.VMEM((1, channels), jnp.int32),
            pltpu.SMEM(sources.shape, jnp.int32),
            padded,
            padded,
            pltpu.SemaphoreType.DMA((3,)),
        ],
        compiler_params=pltpu.CompilerParams(vmem_limit_bytes=12 * MEBI),
        name="encode_and_pick",
    )(*pinned)


def whiten_blocks(blocks):
    segments, (keep, width) = len(blocks), blocks[0].shape
    count, nbins = segments * keep, width // 2
    padded = pltpu.VMEM((count, nbins + 2 * LANES), jnp.bfloat16)
    part = jax.ShapeDtypeStruct((count, nbins), kind_for(keep))
    return pl.pallas_call(
        functools.partial(whiten_kernel, segments),
        out_shape=(part, part, jax.ShapeDtypeStruct((count, LANES), jnp.float32)),
        in_specs=[VMEM] * segments,
        out_specs=(VMEM,) * 3,
        scratch_shapes=[padded, padded],
        compiler_params=pltpu.CompilerParams(vmem_limit_bytes=20 * MEBI),
        cost_estimate=pl.CostEstimate(
            flops=count * width * 1024, bytes_accessed=count * width * 4, transcendentals=0
        ),
        name="whiten_receivers",
    )(*blocks)


def stack_half(segments, slabs, receivers, table, rest=()):
    half, nbins = slabs.shape[0] // (2 * segments), slabs.shape[1]
    keep = receivers[0].shape[0] // segments
    count, rows, lags = segments * half, half * keep, 2 * LAG + 1
    kind = receivers[0].dtype
    groups = total_groups(segments, kind)
    part = pltpu.VMEM((count, nbins), jnp.float32)
    cross = pltpu.VMEM((rows, 2 * groups * BLOCK), kind)
    total = pltpu.VMEM((rows, BLOCK), jnp.float32)
    scratch = [part, part, cross, cross, total, total]
    if rest:
        scratch += [pltpu.VMEM((rows, lags), jnp.float32), pltpu.SemaphoreType.DMA((1 + half,))]
    return pl.pallas_call(
        functools.partial(stack_kernel, segments),
        out_shape=jax.ShapeDtypeStruct((2 * rows if rest else rows, lags), jnp.float32),
        in_specs=[VMEM] * (5 + len(rest)),
        out_specs=HBM if rest else VMEM,
        scratch_shapes=scratch,
        compiler_params=pltpu.CompilerParams(vmem_limit_bytes=20 * MEBI),
        cost_estimate=pl.CostEstimate(
            flops=4 * rows * nbins * 2 * LAG, bytes_accessed=nbins * 2048, transcendentals=0
        ),
        name="stack_other_half" if rest else "stack_own_half",
    )(slabs, *receivers, table, *rest)


def swapped(value, axis, size, step):
    return lax.ppermute(value, axis, [(i, i ^ step) for i in range(size)])


def shards(rcv_size, tm_size, spectra, valid, sources):
    channels, _, width = spectra.shape
    keep = channels // tm_size
    rounds, per_round = sources.shape
    own, other, *receivers = encode(
        tm_size, spectra[:, 0, :], valid.reshape(1, channels), sources
    )
    receivers[-1] = swapped(receivers[-1], "tm", tm_size, tm_size - 1)
    own = own + swapped(other, "rcv", rcv_size, 1)
    step = 2
    while step < rcv_size:
        wide = min(4, rcv_size // step)
        parts = [swapped(own, "rcv", rcv_size, place * step) for place in range(wide - 1, 0, -1)]
        if step == 2:
            parts[-1], later = lax.optimization_barrier((parts[-1], receivers[1:-1]))
            receivers[1:-1] = [
                swapped(block, "tm", tm_size, place) for place, block in enumerate(later, 1)
            ]
            parts[0], receivers[-1] = lax.optimization_barrier((parts[0], receivers[-1]))
        own = functools.reduce(jnp.add, parts[::-1], own)
        step *= wide
    own = [own] + [swapped(own, "tm", tm_size, place) for place in range(1, tm_size)]
    whitened = whiten_blocks(receivers)
    own, whitened = lax.optimization_barrier((own, whitened))
    own = jnp.concatenate(own, axis=0)
    other = swapped(own, "rcv", rcv_size, 1)

    table = jnp.asarray(lag_table(width // 2))
    first = stack_half(tm_size, own, whitened, table)
    stack = stack_half(tm_size, other, whitened, table, (first,))
    return stack.reshape(rounds, per_round, keep, 2 * LAG + 1)


def solution(mesh):
    body = functools.partial(shards, mesh.shape["rcv"], mesh.shape["tm"])
    in_specs = (P("rcv", "tm", None), P("rcv", "tm"), P())
    out_specs = P(None, None, ("rcv", "tm"), None)
    return jax.shard_map(body, mesh=mesh, in_specs=in_specs, out_specs=out_specs, check_vma=False)
```

```python
import functools
import math

import jax
import jax.numpy as jnp
import numpy as np
from jax import lax
from jax.experimental import pallas as pl
from jax.experimental.pallas import tpu as pltpu
from jax.sharding import PartitionSpec as P

NT = 4096
LAG = 150
HALF_WIN = 64
EPSILON = 1e-06

UNUSABLE = 1024.0
USABLE_BELOW = 512.0

LANES = 128
BLOCK = 256
CHUNK = 512
MEBI = 1 << 20
FIRST_LAG = LANES - LAG
VMEM = pl.BlockSpec(memory_space=pltpu.VMEM)
HBM = pl.BlockSpec(memory_space=pltpu.HBM)


def lag_table(nbins):
    winding = np.mod(
        np.arange(1, nbins + 1, dtype=np.int64)[:, None]
        * np.arange(FIRST_LAG, FIRST_LAG + BLOCK, dtype=np.int64)[None, :],
        NT,
    )
    theta = winding * (2.0 * math.pi / NT)
    return np.concatenate([np.cos(theta), -np.sin(theta)], axis=0).astype(jnp.bfloat16)


def kind_for(rows):
    return jnp.bfloat16 if rows % 16 == 0 else jnp.float32


def iota(shape, dim):
    return lax.broadcasted_iota(jnp.int32, shape, dim)


def whitening(real, imag, high, low, unusable=0.0):
    count, nbins = real.shape
    blocks = nbins // BLOCK
    span = BLOCK + 2 * LANES
    amplitude = jnp.sqrt(real * real + imag * imag)
    rounded = amplitude.astype(jnp.bfloat16)
    edge = jnp.zeros((count, LANES), jnp.bfloat16)
    for part, value in (
        (high, rounded),
        (low, (amplitude - rounded.astype(jnp.float32)).astype(jnp.bfloat16)),
    ):
        part[:, :LANES] = edge
        part[:, LANES : LANES + nbins] = value
        part[:, LANES + nbins :] = edge
    near = jnp.abs(iota((span, BLOCK), 0) - LANES - iota((span, BLOCK), 1)) <= HALF_WIN
    band = jnp.where(near, 1.0, 0.0).astype(jnp.bfloat16)
    pieces = [
        part[:, block * BLOCK : block * BLOCK + span] for block in range(blocks) for part in (high, low)
    ]
    windows = jnp.dot(
        jnp.concatenate(pieces, axis=0), band, preferred_element_type=jnp.float32
    )
    for block in range(blocks):
        first = block * BLOCK
        at = 2 * block * count
        window = windows[at : at + count] + windows[at + count : at + 2 * count]
        index = first + iota((1, BLOCK), 1)
        counted = jnp.minimum(index, HALF_WIN) + jnp.minimum(nbins - 1 - index, HALF_WIN) + 1
        factor = 1.0 / (window / counted.astype(jnp.float32) + EPSILON)
        re = real[:, first : first + BLOCK]
        im = imag[:, first : first + BLOCK]
        usable = re < USABLE_BELOW
        re = jnp.where(usable, re * factor, unusable).astype(jnp.bfloat16).astype(jnp.float32)
        im = jnp.where(usable, im * factor, unusable).astype(jnp.bfloat16).astype(jnp.float32)
        yield slice(first, first + BLOCK), re, im


def usable_rows(real):
    return jnp.where(real[:, :LANES] < USABLE_BELOW, 1.0, 0.0)


def encode_kernel(
    segments, spectra_ref, valid_ref, sources_ref, own_ref, other_ref, *refs
):
    blocks, refs = refs[:segments], refs[segments:]
    encoded_ref, spectra, valid, sources, high, low, arrived = refs
    copies = [
        pltpu.make_async_copy(spectra_ref, spectra, arrived.at[0]),
        pltpu.make_async_copy(sources_ref, sources, arrived.at[1]),
        pltpu.make_async_copy(valid_ref, valid, arrived.at[2]),
    ]
    for copy in copies:
        copy.start()
    channels, width = spectra_ref.shape
    nbins = width // 2
    rounds, per_round = sources.shape
    half = rounds * per_round // 2
    index = lax.axis_index("rcv")
    copies[1].wait()
    copies[2].wait()
    diagonal = iota((channels, channels), 0) == iota((channels, channels), 1)
    usable = jnp.sum(jnp.where(diagonal, valid[...], 0), axis=1, keepdims=True) != 0
    row = iota((2 * half, channels), 0)
    local = jnp.zeros((2 * half, channels), jnp.int32)
    for place in range(2 * half):
        number = (index % 2 if place < half else 1 - index % 2) * half + place % half
        here = sources[number // per_round, number % per_round] - index * channels
        local = jnp.where(row == place, here, local)
    onehot = jnp.where(local == iota((2 * half, channels), 1), 1.0, 0.0).astype(jnp.bfloat16)
    copies[0].wait()
    encoded = jnp.where(usable, spectra[...].astype(jnp.float32), UNUSABLE).astype(jnp.bfloat16)
    picked = jnp.dot(onehot, encoded, preferred_element_type=jnp.float32)
    for at, re, im in whitening(picked[:, :nbins], picked[:, nbins:], high, low, UNUSABLE):
        for first, ref in ((0, own_ref), (half, other_ref)):
            rows = slice(first, first + half)
            ref[:, at] = jnp.concatenate([re[rows], im[rows]], axis=0).astype(ref.dtype)
    encoded_ref[...] = encoded.astype(encoded_ref.dtype)
    keep = channels // segments
    for step, block in enumerate(blocks):
        at = pl.multiple_of((lax.axis_index("tm") ^ step) * keep, keep)
        block[...] = encoded_ref[pl.ds(at, keep), :].astype(block.dtype)


def whiten_kernel(segments, *refs):
    blocks, (real_ref, imag_ref, valid_ref, high, low) = refs[:segments], refs[segments:]
    rows = jnp.concatenate([ref[...].astype(jnp.float32) for ref in blocks], axis=0)
    nbins = rows.shape[1] // 2
    real, imag = rows[:, :nbins], rows[:, nbins:]
    for at, re, im in whitening(real, imag, high, low):
        real_ref[:, at] = re.astype(real_ref.dtype)
        imag_ref[:, at] = im.astype(imag_ref.dtype)
    valid_ref[...] = usable_rows(real)


def total_groups(segments, kind):
    return -(-segments // 2) if kind == jnp.bfloat16 and segments % 2 == 0 else 1


def stack_kernel(
    segments, slabs_ref, rcv_re, rcv_im, rcv_valid, table_ref, *refs
):
    *rest, out_ref, src_re, src_im, cross = refs[: 5 if len(refs) == 7 else 4]
    half = slabs_ref.shape[0] // (2 * segments)
    nbins = slabs_ref.shape[1]
    keep = rcv_re.shape[0] // segments
    rows = half * keep
    if rest:
        result, written = refs[5:]
        part = lax.axis_index("rcv") % 2
        pieces = max(1, half // 4)
        at = pl.multiple_of(part * rows, rows)
        copies = [
            pltpu.make_async_copy(rest[0], out_ref.at[pl.ds(at, rows)], written.at[0])
        ]
        copies[0].start()
    else:
        result = out_ref
    slabs = slabs_ref[...].astype(jnp.float32)
    real = jnp.concatenate(
        [slabs[2 * half * t : 2 * half * t + half] for t in range(segments)], axis=0
    )
    imag = jnp.concatenate(
        [slabs[2 * half * t + half : 2 * half * (t + 1)] for t in range(segments)], axis=0
    )
    usable = real < USABLE_BELOW
    for ref, value in ((src_re, real), (src_im, imag)):
        value = jnp.where(usable, value, 0.0)
        for block in range(nbins // LANES):
            ref[block] = value[:, block * LANES : (block + 1) * LANES]
    src_valid = usable_rows(real)
    kind = rcv_re.dtype
    groups = total_groups(segments, kind)

    def spread(ref, block, row):
        tile = ref[block, pl.ds(row, 8, stride=0), :]
        return jnp.concatenate([tile] * (keep // 8), axis=0).astype(kind)

    def multiply(chunk):
        for sub in range(CHUNK // LANES):
            block = chunk * (CHUNK // LANES) + sub
            at = slice(block * LANES, (block + 1) * LANES)
            r_re = [rcv_re[t * keep : (t + 1) * keep, at] for t in range(segments)]
            r_im = [rcv_im[t * keep : (t + 1) * keep, at] for t in range(segments)]
            for source in range(half):
                real, imag = [], []
                for t in range(segments):
                    row = t * half + source
                    s_re, s_im = spread(src_re, block, row), spread(src_im, block, row)
                    real.append(s_re * r_re[t] + s_im * r_im[t])
                    imag.append(s_im * r_re[t] - s_re * r_im[t])
                to = slice(source * keep, (source + 1) * keep)
                share = segments // groups
                for place, part in enumerate((real, imag)):
                    for group in range(groups):
                        value = functools.reduce(jnp.add, part[group * share : (group + 1) * share])
                        first = (place * groups + group) * CHUNK + sub * LANES
                        cross[chunk, to, first : first + LANES] = value

    def project(chunk):
        value = cross[chunk].astype(jnp.bfloat16)
        parts = []
        for place in range(2):
            first = place * nbins + chunk * CHUNK
            table = table_ref[first : first + CHUNK]
            parts.append(
                jnp.dot(
                    value[:, place * groups * CHUNK : (place + 1) * groups * CHUNK],
                    jnp.concatenate([table] * groups, axis=0),
                    preferred_element_type=jnp.float32,
                )
            )
        return parts

    parts = []
    chunks = nbins // CHUNK
    for chunk in range(chunks + 1):
        if chunk < chunks:
            multiply(chunk)
        if chunk > 0:
            parts.append(project(chunk - 1))
    total_re, total_im = (functools.reduce(jnp.add, part) for part in zip(*parts))

    lags = result.shape[1]
    scale = 2.0 / math.sqrt(nbins)
    mirror = LAG - FIRST_LAG - iota((keep, LANES), 1)
    for source in range(half):
        common = 0.0
        for t in range(segments):
            row = t * half + source
            common = common + src_valid[row : row + 1] * rcv_valid[t * keep : (t + 1) * keep, :]
        weight = scale / jnp.maximum(common, 1.0)
        to = slice(source * keep, (source + 1) * keep)
        even, odd = total_re[to], total_im[to]
        ahead = even + odd
        behind = even - odd
        low_part = jnp.take_along_axis(
            behind[:, :LANES], jnp.clip(mirror, 0, LANES - 1), axis=1
        )
        high_part = jnp.take_along_axis(
            behind[:, LANES:], jnp.clip(mirror - LANES, 0, LANES - 1), axis=1
        )
        result[to, :LANES] = jnp.where(mirror < LANES, low_part, high_part) * weight
        for first in range(0, lags - LANES, LANES):
            last = min(first + LANES, lags - LANES)
            value = ahead[:, first : first + LANES] * weight
            result[to, LANES + first : LANES + last] = value[:, : last - first]
        if rest and (source + 1) % pieces == 0:
            first, count = (source + 1 - pieces) * keep, pieces * keep
            at = pl.multiple_of((1 - part) * rows + first, count)
            copies.append(
                pltpu.make_async_copy(
                    result.at[pl.ds(first, count)],
                    out_ref.at[pl.ds(at, count)],
                    written.at[1 + source // pieces],
                )
            )
            copies[-1].start()
    if rest:
        for copy in copies:
            copy.wait()


def encode(segments, spectra, valid, sources):
    channels, width = spectra.shape
    keep = channels // segments
    slab = jax.ShapeDtypeStruct((sources.size, width // 2), jnp.bfloat16)
    block = jax.ShapeDtypeStruct((keep, width), jnp.bfloat16)
    padded = pltpu.VMEM((sources.size, width // 2 + 2 * LANES), jnp.bfloat16)
    pinned = [pltpu.with_memory_space_constraint(x, pltpu.HBM) for x in (spectra, valid, sources)]
    return pl.pallas_call(
        functools.partial(encode_kernel, segments),
        out_shape=(slab, slab) + (block,) * segments,
        in_specs=[HBM] * 3,
        out_specs=(VMEM,) * (2 + segments),
        scratch_shapes=[
            pltpu.VMEM((channels, width), kind_for(keep)),
            pltpu.VMEM((channels, width), jnp.bfloat16),
            pltpu.VMEM((1, channels), jnp.int32),
            pltpu.SMEM(sources.shape, jnp.int32),
            padded,
            padded,
            pltpu.SemaphoreType.DMA((3,)),
        ],
        compiler_params=pltpu.CompilerParams(vmem_limit_bytes=12 * MEBI),
        name="encode_and_pick",
    )(*pinned)


def whiten_blocks(blocks):
    segments, (keep, width) = len(blocks), blocks[0].shape
    count, nbins = segments * keep, width // 2
    padded = pltpu.VMEM((count, nbins + 2 * LANES), jnp.bfloat16)
    part = jax.ShapeDtypeStruct((count, nbins), kind_for(keep))
    return pl.pallas_call(
        functools.partial(whiten_kernel, segments),
        out_shape=(part, part, jax.ShapeDtypeStruct((count, LANES), jnp.float32)),
        in_specs=[VMEM] * segments,
        out_specs=(VMEM,) * 3,
        scratch_shapes=[padded, padded],
        compiler_params=pltpu.CompilerParams(vmem_limit_bytes=20 * MEBI),
        cost_estimate=pl.CostEstimate(
            flops=count * width * 1024, bytes_accessed=count * width * 4, transcendentals=0
        ),
        name="whiten_receivers",
    )(*blocks)


def stack_half(segments, slabs, receivers, table, rest=()):
    half, nbins = slabs.shape[0] // (2 * segments), slabs.shape[1]
    keep = receivers[0].shape[0] // segments
    count, rows, lags = segments * half, half * keep, 2 * LAG + 1
    kind = receivers[0].dtype
    groups = total_groups(segments, kind)
    part = pltpu.VMEM((nbins // LANES, count, LANES), jnp.float32)
    cross = pltpu.VMEM((nbins // CHUNK, rows, 2 * groups * CHUNK), kind)
    scratch = [part, part, cross]
    if rest:
        scratch += [pltpu.VMEM((rows, lags), jnp.float32), pltpu.SemaphoreType.DMA((1 + half,))]
    return pl.pallas_call(
        functools.partial(stack_kernel, segments),
        out_shape=jax.ShapeDtypeStruct((2 * rows if rest else rows, lags), jnp.float32),
        in_specs=[VMEM] * (5 + len(rest)),
        out_specs=HBM if rest else VMEM,
        scratch_shapes=scratch,
        compiler_params=pltpu.CompilerParams(vmem_limit_bytes=20 * MEBI),
        cost_estimate=pl.CostEstimate(
            flops=4 * rows * nbins * 2 * LAG, bytes_accessed=nbins * 2048, transcendentals=0
        ),
        name="stack_other_half" if rest else "stack_own_half",
    )(slabs, *receivers, table, *rest)


def swapped(value, axis, size, step):
    return lax.ppermute(value, axis, [(i, i ^ step) for i in range(size)])


def shards(rcv_size, tm_size, spectra, valid, sources):
    channels, _, width = spectra.shape
    keep = channels // tm_size
    rounds, per_round = sources.shape
    own, other, *receivers = encode(
        tm_size, spectra[:, 0, :], valid.reshape(1, channels), sources
    )
    receivers[-1] = swapped(receivers[-1], "tm", tm_size, tm_size - 1)
    own = own + swapped(other, "rcv", rcv_size, 1)
    step = 2
    while step < rcv_size:
        wide = min(4, rcv_size // step)
        parts = [swapped(own, "rcv", rcv_size, place * step) for place in range(wide - 1, 0, -1)]
        if step == 2:
            parts[-1], later = lax.optimization_barrier((parts[-1], receivers[1:-1]))
            receivers[1:-1] = [
                swapped(block, "tm", tm_size, place) for place, block in enumerate(later, 1)
            ]
            parts[0], receivers[-1] = lax.optimization_barrier((parts[0], receivers[-1]))
        own = functools.reduce(jnp.add, parts[::-1], own)
        step *= wide
    own = [own] + [swapped(own, "tm", tm_size, place) for place in range(1, tm_size)]
    whitened = whiten_blocks(receivers)
    own, whitened = lax.optimization_barrier((own, whitened))
    own = jnp.concatenate(own, axis=0)
    other = swapped(own, "rcv", rcv_size, 1)

    table = jnp.asarray(lag_table(width // 2))
    first = stack_half(tm_size, own, whitened, table)
    stack = stack_half(tm_size, other, whitened, table, (first,))
    return stack.reshape(rounds, per_round, keep, 2 * LAG + 1)


def solution(mesh):
    body = functools.partial(shards, mesh.shape["rcv"], mesh.shape["tm"])
    in_specs = (P("rcv", "tm", None), P("rcv", "tm"), P())
    out_specs = P(None, None, ("rcv", "tm"), None)
    return jax.shard_map(body, mesh=mesh, in_specs=in_specs, out_specs=out_specs, check_vma=False)
```

```python
import functools
import math

import jax
import jax.numpy as jnp
import numpy as np
from jax import lax
from jax.experimental import pallas as pl
from jax.experimental.pallas import tpu as pltpu
from jax.sharding import PartitionSpec as P

NT = 4096
LAG = 150
HALF_WIN = 64
EPSILON = 1e-06

UNUSABLE = 1024.0
USABLE_BELOW = 512.0

LANES = 128
BLOCK = 256
CHUNK = 512
MEBI = 1 << 20
FIRST_LAG = LANES - LAG
VMEM = pl.BlockSpec(memory_space=pltpu.VMEM)
HBM = pl.BlockSpec(memory_space=pltpu.HBM)


def lag_table(nbins):
    winding = np.mod(
        np.arange(1, nbins + 1, dtype=np.int64)[:, None]
        * np.arange(FIRST_LAG, FIRST_LAG + BLOCK, dtype=np.int64)[None, :],
        NT,
    )
    theta = winding * (2.0 * math.pi / NT)
    return np.concatenate([np.cos(theta), -np.sin(theta)], axis=0).astype(jnp.bfloat16)


def kind_for(rows):
    return jnp.bfloat16 if rows % 16 == 0 else jnp.float32


def iota(shape, dim):
    return lax.broadcasted_iota(jnp.int32, shape, dim)


def whitening(real, imag, high, low, unusable=0.0):
    count, nbins = real.shape
    blocks = nbins // BLOCK
    span = BLOCK + 2 * LANES
    amplitude = jnp.sqrt(real * real + imag * imag)
    rounded = amplitude.astype(jnp.bfloat16)
    edge = jnp.zeros((count, LANES), jnp.bfloat16)
    for part, value in (
        (high, rounded),
        (low, (amplitude - rounded.astype(jnp.float32)).astype(jnp.bfloat16)),
    ):
        part[:, :LANES] = edge
        part[:, LANES : LANES + nbins] = value
        part[:, LANES + nbins :] = edge
    near = jnp.abs(iota((span, BLOCK), 0) - LANES - iota((span, BLOCK), 1)) <= HALF_WIN
    band = jnp.where(near, 1.0, 0.0).astype(jnp.bfloat16)
    pieces = [
        part[:, block * BLOCK : block * BLOCK + span] for block in range(blocks) for part in (high, low)
    ]
    windows = jnp.dot(
        jnp.concatenate(pieces, axis=0), band, preferred_element_type=jnp.float32
    )
    for block in range(blocks):
        first = block * BLOCK
        at = 2 * block * count
        window = windows[at : at + count] + windows[at + count : at + 2 * count]
        index = first + iota((1, BLOCK), 1)
        counted = jnp.minimum(index, HALF_WIN) + jnp.minimum(nbins - 1 - index, HALF_WIN) + 1
        factor = 1.0 / (window / counted.astype(jnp.float32) + EPSILON)
        re = real[:, first : first + BLOCK]
        im = imag[:, first : first + BLOCK]
        usable = re < USABLE_BELOW
        re = jnp.where(usable, re * factor, unusable).astype(jnp.bfloat16).astype(jnp.float32)
        im = jnp.where(usable, im * factor, unusable).astype(jnp.bfloat16).astype(jnp.float32)
        yield slice(first, first + BLOCK), re, im


def usable_rows(real):
    return jnp.where(real[:, :LANES] < USABLE_BELOW, 1.0, 0.0)


def encode_kernel(
    segments, spectra_ref, valid_ref, sources_ref, picked_ref, *refs
):
    blocks, refs = refs[:segments], refs[segments:]
    encoded_ref, spectra, valid, sources, high, low, arrived = refs
    copies = [
        pltpu.make_async_copy(spectra_ref, spectra, arrived.at[0]),
        pltpu.make_async_copy(sources_ref, sources, arrived.at[1]),
        pltpu.make_async_copy(valid_ref, valid, arrived.at[2]),
    ]
    for copy in copies:
        copy.start()
    channels, width = spectra_ref.shape
    nbins = width // 2
    rounds, per_round = sources.shape
    count = rounds * per_round
    first_channel = lax.axis_index("rcv") * channels
    copies[1].wait()
    copies[2].wait()
    diagonal = iota((channels, channels), 0) == iota((channels, channels), 1)
    usable = jnp.sum(jnp.where(diagonal, valid[...], 0), axis=1, keepdims=True) != 0
    row = iota((count, channels), 0)
    local = jnp.zeros((count, channels), jnp.int32)
    for place in range(count):
        here = sources[place // per_round, place % per_round] - first_channel
        local = jnp.where(row == place, here, local)
    onehot = jnp.where(local == iota((count, channels), 1), 1.0, 0.0).astype(jnp.bfloat16)
    copies[0].wait()
    encoded = jnp.where(usable, spectra[...].astype(jnp.float32), UNUSABLE).astype(jnp.bfloat16)
    picked = jnp.dot(onehot, encoded, preferred_element_type=jnp.float32)
    for at, re, im in whitening(picked[:, :nbins], picked[:, nbins:], high, low, UNUSABLE):
        picked_ref[:count, at] = re.astype(picked_ref.dtype)
        picked_ref[count:, at] = im.astype(picked_ref.dtype)
    encoded_ref[...] = encoded.astype(encoded_ref.dtype)
    keep = channels // segments
    for step, block in enumerate(blocks):
        at = pl.multiple_of((lax.axis_index("tm") ^ step) * keep, keep)
        block[...] = encoded_ref[pl.ds(at, keep), :].astype(block.dtype)


def whiten_kernel(segments, *refs):
    blocks, (real_ref, imag_ref, valid_ref, high, low) = refs[:segments], refs[segments:]
    rows = jnp.concatenate([ref[...].astype(jnp.float32) for ref in blocks], axis=0)
    nbins = rows.shape[1] // 2
    real, imag = rows[:, :nbins], rows[:, nbins:]
    for at, re, im in whitening(real, imag, high, low):
        real_ref[:, at] = re.astype(real_ref.dtype)
        imag_ref[:, at] = im.astype(imag_ref.dtype)
    valid_ref[...] = usable_rows(real)


def total_groups(segments, kind):
    return -(-segments // 2) if kind == jnp.bfloat16 and segments % 2 == 0 else 1


def stack_kernel(
    segments, slabs_ref, rcv_re, rcv_im, rcv_valid, table_ref, out_ref,
    src_re, src_im, cross, result, written
):
    half = slabs_ref.shape[0] // (2 * segments)
    nbins = slabs_ref.shape[1]
    keep = rcv_re.shape[0] // segments
    pieces = max(1, half // 8)
    copies = []
    slabs = slabs_ref[...].astype(jnp.float32)
    real = jnp.concatenate(
        [slabs[2 * half * t : 2 * half * t + half] for t in range(segments)], axis=0
    )
    imag = jnp.concatenate(
        [slabs[2 * half * t + half : 2 * half * (t + 1)] for t in range(segments)], axis=0
    )
    usable = real < USABLE_BELOW
    for ref, value in ((src_re, real), (src_im, imag)):
        value = jnp.where(usable, value, 0.0)
        for block in range(nbins // LANES):
            ref[block] = value[:, block * LANES : (block + 1) * LANES]
    src_valid = usable_rows(real)
    kind = rcv_re.dtype
    groups = total_groups(segments, kind)

    def spread(ref, block, row):
        tile = ref[block, pl.ds(row, 8, stride=0), :]
        return jnp.concatenate([tile] * (keep // 8), axis=0).astype(kind)

    def multiply(chunk):
        for sub in range(CHUNK // LANES):
            block = chunk * (CHUNK // LANES) + sub
            at = slice(block * LANES, (block + 1) * LANES)
            r_re = [rcv_re[t * keep : (t + 1) * keep, at] for t in range(segments)]
            r_im = [rcv_im[t * keep : (t + 1) * keep, at] for t in range(segments)]
            for source in range(half):
                real, imag = [], []
                for t in range(segments):
                    row = t * half + source
                    s_re, s_im = spread(src_re, block, row), spread(src_im, block, row)
                    real.append(s_re * r_re[t] + s_im * r_im[t])
                    imag.append(s_im * r_re[t] - s_re * r_im[t])
                to = slice(source * keep, (source + 1) * keep)
                share = segments // groups
                for place, part in enumerate((real, imag)):
                    for group in range(groups):
                        value = functools.reduce(jnp.add, part[group * share : (group + 1) * share])
                        first = (place * groups + group) * CHUNK + sub * LANES
                        cross[chunk, to, first : first + LANES] = value

    def project(chunk):
        value = cross[chunk].astype(jnp.bfloat16)
        parts = []
        for place in range(2):
            first = place * nbins + chunk * CHUNK
            table = table_ref[first : first + CHUNK]
            parts.append(
                jnp.dot(
                    value[:, place * groups * CHUNK : (place + 1) * groups * CHUNK],
                    jnp.concatenate([table] * groups, axis=0),
                    preferred_element_type=jnp.float32,
                )
            )
        return parts

    parts = []
    chunks = nbins // CHUNK
    for chunk in range(chunks + 1):
        if chunk < chunks:
            multiply(chunk)
        if chunk > 0:
            parts.append(project(chunk - 1))
    total_re, total_im = (functools.reduce(jnp.add, part) for part in zip(*parts))

    lags = result.shape[1]
    scale = 2.0 / math.sqrt(nbins)
    mirror = LAG - FIRST_LAG - iota((keep, LANES), 1)
    for source in range(half):
        common = 0.0
        for t in range(segments):
            row = t * half + source
            common = common + src_valid[row : row + 1] * rcv_valid[t * keep : (t + 1) * keep, :]
        weight = scale / jnp.maximum(common, 1.0)
        to = slice(source * keep, (source + 1) * keep)
        even, odd = total_re[to], total_im[to]
        ahead = even + odd
        behind = even - odd
        low_part = jnp.take_along_axis(
            behind[:, :LANES], jnp.clip(mirror, 0, LANES - 1), axis=1
        )
        high_part = jnp.take_along_axis(
            behind[:, LANES:], jnp.clip(mirror - LANES, 0, LANES - 1), axis=1
        )
        result[to, :LANES] = jnp.where(mirror < LANES, low_part, high_part) * weight
        for first in range(0, lags - LANES, LANES):
            last = min(first + LANES, lags - LANES)
            value = ahead[:, first : first + LANES] * weight
            result[to, LANES + first : LANES + last] = value[:, : last - first]
        if (source + 1) % pieces == 0:
            at = pl.ds((source + 1 - pieces) * keep, pieces * keep)
            copies.append(
                pltpu.make_async_copy(
                    result.at[at], out_ref.at[at], written.at[source // pieces]
                )
            )
            copies[-1].start()
    for copy in copies:
        copy.wait()


def encode(segments, spectra, valid, sources):
    channels, width = spectra.shape
    keep = channels // segments
    slab = jax.ShapeDtypeStruct((2 * sources.size, width // 2), jnp.bfloat16)
    block = jax.ShapeDtypeStruct((keep, width), jnp.bfloat16)
    padded = pltpu.VMEM((sources.size, width // 2 + 2 * LANES), jnp.bfloat16)
    pinned = [pltpu.with_memory_space_constraint(x, pltpu.HBM) for x in (spectra, valid, sources)]
    return pl.pallas_call(
        functools.partial(encode_kernel, segments),
        out_shape=(slab,) + (block,) * segments,
        in_specs=[HBM] * 3,
        out_specs=(VMEM,) * (1 + segments),
        scratch_shapes=[
            pltpu.VMEM((channels, width), kind_for(keep)),
            pltpu.VMEM((channels, width), jnp.bfloat16),
            pltpu.VMEM((1, channels), jnp.int32),
            pltpu.SMEM(sources.shape, jnp.int32),
            padded,
            padded,
            pltpu.SemaphoreType.DMA((3,)),
        ],
        compiler_params=pltpu.CompilerParams(vmem_limit_bytes=12 * MEBI),
        name="encode_and_pick",
    )(*pinned)


def whiten_blocks(blocks):
    segments, (keep, width) = len(blocks), blocks[0].shape
    count, nbins = segments * keep, width // 2
    padded = pltpu.VMEM((count, nbins + 2 * LANES), jnp.bfloat16)
    part = jax.ShapeDtypeStruct((count, nbins), kind_for(keep))
    return pl.pallas_call(
        functools.partial(whiten_kernel, segments),
        out_shape=(part, part, jax.ShapeDtypeStruct((count, LANES), jnp.float32)),
        in_specs=[VMEM] * segments,
        out_specs=(VMEM,) * 3,
        scratch_shapes=[padded, padded],
        compiler_params=pltpu.CompilerParams(vmem_limit_bytes=20 * MEBI),
        cost_estimate=pl.CostEstimate(
            flops=count * width * 1024, bytes_accessed=count * width * 4, transcendentals=0
        ),
        name="whiten_receivers",
    )(*blocks)


def stack_all(segments, slabs, receivers, table):
    count, nbins = slabs.shape[0] // 2, slabs.shape[1]
    keep = receivers[0].shape[0] // segments
    sources = count // segments
    rows, lags = sources * keep, 2 * LAG + 1
    kind = receivers[0].dtype
    groups = total_groups(segments, kind)
    part = pltpu.VMEM((nbins // LANES, count, LANES), jnp.float32)
    return pl.pallas_call(
        functools.partial(stack_kernel, segments),
        out_shape=jax.ShapeDtypeStruct((rows, lags), jnp.float32),
        in_specs=[VMEM] * 5,
        out_specs=HBM,
        scratch_shapes=[
            part,
            part,
            pltpu.VMEM((nbins // CHUNK, rows, 2 * groups * CHUNK), kind),
            pltpu.VMEM((rows, lags), jnp.float32),
            pltpu.SemaphoreType.DMA((sources,)),
        ],
        compiler_params=pltpu.CompilerParams(vmem_limit_bytes=28 * MEBI),
        cost_estimate=pl.CostEstimate(
            flops=4 * rows * nbins * 2 * LAG, bytes_accessed=nbins * 2048, transcendentals=0
        ),
        name="stack_sources",
    )(slabs, *receivers, table)


def swapped(value, axis, size, step):
    return lax.ppermute(value, axis, [(i, i ^ step) for i in range(size)])


def shards(rcv_size, tm_size, spectra, valid, sources):
    channels, _, width = spectra.shape
    keep = channels // tm_size
    rounds, per_round = sources.shape
    picked, *receivers = encode(
        tm_size, spectra[:, 0, :], valid.reshape(1, channels), sources
    )
    axes = ("rcv", "tm")
    seconds = range(1, rcv_size, 2)

    def among_seconds(value, rcv_step, tm_step):
        pairs = [
            (rcv * tm_size + tm, (rcv ^ rcv_step) * tm_size + (tm ^ tm_step))
            for rcv in seconds
            for tm in range(tm_size)
        ]
        return lax.ppermute(value, axes, pairs)

    receivers[-1] = swapped(receivers[-1], "tm", tm_size, tm_size - 1)
    own = picked + lax.ppermute(picked, "rcv", [(rcv - 1, rcv) for rcv in seconds])
    step = 2
    while step < rcv_size:
        wide = min(4, rcv_size // step)
        parts = [among_seconds(own, place * step, 0) for place in range(wide - 1, 0, -1)]
        if step == 2:
            parts[-1], later = lax.optimization_barrier((parts[-1], receivers[1:-1]))
            receivers[1:-1] = [
                swapped(block, "tm", tm_size, place) for place, block in enumerate(later, 1)
            ]
            parts[0], receivers[-1] = lax.optimization_barrier((parts[0], receivers[-1]))
        own = functools.reduce(jnp.add, parts[::-1], own)
        step *= wide
    own = [own] + [among_seconds(own, 0, place) for place in range(1, tm_size)]
    whitened = whiten_blocks(receivers)
    own, whitened = lax.optimization_barrier((own, whitened))
    own = jnp.concatenate(own, axis=0)
    handed = lax.ppermute(own, "rcv", [(rcv, rcv - 1) for rcv in seconds])
    own = jnp.where(lax.axis_index("rcv") % 2 == 1, own, handed)

    stack = stack_all(tm_size, own, whitened, jnp.asarray(lag_table(width // 2)))
    return stack.reshape(rounds, per_round, keep, 2 * LAG + 1)


def solution(mesh):
    body = functools.partial(shards, mesh.shape["rcv"], mesh.shape["tm"])
    in_specs = (P("rcv", "tm", None), P("rcv", "tm"), P())
    out_specs = P(None, None, ("rcv", "tm"), None)
    return jax.shard_map(body, mesh=mesh, in_specs=in_specs, out_specs=out_specs, check_vma=False)
```

```python
import functools
import math

import jax
import jax.numpy as jnp
import numpy as np
from jax import lax
from jax.experimental import pallas as pl
from jax.experimental.pallas import tpu as pltpu
from jax.sharding import PartitionSpec as P

NT = 4096
LAG = 150
HALF_WIN = 64
EPSILON = 1e-06

UNUSABLE = 1024.0
USABLE_BELOW = 512.0

LANES = 128
BLOCK = 256
CHUNK = 512
MEBI = 1 << 20
FIRST_LAG = LANES - LAG
VMEM = pl.BlockSpec(memory_space=pltpu.VMEM)
HBM = pl.BlockSpec(memory_space=pltpu.HBM)


def lag_table(nbins):
    winding = np.mod(
        np.arange(1, nbins + 1, dtype=np.int64)[:, None]
        * np.arange(FIRST_LAG, FIRST_LAG + BLOCK, dtype=np.int64)[None, :],
        NT,
    )
    theta = winding * (2.0 * math.pi / NT)
    return np.concatenate([np.cos(theta), -np.sin(theta)], axis=0).astype(jnp.bfloat16)


def kind_for(rows):
    return jnp.bfloat16 if rows % 16 == 0 else jnp.float32


def iota(shape, dim):
    return lax.broadcasted_iota(jnp.int32, shape, dim)


def whitening(real, imag, high, low, unusable=0.0):
    count, nbins = real.shape
    blocks = nbins // BLOCK
    span = BLOCK + 2 * LANES
    amplitude = jnp.sqrt(real * real + imag * imag)
    rounded = amplitude.astype(jnp.bfloat16)
    edge = jnp.zeros((count, LANES), jnp.bfloat16)
    for part, value in (
        (high, rounded),
        (low, (amplitude - rounded.astype(jnp.float32)).astype(jnp.bfloat16)),
    ):
        part[:, :LANES] = edge
        part[:, LANES : LANES + nbins] = value
        part[:, LANES + nbins :] = edge
    near = jnp.abs(iota((span, BLOCK), 0) - LANES - iota((span, BLOCK), 1)) <= HALF_WIN
    band = jnp.where(near, 1.0, 0.0).astype(jnp.bfloat16)
    pieces = [
        part[:, block * BLOCK : block * BLOCK + span] for block in range(blocks) for part in (high, low)
    ]
    windows = jnp.dot(
        jnp.concatenate(pieces, axis=0), band, preferred_element_type=jnp.float32
    )
    for block in range(blocks):
        first = block * BLOCK
        at = 2 * block * count
        window = windows[at : at + count] + windows[at + count : at + 2 * count]
        index = first + iota((1, BLOCK), 1)
        counted = jnp.minimum(index, HALF_WIN) + jnp.minimum(nbins - 1 - index, HALF_WIN) + 1
        factor = 1.0 / (window / counted.astype(jnp.float32) + EPSILON)
        re = real[:, first : first + BLOCK]
        im = imag[:, first : first + BLOCK]
        usable = re < USABLE_BELOW
        re = jnp.where(usable, re * factor, unusable).astype(jnp.bfloat16).astype(jnp.float32)
        im = jnp.where(usable, im * factor, unusable).astype(jnp.bfloat16).astype(jnp.float32)
        yield slice(first, first + BLOCK), re, im


def usable_rows(real):
    return jnp.where(real[:, :LANES] < USABLE_BELOW, 1.0, 0.0)


def encode_kernel(
    segments, spectra_ref, valid_ref, sources_ref, own_ref, other_ref, *refs
):
    blocks, refs = refs[:segments], refs[segments:]
    encoded_ref, spectra, valid, sources, high, low, arrived = refs
    copies = [
        pltpu.make_async_copy(spectra_ref, spectra, arrived.at[0]),
        pltpu.make_async_copy(sources_ref, sources, arrived.at[1]),
        pltpu.make_async_copy(valid_ref, valid, arrived.at[2]),
    ]
    for copy in copies:
        copy.start()
    channels, width = spectra_ref.shape
    nbins = width // 2
    rounds, per_round = sources.shape
    half = rounds * per_round // 2
    index = lax.axis_index("rcv")
    copies[1].wait()
    copies[2].wait()
    diagonal = iota((channels, channels), 0) == iota((channels, channels), 1)
    usable = jnp.sum(jnp.where(diagonal, valid[...], 0), axis=1, keepdims=True) != 0
    row = iota((2 * half, channels), 0)
    local = jnp.zeros((2 * half, channels), jnp.int32)
    for place in range(2 * half):
        number = (index % 2 if place < half else 1 - index % 2) * half + place % half
        here = sources[number // per_round, number % per_round] - index * channels
        local = jnp.where(row == place, here, local)
    onehot = jnp.where(local == iota((2 * half, channels), 1), 1.0, 0.0).astype(jnp.bfloat16)
    copies[0].wait()
    encoded = jnp.where(usable, spectra[...].astype(jnp.float32), UNUSABLE).astype(jnp.bfloat16)
    picked = jnp.dot(onehot, encoded, preferred_element_type=jnp.float32)
    for at, re, im in whitening(picked[:, :nbins], picked[:, nbins:], high, low, UNUSABLE):
        for first, ref in ((0, own_ref), (half, other_ref)):
            rows = slice(first, first + half)
            ref[:, at] = jnp.concatenate([re[rows], im[rows]], axis=0).astype(ref.dtype)
    encoded_ref[...] = encoded.astype(encoded_ref.dtype)
    keep = channels // segments
    for step, block in enumerate(blocks):
        at = pl.multiple_of((lax.axis_index("tm") ^ step) * keep, keep)
        block[...] = encoded_ref[pl.ds(at, keep), :].astype(block.dtype)


def whiten_kernel(segments, *refs):
    blocks, refs = refs[:segments], refs[segments:]
    real_ref, imag_ref, both_ref, valid_ref, high, low = refs
    rows = jnp.concatenate([ref[...].astype(jnp.float32) for ref in blocks], axis=0)
    nbins = rows.shape[1] // 2
    real, imag = rows[:, :nbins], rows[:, nbins:]
    for at, re, im in whitening(real, imag, high, low):
        real_ref[:, at] = re
        imag_ref[:, at] = im
        both_ref[:, at] = re + im
    valid_ref[...] = usable_rows(real)


def stack_kernel(
    segments, slabs_ref, rcv_re, rcv_im, rcv_both, rcv_valid, table_ref, *refs
):
    *rest, out_ref, src_re, src_diff, src_sum, cross = refs[: 6 if len(refs) == 8 else 5]
    half = slabs_ref.shape[0] // (2 * segments)
    nbins = slabs_ref.shape[1]
    keep = rcv_re.shape[0] // segments
    rows = half * keep
    if rest:
        result, written = refs[6:]
        part = lax.axis_index("rcv") % 2
        pieces = max(1, half // 4)
        at = pl.multiple_of(part * rows, rows)
        copies = [
            pltpu.make_async_copy(rest[0], out_ref.at[pl.ds(at, rows)], written.at[0])
        ]
        copies[0].start()
    else:
        result = out_ref
    slabs = slabs_ref[...].astype(jnp.float32)
    real = jnp.concatenate(
        [slabs[2 * half * t : 2 * half * t + half] for t in range(segments)], axis=0
    )
    imag = jnp.concatenate(
        [slabs[2 * half * t + half : 2 * half * (t + 1)] for t in range(segments)], axis=0
    )
    usable = real < USABLE_BELOW
    real, imag = jnp.where(usable, real, 0.0), jnp.where(usable, imag, 0.0)
    src_valid = jnp.where(usable[:, :LANES], 1.0, 0.0)
    for ref, value in ((src_re, real), (src_diff, imag - real), (src_sum, imag + real)):
        for block in range(nbins // LANES):
            ref[block] = value[:, block * LANES : (block + 1) * LANES]
    tile = min(keep, 16)

    def spread(ref, block, row):
        return jnp.concatenate([ref[block, pl.ds(row, 8, stride=0), :]] * (tile // 8), axis=0)

    def multiply(chunk):
        for sub in range(CHUNK // LANES):
            block = chunk * (CHUNK // LANES) + sub
            at = slice(block * LANES, (block + 1) * LANES)
            for first in range(0, keep, tile):
                rows = [slice(t * keep + first, t * keep + first + tile) for t in range(segments)]
                r_re = [rcv_re[row, at] for row in rows]
                r_im = [rcv_im[row, at] for row in rows]
                r_both = [rcv_both[row, at] for row in rows]
                for source in range(half):
                    p, q, w = [], [], []
                    for t in range(segments):
                        row = t * half + source
                        p.append(spread(src_re, block, row) * r_both[t])
                        q.append(spread(src_diff, block, row) * r_im[t])
                        w.append(spread(src_sum, block, row) * r_re[t])
                    p, q, w = (functools.reduce(jnp.add, part) for part in (p, q, w))
                    to = slice(source * keep + first, source * keep + first + tile)
                    lanes = slice(sub * LANES, (sub + 1) * LANES)
                    cross[chunk, 0, to, lanes] = (p + q).astype(cross.dtype)
                    cross[chunk, 1, to, lanes] = (w - p).astype(cross.dtype)

    def project(chunk):
        parts = []
        for place in range(2):
            first = place * nbins + chunk * CHUNK
            parts.append(
                jnp.dot(
                    cross[chunk, place].astype(jnp.bfloat16),
                    table_ref[first : first + CHUNK],
                    preferred_element_type=jnp.float32,
                )
            )
        return parts

    parts = []
    chunks = nbins // CHUNK
    for chunk in range(chunks + 1):
        if chunk < chunks:
            multiply(chunk)
        if chunk > 0:
            parts.append(project(chunk - 1))
    total_re, total_im = (functools.reduce(jnp.add, part) for part in zip(*parts))

    lags = result.shape[1]
    scale = 2.0 / math.sqrt(nbins)
    mirror = LAG - FIRST_LAG - iota((keep, LANES), 1)
    for source in range(half):
        common = 0.0
        for t in range(segments):
            row = t * half + source
            common = common + src_valid[row : row + 1] * rcv_valid[t * keep : (t + 1) * keep, :]
        weight = scale / jnp.maximum(common, 1.0)
        to = slice(source * keep, (source + 1) * keep)
        even, odd = total_re[to], total_im[to]
        ahead = even + odd
        behind = even - odd
        low_part = jnp.take_along_axis(
            behind[:, :LANES], jnp.clip(mirror, 0, LANES - 1), axis=1
        )
        high_part = jnp.take_along_axis(
            behind[:, LANES:], jnp.clip(mirror - LANES, 0, LANES - 1), axis=1
        )
        result[to, :LANES] = jnp.where(mirror < LANES, low_part, high_part) * weight
        for first in range(0, lags - LANES, LANES):
            last = min(first + LANES, lags - LANES)
            value = ahead[:, first : first + LANES] * weight
            result[to, LANES + first : LANES + last] = value[:, : last - first]
        if rest and (source + 1) % pieces == 0:
            first, count = (source + 1 - pieces) * keep, pieces * keep
            at = pl.multiple_of((1 - part) * rows + first, count)
            copies.append(
                pltpu.make_async_copy(
                    result.at[pl.ds(first, count)],
                    out_ref.at[pl.ds(at, count)],
                    written.at[1 + source // pieces],
                )
            )
            copies[-1].start()
    if rest:
        for copy in copies:
            copy.wait()


def encode(segments, spectra, valid, sources):
    channels, width = spectra.shape
    keep = channels // segments
    slab = jax.ShapeDtypeStruct((sources.size, width // 2), jnp.bfloat16)
    block = jax.ShapeDtypeStruct((keep, width), jnp.bfloat16)
    padded = pltpu.VMEM((sources.size, width // 2 + 2 * LANES), jnp.bfloat16)
    pinned = [pltpu.with_memory_space_constraint(x, pltpu.HBM) for x in (spectra, valid, sources)]
    return pl.pallas_call(
        functools.partial(encode_kernel, segments),
        out_shape=(slab, slab) + (block,) * segments,
        in_specs=[HBM] * 3,
        out_specs=(VMEM,) * (2 + segments),
        scratch_shapes=[
            pltpu.VMEM((channels, width), kind_for(keep)),
            pltpu.VMEM((channels, width), jnp.bfloat16),
            pltpu.VMEM((1, channels), jnp.int32),
            pltpu.SMEM(sources.shape, jnp.int32),
            padded,
            padded,
            pltpu.SemaphoreType.DMA((3,)),
        ],
        compiler_params=pltpu.CompilerParams(vmem_limit_bytes=12 * MEBI),
        name="encode_and_pick",
    )(*pinned)


def whiten_blocks(blocks):
    segments, (keep, width) = len(blocks), blocks[0].shape
    count, nbins = segments * keep, width // 2
    padded = pltpu.VMEM((count, nbins + 2 * LANES), jnp.bfloat16)
    part = jax.ShapeDtypeStruct((count, nbins), jnp.float32)
    return pl.pallas_call(
        functools.partial(whiten_kernel, segments),
        out_shape=(part, part, part, jax.ShapeDtypeStruct((count, LANES), jnp.float32)),
        in_specs=[VMEM] * segments,
        out_specs=(VMEM,) * 4,
        scratch_shapes=[padded, padded],
        compiler_params=pltpu.CompilerParams(vmem_limit_bytes=20 * MEBI),
        cost_estimate=pl.CostEstimate(
            flops=count * width * 1024, bytes_accessed=count * width * 4, transcendentals=0
        ),
        name="whiten_receivers",
    )(*blocks)


def stack_half(segments, slabs, receivers, table, rest=()):
    half, nbins = slabs.shape[0] // (2 * segments), slabs.shape[1]
    keep = receivers[0].shape[0] // segments
    count, rows, lags = segments * half, half * keep, 2 * LAG + 1
    part = pltpu.VMEM((nbins // LANES, count, LANES), jnp.float32)
    cross = pltpu.VMEM((nbins // CHUNK, 2, rows, CHUNK), kind_for(keep))
    scratch = [part, part, part, cross]
    if rest:
        scratch += [pltpu.VMEM((rows, lags), jnp.float32), pltpu.SemaphoreType.DMA((1 + half,))]
    return pl.pallas_call(
        functools.partial(stack_kernel, segments),
        out_shape=jax.ShapeDtypeStruct((2 * rows if rest else rows, lags), jnp.float32),
        in_specs=[VMEM] * (6 + len(rest)),
        out_specs=HBM if rest else VMEM,
        scratch_shapes=scratch,
        compiler_params=pltpu.CompilerParams(vmem_limit_bytes=20 * MEBI),
        cost_estimate=pl.CostEstimate(
            flops=4 * rows * nbins * 2 * LAG, bytes_accessed=nbins * 2048, transcendentals=0
        ),
        name="stack_other_half" if rest else "stack_own_half",
    )(slabs, *receivers, table, *rest)


def swapped(value, axis, size, step):
    return lax.ppermute(value, axis, [(i, i ^ step) for i in range(size)])


def shards(rcv_size, tm_size, spectra, valid, sources):
    channels, _, width = spectra.shape
    keep = channels // tm_size
    rounds, per_round = sources.shape
    own, other, *receivers = encode(
        tm_size, spectra[:, 0, :], valid.reshape(1, channels), sources
    )
    receivers[-1] = swapped(receivers[-1], "tm", tm_size, tm_size - 1)
    own = own + swapped(other, "rcv", rcv_size, 1)
    step = 2
    while step < rcv_size:
        wide = min(4, rcv_size // step)
        parts = [swapped(own, "rcv", rcv_size, place * step) for place in range(wide - 1, 0, -1)]
        if step == 2:
            parts[-1], later = lax.optimization_barrier((parts[-1], receivers[1:-1]))
            receivers[1:-1] = [
                swapped(block, "tm", tm_size, place) for place, block in enumerate(later, 1)
            ]
            parts[0], receivers[-1] = lax.optimization_barrier((parts[0], receivers[-1]))
        own = functools.reduce(jnp.add, parts[::-1], own)
        step *= wide
    own = [own] + [swapped(own, "tm", tm_size, place) for place in range(1, tm_size)]
    whitened = whiten_blocks(receivers)
    own, whitened = lax.optimization_barrier((own, whitened))
    own = jnp.concatenate(own, axis=0)
    other = swapped(own, "rcv", rcv_size, 1)

    table = jnp.asarray(lag_table(width // 2))
    first = stack_half(tm_size, own, whitened, table)
    stack = stack_half(tm_size, other, whitened, table, (first,))
    return stack.reshape(rounds, per_round, keep, 2 * LAG + 1)


def solution(mesh):
    body = functools.partial(shards, mesh.shape["rcv"], mesh.shape["tm"])
    in_specs = (P("rcv", "tm", None), P("rcv", "tm"), P())
    out_specs = P(None, None, ("rcv", "tm"), None)
    return jax.shard_map(body, mesh=mesh, in_specs=in_specs, out_specs=out_specs, check_vma=False)
```

```python
import functools
import math

import jax
import jax.numpy as jnp
import numpy as np
from jax import lax
from jax.experimental import pallas as pl
from jax.experimental.pallas import tpu as pltpu
from jax.sharding import PartitionSpec as P

NT = 4096
LAG = 150
HALF_WIN = 64
EPSILON = 1e-06

UNUSABLE = 1024.0
USABLE_BELOW = 512.0

LANES = 128
BLOCK = 256
CHUNK = 512
MEBI = 1 << 20
FIRST_LAG = LANES - LAG
VMEM = pl.BlockSpec(memory_space=pltpu.VMEM)
HBM = pl.BlockSpec(memory_space=pltpu.HBM)


def lag_table(nbins):
    winding = np.mod(
        np.arange(1, nbins + 1, dtype=np.int64)[:, None]
        * np.arange(FIRST_LAG, FIRST_LAG + BLOCK, dtype=np.int64)[None, :],
        NT,
    )
    theta = winding * (2.0 * math.pi / NT)
    return np.concatenate([np.cos(theta), -np.sin(theta)], axis=0).astype(jnp.bfloat16)


def kind_for(rows):
    return jnp.bfloat16 if rows % 16 == 0 else jnp.float32


def iota(shape, dim):
    return lax.broadcasted_iota(jnp.int32, shape, dim)


def whitening(real, imag, high, low, unusable=0.0):
    count, nbins = real.shape
    blocks = nbins // BLOCK
    span = BLOCK + 2 * LANES
    amplitude = jnp.sqrt(real * real + imag * imag)
    rounded = amplitude.astype(jnp.bfloat16)
    edge = jnp.zeros((count, LANES), jnp.bfloat16)
    for part, value in (
        (high, rounded),
        (low, (amplitude - rounded.astype(jnp.float32)).astype(jnp.bfloat16)),
    ):
        part[:, :LANES] = edge
        part[:, LANES : LANES + nbins] = value
        part[:, LANES + nbins :] = edge
    near = jnp.abs(iota((span, BLOCK), 0) - LANES - iota((span, BLOCK), 1)) <= HALF_WIN
    band = jnp.where(near, 1.0, 0.0).astype(jnp.bfloat16)
    pieces = [
        part[:, block * BLOCK : block * BLOCK + span] for block in range(blocks) for part in (high, low)
    ]
    windows = jnp.dot(
        jnp.concatenate(pieces, axis=0), band, preferred_element_type=jnp.float32
    )
    for block in range(blocks):
        first = block * BLOCK
        at = 2 * block * count
        window = windows[at : at + count] + windows[at + count : at + 2 * count]
        index = first + iota((1, BLOCK), 1)
        counted = jnp.minimum(index, HALF_WIN) + jnp.minimum(nbins - 1 - index, HALF_WIN) + 1
        factor = 1.0 / (window / counted.astype(jnp.float32) + EPSILON)
        re = real[:, first : first + BLOCK]
        im = imag[:, first : first + BLOCK]
        usable = re < USABLE_BELOW
        re = jnp.where(usable, re * factor, unusable).astype(jnp.bfloat16).astype(jnp.float32)
        im = jnp.where(usable, im * factor, unusable).astype(jnp.bfloat16).astype(jnp.float32)
        yield slice(first, first + BLOCK), re, im


def usable_rows(real):
    return jnp.where(real[:, :LANES] < USABLE_BELOW, 1.0, 0.0)


def encode_kernel(
    segments, spectra_ref, valid_ref, sources_ref, own_ref, other_ref, *refs
):
    blocks, refs = refs[:segments], refs[segments:]
    encoded_ref, spectra, valid, sources, high, low, arrived = refs
    copies = [
        pltpu.make_async_copy(spectra_ref, spectra, arrived.at[0]),
        pltpu.make_async_copy(sources_ref, sources, arrived.at[1]),
        pltpu.make_async_copy(valid_ref, valid, arrived.at[2]),
    ]
    for copy in copies:
        copy.start()
    channels, width = spectra_ref.shape
    nbins = width // 2
    rounds, per_round = sources.shape
    half = rounds * per_round // 2
    index = lax.axis_index("rcv")
    copies[1].wait()
    copies[2].wait()
    diagonal = iota((channels, channels), 0) == iota((channels, channels), 1)
    usable = jnp.sum(jnp.where(diagonal, valid[...], 0), axis=1, keepdims=True) != 0
    row = iota((2 * half, channels), 0)
    local = jnp.zeros((2 * half, channels), jnp.int32)
    for place in range(2 * half):
        number = (index % 2 if place < half else 1 - index % 2) * half + place % half
        here = sources[number // per_round, number % per_round] - index * channels
        local = jnp.where(row == place, here, local)
    onehot = jnp.where(local == iota((2 * half, channels), 1), 1.0, 0.0).astype(jnp.bfloat16)
    copies[0].wait()
    encoded = jnp.where(usable, spectra[...].astype(jnp.float32), UNUSABLE).astype(jnp.bfloat16)
    picked = jnp.dot(onehot, encoded, preferred_element_type=jnp.float32)
    for at, re, im in whitening(picked[:, :nbins], picked[:, nbins:], high, low, UNUSABLE):
        for first, ref in ((0, own_ref), (half, other_ref)):
            rows = slice(first, first + half)
            ref[:, at] = jnp.concatenate([re[rows], im[rows]], axis=0).astype(ref.dtype)
    encoded_ref[...] = encoded.astype(encoded_ref.dtype)
    keep = channels // segments
    for step, block in enumerate(blocks):
        at = pl.multiple_of((lax.axis_index("tm") ^ step) * keep, keep)
        block[...] = encoded_ref[pl.ds(at, keep), :].astype(block.dtype)


def whiten_kernel(segments, *refs):
    blocks, refs = refs[:segments], refs[segments:]
    real_ref, imag_ref, both_ref, valid_ref, high, low = refs
    rows = jnp.concatenate([ref[...].astype(jnp.float32) for ref in blocks], axis=0)
    nbins = rows.shape[1] // 2
    real, imag = rows[:, :nbins], rows[:, nbins:]
    for at, re, im in whitening(real, imag, high, low):
        real_ref[:, at] = re
        imag_ref[:, at] = im
        both_ref[:, at] = re + im
    valid_ref[...] = usable_rows(real)


def stack_kernel(
    segments, slabs_ref, rcv_re, rcv_im, rcv_both, rcv_valid, table_ref, *refs
):
    *rest, out_ref, src_re, src_diff, src_sum, cross = refs[: 6 if len(refs) == 8 else 5]
    half = slabs_ref.shape[0] // (2 * segments)
    nbins = slabs_ref.shape[1]
    keep = rcv_re.shape[0] // segments
    rows = half * keep
    if rest:
        result, written = refs[6:]
        part = lax.axis_index("rcv") % 2
        pieces = max(1, half // 4)
        at = pl.multiple_of(part * rows, rows)
        copies = [
            pltpu.make_async_copy(rest[0], out_ref.at[pl.ds(at, rows)], written.at[0])
        ]
        copies[0].start()
    else:
        result = out_ref
    slabs = slabs_ref[...].astype(jnp.float32)
    real = jnp.concatenate(
        [slabs[2 * half * t : 2 * half * t + half] for t in range(segments)], axis=0
    )
    imag = jnp.concatenate(
        [slabs[2 * half * t + half : 2 * half * (t + 1)] for t in range(segments)], axis=0
    )
    usable = real < USABLE_BELOW
    real, imag = jnp.where(usable, real, 0.0), jnp.where(usable, imag, 0.0)
    src_valid = jnp.where(usable[:, :LANES], 1.0, 0.0)
    for ref, value in ((src_re, real), (src_diff, imag - real), (src_sum, imag + real)):
        for block in range(nbins // LANES):
            ref[block] = value[:, block * LANES : (block + 1) * LANES]
    tile = min(keep, 16)

    def spread(ref, block, row):
        return jnp.concatenate([ref[block, pl.ds(row, 8, stride=0), :]] * (tile // 8), axis=0)

    def multiply(chunk, sub):
        block = chunk * (CHUNK // LANES) + sub
        at = slice(block * LANES, (block + 1) * LANES)
        lanes = slice(sub * LANES, (sub + 1) * LANES)
        for first in range(0, keep, tile):
            rows = [slice(t * keep + first, t * keep + first + tile) for t in range(segments)]
            r_re = [rcv_re[row, at] for row in rows]
            r_im = [rcv_im[row, at] for row in rows]
            r_both = [rcv_both[row, at] for row in rows]
            for source in range(half):
                p, q, w = [], [], []
                for t in range(segments):
                    row = t * half + source
                    p.append(spread(src_re, block, row) * r_both[t])
                    q.append(spread(src_diff, block, row) * r_im[t])
                    w.append(spread(src_sum, block, row) * r_re[t])
                p, q, w = (functools.reduce(jnp.add, part) for part in (p, q, w))
                to = slice(source * keep + first, source * keep + first + tile)
                cross[chunk, 0, to, lanes] = (p + q).astype(cross.dtype)
                cross[chunk, 1, to, lanes] = (w - p).astype(cross.dtype)

    def project(chunk, place, part):
        first = place * nbins + chunk * CHUNK
        return jnp.dot(
            cross[chunk, place, part].astype(jnp.bfloat16),
            table_ref[first : first + CHUNK],
            preferred_element_type=jnp.float32,
        )

    chunks, subs = nbins // CHUNK, CHUNK // LANES
    totals = [[], []]
    for chunk in range(chunks):
        for sub in range(subs):
            multiply(chunk, sub)
            if chunk > 0 and sub % (subs // 2) == 0:
                place = sub // (subs // 2)
                totals[place].append(project(chunk - 1, place, slice(None)))
    tops = [functools.reduce(jnp.add, part) for part in totals]
    ends = []
    for first in (0, half // 2):
        at = slice(first * keep, (first + half // 2) * keep)
        ends.append([tops[place][at] + project(chunks - 1, place, at) for place in range(2)])

    lags = result.shape[1]
    scale = 2.0 / math.sqrt(nbins)
    mirror = LAG - FIRST_LAG - iota((keep, LANES), 1)
    for source in range(half):
        common = 0.0
        for t in range(segments):
            row = t * half + source
            common = common + src_valid[row : row + 1] * rcv_valid[t * keep : (t + 1) * keep, :]
        weight = scale / jnp.maximum(common, 1.0)
        to = slice(source * keep, (source + 1) * keep)
        inside = slice(source % (half // 2) * keep, (source % (half // 2) + 1) * keep)
        even, odd = (total[inside] for total in ends[source // (half // 2)])
        ahead = even + odd
        behind = even - odd
        low_part = jnp.take_along_axis(
            behind[:, :LANES], jnp.clip(mirror, 0, LANES - 1), axis=1
        )
        high_part = jnp.take_along_axis(
            behind[:, LANES:], jnp.clip(mirror - LANES, 0, LANES - 1), axis=1
        )
        result[to, :LANES] = jnp.where(mirror < LANES, low_part, high_part) * weight
        for first in range(0, lags - LANES, LANES):
            last = min(first + LANES, lags - LANES)
            value = ahead[:, first : first + LANES] * weight
            result[to, LANES + first : LANES + last] = value[:, : last - first]
        if rest and (source + 1) % pieces == 0:
            first, count = (source + 1 - pieces) * keep, pieces * keep
            at = pl.multiple_of((1 - part) * rows + first, count)
            copies.append(
                pltpu.make_async_copy(
                    result.at[pl.ds(first, count)],
                    out_ref.at[pl.ds(at, count)],
                    written.at[1 + source // pieces],
                )
            )
            copies[-1].start()
    if rest:
        for copy in copies:
            copy.wait()


def encode(segments, spectra, valid, sources):
    channels, width = spectra.shape
    keep = channels // segments
    slab = jax.ShapeDtypeStruct((sources.size, width // 2), jnp.bfloat16)
    block = jax.ShapeDtypeStruct((keep, width), jnp.bfloat16)
    padded = pltpu.VMEM((sources.size, width // 2 + 2 * LANES), jnp.bfloat16)
    pinned = [pltpu.with_memory_space_constraint(x, pltpu.HBM) for x in (spectra, valid, sources)]
    return pl.pallas_call(
        functools.partial(encode_kernel, segments),
        out_shape=(slab, slab) + (block,) * segments,
        in_specs=[HBM] * 3,
        out_specs=(VMEM,) * (2 + segments),
        scratch_shapes=[
            pltpu.VMEM((channels, width), kind_for(keep)),
            pltpu.VMEM((channels, width), jnp.bfloat16),
            pltpu.VMEM((1, channels), jnp.int32),
            pltpu.SMEM(sources.shape, jnp.int32),
            padded,
            padded,
            pltpu.SemaphoreType.DMA((3,)),
        ],
        compiler_params=pltpu.CompilerParams(vmem_limit_bytes=12 * MEBI),
        name="encode_and_pick",
    )(*pinned)


def whiten_blocks(blocks):
    segments, (keep, width) = len(blocks), blocks[0].shape
    count, nbins = segments * keep, width // 2
    padded = pltpu.VMEM((count, nbins + 2 * LANES), jnp.bfloat16)
    part = jax.ShapeDtypeStruct((count, nbins), jnp.float32)
    return pl.pallas_call(
        functools.partial(whiten_kernel, segments),
        out_shape=(part, part, part, jax.ShapeDtypeStruct((count, LANES), jnp.float32)),
        in_specs=[VMEM] * segments,
        out_specs=(VMEM,) * 4,
        scratch_shapes=[padded, padded],
        compiler_params=pltpu.CompilerParams(vmem_limit_bytes=20 * MEBI),
        cost_estimate=pl.CostEstimate(
            flops=count * width * 1024, bytes_accessed=count * width * 4, transcendentals=0
        ),
        name="whiten_receivers",
    )(*blocks)


def stack_half(segments, slabs, receivers, table, rest=()):
    half, nbins = slabs.shape[0] // (2 * segments), slabs.shape[1]
    keep = receivers[0].shape[0] // segments
    count, rows, lags = segments * half, half * keep, 2 * LAG + 1
    part = pltpu.VMEM((nbins // LANES, count, LANES), jnp.float32)
    cross = pltpu.VMEM((nbins // CHUNK, 2, rows, CHUNK), kind_for(keep))
    scratch = [part, part, part, cross]
    if rest:
        scratch += [pltpu.VMEM((rows, lags), jnp.float32), pltpu.SemaphoreType.DMA((1 + half,))]
    return pl.pallas_call(
        functools.partial(stack_kernel, segments),
        out_shape=jax.ShapeDtypeStruct((2 * rows if rest else rows, lags), jnp.float32),
        in_specs=[VMEM] * (6 + len(rest)),
        out_specs=HBM if rest else VMEM,
        scratch_shapes=scratch,
        compiler_params=pltpu.CompilerParams(vmem_limit_bytes=20 * MEBI),
        cost_estimate=pl.CostEstimate(
            flops=4 * rows * nbins * 2 * LAG, bytes_accessed=nbins * 2048, transcendentals=0
        ),
        name="stack_other_half" if rest else "stack_own_half",
    )(slabs, *receivers, table, *rest)


def swapped(value, axis, size, step):
    return lax.ppermute(value, axis, [(i, i ^ step) for i in range(size)])


def shards(rcv_size, tm_size, spectra, valid, sources):
    channels, _, width = spectra.shape
    keep = channels // tm_size
    rounds, per_round = sources.shape
    own, other, *receivers = encode(
        tm_size, spectra[:, 0, :], valid.reshape(1, channels), sources
    )
    receivers[-1] = swapped(receivers[-1], "tm", tm_size, tm_size - 1)
    own = own + swapped(other, "rcv", rcv_size, 1)
    own, later = lax.optimization_barrier((own, receivers[1:-1]))
    receivers[1:-1] = [
        swapped(block, "tm", tm_size, place) for place, block in enumerate(later, 1)
    ]
    step = 2
    while step < rcv_size:
        wide = min(4, rcv_size // step)
        parts = [swapped(own, "rcv", rcv_size, place * step) for place in range(1, wide)]
        if step == 2:
            parts[-1], receivers[-1] = lax.optimization_barrier((parts[-1], receivers[-1]))
        own = functools.reduce(jnp.add, parts, own)
        step *= wide
    own = [own] + [swapped(own, "tm", tm_size, place) for place in range(1, tm_size)]
    whitened = whiten_blocks(receivers)
    own, whitened = lax.optimization_barrier((own, whitened))
    own = jnp.concatenate(own, axis=0)
    other = swapped(own, "rcv", rcv_size, 1)

    table = jnp.asarray(lag_table(width // 2))
    first = stack_half(tm_size, own, whitened, table)
    stack = stack_half(tm_size, other, whitened, table, (first,))
    return stack.reshape(rounds, per_round, keep, 2 * LAG + 1)


def solution(mesh):
    body = functools.partial(shards, mesh.shape["rcv"], mesh.shape["tm"])
    in_specs = (P("rcv", "tm", None), P("rcv", "tm"), P())
    out_specs = P(None, None, ("rcv", "tm"), None)
    return jax.shard_map(body, mesh=mesh, in_specs=in_specs, out_specs=out_specs, check_vma=False)
```

```python
import functools
import math

import jax
import jax.numpy as jnp
import numpy as np
from jax import lax
from jax.experimental import pallas as pl
from jax.experimental.pallas import tpu as pltpu
from jax.sharding import PartitionSpec as P

NT = 4096
LAG = 150
HALF_WIN = 64
EPSILON = 1e-06

UNUSABLE = 1024.0
USABLE_BELOW = 512.0

LANES = 128
BLOCK = 256
CHUNK = 512
MEBI = 1 << 20
VMEM = pl.BlockSpec(memory_space=pltpu.VMEM)
HBM = pl.BlockSpec(memory_space=pltpu.HBM)


def lag_table(nbins):
    winding = np.mod(
        np.arange(1, nbins + 1, dtype=np.int64)[:, None]
        * np.arange(-LAG, LAG + 1, dtype=np.int64)[None, :],
        NT,
    )
    theta = winding * (2.0 * math.pi / NT)
    table = np.stack([np.cos(theta), -np.sin(theta)]).reshape(2, nbins // CHUNK, CHUNK, -1)
    table = np.swapaxes(table, 0, 1).reshape(2 * nbins, -1)
    columns = table.shape[1]
    padded = -(-columns // LANES) * LANES
    return np.pad(table, ((0, 0), (0, padded - columns))).astype(jnp.bfloat16)


def kind_for(rows):
    return jnp.bfloat16 if rows % 16 == 0 else jnp.float32


def iota(shape, dim):
    return lax.broadcasted_iota(jnp.int32, shape, dim)


def whitening(real, imag, high, low, unusable=0.0):
    count, nbins = real.shape
    blocks = nbins // BLOCK
    span = BLOCK + 2 * LANES
    amplitude = jnp.sqrt(real * real + imag * imag)
    rounded = amplitude.astype(jnp.bfloat16)
    edge = jnp.zeros((count, LANES), jnp.bfloat16)
    for part, value in (
        (high, rounded),
        (low, (amplitude - rounded.astype(jnp.float32)).astype(jnp.bfloat16)),
    ):
        part[:, :LANES] = edge
        part[:, LANES : LANES + nbins] = value
        part[:, LANES + nbins :] = edge
    near = jnp.abs(iota((span, BLOCK), 0) - LANES - iota((span, BLOCK), 1)) <= HALF_WIN
    band = jnp.where(near, 1.0, 0.0).astype(jnp.bfloat16)
    pieces = [
        part[:, block * BLOCK : block * BLOCK + span] for block in range(blocks) for part in (high, low)
    ]
    windows = jnp.dot(
        jnp.concatenate(pieces, axis=0), band, preferred_element_type=jnp.float32
    )
    for block in range(blocks):
        first = block * BLOCK
        at = 2 * block * count
        window = windows[at : at + count] + windows[at + count : at + 2 * count]
        index = first + iota((1, BLOCK), 1)
        counted = jnp.minimum(index, HALF_WIN) + jnp.minimum(nbins - 1 - index, HALF_WIN) + 1
        factor = 1.0 / (window / counted.astype(jnp.float32) + EPSILON)
        re = real[:, first : first + BLOCK]
        im = imag[:, first : first + BLOCK]
        usable = re < USABLE_BELOW
        re = jnp.where(usable, re * factor, unusable).astype(jnp.bfloat16).astype(jnp.float32)
        im = jnp.where(usable, im * factor, unusable).astype(jnp.bfloat16).astype(jnp.float32)
        yield slice(first, first + BLOCK), re, im


def usable_rows(real):
    return jnp.where(real[:, :LANES] < USABLE_BELOW, 1.0, 0.0)


def encode_kernel(
    segments, spectra_ref, valid_ref, sources_ref, own_ref, other_ref, *refs
):
    blocks, refs = refs[:segments], refs[segments:]
    encoded_ref, spectra, valid, sources, high, low, arrived = refs
    copies = [
        pltpu.make_async_copy(spectra_ref, spectra, arrived.at[0]),
        pltpu.make_async_copy(sources_ref, sources, arrived.at[1]),
        pltpu.make_async_copy(valid_ref, valid, arrived.at[2]),
    ]
    for copy in copies:
        copy.start()
    channels, width = spectra_ref.shape
    nbins = width // 2
    rounds, per_round = sources.shape
    half = rounds * per_round // 2
    index = lax.axis_index("rcv")
    copies[1].wait()
    copies[2].wait()
    diagonal = iota((channels, channels), 0) == iota((channels, channels), 1)
    usable = jnp.sum(jnp.where(diagonal, valid[...], 0), axis=1, keepdims=True) != 0
    row = iota((2 * half, channels), 0)
    local = jnp.zeros((2 * half, channels), jnp.int32)
    for place in range(2 * half):
        number = (index % 2 if place < half else 1 - index % 2) * half + place % half
        here = sources[number // per_round, number % per_round] - index * channels
        local = jnp.where(row == place, here, local)
    onehot = jnp.where(local == iota((2 * half, channels), 1), 1.0, 0.0).astype(jnp.bfloat16)
    copies[0].wait()
    encoded = jnp.where(usable, spectra[...].astype(jnp.float32), UNUSABLE).astype(jnp.bfloat16)
    picked = jnp.dot(onehot, encoded, preferred_element_type=jnp.float32)
    for at, re, im in whitening(picked[:, :nbins], picked[:, nbins:], high, low, UNUSABLE):
        for first, ref in ((0, own_ref), (half, other_ref)):
            rows = slice(first, first + half)
            ref[:, at] = jnp.concatenate([re[rows], im[rows]], axis=0).astype(ref.dtype)
    encoded_ref[...] = encoded.astype(encoded_ref.dtype)
    keep = channels // segments
    for step, block in enumerate(blocks):
        at = pl.multiple_of((lax.axis_index("tm") ^ step) * keep, keep)
        block[...] = encoded_ref[pl.ds(at, keep), :].astype(block.dtype)


def whiten_kernel(segments, *refs):
    blocks, refs = refs[:segments], refs[segments:]
    real_ref, imag_ref, both_ref, valid_ref, high, low = refs
    rows = jnp.concatenate([ref[...].astype(jnp.float32) for ref in blocks], axis=0)
    nbins = rows.shape[1] // 2
    real, imag = rows[:, :nbins], rows[:, nbins:]
    for at, re, im in whitening(real, imag, high, low):
        real_ref[:, at] = re
        imag_ref[:, at] = im
        both_ref[:, at] = re + im
    valid_ref[...] = usable_rows(real)


def stack_kernel(
    segments, slabs_ref, rcv_re, rcv_im, rcv_both, rcv_valid, table_ref, *refs
):
    *rest, out_ref, src_re, src_diff, src_sum, cross = refs[: 6 if len(refs) == 8 else 5]
    half = slabs_ref.shape[0] // (2 * segments)
    nbins = slabs_ref.shape[1]
    keep = rcv_re.shape[0] // segments
    rows = half * keep
    if rest:
        result, written = refs[6:]
        part = lax.axis_index("rcv") % 2
        pieces = max(1, half // 4)
        at = pl.multiple_of(part * rows, rows)
        copies = [
            pltpu.make_async_copy(rest[0], out_ref.at[pl.ds(at, rows)], written.at[0])
        ]
        copies[0].start()
    else:
        result = out_ref
    slabs = slabs_ref[...].astype(jnp.float32)
    real = jnp.concatenate(
        [slabs[2 * half * t : 2 * half * t + half] for t in range(segments)], axis=0
    )
    imag = jnp.concatenate(
        [slabs[2 * half * t + half : 2 * half * (t + 1)] for t in range(segments)], axis=0
    )
    usable = real < USABLE_BELOW
    real, imag = jnp.where(usable, real, 0.0), jnp.where(usable, imag, 0.0)
    src_valid = jnp.where(usable[:, :LANES], 1.0, 0.0)
    for ref, value in ((src_re, real), (src_diff, imag - real), (src_sum, imag + real)):
        for block in range(nbins // LANES):
            ref[block] = value[:, block * LANES : (block + 1) * LANES]
    tile = min(keep, 16)

    def spread(ref, block, row):
        return jnp.concatenate([ref[block, pl.ds(row, 8, stride=0), :]] * (tile // 8), axis=0)

    def multiply(chunk, sub):
        block = chunk * (CHUNK // LANES) + sub
        at = slice(block * LANES, (block + 1) * LANES)
        for first in range(0, keep, tile):
            rows = [slice(t * keep + first, t * keep + first + tile) for t in range(segments)]
            r_re = [rcv_re[row, at] for row in rows]
            r_im = [rcv_im[row, at] for row in rows]
            r_both = [rcv_both[row, at] for row in rows]
            for source in range(half):
                p, q, w = [], [], []
                for t in range(segments):
                    row = t * half + source
                    p.append(spread(src_re, block, row) * r_both[t])
                    q.append(spread(src_diff, block, row) * r_im[t])
                    w.append(spread(src_sum, block, row) * r_re[t])
                p, q, w = (functools.reduce(jnp.add, part) for part in (p, q, w))
                to = slice(source * keep + first, source * keep + first + tile)
                cross[chunk, to, sub * LANES : (sub + 1) * LANES] = (p + q).astype(cross.dtype)
                first_im = CHUNK + sub * LANES
                cross[chunk, to, first_im : first_im + LANES] = (w - p).astype(cross.dtype)

    def project(chunk, part):
        first = 2 * chunk * CHUNK
        return jnp.dot(
            cross[chunk, part].astype(jnp.bfloat16),
            table_ref[first : first + 2 * CHUNK],
            preferred_element_type=jnp.float32,
        )

    chunks, subs = nbins // CHUNK, CHUNK // LANES
    totals = []
    for chunk in range(chunks):
        for sub in range(subs):
            multiply(chunk, sub)
            if chunk > 0 and sub == 0:
                totals.append(project(chunk - 1, slice(None)))
    total = functools.reduce(jnp.add, totals)
    ends = []
    for first in (0, half // 2):
        at = slice(first * keep, (first + half // 2) * keep)
        ends.append(total[at] + project(chunks - 1, at))

    lags = result.shape[1]
    scale = 2.0 / math.sqrt(nbins)
    for source in range(half):
        common = 0.0
        for t in range(segments):
            row = t * half + source
            common = common + src_valid[row : row + 1] * rcv_valid[t * keep : (t + 1) * keep, :]
        weight = scale / jnp.maximum(common, 1.0)
        to = slice(source * keep, (source + 1) * keep)
        inside = slice(source % (half // 2) * keep, (source % (half // 2) + 1) * keep)
        value = ends[source // (half // 2)][inside]
        for first in range(0, lags, LANES):
            last = min(first + LANES, lags)
            result[to, first:last] = (value[:, first : first + LANES] * weight)[:, : last - first]
        if rest and (source + 1) % pieces == 0:
            first, count = (source + 1 - pieces) * keep, pieces * keep
            at = pl.multiple_of((1 - part) * rows + first, count)
            copies.append(
                pltpu.make_async_copy(
                    result.at[pl.ds(first, count)],
                    out_ref.at[pl.ds(at, count)],
                    written.at[1 + source // pieces],
                )
            )
            copies[-1].start()
    if rest:
        for copy in copies:
            copy.wait()


def encode(segments, spectra, valid, sources):
    channels, width = spectra.shape
    keep = channels // segments
    slab = jax.ShapeDtypeStruct((sources.size, width // 2), jnp.bfloat16)
    block = jax.ShapeDtypeStruct((keep, width), jnp.bfloat16)
    padded = pltpu.VMEM((sources.size, width // 2 + 2 * LANES), jnp.bfloat16)
    pinned = [pltpu.with_memory_space_constraint(x, pltpu.HBM) for x in (spectra, valid, sources)]
    return pl.pallas_call(
        functools.partial(encode_kernel, segments),
        out_shape=(slab, slab) + (block,) * segments,
        in_specs=[HBM] * 3,
        out_specs=(VMEM,) * (2 + segments),
        scratch_shapes=[
            pltpu.VMEM((channels, width), kind_for(keep)),
            pltpu.VMEM((channels, width), jnp.bfloat16),
            pltpu.VMEM((1, channels), jnp.int32),
            pltpu.SMEM(sources.shape, jnp.int32),
            padded,
            padded,
            pltpu.SemaphoreType.DMA((3,)),
        ],
        compiler_params=pltpu.CompilerParams(vmem_limit_bytes=12 * MEBI),
        name="encode_and_pick",
    )(*pinned)


def whiten_blocks(blocks):
    segments, (keep, width) = len(blocks), blocks[0].shape
    count, nbins = segments * keep, width // 2
    padded = pltpu.VMEM((count, nbins + 2 * LANES), jnp.bfloat16)
    part = jax.ShapeDtypeStruct((count, nbins), jnp.float32)
    return pl.pallas_call(
        functools.partial(whiten_kernel, segments),
        out_shape=(part, part, part, jax.ShapeDtypeStruct((count, LANES), jnp.float32)),
        in_specs=[VMEM] * segments,
        out_specs=(VMEM,) * 4,
        scratch_shapes=[padded, padded],
        compiler_params=pltpu.CompilerParams(vmem_limit_bytes=20 * MEBI),
        cost_estimate=pl.CostEstimate(
            flops=count * width * 1024, bytes_accessed=count * width * 4, transcendentals=0
        ),
        name="whiten_receivers",
    )(*blocks)


def stack_half(segments, slabs, receivers, table, rest=()):
    half, nbins = slabs.shape[0] // (2 * segments), slabs.shape[1]
    keep = receivers[0].shape[0] // segments
    count, rows, lags = segments * half, half * keep, 2 * LAG + 1
    part = pltpu.VMEM((nbins // LANES, count, LANES), jnp.float32)
    cross = pltpu.VMEM((nbins // CHUNK, rows, 2 * CHUNK), kind_for(keep))
    scratch = [part, part, part, cross]
    if rest:
        scratch += [pltpu.VMEM((rows, lags), jnp.float32), pltpu.SemaphoreType.DMA((1 + half,))]
    return pl.pallas_call(
        functools.partial(stack_kernel, segments),
        out_shape=jax.ShapeDtypeStruct((2 * rows if rest else rows, lags), jnp.float32),
        in_specs=[VMEM] * (6 + len(rest)),
        out_specs=HBM if rest else VMEM,
        scratch_shapes=scratch,
        compiler_params=pltpu.CompilerParams(vmem_limit_bytes=20 * MEBI),
        cost_estimate=pl.CostEstimate(
            flops=4 * rows * nbins * 2 * LAG, bytes_accessed=nbins * 2048, transcendentals=0
        ),
        name="stack_other_half" if rest else "stack_own_half",
    )(slabs, *receivers, table, *rest)


def swapped(value, axis, size, step):
    return lax.ppermute(value, axis, [(i, i ^ step) for i in range(size)])


def shards(rcv_size, tm_size, spectra, valid, sources):
    channels, _, width = spectra.shape
    keep = channels // tm_size
    rounds, per_round = sources.shape
    own, other, *receivers = encode(
        tm_size, spectra[:, 0, :], valid.reshape(1, channels), sources
    )
    receivers[-1] = swapped(receivers[-1], "tm", tm_size, tm_size - 1)
    own = own + swapped(other, "rcv", rcv_size, 1)
    own, later = lax.optimization_barrier((own, receivers[1:-1]))
    receivers[1:-1] = [
        swapped(block, "tm", tm_size, place) for place, block in enumerate(later, 1)
    ]
    step = 2
    while step < rcv_size:
        wide = min(4, rcv_size // step)
        parts = [swapped(own, "rcv", rcv_size, place * step) for place in range(1, wide)]
        if step == 2:
            parts[-1], receivers[-1] = lax.optimization_barrier((parts[-1], receivers[-1]))
        own = functools.reduce(jnp.add, parts, own)
        step *= wide
    own = [own] + [swapped(own, "tm", tm_size, place) for place in range(1, tm_size)]
    whitened = whiten_blocks(receivers)
    own, whitened = lax.optimization_barrier((own, whitened))
    own = jnp.concatenate(own, axis=0)
    other = swapped(own, "rcv", rcv_size, 1)

    table = jnp.asarray(lag_table(width // 2))
    first = stack_half(tm_size, own, whitened, table)
    stack = stack_half(tm_size, other, whitened, table, (first,))
    return stack.reshape(rounds, per_round, keep, 2 * LAG + 1)


def solution(mesh):
    body = functools.partial(shards, mesh.shape["rcv"], mesh.shape["tm"])
    in_specs = (P("rcv", "tm", None), P("rcv", "tm"), P())
    out_specs = P(None, None, ("rcv", "tm"), None)
    return jax.shard_map(body, mesh=mesh, in_specs=in_specs, out_specs=out_specs, check_vma=False)
```

```python
import functools
import math

import jax
import jax.numpy as jnp
import numpy as np
from jax import lax
from jax.experimental import pallas as pl
from jax.experimental.pallas import tpu as pltpu
from jax.sharding import PartitionSpec as P

NT = 4096
LAG = 150
HALF_WIN = 64
EPSILON = 1e-06

UNUSABLE = 1024.0
USABLE_BELOW = 512.0

LANES = 128
BLOCK = 256
MEBI = 1 << 20
FIRST_LAG = LANES - LAG
VMEM = pl.BlockSpec(memory_space=pltpu.VMEM)
HBM = pl.BlockSpec(memory_space=pltpu.HBM)


def lag_table(nbins):
    winding = np.mod(
        np.arange(1, nbins + 1, dtype=np.int64)[:, None]
        * np.arange(FIRST_LAG, FIRST_LAG + BLOCK, dtype=np.int64)[None, :],
        NT,
    )
    theta = winding * (2.0 * math.pi / NT)
    return np.concatenate([np.cos(theta), -np.sin(theta)], axis=0).astype(jnp.bfloat16)


def kind_for(rows):
    return jnp.bfloat16 if rows % 16 == 0 else jnp.float32


def iota(shape, dim):
    return lax.broadcasted_iota(jnp.int32, shape, dim)


def whitening(real, imag, high, low, unusable=0.0):
    count, nbins = real.shape
    blocks = nbins // BLOCK
    span = BLOCK + 2 * LANES
    amplitude = jnp.sqrt(real * real + imag * imag)
    rounded = amplitude.astype(jnp.bfloat16)
    edge = jnp.zeros((count, LANES), jnp.bfloat16)
    for part, value in (
        (high, rounded),
        (low, (amplitude - rounded.astype(jnp.float32)).astype(jnp.bfloat16)),
    ):
        part[:, :LANES] = edge
        part[:, LANES : LANES + nbins] = value
        part[:, LANES + nbins :] = edge
    near = jnp.abs(iota((span, BLOCK), 0) - LANES - iota((span, BLOCK), 1)) <= HALF_WIN
    band = jnp.where(near, 1.0, 0.0).astype(jnp.bfloat16)
    pieces = [
        part[:, block * BLOCK : block * BLOCK + span] for block in range(blocks) for part in (high, low)
    ]
    windows = jnp.dot(
        jnp.concatenate(pieces, axis=0), band, preferred_element_type=jnp.float32
    )
    for block in range(blocks):
        first = block * BLOCK
        at = 2 * block * count
        window = windows[at : at + count] + windows[at + count : at + 2 * count]
        index = first + iota((1, BLOCK), 1)
        counted = jnp.minimum(index, HALF_WIN) + jnp.minimum(nbins - 1 - index, HALF_WIN) + 1
        factor = 1.0 / (window / counted.astype(jnp.float32) + EPSILON)
        re = real[:, first : first + BLOCK]
        im = imag[:, first : first + BLOCK]
        usable = re < USABLE_BELOW
        re = jnp.where(usable, re * factor, unusable).astype(jnp.bfloat16).astype(jnp.float32)
        im = jnp.where(usable, im * factor, unusable).astype(jnp.bfloat16).astype(jnp.float32)
        yield slice(first, first + BLOCK), re, im


def usable_rows(real):
    return jnp.where(real[:, :LANES] < USABLE_BELOW, 1.0, 0.0)


def encode_kernel(
    segments, spectra_ref, valid_ref, sources_ref, own_ref, other_ref, *refs
):
    blocks, refs = refs[:segments], refs[segments:]
    encoded_ref, spectra, valid, sources, high, low, arrived = refs
    copies = [
        pltpu.make_async_copy(spectra_ref, spectra, arrived.at[0]),
        pltpu.make_async_copy(sources_ref, sources, arrived.at[1]),
        pltpu.make_async_copy(valid_ref, valid, arrived.at[2]),
    ]
    for copy in copies:
        copy.start()
    channels, width = spectra_ref.shape
    nbins = width // 2
    rounds, per_round = sources.shape
    half = rounds * per_round // 2
    index = lax.axis_index("rcv")
    copies[1].wait()
    copies[2].wait()
    diagonal = iota((channels, channels), 0) == iota((channels, channels), 1)
    usable = jnp.sum(jnp.where(diagonal, valid[...], 0), axis=1, keepdims=True) != 0
    row = iota((2 * half, channels), 0)
    local = jnp.zeros((2 * half, channels), jnp.int32)
    for place in range(2 * half):
        number = (index % 2 if place < half else 1 - index % 2) * half + place % half
        here = sources[number // per_round, number % per_round] - index * channels
        local = jnp.where(row == place, here, local)
    onehot = jnp.where(local == iota((2 * half, channels), 1), 1.0, 0.0).astype(jnp.bfloat16)
    copies[0].wait()
    encoded = jnp.where(usable, spectra[...].astype(jnp.float32), UNUSABLE).astype(jnp.bfloat16)
    picked = jnp.dot(onehot, encoded, preferred_element_type=jnp.float32)
    for at, re, im in whitening(picked[:, :nbins], picked[:, nbins:], high, low, UNUSABLE):
        for first, ref in ((0, own_ref), (half, other_ref)):
            rows = slice(first, first + half)
            ref[:, at] = jnp.concatenate([re[rows], im[rows]], axis=0).astype(ref.dtype)
    encoded_ref[...] = encoded.astype(encoded_ref.dtype)
    keep = channels // segments
    for step, block in enumerate(blocks):
        at = pl.multiple_of((lax.axis_index("tm") ^ step) * keep, keep)
        block[...] = encoded_ref[pl.ds(at, keep), :].astype(block.dtype)


def whiten_kernel(segments, *refs):
    blocks, refs = refs[:segments], refs[segments:]
    real_ref, imag_ref, both_ref, valid_ref, high, low = refs
    rows = jnp.concatenate([ref[...].astype(jnp.float32) for ref in blocks], axis=0)
    nbins = rows.shape[1] // 2
    real, imag = rows[:, :nbins], rows[:, nbins:]
    for at, re, im in whitening(real, imag, high, low):
        real_ref[:, at] = re
        imag_ref[:, at] = im
        both_ref[:, at] = re + im
    valid_ref[...] = usable_rows(real)


def stack_kernel(
    segments, slabs_ref, rcv_re, rcv_im, rcv_both, rcv_valid, table_ref, *refs
):
    *rest, out_ref, src_re, src_diff, src_sum, cross = refs[: 6 if len(refs) == 8 else 5]
    half = slabs_ref.shape[0] // (2 * segments)
    nbins = slabs_ref.shape[1]
    keep = rcv_re.shape[0] // segments
    rows = half * keep
    if rest:
        result, written = refs[6:]
        part = lax.axis_index("rcv") % 2
        pieces = max(1, half // 4)
        at = pl.multiple_of(part * rows, rows)
        copies = [
            pltpu.make_async_copy(rest[0], out_ref.at[pl.ds(at, rows)], written.at[0])
        ]
        copies[0].start()
    else:
        result = out_ref
    slabs = slabs_ref[...].astype(jnp.float32)
    real = jnp.concatenate(
        [slabs[2 * half * t : 2 * half * t + half] for t in range(segments)], axis=0
    )
    imag = jnp.concatenate(
        [slabs[2 * half * t + half : 2 * half * (t + 1)] for t in range(segments)], axis=0
    )
    usable = real < USABLE_BELOW
    real, imag = jnp.where(usable, real, 0.0), jnp.where(usable, imag, 0.0)
    src_valid = jnp.where(usable[:, :LANES], 1.0, 0.0)
    for ref, value in ((src_re, real), (src_diff, imag - real), (src_sum, imag + real)):
        for block in range(nbins // LANES):
            ref[block] = value[:, block * LANES : (block + 1) * LANES]
    tile = min(keep, 16)

    def spread(ref, block, row):
        return jnp.concatenate([ref[block, pl.ds(row, 8, stride=0), :]] * (tile // 8), axis=0)

    def multiply(block, carry):
        at = pl.ds(pl.multiple_of(block * LANES, LANES), LANES)
        for first in range(0, keep, tile):
            rows = [slice(t * keep + first, t * keep + first + tile) for t in range(segments)]
            r_re = [rcv_re[row, at] for row in rows]
            r_im = [rcv_im[row, at] for row in rows]
            r_both = [rcv_both[row, at] for row in rows]
            for source in range(half):
                p, q, w = [], [], []
                for t in range(segments):
                    row = t * half + source
                    p.append(spread(src_re, block, row) * r_both[t])
                    q.append(spread(src_diff, block, row) * r_im[t])
                    w.append(spread(src_sum, block, row) * r_re[t])
                p, q, w = (functools.reduce(jnp.add, part) for part in (p, q, w))
                to = slice(source * keep + first, source * keep + first + tile)
                cross[0, block, to] = (p + q).astype(cross.dtype)
                cross[1, block, to] = (w - p).astype(cross.dtype)
        return carry

    lax.fori_loop(0, nbins // LANES, multiply, 0)

    def project(place, part):
        value = [cross[place, block, part] for block in range(nbins // LANES)]
        return jnp.dot(
            jnp.concatenate(value, axis=1).astype(jnp.bfloat16),
            table_ref[place * nbins : (place + 1) * nbins],
            preferred_element_type=jnp.float32,
        )

    ends = []
    for first in (0, half // 2):
        at = slice(first * keep, (first + half // 2) * keep)
        ends.append([project(place, at) for place in range(2)])

    lags = result.shape[1]
    scale = 2.0 / math.sqrt(nbins)
    mirror = LAG - FIRST_LAG - iota((keep, LANES), 1)
    for source in range(half):
        common = 0.0
        for t in range(segments):
            row = t * half + source
            common = common + src_valid[row : row + 1] * rcv_valid[t * keep : (t + 1) * keep, :]
        weight = scale / jnp.maximum(common, 1.0)
        to = slice(source * keep, (source + 1) * keep)
        inside = slice(source % (half // 2) * keep, (source % (half // 2) + 1) * keep)
        even, odd = (total[inside] for total in ends[source // (half // 2)])
        ahead = even + odd
        behind = even - odd
        low_part = jnp.take_along_axis(
            behind[:, :LANES], jnp.clip(mirror, 0, LANES - 1), axis=1
        )
        high_part = jnp.take_along_axis(
            behind[:, LANES:], jnp.clip(mirror - LANES, 0, LANES - 1), axis=1
        )
        result[to, :LANES] = jnp.where(mirror < LANES, low_part, high_part) * weight
        for first in range(0, lags - LANES, LANES):
            last = min(first + LANES, lags - LANES)
            value = ahead[:, first : first + LANES] * weight
            result[to, LANES + first : LANES + last] = value[:, : last - first]
        if rest and (source + 1) % pieces == 0:
            first, count = (source + 1 - pieces) * keep, pieces * keep
            at = pl.multiple_of((1 - part) * rows + first, count)
            copies.append(
                pltpu.make_async_copy(
                    result.at[pl.ds(first, count)],
                    out_ref.at[pl.ds(at, count)],
                    written.at[1 + source // pieces],
                )
            )
            copies[-1].start()
    if rest:
        for copy in copies:
            copy.wait()


def encode(segments, spectra, valid, sources):
    channels, width = spectra.shape
    keep = channels // segments
    slab = jax.ShapeDtypeStruct((sources.size, width // 2), jnp.bfloat16)
    block = jax.ShapeDtypeStruct((keep, width), jnp.bfloat16)
    padded = pltpu.VMEM((sources.size, width // 2 + 2 * LANES), jnp.bfloat16)
    pinned = [pltpu.with_memory_space_constraint(x, pltpu.HBM) for x in (spectra, valid, sources)]
    return pl.pallas_call(
        functools.partial(encode_kernel, segments),
        out_shape=(slab, slab) + (block,) * segments,
        in_specs=[HBM] * 3,
        out_specs=(VMEM,) * (2 + segments),
        scratch_shapes=[
            pltpu.VMEM((channels, width), kind_for(keep)),
            pltpu.VMEM((channels, width), jnp.bfloat16),
            pltpu.VMEM((1, channels), jnp.int32),
            pltpu.SMEM(sources.shape, jnp.int32),
            padded,
            padded,
            pltpu.SemaphoreType.DMA((3,)),
        ],
        compiler_params=pltpu.CompilerParams(vmem_limit_bytes=12 * MEBI),
        name="encode_and_pick",
    )(*pinned)


def whiten_blocks(blocks):
    segments, (keep, width) = len(blocks), blocks[0].shape
    count, nbins = segments * keep, width // 2
    padded = pltpu.VMEM((count, nbins + 2 * LANES), jnp.bfloat16)
    part = jax.ShapeDtypeStruct((count, nbins), jnp.float32)
    return pl.pallas_call(
        functools.partial(whiten_kernel, segments),
        out_shape=(part, part, part, jax.ShapeDtypeStruct((count, LANES), jnp.float32)),
        in_specs=[VMEM] * segments,
        out_specs=(VMEM,) * 4,
        scratch_shapes=[padded, padded],
        compiler_params=pltpu.CompilerParams(vmem_limit_bytes=20 * MEBI),
        cost_estimate=pl.CostEstimate(
            flops=count * width * 1024, bytes_accessed=count * width * 4, transcendentals=0
        ),
        name="whiten_receivers",
    )(*blocks)


def stack_half(segments, slabs, receivers, table, rest=()):
    half, nbins = slabs.shape[0] // (2 * segments), slabs.shape[1]
    keep = receivers[0].shape[0] // segments
    count, rows, lags = segments * half, half * keep, 2 * LAG + 1
    part = pltpu.VMEM((nbins // LANES, count, LANES), jnp.float32)
    cross = pltpu.VMEM((2, nbins // LANES, rows, LANES), kind_for(keep))
    scratch = [part, part, part, cross]
    if rest:
        scratch += [pltpu.VMEM((rows, lags), jnp.float32), pltpu.SemaphoreType.DMA((1 + half,))]
    return pl.pallas_call(
        functools.partial(stack_kernel, segments),
        out_shape=jax.ShapeDtypeStruct((2 * rows if rest else rows, lags), jnp.float32),
        in_specs=[VMEM] * (6 + len(rest)),
        out_specs=HBM if rest else VMEM,
        scratch_shapes=scratch,
        compiler_params=pltpu.CompilerParams(vmem_limit_bytes=20 * MEBI),
        cost_estimate=pl.CostEstimate(
            flops=4 * rows * nbins * 2 * LAG, bytes_accessed=nbins * 2048, transcendentals=0
        ),
        name="stack_other_half" if rest else "stack_own_half",
    )(slabs, *receivers, table, *rest)


def swapped(value, axis, size, step):
    return lax.ppermute(value, axis, [(i, i ^ step) for i in range(size)])


def shards(rcv_size, tm_size, spectra, valid, sources):
    channels, _, width = spectra.shape
    keep = channels // tm_size
    rounds, per_round = sources.shape
    own, other, *receivers = encode(
        tm_size, spectra[:, 0, :], valid.reshape(1, channels), sources
    )
    receivers[-1] = swapped(receivers[-1], "tm", tm_size, tm_size - 1)
    own = own + swapped(other, "rcv", rcv_size, 1)
    own, later = lax.optimization_barrier((own, receivers[1:-1]))
    receivers[1:-1] = [
        swapped(block, "tm", tm_size, place) for place, block in enumerate(later, 1)
    ]
    step = 2
    while step < rcv_size:
        wide = min(4, rcv_size // step)
        parts = [swapped(own, "rcv", rcv_size, place * step) for place in range(1, wide)]
        if step == 2:
            parts[-1], receivers[-1] = lax.optimization_barrier((parts[-1], receivers[-1]))
        own = functools.reduce(jnp.add, parts, own)
        step *= wide
    own = [own] + [swapped(own, "tm", tm_size, place) for place in range(1, tm_size)]
    whitened = whiten_blocks(receivers)
    own, whitened = lax.optimization_barrier((own, whitened))
    own = jnp.concatenate(own, axis=0)
    other = swapped(own, "rcv", rcv_size, 1)

    table = jnp.asarray(lag_table(width // 2))
    first = stack_half(tm_size, own, whitened, table)
    stack = stack_half(tm_size, other, whitened, table, (first,))
    return stack.reshape(rounds, per_round, keep, 2 * LAG + 1)


def solution(mesh):
    body = functools.partial(shards, mesh.shape["rcv"], mesh.shape["tm"])
    in_specs = (P("rcv", "tm", None), P("rcv", "tm"), P())
    out_specs = P(None, None, ("rcv", "tm"), None)
    return jax.shard_map(body, mesh=mesh, in_specs=in_specs, out_specs=out_specs, check_vma=False)
```

```python
import functools
import math

import jax
import jax.numpy as jnp
import numpy as np
from jax import lax
from jax.experimental import pallas as pl
from jax.experimental.pallas import tpu as pltpu
from jax.sharding import PartitionSpec as P

NT = 4096
LAG = 150
HALF_WIN = 64
EPSILON = 1e-06

UNUSABLE = 1024.0
USABLE_BELOW = 512.0

LANES = 128
BLOCK = 256
MEBI = 1 << 20
FIRST_LAG = LANES - LAG
VMEM = pl.BlockSpec(memory_space=pltpu.VMEM)
HBM = pl.BlockSpec(memory_space=pltpu.HBM)


def lag_table(nbins):
    winding = np.mod(
        np.arange(1, nbins + 1, dtype=np.int64)[:, None]
        * np.arange(FIRST_LAG, FIRST_LAG + BLOCK, dtype=np.int64)[None, :],
        NT,
    )
    theta = winding * (2.0 * math.pi / NT)
    return np.concatenate([np.cos(theta), -np.sin(theta)], axis=0).astype(jnp.bfloat16)


def kind_for(rows):
    return jnp.bfloat16 if rows % 16 == 0 else jnp.float32


def iota(shape, dim):
    return lax.broadcasted_iota(jnp.int32, shape, dim)


def whitening(real, imag, high, low, unusable=0.0):
    count, nbins = real.shape
    blocks = nbins // BLOCK
    span = BLOCK + 2 * LANES
    amplitude = jnp.sqrt(real * real + imag * imag)
    rounded = amplitude.astype(jnp.bfloat16)
    edge = jnp.zeros((count, LANES), jnp.bfloat16)
    for part, value in (
        (high, rounded),
        (low, (amplitude - rounded.astype(jnp.float32)).astype(jnp.bfloat16)),
    ):
        part[:, :LANES] = edge
        part[:, LANES : LANES + nbins] = value
        part[:, LANES + nbins :] = edge
    near = jnp.abs(iota((span, BLOCK), 0) - LANES - iota((span, BLOCK), 1)) <= HALF_WIN
    band = jnp.where(near, 1.0, 0.0).astype(jnp.bfloat16)
    pieces = [
        part[:, block * BLOCK : block * BLOCK + span] for block in range(blocks) for part in (high, low)
    ]
    windows = jnp.dot(
        jnp.concatenate(pieces, axis=0), band, preferred_element_type=jnp.float32
    )
    for block in range(blocks):
        first = block * BLOCK
        at = 2 * block * count
        window = windows[at : at + count] + windows[at + count : at + 2 * count]
        index = first + iota((1, BLOCK), 1)
        counted = jnp.minimum(index, HALF_WIN) + jnp.minimum(nbins - 1 - index, HALF_WIN) + 1
        factor = 1.0 / (window / counted.astype(jnp.float32) + EPSILON)
        re = real[:, first : first + BLOCK]
        im = imag[:, first : first + BLOCK]
        usable = re < USABLE_BELOW
        re = jnp.where(usable, re * factor, unusable).astype(jnp.bfloat16).astype(jnp.float32)
        im = jnp.where(usable, im * factor, unusable).astype(jnp.bfloat16).astype(jnp.float32)
        yield slice(first, first + BLOCK), re, im


def usable_rows(real):
    return jnp.where(real[:, :LANES] < USABLE_BELOW, 1.0, 0.0)


def encode_kernel(
    segments, spectra_ref, valid_ref, sources_ref, picked_ref, *refs
):
    blocks, refs = refs[:segments], refs[segments:]
    encoded_ref, spectra, valid, sources, high, low, arrived = refs
    copies = [
        pltpu.make_async_copy(spectra_ref, spectra, arrived.at[0]),
        pltpu.make_async_copy(sources_ref, sources, arrived.at[1]),
        pltpu.make_async_copy(valid_ref, valid, arrived.at[2]),
    ]
    for copy in copies:
        copy.start()
    channels, width = spectra_ref.shape
    nbins = width // 2
    rounds, per_round = sources.shape
    count = rounds * per_round
    first_channel = lax.axis_index("rcv") * channels
    copies[1].wait()
    copies[2].wait()
    diagonal = iota((channels, channels), 0) == iota((channels, channels), 1)
    usable = jnp.sum(jnp.where(diagonal, valid[...], 0), axis=1, keepdims=True) != 0
    row = iota((count, channels), 0)
    local = jnp.zeros((count, channels), jnp.int32)
    for place in range(count):
        here = sources[place // per_round, place % per_round] - first_channel
        local = jnp.where(row == place, here, local)
    onehot = jnp.where(local == iota((count, channels), 1), 1.0, 0.0).astype(jnp.bfloat16)
    copies[0].wait()
    encoded = jnp.where(usable, spectra[...].astype(jnp.float32), UNUSABLE).astype(jnp.bfloat16)
    picked = jnp.dot(onehot, encoded, preferred_element_type=jnp.float32)
    for at, re, im in whitening(picked[:, :nbins], picked[:, nbins:], high, low, UNUSABLE):
        picked_ref[:count, at] = re.astype(picked_ref.dtype)
        picked_ref[count:, at] = im.astype(picked_ref.dtype)
    encoded_ref[...] = encoded.astype(encoded_ref.dtype)
    keep = channels // segments
    for step, block in enumerate(blocks):
        at = pl.multiple_of((lax.axis_index("tm") ^ step) * keep, keep)
        block[...] = encoded_ref[pl.ds(at, keep), :].astype(block.dtype)


def whiten_kernel(segments, *refs):
    blocks, refs = refs[:segments], refs[segments:]
    real_ref, imag_ref, both_ref, valid_ref, high, low = refs
    rows = jnp.concatenate([ref[...].astype(jnp.float32) for ref in blocks], axis=0)
    nbins = rows.shape[1] // 2
    real, imag = rows[:, :nbins], rows[:, nbins:]
    for at, re, im in whitening(real, imag, high, low):
        real_ref[:, at] = re
        imag_ref[:, at] = im
        both_ref[:, at] = re + im
    valid_ref[...] = usable_rows(real)


def stack_kernel(places, stage, *refs):
    first_stage, last_stage = stage
    segments = len(places)
    slabs, refs = refs[:segments], refs[segments:]
    rcv_re, rcv_im, rcv_both, rcv_valid, table_ref, *refs = refs
    before, refs = ([], refs) if first_stage else (refs[:2], refs[2:])
    after, refs = (refs[:1], refs[1:]) if last_stage else (refs[:2], refs[2:])
    src_re, src_diff, src_sum, cross, *refs = refs
    count, nbins = slabs[0].shape[0] // 2, slabs[0].shape[1]
    rows = cross.shape[2]
    keep = rows // count
    core = lax.axis_index("rcv") % 2
    at_rows = [pl.multiple_of(place(core) * keep, keep) for place in places]
    values = [slab[...].astype(jnp.float32) for slab in slabs]
    real = jnp.concatenate([value[:count] for value in values], axis=0)
    imag = jnp.concatenate([value[count:] for value in values], axis=0)
    usable = real < USABLE_BELOW
    real, imag = jnp.where(usable, real, 0.0), jnp.where(usable, imag, 0.0)
    src_valid = jnp.where(usable[:, :LANES], 1.0, 0.0)
    for ref, value in ((src_re, real), (src_diff, imag - real), (src_sum, imag + real)):
        for block in range(nbins // LANES):
            ref[block] = value[:, block * LANES : (block + 1) * LANES]
    tile = keep if segments <= 2 else min(keep, 16)

    def spread(ref, block, row):
        return jnp.concatenate([ref[block, pl.ds(row, 8, stride=0), :]] * (tile // 8), axis=0)

    def multiply(block, carry):
        at = pl.ds(pl.multiple_of(block * LANES, LANES), LANES)
        for first in range(0, keep, tile):
            rcv_rows = [pl.ds(pl.multiple_of(row + first, 8), tile) for row in at_rows]
            r_re = [rcv_re[row, at] for row in rcv_rows]
            r_im = [rcv_im[row, at] for row in rcv_rows]
            r_both = [rcv_both[row, at] for row in rcv_rows]
            for source in range(count):
                p, q, w = [], [], []
                for t in range(segments):
                    row = t * count + source
                    p.append(spread(src_re, block, row) * r_both[t])
                    q.append(spread(src_diff, block, row) * r_im[t])
                    w.append(spread(src_sum, block, row) * r_re[t])
                p, q, w = (functools.reduce(jnp.add, part) for part in (p, q, w))
                to = slice(source * keep + first, source * keep + first + tile)
                cross[0, block, to] = (p + q).astype(cross.dtype)
                cross[1, block, to] = (w - p).astype(cross.dtype)
        return carry

    lax.fori_loop(0, nbins // LANES, multiply, 0)

    def project(place, part):
        value = [cross[place, block, part] for block in range(nbins // LANES)]
        return jnp.dot(
            jnp.concatenate(value, axis=1).astype(jnp.bfloat16),
            table_ref[place * nbins : (place + 1) * nbins],
            preferred_element_type=jnp.float32,
        )

    ends = []
    for first in (0, count // 2):
        at = slice(first * keep, (first + count // 2) * keep)
        sums = [project(place, at) for place in range(2)]
        if not first_stage:
            sums = [before[0][place, at] + sums[place] for place in range(2)]
        if not last_stage:
            for place in range(2):
                after[0][place, at] = sums[place]
        ends.append(sums)

    lags = 2 * LAG + 1
    scale = 2.0 / math.sqrt(nbins)
    mirror = LAG - FIRST_LAG - iota((keep, LANES), 1)
    pieces = max(1, count // 8)
    copies = []
    for source in range(count):
        to = slice(source * keep, (source + 1) * keep)
        common = [
            src_valid[t * count + source : t * count + source + 1]
            * rcv_valid[pl.ds(at_rows[t], keep), :]
            for t in range(segments)
        ] + ([] if first_stage else [before[1][to]])
        common = functools.reduce(jnp.add, common)
        if not last_stage:
            after[1][to] = common
            continue
        result, written = refs
        weight = scale / jnp.maximum(common, 1.0)
        inside = slice(source % (count // 2) * keep, (source % (count // 2) + 1) * keep)
        even, odd = (total[inside] for total in ends[source // (count // 2)])
        ahead = even + odd
        behind = even - odd
        low_part = jnp.take_along_axis(
            behind[:, :LANES], jnp.clip(mirror, 0, LANES - 1), axis=1
        )
        high_part = jnp.take_along_axis(
            behind[:, LANES:], jnp.clip(mirror - LANES, 0, LANES - 1), axis=1
        )
        result[to, :LANES] = jnp.where(mirror < LANES, low_part, high_part) * weight
        for first in range(0, lags - LANES, LANES):
            last = min(first + LANES, lags - LANES)
            value = ahead[:, first : first + LANES] * weight
            result[to, LANES + first : LANES + last] = value[:, : last - first]
        if (source + 1) % pieces == 0:
            at = pl.ds((source + 1 - pieces) * keep, pieces * keep)
            copies.append(
                pltpu.make_async_copy(
                    result.at[at], after[0].at[at], written.at[source // pieces]
                )
            )
            copies[-1].start()
    for copy in copies:
        copy.wait()


def encode(segments, spectra, valid, sources):
    channels, width = spectra.shape
    keep = channels // segments
    slab = jax.ShapeDtypeStruct((2 * sources.size, width // 2), jnp.bfloat16)
    block = jax.ShapeDtypeStruct((keep, width), jnp.bfloat16)
    padded = pltpu.VMEM((sources.size, width // 2 + 2 * LANES), jnp.bfloat16)
    pinned = [pltpu.with_memory_space_constraint(x, pltpu.HBM) for x in (spectra, valid, sources)]
    return pl.pallas_call(
        functools.partial(encode_kernel, segments),
        out_shape=(slab,) + (block,) * segments,
        in_specs=[HBM] * 3,
        out_specs=(VMEM,) * (1 + segments),
        scratch_shapes=[
            pltpu.VMEM((channels, width), kind_for(keep)),
            pltpu.VMEM((channels, width), jnp.bfloat16),
            pltpu.VMEM((1, channels), jnp.int32),
            pltpu.SMEM(sources.shape, jnp.int32),
            padded,
            padded,
            pltpu.SemaphoreType.DMA((3,)),
        ],
        compiler_params=pltpu.CompilerParams(vmem_limit_bytes=12 * MEBI),
        name="encode_and_pick",
    )(*pinned)


def whiten_blocks(blocks):
    segments, (keep, width) = len(blocks), blocks[0].shape
    count, nbins = segments * keep, width // 2
    padded = pltpu.VMEM((count, nbins + 2 * LANES), jnp.bfloat16)
    part = jax.ShapeDtypeStruct((count, nbins), jnp.float32)
    return pl.pallas_call(
        functools.partial(whiten_kernel, segments),
        out_shape=(part, part, part, jax.ShapeDtypeStruct((count, LANES), jnp.float32)),
        in_specs=[VMEM] * segments,
        out_specs=(VMEM,) * 4,
        scratch_shapes=[padded, padded],
        compiler_params=pltpu.CompilerParams(vmem_limit_bytes=20 * MEBI),
        cost_estimate=pl.CostEstimate(
            flops=count * width * 1024, bytes_accessed=count * width * 4, transcendentals=0
        ),
        name="whiten_receivers",
    )(*blocks)


def stack_stage(keep, slabs, places, receivers, table, before=(), last=True):
    count, nbins = slabs[0].shape[0] // 2, slabs[0].shape[1]
    rows, lags = count * keep, 2 * LAG + 1
    part = pltpu.VMEM((nbins // LANES, len(slabs) * count, LANES), jnp.float32)
    cross = pltpu.VMEM((2, nbins // LANES, rows, LANES), kind_for(keep))
    scratch = [part, part, part, cross]
    sums = (
        jax.ShapeDtypeStruct((2, rows, BLOCK), jnp.float32),
        jax.ShapeDtypeStruct((rows, LANES), jnp.float32),
    )
    if last:
        scratch += [pltpu.VMEM((rows, lags), jnp.float32), pltpu.SemaphoreType.DMA((count,))]
    return pl.pallas_call(
        functools.partial(stack_kernel, places, (not before, last)),
        out_shape=jax.ShapeDtypeStruct((rows, lags), jnp.float32) if last else sums,
        in_specs=[VMEM] * (len(slabs) + len(receivers) + 1 + len(before)),
        out_specs=HBM if last else (VMEM, VMEM),
        scratch_shapes=scratch,
        compiler_params=pltpu.CompilerParams(vmem_limit_bytes=26 * MEBI),
        cost_estimate=pl.CostEstimate(
            flops=4 * rows * nbins * 2 * LAG, bytes_accessed=nbins * 2048, transcendentals=0
        ),
        name="stack_last" if last else "stack_first",
    )(*slabs, *receivers, table, *before)


def swapped(value, axis, size, step):
    return lax.ppermute(value, axis, [(i, i ^ step) for i in range(size)])


def gather_shared(picked, receivers, rcv_size, tm_size):
    core = lax.axis_index("rcv") % 2
    receivers[3] = swapped(receivers[3], "tm", tm_size, 3)
    own = picked + swapped(picked, "rcv", rcv_size, 1)
    own, near = lax.optimization_barrier((own, receivers[1:3]))
    receivers[1:3] = [swapped(block, "tm", tm_size, place) for place, block in enumerate(near, 1)]
    far = lax.ppermute(own, "rcv", [(i, i ^ (6 if i % 2 else 4)) for i in range(rcv_size)])
    near = swapped(own, "rcv", rcv_size, 2)
    far, receivers[3] = lax.optimization_barrier((far, receivers[3]))
    partial = far + jnp.where(core == 0, own, jnp.zeros_like(own))
    own = near + (partial + swapped(partial, "rcv", rcv_size, 1))
    pairs = [
        (rcv * tm_size + tm, rcv * tm_size + (tm ^ (2 if rcv % 2 else 1)))
        for rcv in range(rcv_size)
        for tm in range(tm_size)
    ]
    beside = lax.ppermute(own, ("rcv", "tm"), pairs)
    late, receivers[1:3] = lax.optimization_barrier((own, receivers[1:3]))
    across = swapped(late, "tm", tm_size, 3)
    handed = swapped(beside, "rcv", rcv_size, 1)
    return own, beside, handed, across


def shards(rcv_size, tm_size, spectra, valid, sources):
    channels, _, width = spectra.shape
    keep = channels // tm_size
    rounds, per_round = sources.shape
    table = jnp.asarray(lag_table(width // 2))
    picked, *receivers = encode(
        tm_size, spectra[:, 0, :], valid.reshape(1, channels), sources
    )
    if (rcv_size, tm_size) == (8, 4):
        own, beside, handed, across = gather_shared(picked, receivers, rcv_size, tm_size)
        whitened = whiten_blocks(receivers)
        sums = stack_stage(
            keep, [own, beside], [lambda core: 0, lambda core: 1 + core], whitened, table, last=False
        )
        stack = stack_stage(
            keep, [handed, across], [lambda core: 2 - core, lambda core: 3], whitened, table, sums
        )
    else:
        receivers[1:] = [
            swapped(receivers[place], "tm", tm_size, place) for place in range(1, tm_size)
        ]
        step = 1
        while step < rcv_size:
            picked = picked + swapped(picked, "rcv", rcv_size, step)
            step *= 2
        slabs = [picked] + [swapped(picked, "tm", tm_size, place) for place in range(1, tm_size)]
        places = [functools.partial(lambda place, core: place, place) for place in range(tm_size)]
        stack = stack_stage(keep, slabs, places, whiten_blocks(receivers), table)
    return stack.reshape(rounds, per_round, keep, 2 * LAG + 1)


def solution(mesh):
    body = functools.partial(shards, mesh.shape["rcv"], mesh.shape["tm"])
    in_specs = (P("rcv", "tm", None), P("rcv", "tm"), P())
    out_specs = P(None, None, ("rcv", "tm"), None)
    return jax.shard_map(body, mesh=mesh, in_specs=in_specs, out_specs=out_specs, check_vma=False)
```

```python
import functools
import math

import jax
import jax.numpy as jnp
import numpy as np
from jax import lax
from jax.experimental import pallas as pl
from jax.experimental.pallas import tpu as pltpu
from jax.sharding import PartitionSpec as P

NT = 4096
LAG = 150
HALF_WIN = 64
EPSILON = 1e-06

UNUSABLE = 1024.0
USABLE_BELOW = 512.0

LANES = 128
BLOCK = 256
MEBI = 1 << 20
FIRST_LAG = LANES - LAG
VMEM = pl.BlockSpec(memory_space=pltpu.VMEM)
HBM = pl.BlockSpec(memory_space=pltpu.HBM)


def lag_table(nbins):
    winding = np.mod(
        np.arange(1, nbins + 1, dtype=np.int64)[:, None]
        * np.arange(FIRST_LAG, FIRST_LAG + BLOCK, dtype=np.int64)[None, :],
        NT,
    )
    theta = winding * (2.0 * math.pi / NT)
    return np.concatenate([np.cos(theta), -np.sin(theta)], axis=0).astype(jnp.bfloat16)


def kind_for(rows):
    return jnp.bfloat16 if rows % 16 == 0 else jnp.float32


def iota(shape, dim):
    return lax.broadcasted_iota(jnp.int32, shape, dim)


def whitening(real, imag, high, low, unusable=0.0):
    count, nbins = real.shape
    blocks = nbins // BLOCK
    span = BLOCK + 2 * LANES
    amplitude = jnp.sqrt(real * real + imag * imag)
    rounded = amplitude.astype(jnp.bfloat16)
    edge = jnp.zeros((count, LANES), jnp.bfloat16)
    for part, value in (
        (high, rounded),
        (low, (amplitude - rounded.astype(jnp.float32)).astype(jnp.bfloat16)),
    ):
        part[:, :LANES] = edge
        part[:, LANES : LANES + nbins] = value
        part[:, LANES + nbins :] = edge
    near = jnp.abs(iota((span, BLOCK), 0) - LANES - iota((span, BLOCK), 1)) <= HALF_WIN
    band = jnp.where(near, 1.0, 0.0).astype(jnp.bfloat16)
    pieces = [
        part[:, block * BLOCK : block * BLOCK + span] for block in range(blocks) for part in (high, low)
    ]
    windows = jnp.dot(
        jnp.concatenate(pieces, axis=0), band, preferred_element_type=jnp.float32
    )
    for block in range(blocks):
        first = block * BLOCK
        at = 2 * block * count
        window = windows[at : at + count] + windows[at + count : at + 2 * count]
        index = first + iota((1, BLOCK), 1)
        counted = jnp.minimum(index, HALF_WIN) + jnp.minimum(nbins - 1 - index, HALF_WIN) + 1
        factor = 1.0 / (window / counted.astype(jnp.float32) + EPSILON)
        re = real[:, first : first + BLOCK]
        im = imag[:, first : first + BLOCK]
        usable = re < USABLE_BELOW
        re = jnp.where(usable, re * factor, unusable).astype(jnp.bfloat16).astype(jnp.float32)
        im = jnp.where(usable, im * factor, unusable).astype(jnp.bfloat16).astype(jnp.float32)
        yield slice(first, first + BLOCK), re, im


def usable_rows(real):
    return jnp.where(real[:, :LANES] < USABLE_BELOW, 1.0, 0.0)


def encode_kernel(
    segments, spectra_ref, valid_ref, sources_ref, picked_ref, *refs
):
    blocks, refs = refs[:segments], refs[segments:]
    encoded_ref, spectra, valid, sources, high, low, arrived = refs
    copies = [
        pltpu.make_async_copy(spectra_ref, spectra, arrived.at[0]),
        pltpu.make_async_copy(sources_ref, sources, arrived.at[1]),
        pltpu.make_async_copy(valid_ref, valid, arrived.at[2]),
    ]
    for copy in copies:
        copy.start()
    channels, width = spectra_ref.shape
    nbins = width // 2
    rounds, per_round = sources.shape
    count = rounds * per_round
    first_channel = lax.axis_index("rcv") * channels
    copies[1].wait()
    copies[2].wait()
    diagonal = iota((channels, channels), 0) == iota((channels, channels), 1)
    usable = jnp.sum(jnp.where(diagonal, valid[...], 0), axis=1, keepdims=True) != 0
    row = iota((count, channels), 0)
    local = jnp.zeros((count, channels), jnp.int32)
    for place in range(count):
        here = sources[place // per_round, place % per_round] - first_channel
        local = jnp.where(row == place, here, local)
    onehot = jnp.where(local == iota((count, channels), 1), 1.0, 0.0).astype(jnp.bfloat16)
    copies[0].wait()
    encoded = jnp.where(usable, spectra[...].astype(jnp.float32), UNUSABLE).astype(jnp.bfloat16)
    picked = jnp.dot(onehot, encoded, preferred_element_type=jnp.float32)
    for at, re, im in whitening(picked[:, :nbins], picked[:, nbins:], high, low, UNUSABLE):
        picked_ref[:count, at] = re.astype(picked_ref.dtype)
        picked_ref[count:, at] = im.astype(picked_ref.dtype)
    encoded_ref[...] = encoded.astype(encoded_ref.dtype)
    keep = channels // segments
    for step, block in enumerate(blocks):
        at = pl.multiple_of((lax.axis_index("tm") ^ step) * keep, keep)
        block[...] = encoded_ref[pl.ds(at, keep), :].astype(block.dtype)


def whiten_kernel(segments, *refs):
    blocks, refs = refs[:segments], refs[segments:]
    real_ref, imag_ref, both_ref, valid_ref, high, low = refs
    rows = jnp.concatenate([ref[...].astype(jnp.float32) for ref in blocks], axis=0)
    nbins = rows.shape[1] // 2
    real, imag = rows[:, :nbins], rows[:, nbins:]
    for at, re, im in whitening(real, imag, high, low):
        real_ref[:, at] = re
        imag_ref[:, at] = im
        both_ref[:, at] = re + im
    valid_ref[...] = usable_rows(real)


def stack_kernel(places, stage, *refs):
    first_stage, last_stage = stage
    segments = len(places)
    slabs, refs = refs[:segments], refs[segments:]
    rcv_re, rcv_im, rcv_both, rcv_valid, table_ref, *refs = refs
    before, refs = ([], refs) if first_stage else (refs[:2], refs[2:])
    after, refs = (refs[:1], refs[1:]) if last_stage else (refs[:2], refs[2:])
    src_re, src_diff, src_sum, cross, *refs = refs
    count, nbins = slabs[0].shape[0] // 2, slabs[0].shape[1]
    rows = cross.shape[2]
    keep = rows // count
    core = lax.axis_index("rcv") % 2
    at_rows = [pl.multiple_of(place(core) * keep, keep) for place in places]
    values = [slab[...].astype(jnp.float32) for slab in slabs]
    real = jnp.concatenate([value[:count] for value in values], axis=0)
    imag = jnp.concatenate([value[count:] for value in values], axis=0)
    usable = real < USABLE_BELOW
    real, imag = jnp.where(usable, real, 0.0), jnp.where(usable, imag, 0.0)
    src_valid = jnp.where(usable[:, :LANES], 1.0, 0.0)
    for ref, value in ((src_re, real), (src_diff, imag - real), (src_sum, imag + real)):
        for block in range(nbins // LANES):
            ref[block] = value[:, block * LANES : (block + 1) * LANES]
    tile = keep if segments <= 2 else min(keep, 16)

    def spread(ref, block, row):
        return jnp.concatenate([ref[block, pl.ds(row, 8, stride=0), :]] * (tile // 8), axis=0)

    def multiply(block, carry):
        at = pl.ds(pl.multiple_of(block * LANES, LANES), LANES)
        for first in range(0, keep, tile):
            rcv_rows = [pl.ds(pl.multiple_of(row + first, 8), tile) for row in at_rows]
            r_re = [rcv_re[row, at] for row in rcv_rows]
            r_im = [rcv_im[row, at] for row in rcv_rows]
            r_both = [rcv_both[row, at] for row in rcv_rows]
            for source in range(count):
                p, q, w = [], [], []
                for t in range(segments):
                    row = t * count + source
                    p.append(spread(src_re, block, row) * r_both[t])
                    q.append(spread(src_diff, block, row) * r_im[t])
                    w.append(spread(src_sum, block, row) * r_re[t])
                p, q, w = (functools.reduce(jnp.add, part) for part in (p, q, w))
                to = slice(source * keep + first, source * keep + first + tile)
                cross[0, block, to] = (p + q).astype(cross.dtype)
                cross[1, block, to] = (w - p).astype(cross.dtype)
        return carry

    lax.fori_loop(0, nbins // LANES, multiply, 0)

    def project(place, part):
        value = [cross[place, block, part] for block in range(nbins // LANES)]
        return jnp.dot(
            jnp.concatenate(value, axis=1).astype(jnp.bfloat16),
            table_ref[place * nbins : (place + 1) * nbins],
            preferred_element_type=jnp.float32,
        )

    ends = []
    for first in (0, count // 2):
        at = slice(first * keep, (first + count // 2) * keep)
        sums = [project(place, at) for place in range(2)]
        if not first_stage:
            sums = [before[0][place, at] + sums[place] for place in range(2)]
        if not last_stage:
            for place in range(2):
                after[0][place, at] = sums[place]
        ends.append(sums)

    lags = 2 * LAG + 1
    scale = 2.0 / math.sqrt(nbins)
    mirror = LAG - FIRST_LAG - iota((keep, LANES), 1)
    pieces = max(1, count // 8)
    copies = []
    for source in range(count):
        to = slice(source * keep, (source + 1) * keep)
        common = [
            src_valid[t * count + source : t * count + source + 1]
            * rcv_valid[pl.ds(at_rows[t], keep), :]
            for t in range(segments)
        ] + ([] if first_stage else [before[1][to]])
        common = functools.reduce(jnp.add, common)
        if not last_stage:
            after[1][to] = common
            continue
        result, written = refs
        weight = scale / jnp.maximum(common, 1.0)
        inside = slice(source % (count // 2) * keep, (source % (count // 2) + 1) * keep)
        even, odd = (total[inside] for total in ends[source // (count // 2)])
        ahead = even + odd
        behind = even - odd
        low_part = jnp.take_along_axis(
            behind[:, :LANES], jnp.clip(mirror, 0, LANES - 1), axis=1
        )
        high_part = jnp.take_along_axis(
            behind[:, LANES:], jnp.clip(mirror - LANES, 0, LANES - 1), axis=1
        )
        result[to, :LANES] = jnp.where(mirror < LANES, low_part, high_part) * weight
        for first in range(0, lags - LANES, LANES):
            last = min(first + LANES, lags - LANES)
            value = ahead[:, first : first + LANES] * weight
            result[to, LANES + first : LANES + last] = value[:, : last - first]
        if (source + 1) % pieces == 0:
            at = pl.ds((source + 1 - pieces) * keep, pieces * keep)
            copies.append(
                pltpu.make_async_copy(
                    result.at[at], after[0].at[at], written.at[source // pieces]
                )
            )
            copies[-1].start()
    for copy in copies:
        copy.wait()


def encode(segments, spectra, valid, sources):
    channels, width = spectra.shape
    keep = channels // segments
    slab = jax.ShapeDtypeStruct((2 * sources.size, width // 2), jnp.bfloat16)
    block = jax.ShapeDtypeStruct((keep, width), jnp.bfloat16)
    padded = pltpu.VMEM((sources.size, width // 2 + 2 * LANES), jnp.bfloat16)
    pinned = [pltpu.with_memory_space_constraint(x, pltpu.HBM) for x in (spectra, valid, sources)]
    return pl.pallas_call(
        functools.partial(encode_kernel, segments),
        out_shape=(slab,) + (block,) * segments,
        in_specs=[HBM] * 3,
        out_specs=(VMEM,) * (1 + segments),
        scratch_shapes=[
            pltpu.VMEM((channels, width), kind_for(keep)),
            pltpu.VMEM((channels, width), jnp.bfloat16),
            pltpu.VMEM((1, channels), jnp.int32),
            pltpu.SMEM(sources.shape, jnp.int32),
            padded,
            padded,
            pltpu.SemaphoreType.DMA((3,)),
        ],
        compiler_params=pltpu.CompilerParams(vmem_limit_bytes=12 * MEBI),
        name="encode_and_pick",
    )(*pinned)


def whiten_blocks(blocks):
    segments, (keep, width) = len(blocks), blocks[0].shape
    count, nbins = segments * keep, width // 2
    padded = pltpu.VMEM((count, nbins + 2 * LANES), jnp.bfloat16)
    part = jax.ShapeDtypeStruct((count, nbins), jnp.float32)
    return pl.pallas_call(
        functools.partial(whiten_kernel, segments),
        out_shape=(part, part, part, jax.ShapeDtypeStruct((count, LANES), jnp.float32)),
        in_specs=[VMEM] * segments,
        out_specs=(VMEM,) * 4,
        scratch_shapes=[padded, padded],
        compiler_params=pltpu.CompilerParams(vmem_limit_bytes=20 * MEBI),
        cost_estimate=pl.CostEstimate(
            flops=count * width * 1024, bytes_accessed=count * width * 4, transcendentals=0
        ),
        name="whiten_receivers",
    )(*blocks)


def stack_stage(keep, slabs, places, receivers, table, before=(), last=True):
    count, nbins = slabs[0].shape[0] // 2, slabs[0].shape[1]
    rows, lags = count * keep, 2 * LAG + 1
    part = pltpu.VMEM((nbins // LANES, len(slabs) * count, LANES), jnp.float32)
    cross = pltpu.VMEM((2, nbins // LANES, rows, LANES), kind_for(keep))
    scratch = [part, part, part, cross]
    sums = (
        jax.ShapeDtypeStruct((2, rows, BLOCK), jnp.float32),
        jax.ShapeDtypeStruct((rows, LANES), jnp.float32),
    )
    if last:
        scratch += [pltpu.VMEM((rows, lags), jnp.float32), pltpu.SemaphoreType.DMA((count,))]
    return pl.pallas_call(
        functools.partial(stack_kernel, places, (not before, last)),
        out_shape=jax.ShapeDtypeStruct((rows, lags), jnp.float32) if last else sums,
        in_specs=[VMEM] * (len(slabs) + len(receivers) + 1 + len(before)),
        out_specs=HBM if last else (VMEM, VMEM),
        scratch_shapes=scratch,
        compiler_params=pltpu.CompilerParams(vmem_limit_bytes=26 * MEBI),
        cost_estimate=pl.CostEstimate(
            flops=4 * rows * nbins * 2 * LAG, bytes_accessed=nbins * 2048, transcendentals=0
        ),
        name="stack_last" if last else "stack_first",
    )(*slabs, *receivers, table, *before)


def swapped(value, axis, size, step):
    return lax.ppermute(value, axis, [(i, i ^ step) for i in range(size)])


def gather_shared(picked, receivers, rcv_size, tm_size):
    core = lax.axis_index("rcv") % 2
    receivers[3] = swapped(receivers[3], "tm", tm_size, 3)
    own = picked + swapped(picked, "rcv", rcv_size, 1)
    own, near = lax.optimization_barrier((own, receivers[1:3]))
    receivers[1:3] = [swapped(block, "tm", tm_size, place) for place, block in enumerate(near, 1)]
    far = lax.ppermute(own, "rcv", [(i, i ^ (6 if i % 2 else 4)) for i in range(rcv_size)])
    near = swapped(own, "rcv", rcv_size, 2)
    far, receivers[3] = lax.optimization_barrier((far, receivers[3]))
    near, receivers[1:3] = lax.optimization_barrier((near, receivers[1:3]))
    partial = far + jnp.where(core == 0, own, jnp.zeros_like(own))
    own = near + (partial + swapped(partial, "rcv", rcv_size, 1))
    pairs = [
        (rcv * tm_size + tm, rcv * tm_size + (tm ^ (2 if rcv % 2 else 1)))
        for rcv in range(rcv_size)
        for tm in range(tm_size)
    ]
    beside = lax.ppermute(own, ("rcv", "tm"), pairs)
    across = swapped(own, "tm", tm_size, 3)
    beside, whitened = lax.optimization_barrier((beside, whiten_blocks(receivers)))
    handed = swapped(beside, "rcv", rcv_size, 1)
    return (own, beside), (handed, across), whitened


def shards(rcv_size, tm_size, spectra, valid, sources):
    channels, _, width = spectra.shape
    keep = channels // tm_size
    rounds, per_round = sources.shape
    table = jnp.asarray(lag_table(width // 2))
    picked, *receivers = encode(
        tm_size, spectra[:, 0, :], valid.reshape(1, channels), sources
    )
    if (rcv_size, tm_size) == (8, 4):
        first, rest, whitened = gather_shared(picked, receivers, rcv_size, tm_size)
        places = [lambda core: 0, lambda core: 1 + core]
        sums = stack_stage(keep, first, places, whitened, table, last=False)
        places = [lambda core: 2 - core, lambda core: 3]
        stack = stack_stage(keep, rest, places, whitened, table, sums)
    else:
        receivers[1:] = [
            swapped(receivers[place], "tm", tm_size, place) for place in range(1, tm_size)
        ]
        step = 1
        while step < rcv_size:
            picked = picked + swapped(picked, "rcv", rcv_size, step)
            step *= 2
        slabs = [picked] + [swapped(picked, "tm", tm_size, place) for place in range(1, tm_size)]
        places = [functools.partial(lambda place, core: place, place) for place in range(tm_size)]
        stack = stack_stage(keep, slabs, places, whiten_blocks(receivers), table)
    return stack.reshape(rounds, per_round, keep, 2 * LAG + 1)


def solution(mesh):
    body = functools.partial(shards, mesh.shape["rcv"], mesh.shape["tm"])
    in_specs = (P("rcv", "tm", None), P("rcv", "tm"), P())
    out_specs = P(None, None, ("rcv", "tm"), None)
    return jax.shard_map(body, mesh=mesh, in_specs=in_specs, out_specs=out_specs, check_vma=False)
```

```python
import functools
import math

import jax
import jax.numpy as jnp
import numpy as np
from jax import lax
from jax.experimental import pallas as pl
from jax.experimental.pallas import tpu as pltpu
from jax.sharding import PartitionSpec as P

NT = 4096
LAG = 150
HALF_WIN = 64
EPSILON = 1e-06

UNUSABLE = 1024.0
USABLE_BELOW = 512.0

LANES = 128
BLOCK = 256
MEBI = 1 << 20
FIRST_LAG = LANES - LAG
VMEM = pl.BlockSpec(memory_space=pltpu.VMEM)
HBM = pl.BlockSpec(memory_space=pltpu.HBM)


def lag_table(nbins):
    winding = np.mod(
        np.arange(1, nbins + 1, dtype=np.int64)[:, None]
        * np.arange(FIRST_LAG, FIRST_LAG + BLOCK, dtype=np.int64)[None, :],
        NT,
    )
    theta = winding * (2.0 * math.pi / NT)
    return np.concatenate([np.cos(theta), -np.sin(theta)], axis=0).astype(jnp.bfloat16)


def kind_for(rows):
    return jnp.bfloat16 if rows % 16 == 0 else jnp.float32


def iota(shape, dim):
    return lax.broadcasted_iota(jnp.int32, shape, dim)


def band_matrix():
    shape = (BLOCK + 2 * LANES, BLOCK)
    near = jnp.abs(iota(shape, 0) - LANES - iota(shape, 1)) <= HALF_WIN
    return jnp.where(near, 1.0, 0.0).astype(jnp.bfloat16)


def whitening(real, imag, high, low, unusable=0.0, band=None):
    count, nbins = real.shape
    blocks = nbins // BLOCK
    span = BLOCK + 2 * LANES
    amplitude = jnp.sqrt(real * real + imag * imag)
    rounded = amplitude.astype(jnp.bfloat16)
    edge = jnp.zeros((count, LANES), jnp.bfloat16)
    for part, value in (
        (high, rounded),
        (low, (amplitude - rounded.astype(jnp.float32)).astype(jnp.bfloat16)),
    ):
        part[:, :LANES] = edge
        part[:, LANES : LANES + nbins] = value
        part[:, LANES + nbins :] = edge
    band = band_matrix() if band is None else band[...]
    pieces = [
        part[:, block * BLOCK : block * BLOCK + span] for block in range(blocks) for part in (high, low)
    ]
    windows = jnp.dot(
        jnp.concatenate(pieces, axis=0), band, preferred_element_type=jnp.float32
    )
    for block in range(blocks):
        first = block * BLOCK
        at = 2 * block * count
        window = windows[at : at + count] + windows[at + count : at + 2 * count]
        index = first + iota((1, BLOCK), 1)
        counted = jnp.minimum(index, HALF_WIN) + jnp.minimum(nbins - 1 - index, HALF_WIN) + 1
        factor = 1.0 / (window / counted.astype(jnp.float32) + EPSILON)
        re = real[:, first : first + BLOCK]
        im = imag[:, first : first + BLOCK]
        usable = re < USABLE_BELOW
        re = jnp.where(usable, re * factor, unusable).astype(jnp.bfloat16).astype(jnp.float32)
        im = jnp.where(usable, im * factor, unusable).astype(jnp.bfloat16).astype(jnp.float32)
        yield slice(first, first + BLOCK), re, im


def usable_rows(real):
    return jnp.where(real[:, :LANES] < USABLE_BELOW, 1.0, 0.0)


def encode_kernel(
    segments, spectra_ref, valid_ref, sources_ref, own_ref, other_ref, *refs
):
    blocks, refs = refs[:segments], refs[segments:]
    encoded_ref, spectra, valid, sources, high, low, band, arrived = refs
    copies = [
        pltpu.make_async_copy(spectra_ref, spectra, arrived.at[0]),
        pltpu.make_async_copy(sources_ref, sources, arrived.at[1]),
        pltpu.make_async_copy(valid_ref, valid, arrived.at[2]),
    ]
    for copy in copies:
        copy.start()
    channels, width = spectra_ref.shape
    nbins = width // 2
    rounds, per_round = sources.shape
    half = rounds * per_round // 2
    index = lax.axis_index("rcv")
    copies[1].wait()
    copies[2].wait()
    diagonal = iota((channels, channels), 0) == iota((channels, channels), 1)
    usable = jnp.sum(jnp.where(diagonal, valid[...], 0), axis=1, keepdims=True) != 0
    row = iota((2 * half, channels), 0)
    local = jnp.zeros((2 * half, channels), jnp.int32)
    for place in range(2 * half):
        number = (index % 2 if place < half else 1 - index % 2) * half + place % half
        here = sources[number // per_round, number % per_round] - index * channels
        local = jnp.where(row == place, here, local)
    onehot = jnp.where(local == iota((2 * half, channels), 1), 1.0, 0.0).astype(jnp.bfloat16)
    band[...] = band_matrix()
    copies[0].wait()
    encoded = jnp.where(usable, spectra[...].astype(jnp.float32), UNUSABLE).astype(jnp.bfloat16)
    picked = jnp.dot(onehot, encoded, preferred_element_type=jnp.float32)
    for at, re, im in whitening(picked[:, :nbins], picked[:, nbins:], high, low, UNUSABLE, band):
        for first, ref in ((0, own_ref), (half, other_ref)):
            rows = slice(first, first + half)
            ref[:, at] = jnp.concatenate([re[rows], im[rows]], axis=0).astype(ref.dtype)
    encoded_ref[...] = encoded.astype(encoded_ref.dtype)
    keep = channels // segments
    for step, block in enumerate(blocks):
        at = pl.multiple_of((lax.axis_index("tm") ^ step) * keep, keep)
        block[...] = encoded_ref[pl.ds(at, keep), :].astype(block.dtype)


def whiten_kernel(segments, *refs):
    blocks, refs = refs[:segments], refs[segments:]
    real_ref, imag_ref, both_ref, valid_ref, high, low = refs
    rows = jnp.concatenate([ref[...].astype(jnp.float32) for ref in blocks], axis=0)
    nbins = rows.shape[1] // 2
    real, imag = rows[:, :nbins], rows[:, nbins:]
    for at, re, im in whitening(real, imag, high, low):
        real_ref[:, at] = re
        imag_ref[:, at] = im
        both_ref[:, at] = re + im
    valid_ref[...] = usable_rows(real)


def stack_kernel(places, halves, stage, *refs):
    first_stage, last_stage = stage
    segments, inputs = len(places), 1 + max(slab for pair in halves for slab, _ in pair)
    slabs, refs = refs[:inputs], refs[inputs:]
    rcv_re, rcv_im, rcv_both, rcv_valid, table_ref, *refs = refs
    before, refs = ([], refs) if first_stage else (refs[:2], refs[2:])
    after, refs = (refs[:1], refs[1:]) if last_stage else (refs[:2], refs[2:])
    src_re, src_diff, src_sum, cross, *refs = refs
    nbins, rows = slabs[0].shape[1], cross.shape[2]
    count = src_re.shape[1] // segments
    keep, half = rows // count, count // 2
    core = lax.axis_index("rcv") % 2
    at_rows = [pl.multiple_of(place(core) * keep, keep) for place in places]
    values = [
        slabs[slab][first : first + count].astype(jnp.float32)
        for pair in halves
        for slab, first in pair
    ]
    real = jnp.concatenate([value[:half] for value in values], axis=0)
    imag = jnp.concatenate([value[half:] for value in values], axis=0)
    usable = real < USABLE_BELOW
    real, imag = jnp.where(usable, real, 0.0), jnp.where(usable, imag, 0.0)
    src_valid = jnp.where(usable[:, :LANES], 1.0, 0.0)
    for ref, value in ((src_re, real), (src_diff, imag - real), (src_sum, imag + real)):
        for block in range(nbins // LANES):
            ref[block] = value[:, block * LANES : (block + 1) * LANES]
    tile = keep if segments <= 2 else min(keep, 16)

    def spread(ref, block, row):
        return jnp.concatenate([ref[block, pl.ds(row, 8, stride=0), :]] * (tile // 8), axis=0)

    def multiply(block, carry):
        at = pl.ds(pl.multiple_of(block * LANES, LANES), LANES)
        for first in range(0, keep, tile):
            rcv_rows = [pl.ds(pl.multiple_of(row + first, 8), tile) for row in at_rows]
            r_re = [rcv_re[row, at] for row in rcv_rows]
            r_im = [rcv_im[row, at] for row in rcv_rows]
            r_both = [rcv_both[row, at] for row in rcv_rows]
            for source in range(count):
                p, q, w = [], [], []
                for t in range(segments):
                    row = t * count + source
                    p.append(spread(src_re, block, row) * r_both[t])
                    q.append(spread(src_diff, block, row) * r_im[t])
                    w.append(spread(src_sum, block, row) * r_re[t])
                p, q, w = (functools.reduce(jnp.add, part) for part in (p, q, w))
                to = slice(source * keep + first, source * keep + first + tile)
                cross[0, block, to] = (p + q).astype(cross.dtype)
                cross[1, block, to] = (w - p).astype(cross.dtype)
        return carry

    lax.fori_loop(0, nbins // LANES, multiply, 0)

    def project(place, part):
        value = [cross[place, block, part] for block in range(nbins // LANES)]
        return jnp.dot(
            jnp.concatenate(value, axis=1).astype(jnp.bfloat16),
            table_ref[place * nbins : (place + 1) * nbins],
            preferred_element_type=jnp.float32,
        )

    ends = []
    for first in (0, count // 2):
        at = slice(first * keep, (first + count // 2) * keep)
        sums = [project(place, at) for place in range(2)]
        if not first_stage:
            sums = [before[0][place, at] + sums[place] for place in range(2)]
        if not last_stage:
            for place in range(2):
                after[0][place, at] = sums[place]
        ends.append(sums)

    lags = 2 * LAG + 1
    scale = 2.0 / math.sqrt(nbins)
    mirror = LAG - FIRST_LAG - iota((keep, LANES), 1)
    pieces = max(1, count // 8)
    copies = []
    for source in range(count):
        to = slice(source * keep, (source + 1) * keep)
        common = [
            src_valid[t * count + source : t * count + source + 1]
            * rcv_valid[pl.ds(at_rows[t], keep), :]
            for t in range(segments)
        ] + ([] if first_stage else [before[1][to]])
        common = functools.reduce(jnp.add, common)
        if not last_stage:
            after[1][to] = common
            continue
        result, written = refs
        weight = scale / jnp.maximum(common, 1.0)
        inside = slice(source % (count // 2) * keep, (source % (count // 2) + 1) * keep)
        even, odd = (total[inside] for total in ends[source // (count // 2)])
        ahead = even + odd
        behind = even - odd
        low_part = jnp.take_along_axis(
            behind[:, :LANES], jnp.clip(mirror, 0, LANES - 1), axis=1
        )
        high_part = jnp.take_along_axis(
            behind[:, LANES:], jnp.clip(mirror - LANES, 0, LANES - 1), axis=1
        )
        result[to, :LANES] = jnp.where(mirror < LANES, low_part, high_part) * weight
        for first in range(0, lags - LANES, LANES):
            last = min(first + LANES, lags - LANES)
            value = ahead[:, first : first + LANES] * weight
            result[to, LANES + first : LANES + last] = value[:, : last - first]
        if (source + 1) % pieces == 0:
            first, size = (source + 1 - pieces) * keep, pieces * keep
            to = (first + core * half * keep) % rows
            copies.append(
                pltpu.make_async_copy(
                    result.at[pl.ds(first, size)],
                    after[0].at[pl.ds(pl.multiple_of(to, size), size)],
                    written.at[source // pieces],
                )
            )
            copies[-1].start()
    for copy in copies:
        copy.wait()


def encode(segments, spectra, valid, sources):
    channels, width = spectra.shape
    keep = channels // segments
    slab = jax.ShapeDtypeStruct((sources.size, width // 2), jnp.bfloat16)
    block = jax.ShapeDtypeStruct((keep, width), jnp.bfloat16)
    padded = pltpu.VMEM((sources.size, width // 2 + 2 * LANES), jnp.bfloat16)
    pinned = [pltpu.with_memory_space_constraint(x, pltpu.HBM) for x in (spectra, valid, sources)]
    return pl.pallas_call(
        functools.partial(encode_kernel, segments),
        out_shape=(slab, slab) + (block,) * segments,
        in_specs=[HBM] * 3,
        out_specs=(VMEM,) * (2 + segments),
        scratch_shapes=[
            pltpu.VMEM((channels, width), kind_for(keep)),
            pltpu.VMEM((channels, width), jnp.bfloat16),
            pltpu.VMEM((1, channels), jnp.int32),
            pltpu.SMEM(sources.shape, jnp.int32),
            padded,
            padded,
            pltpu.VMEM((BLOCK + 2 * LANES, BLOCK), jnp.bfloat16),
            pltpu.SemaphoreType.DMA((3,)),
        ],
        compiler_params=pltpu.CompilerParams(vmem_limit_bytes=12 * MEBI),
        name="encode_and_pick",
    )(*pinned)


def whiten_blocks(blocks):
    segments, (keep, width) = len(blocks), blocks[0].shape
    count, nbins = segments * keep, width // 2
    padded = pltpu.VMEM((count, nbins + 2 * LANES), jnp.bfloat16)
    part = jax.ShapeDtypeStruct((count, nbins), jnp.float32)
    return pl.pallas_call(
        functools.partial(whiten_kernel, segments),
        out_shape=(part, part, part, jax.ShapeDtypeStruct((count, LANES), jnp.float32)),
        in_specs=[VMEM] * segments,
        out_specs=(VMEM,) * 4,
        scratch_shapes=[padded, padded],
        compiler_params=pltpu.CompilerParams(vmem_limit_bytes=20 * MEBI),
        cost_estimate=pl.CostEstimate(
            flops=count * width * 1024, bytes_accessed=count * width * 4, transcendentals=0
        ),
        name="whiten_receivers",
    )(*blocks)


def stack_stage(count, keep, slabs, halves, places, receivers, table, before=(), last=True):
    nbins = slabs[0].shape[1]
    rows, lags = count * keep, 2 * LAG + 1
    part = pltpu.VMEM((nbins // LANES, len(places) * count, LANES), jnp.float32)
    cross = pltpu.VMEM((2, nbins // LANES, rows, LANES), kind_for(keep))
    scratch = [part, part, part, cross]
    sums = (
        jax.ShapeDtypeStruct((2, rows, BLOCK), jnp.float32),
        jax.ShapeDtypeStruct((rows, LANES), jnp.float32),
    )
    if last:
        scratch += [pltpu.VMEM((rows, lags), jnp.float32), pltpu.SemaphoreType.DMA((count,))]
    return pl.pallas_call(
        functools.partial(stack_kernel, places, halves, (not before, last)),
        out_shape=jax.ShapeDtypeStruct((rows, lags), jnp.float32) if last else sums,
        in_specs=[VMEM] * (len(slabs) + len(receivers) + 1 + len(before)),
        out_specs=HBM if last else (VMEM, VMEM),
        scratch_shapes=scratch,
        compiler_params=pltpu.CompilerParams(vmem_limit_bytes=26 * MEBI),
        cost_estimate=pl.CostEstimate(
            flops=4 * rows * nbins * 2 * LAG, bytes_accessed=nbins * 2048, transcendentals=0
        ),
        name="stack_last" if last else "stack_first",
    )(*slabs, *receivers, table, *before)


def swapped(value, axis, size, step):
    return lax.ppermute(value, axis, [(i, i ^ step) for i in range(size)])


def gather_shared(own, other, receivers, rcv_size, tm_size):
    def both(one, two):
        return jnp.concatenate([one, two], axis=0)

    core, count = lax.axis_index("rcv") % 2, own.shape[0]
    receivers[3] = swapped(receivers[3], "tm", tm_size, 3)
    rows = both(own, other) + swapped(both(other, own), "rcv", rcv_size, 1)
    rows, near = lax.optimization_barrier((rows, receivers[1:3]))
    receivers[1:3] = [swapped(block, "tm", tm_size, place) for place, block in enumerate(near, 1)]
    far = lax.ppermute(rows, "rcv", [(i, i ^ (6 if i % 2 else 4)) for i in range(rcv_size)])
    near = swapped(rows, "rcv", rcv_size, 2)
    far, receivers[3] = lax.optimization_barrier((far, receivers[3]))
    near, receivers[1:3] = lax.optimization_barrier((near, receivers[1:3]))
    partial = far + jnp.where(core == 0, rows, jnp.zeros_like(rows))
    handed = swapped(both(partial[count:], partial[:count]), "rcv", rcv_size, 1)
    rows = near + (partial + handed)
    pairs = [
        (rcv * tm_size + tm, rcv * tm_size + (tm ^ (2 if rcv % 2 else 1)))
        for rcv in range(rcv_size)
        for tm in range(tm_size)
    ]
    beside = lax.ppermute(rows, ("rcv", "tm"), pairs)
    across = swapped(rows[:count], "tm", tm_size, 3)
    beside, across, whitened = lax.optimization_barrier(
        (beside, across, whiten_blocks(receivers))
    )
    handed = swapped(
        both(both(beside[count:], beside[:count]), across), "rcv", rcv_size, 1
    )
    return (rows, beside), (handed, across), whitened


def shards(rcv_size, tm_size, spectra, valid, sources):
    channels, _, width = spectra.shape
    keep, count = channels // tm_size, sources.size
    table = jnp.asarray(lag_table(width // 2))
    own, other, *receivers = encode(
        tm_size, spectra[:, 0, :], valid.reshape(1, channels), sources
    )
    if (rcv_size, tm_size) == (8, 4):
        first, rest, whitened = gather_shared(own, other, receivers, rcv_size, tm_size)
        places = [lambda core: 0, lambda core: 1 + core]
        halves = [((0, 0), (0, count)), ((1, 0), (1, count))]
        sums = stack_stage(count, keep, first, halves, places, whitened, table, last=False)
        places = [lambda core: 2 - core, lambda core: 3]
        halves = [((0, 0), (0, count)), ((1, 0), (0, 2 * count))]
        stack = stack_stage(count, keep, rest, halves, places, whitened, table, sums)
    else:
        receivers[1:] = [
            swapped(receivers[place], "tm", tm_size, place) for place in range(1, tm_size)
        ]
        both = jnp.concatenate(
            [own + swapped(other, "rcv", rcv_size, 1), other + swapped(own, "rcv", rcv_size, 1)],
            axis=0,
        )
        step = 2
        while step < rcv_size:
            both = both + swapped(both, "rcv", rcv_size, step)
            step *= 2
        slabs = [both] + [swapped(both, "tm", tm_size, place) for place in range(1, tm_size)]
        places = [functools.partial(lambda place, core: place, place) for place in range(tm_size)]
        halves = [((place, 0), (place, count)) for place in range(tm_size)]
        whitened = whiten_blocks(receivers)
        stack = stack_stage(count, keep, slabs, halves, places, whitened, table)
    return stack.reshape(sources.shape + (keep, 2 * LAG + 1))


def solution(mesh):
    body = functools.partial(shards, mesh.shape["rcv"], mesh.shape["tm"])
    in_specs = (P("rcv", "tm", None), P("rcv", "tm"), P())
    out_specs = P(None, None, ("rcv", "tm"), None)
    return jax.shard_map(body, mesh=mesh, in_specs=in_specs, out_specs=out_specs, check_vma=False)
```

```python
import functools
import math

import jax
import jax.numpy as jnp
import numpy as np
from jax import lax
from jax.experimental import pallas as pl
from jax.experimental.pallas import tpu as pltpu
from jax.sharding import PartitionSpec as P

NT = 4096
LAG = 150
HALF_WIN = 64
EPSILON = 1e-06

UNUSABLE = 1024.0
USABLE_BELOW = 512.0

LANES = 128
BLOCK = 256
MEBI = 1 << 20
FIRST_LAG = LANES - LAG
VMEM = pl.BlockSpec(memory_space=pltpu.VMEM)
HBM = pl.BlockSpec(memory_space=pltpu.HBM)


def lag_table(nbins):
    winding = np.mod(
        np.arange(1, nbins + 1, dtype=np.int64)[:, None]
        * np.arange(FIRST_LAG, FIRST_LAG + BLOCK, dtype=np.int64)[None, :],
        NT,
    )
    theta = winding * (2.0 * math.pi / NT)
    return np.concatenate([np.cos(theta), -np.sin(theta)], axis=0).astype(jnp.bfloat16)


def kind_for(rows):
    return jnp.bfloat16 if rows % 16 == 0 else jnp.float32


def iota(shape, dim):
    return lax.broadcasted_iota(jnp.int32, shape, dim)


def band_matrix():
    shape = (BLOCK + 2 * LANES, BLOCK)
    near = jnp.abs(iota(shape, 0) - LANES - iota(shape, 1)) <= HALF_WIN
    return jnp.where(near, 1.0, 0.0).astype(jnp.bfloat16)


def whitening(real, imag, high, low, unusable=0.0, band=None):
    count, nbins = real.shape
    blocks = nbins // BLOCK
    span = BLOCK + 2 * LANES
    amplitude = jnp.sqrt(real * real + imag * imag)
    rounded = amplitude.astype(jnp.bfloat16)
    edge = jnp.zeros((count, LANES), jnp.bfloat16)
    for part, value in (
        (high, rounded),
        (low, (amplitude - rounded.astype(jnp.float32)).astype(jnp.bfloat16)),
    ):
        part[:, :LANES] = edge
        part[:, LANES : LANES + nbins] = value
        part[:, LANES + nbins :] = edge
    band = band_matrix() if band is None else band[...]
    pieces = [
        part[:, block * BLOCK : block * BLOCK + span] for block in range(blocks) for part in (high, low)
    ]
    windows = jnp.dot(
        jnp.concatenate(pieces, axis=0), band, preferred_element_type=jnp.float32
    )
    for block in range(blocks):
        first = block * BLOCK
        at = 2 * block * count
        window = windows[at : at + count] + windows[at + count : at + 2 * count]
        index = first + iota((1, BLOCK), 1)
        counted = jnp.minimum(index, HALF_WIN) + jnp.minimum(nbins - 1 - index, HALF_WIN) + 1
        factor = 1.0 / (window / counted.astype(jnp.float32) + EPSILON)
        re = real[:, first : first + BLOCK]
        im = imag[:, first : first + BLOCK]
        usable = re < USABLE_BELOW
        re = jnp.where(usable, re * factor, unusable).astype(jnp.bfloat16).astype(jnp.float32)
        im = jnp.where(usable, im * factor, unusable).astype(jnp.bfloat16).astype(jnp.float32)
        yield slice(first, first + BLOCK), re, im


def usable_rows(real):
    return jnp.where(real[:, :LANES] < USABLE_BELOW, 1.0, 0.0)


def encode_kernel(
    segments, spectra_ref, valid_ref, sources_ref, own_ref, other_ref, *refs
):
    blocks, refs = refs[:segments], refs[segments:]
    encoded_ref, spectra, valid, sources, high, low, band, arrived = refs
    copies = [
        pltpu.make_async_copy(spectra_ref, spectra, arrived.at[0]),
        pltpu.make_async_copy(sources_ref, sources, arrived.at[1]),
        pltpu.make_async_copy(valid_ref, valid, arrived.at[2]),
    ]
    for copy in copies:
        copy.start()
    channels, width = spectra_ref.shape
    nbins = width // 2
    rounds, per_round = sources.shape
    half = rounds * per_round // 2
    index = lax.axis_index("rcv")
    copies[1].wait()
    copies[2].wait()
    diagonal = iota((channels, channels), 0) == iota((channels, channels), 1)
    usable = jnp.sum(jnp.where(diagonal, valid[...], 0), axis=1, keepdims=True) != 0
    row = iota((2 * half, channels), 0)
    local = jnp.zeros((2 * half, channels), jnp.int32)
    for place in range(2 * half):
        number = (index % 2 if place < half else 1 - index % 2) * half + place % half
        here = sources[number // per_round, number % per_round] - index * channels
        local = jnp.where(row == place, here, local)
    onehot = jnp.where(local == iota((2 * half, channels), 1), 1.0, 0.0).astype(jnp.bfloat16)
    band[...] = band_matrix()
    copies[0].wait()
    encoded = jnp.where(usable, spectra[...].astype(jnp.float32), UNUSABLE).astype(jnp.bfloat16)
    picked = jnp.dot(onehot, encoded, preferred_element_type=jnp.float32)
    for at, re, im in whitening(picked[:, :nbins], picked[:, nbins:], high, low, UNUSABLE, band):
        for first, ref in ((0, own_ref), (half, other_ref)):
            rows = slice(first, first + half)
            ref[:, at] = jnp.concatenate([re[rows], im[rows]], axis=0).astype(ref.dtype)
    encoded_ref[...] = encoded.astype(encoded_ref.dtype)
    keep = channels // segments
    for step, block in enumerate(blocks):
        at = pl.multiple_of((lax.axis_index("tm") ^ step) * keep, keep)
        block[...] = encoded_ref[pl.ds(at, keep), :].astype(block.dtype)


def whiten_kernel(segments, *refs):
    blocks, refs = refs[:segments], refs[segments:]
    real_ref, imag_ref, both_ref, valid_ref, high, low = refs
    rows = jnp.concatenate([ref[...].astype(jnp.float32) for ref in blocks], axis=0)
    nbins = rows.shape[1] // 2
    real, imag = rows[:, :nbins], rows[:, nbins:]
    for at, re, im in whitening(real, imag, high, low):
        real_ref[:, at] = re
        imag_ref[:, at] = im
        both_ref[:, at] = re + im
    valid_ref[...] = usable_rows(real)


def stack_kernel(places, stage, *refs):
    segments, sets = len(places), 1 + max(which for which, _ in places)
    slabs, refs = refs[0], refs[1:]
    receivers = [refs[4 * which : 4 * which + 4] for which in range(sets)]
    table_ref, refs = refs[4 * sets], refs[4 * sets + 1 :]
    first_stage, stage = stage
    before, refs = ([], refs) if first_stage else (refs[:2], refs[2:])
    ready, refs = (refs[0], refs[1:]) if stage == "store" else (None, refs)
    after, refs = (refs[:2], refs[2:]) if stage == "sums" else (refs[:1], refs[1:])
    src_re, src_diff, src_sum, cross, *refs = refs
    nbins, rows = slabs.shape[1], cross.shape[2]
    count = slabs.shape[0] // (2 * segments)
    keep = rows // count
    copies = []
    if stage == "store":
        result, written = refs
        part = lax.axis_index("rcv") % 2
        at = pl.multiple_of(part * rows, rows)
        copies.append(
            pltpu.make_async_copy(ready, after[0].at[pl.ds(at, rows)], written.at[count])
        )
        copies[0].start()
    elif stage == "result":
        result = after[0]
    values = slabs[...].astype(jnp.float32)
    real = jnp.concatenate(
        [values[2 * count * t : 2 * count * t + count] for t in range(segments)], axis=0
    )
    imag = jnp.concatenate(
        [values[2 * count * t + count : 2 * count * (t + 1)] for t in range(segments)], axis=0
    )
    usable = real < USABLE_BELOW
    real, imag = jnp.where(usable, real, 0.0), jnp.where(usable, imag, 0.0)
    src_valid = jnp.where(usable[:, :LANES], 1.0, 0.0)
    for ref, value in ((src_re, real), (src_diff, imag - real), (src_sum, imag + real)):
        for block in range(nbins // LANES):
            ref[block] = value[:, block * LANES : (block + 1) * LANES]
    tile = keep if segments <= 2 else min(keep, 16)

    def spread(ref, block, row):
        return jnp.concatenate([ref[block, pl.ds(row, 8, stride=0), :]] * (tile // 8), axis=0)

    def multiply(block, carry):
        at = pl.ds(pl.multiple_of(block * LANES, LANES), LANES)
        for first in range(0, keep, tile):
            taken = [
                (receivers[which], slice(place * keep + first, place * keep + first + tile))
                for which, place in places
            ]
            r_re = [block_refs[0][row, at] for block_refs, row in taken]
            r_im = [block_refs[1][row, at] for block_refs, row in taken]
            r_both = [block_refs[2][row, at] for block_refs, row in taken]
            for source in range(count):
                p, q, w = [], [], []
                for t in range(segments):
                    row = t * count + source
                    p.append(spread(src_re, block, row) * r_both[t])
                    q.append(spread(src_diff, block, row) * r_im[t])
                    w.append(spread(src_sum, block, row) * r_re[t])
                p, q, w = (functools.reduce(jnp.add, part) for part in (p, q, w))
                to = slice(source * keep + first, source * keep + first + tile)
                cross[0, block, to] = (p + q).astype(cross.dtype)
                cross[1, block, to] = (w - p).astype(cross.dtype)
        return carry

    lax.fori_loop(0, nbins // LANES, multiply, 0)

    def project(place, part):
        value = [cross[place, block, part] for block in range(nbins // LANES)]
        return jnp.dot(
            jnp.concatenate(value, axis=1).astype(jnp.bfloat16),
            table_ref[place * nbins : (place + 1) * nbins],
            preferred_element_type=jnp.float32,
        )

    ends = []
    for first in (0, count // 2):
        at = slice(first * keep, (first + count // 2) * keep)
        sums = [project(place, at) for place in range(2)]
        if not first_stage:
            sums = [before[0][place, at] + sums[place] for place in range(2)]
        if stage == "sums":
            for place in range(2):
                after[0][place, at] = sums[place]
        ends.append(sums)

    lags = 2 * LAG + 1
    scale = 2.0 / math.sqrt(nbins)
    mirror = LAG - FIRST_LAG - iota((keep, LANES), 1)
    pieces = max(1, count // 4)
    for source in range(count):
        to = slice(source * keep, (source + 1) * keep)
        common = [
            src_valid[t * count + source : t * count + source + 1]
            * receivers[which][3][place * keep : (place + 1) * keep, :]
            for t, (which, place) in enumerate(places)
        ] + ([] if first_stage else [before[1][to]])
        common = functools.reduce(jnp.add, common)
        if stage == "sums":
            after[1][to] = common
            continue
        weight = scale / jnp.maximum(common, 1.0)
        inside = slice(source % (count // 2) * keep, (source % (count // 2) + 1) * keep)
        even, odd = (total[inside] for total in ends[source // (count // 2)])
        ahead = even + odd
        behind = even - odd
        low_part = jnp.take_along_axis(
            behind[:, :LANES], jnp.clip(mirror, 0, LANES - 1), axis=1
        )
        high_part = jnp.take_along_axis(
            behind[:, LANES:], jnp.clip(mirror - LANES, 0, LANES - 1), axis=1
        )
        result[to, :LANES] = jnp.where(mirror < LANES, low_part, high_part) * weight
        for first in range(0, lags - LANES, LANES):
            last = min(first + LANES, lags - LANES)
            value = ahead[:, first : first + LANES] * weight
            result[to, LANES + first : LANES + last] = value[:, : last - first]
        if stage == "store" and (source + 1) % pieces == 0:
            first, size = (source + 1 - pieces) * keep, pieces * keep
            at = pl.multiple_of((1 - part) * rows + first, size)
            copies.append(
                pltpu.make_async_copy(
                    result.at[pl.ds(first, size)],
                    after[0].at[pl.ds(at, size)],
                    written.at[source // pieces],
                )
            )
            copies[-1].start()
    for copy in copies:
        copy.wait()


def encode(segments, spectra, valid, sources):
    channels, width = spectra.shape
    keep = channels // segments
    slab = jax.ShapeDtypeStruct((sources.size, width // 2), jnp.bfloat16)
    block = jax.ShapeDtypeStruct((keep, width), jnp.bfloat16)
    padded = pltpu.VMEM((sources.size, width // 2 + 2 * LANES), jnp.bfloat16)
    pinned = [pltpu.with_memory_space_constraint(x, pltpu.HBM) for x in (spectra, valid, sources)]
    return pl.pallas_call(
        functools.partial(encode_kernel, segments),
        out_shape=(slab, slab) + (block,) * segments,
        in_specs=[HBM] * 3,
        out_specs=(VMEM,) * (2 + segments),
        scratch_shapes=[
            pltpu.VMEM((channels, width), kind_for(keep)),
            pltpu.VMEM((channels, width), jnp.bfloat16),
            pltpu.VMEM((1, channels), jnp.int32),
            pltpu.SMEM(sources.shape, jnp.int32),
            padded,
            padded,
            pltpu.VMEM((BLOCK + 2 * LANES, BLOCK), jnp.bfloat16),
            pltpu.SemaphoreType.DMA((3,)),
        ],
        compiler_params=pltpu.CompilerParams(vmem_limit_bytes=12 * MEBI),
        name="encode_and_pick",
    )(*pinned)


def whiten_blocks(blocks):
    segments, (keep, width) = len(blocks), blocks[0].shape
    count, nbins = segments * keep, width // 2
    padded = pltpu.VMEM((count, nbins + 2 * LANES), jnp.bfloat16)
    part = jax.ShapeDtypeStruct((count, nbins), jnp.float32)
    return pl.pallas_call(
        functools.partial(whiten_kernel, segments),
        out_shape=(part, part, part, jax.ShapeDtypeStruct((count, LANES), jnp.float32)),
        in_specs=[VMEM] * segments,
        out_specs=(VMEM,) * 4,
        scratch_shapes=[padded, padded],
        compiler_params=pltpu.CompilerParams(vmem_limit_bytes=20 * MEBI),
        cost_estimate=pl.CostEstimate(
            flops=count * width * 1024, bytes_accessed=count * width * 4, transcendentals=0
        ),
        name="whiten_receivers",
    )(*blocks)


def stack_stage(keep, slabs, places, receivers, table, stage, before=(), ready=()):
    count, nbins = slabs.shape[0] // (2 * len(places)), slabs.shape[1]
    rows, lags = count * keep, 2 * LAG + 1
    part = pltpu.VMEM((nbins // LANES, len(places) * count, LANES), jnp.float32)
    cross = pltpu.VMEM((2, nbins // LANES, rows, LANES), kind_for(keep))
    scratch = [part, part, part, cross]
    sums = (
        jax.ShapeDtypeStruct((2, rows, BLOCK), jnp.float32),
        jax.ShapeDtypeStruct((rows, LANES), jnp.float32),
    )
    if stage == "store":
        scratch += [pltpu.VMEM((rows, lags), jnp.float32), pltpu.SemaphoreType.DMA((count + 1,))]
    out_rows = 2 * rows if stage == "store" else rows
    result = jax.ShapeDtypeStruct((out_rows, lags), jnp.float32)
    inputs = [slabs, *sum(receivers, ()), table, *before, *ready]
    return pl.pallas_call(
        functools.partial(stack_kernel, places, (not before, stage)),
        out_shape=sums if stage == "sums" else result,
        in_specs=[VMEM] * len(inputs),
        out_specs=(VMEM, VMEM) if stage == "sums" else HBM if stage == "store" else VMEM,
        scratch_shapes=scratch,
        compiler_params=pltpu.CompilerParams(vmem_limit_bytes=20 * MEBI),
        cost_estimate=pl.CostEstimate(
            flops=4 * rows * nbins * 2 * LAG, bytes_accessed=nbins * 2048, transcendentals=0
        ),
        name="stack_" + stage,
    )(*inputs)


def swapped(value, axis, size, step):
    return lax.ppermute(value, axis, [(i, i ^ step) for i in range(size)])


def shards(rcv_size, tm_size, spectra, valid, sources):
    channels, _, width = spectra.shape
    keep = channels // tm_size
    rounds, per_round = sources.shape
    own, other, *receivers = encode(
        tm_size, spectra[:, 0, :], valid.reshape(1, channels), sources
    )
    receivers[-1] = swapped(receivers[-1], "tm", tm_size, tm_size - 1)
    own = own + swapped(other, "rcv", rcv_size, 1)
    own, later = lax.optimization_barrier((own, receivers[1:-1]))
    receivers[1:-1] = [
        swapped(block, "tm", tm_size, place) for place, block in enumerate(later, 1)
    ]
    step = 2
    while step < rcv_size:
        wide = min(4, rcv_size // step)
        parts = [swapped(own, "rcv", rcv_size, place * step) for place in range(1, wide)]
        if step == 2:
            parts[-1], receivers[-1] = lax.optimization_barrier((parts[-1], receivers[-1]))
        own = functools.reduce(jnp.add, parts, own)
        step *= wide
    own = [own] + [swapped(own, "tm", tm_size, place) for place in range(1, tm_size)]
    own[-1], receivers[1:-1] = lax.optimization_barrier((own[-1], receivers[1:-1]))
    table = jnp.asarray(lag_table(width // 2))
    far = tm_size - 1
    early = tuple(whiten_blocks([receivers[0], receivers[far]]))
    sums = stack_stage(
        keep, jnp.concatenate([own[0], own[far]], axis=0), [(0, 0), (0, 1)], [early], table, "sums"
    )
    late = tuple(whiten_blocks(receivers[1:far]))
    rest, sums, late = lax.optimization_barrier((own[1:far], sums, late))
    slabs = jnp.concatenate([own[0], own[far], *rest], axis=0)
    other = swapped(slabs, "rcv", rcv_size, 1)
    places = [(0, place) for place in range(far - 1)]
    first = stack_stage(
        keep, slabs[2 * own[0].shape[0] :], places, [late], table, "result", sums
    )
    places = [(0, 0), (0, 1)] + [(1, place) for place in range(far - 1)]
    stack = stack_stage(keep, other, places, [early, late], table, "store", (), (first,))
    return stack.reshape(rounds, per_round, keep, 2 * LAG + 1)


def solution(mesh):
    body = functools.partial(shards, mesh.shape["rcv"], mesh.shape["tm"])
    in_specs = (P("rcv", "tm", None), P("rcv", "tm"), P())
    out_specs = P(None, None, ("rcv", "tm"), None)
    return jax.shard_map(body, mesh=mesh, in_specs=in_specs, out_specs=out_specs, check_vma=False)
```

```python
import functools
import math

import jax
import jax.numpy as jnp
import numpy as np
from jax import lax
from jax.experimental import pallas as pl
from jax.experimental.pallas import tpu as pltpu
from jax.sharding import PartitionSpec as P

NT = 4096
LAG = 150
HALF_WIN = 64
EPSILON = 1e-06

UNUSABLE = 1024.0
USABLE_BELOW = 512.0

LANES = 128
BLOCK = 256
MEBI = 1 << 20
FIRST_LAG = LANES - LAG
VMEM = pl.BlockSpec(memory_space=pltpu.VMEM)
HBM = pl.BlockSpec(memory_space=pltpu.HBM)


def lag_table(nbins):
    winding = np.mod(
        np.arange(1, nbins + 1, dtype=np.int64)[:, None]
        * np.arange(FIRST_LAG, FIRST_LAG + BLOCK, dtype=np.int64)[None, :],
        NT,
    )
    theta = winding * (2.0 * math.pi / NT)
    return np.concatenate([np.cos(theta), -np.sin(theta)], axis=0).astype(jnp.bfloat16)


def kind_for(rows):
    return jnp.bfloat16 if rows % 16 == 0 else jnp.float32


def iota(shape, dim):
    return lax.broadcasted_iota(jnp.int32, shape, dim)


def band_matrix():
    shape = (BLOCK + 2 * LANES, BLOCK)
    near = jnp.abs(iota(shape, 0) - LANES - iota(shape, 1)) <= HALF_WIN
    return jnp.where(near, 1.0, 0.0).astype(jnp.bfloat16)


def whitening(real, imag, high, low, unusable=0.0, band=None):
    count, nbins = real.shape
    blocks = nbins // BLOCK
    span = BLOCK + 2 * LANES
    amplitude = jnp.sqrt(real * real + imag * imag)
    rounded = amplitude.astype(jnp.bfloat16)
    edge = jnp.zeros((count, LANES), jnp.bfloat16)
    for part, value in (
        (high, rounded),
        (low, (amplitude - rounded.astype(jnp.float32)).astype(jnp.bfloat16)),
    ):
        part[:, :LANES] = edge
        part[:, LANES : LANES + nbins] = value
        part[:, LANES + nbins :] = edge
    band = band_matrix() if band is None else band[...]
    pieces = [
        part[:, block * BLOCK : block * BLOCK + span] for block in range(blocks) for part in (high, low)
    ]
    windows = jnp.dot(
        jnp.concatenate(pieces, axis=0), band, preferred_element_type=jnp.float32
    )
    for block in range(blocks):
        first = block * BLOCK
        at = 2 * block * count
        window = windows[at : at + count] + windows[at + count : at + 2 * count]
        index = first + iota((1, BLOCK), 1)
        counted = jnp.minimum(index, HALF_WIN) + jnp.minimum(nbins - 1 - index, HALF_WIN) + 1
        factor = 1.0 / (window / counted.astype(jnp.float32) + EPSILON)
        re = real[:, first : first + BLOCK]
        im = imag[:, first : first + BLOCK]
        usable = re < USABLE_BELOW
        re = jnp.where(usable, re * factor, unusable).astype(jnp.bfloat16).astype(jnp.float32)
        im = jnp.where(usable, im * factor, unusable).astype(jnp.bfloat16).astype(jnp.float32)
        yield slice(first, first + BLOCK), re, im


def usable_rows(real):
    return jnp.where(real[:, :LANES] < USABLE_BELOW, 1.0, 0.0)


def encode_kernel(
    segments, spectra_ref, valid_ref, sources_ref, own_ref, other_ref, *refs
):
    blocks, refs = refs[:segments], refs[segments:]
    encoded_ref, spectra, valid, sources, high, low, band, arrived = refs
    copies = [
        pltpu.make_async_copy(spectra_ref, spectra, arrived.at[0]),
        pltpu.make_async_copy(sources_ref, sources, arrived.at[1]),
        pltpu.make_async_copy(valid_ref, valid, arrived.at[2]),
    ]
    for copy in copies:
        copy.start()
    channels, width = spectra_ref.shape
    nbins = width // 2
    rounds, per_round = sources.shape
    half = rounds * per_round // 2
    index = lax.axis_index("rcv")
    copies[1].wait()
    copies[2].wait()
    diagonal = iota((channels, channels), 0) == iota((channels, channels), 1)
    usable = jnp.sum(jnp.where(diagonal, valid[...], 0), axis=1, keepdims=True) != 0
    row = iota((2 * half, channels), 0)
    local = jnp.zeros((2 * half, channels), jnp.int32)
    for place in range(2 * half):
        number = (index % 2 if place < half else 1 - index % 2) * half + place % half
        here = sources[number // per_round, number % per_round] - index * channels
        local = jnp.where(row == place, here, local)
    onehot = jnp.where(local == iota((2 * half, channels), 1), 1.0, 0.0).astype(jnp.bfloat16)
    band[...] = band_matrix()
    copies[0].wait()
    encoded = jnp.where(usable, spectra[...].astype(jnp.float32), UNUSABLE).astype(jnp.bfloat16)
    picked = jnp.dot(onehot, encoded, preferred_element_type=jnp.float32)
    for at, re, im in whitening(picked[:, :nbins], picked[:, nbins:], high, low, UNUSABLE, band):
        for first, ref in ((0, own_ref), (half, other_ref)):
            rows = slice(first, first + half)
            ref[:, at] = jnp.concatenate([re[rows], im[rows]], axis=0).astype(ref.dtype)
    encoded_ref[...] = encoded.astype(encoded_ref.dtype)
    keep = channels // segments
    for step, block in enumerate(blocks):
        at = pl.multiple_of((lax.axis_index("tm") ^ step) * keep, keep)
        block[...] = encoded_ref[pl.ds(at, keep), :].astype(block.dtype)


def whiten_kernel(segments, *refs):
    blocks, refs = refs[:segments], refs[segments:]
    real_ref, imag_ref, both_ref, valid_ref, high, low = refs
    rows = jnp.concatenate([ref[...].astype(jnp.float32) for ref in blocks], axis=0)
    nbins = rows.shape[1] // 2
    real, imag = rows[:, :nbins], rows[:, nbins:]
    for at, re, im in whitening(real, imag, high, low):
        real_ref[:, at] = re
        imag_ref[:, at] = im
        both_ref[:, at] = re + im
    valid_ref[...] = usable_rows(real)


def stack_kernel(places, stage, *refs):
    segments, sets = len(places), 1 + max(which for which, _ in places)
    slabs, refs = refs[0], refs[1:]
    receivers = [refs[4 * which : 4 * which + 4] for which in range(sets)]
    table_ref, refs = refs[4 * sets], refs[4 * sets + 1 :]
    first_stage, stage = stage
    before, refs = ([], refs) if first_stage else (refs[:2], refs[2:])
    ready, refs = (refs[0], refs[1:]) if stage == "store" else (None, refs)
    after, refs = (refs[:2], refs[2:]) if stage == "sums" else (refs[:1], refs[1:])
    src_re, src_diff, src_sum, cross, *refs = refs
    nbins, rows = slabs.shape[1], cross.shape[2]
    count = slabs.shape[0] // (2 * segments)
    keep = rows // count
    copies = []
    if stage == "store":
        result, written = refs
        part = lax.axis_index("rcv") % 2
        at = pl.multiple_of(part * rows, rows)
        copies.append(
            pltpu.make_async_copy(ready, after[0].at[pl.ds(at, rows)], written.at[count])
        )
        copies[0].start()
    elif stage == "result":
        result = after[0]
    values = slabs[...].astype(jnp.float32)
    real = jnp.concatenate(
        [values[2 * count * t : 2 * count * t + count] for t in range(segments)], axis=0
    )
    imag = jnp.concatenate(
        [values[2 * count * t + count : 2 * count * (t + 1)] for t in range(segments)], axis=0
    )
    usable = real < USABLE_BELOW
    real, imag = jnp.where(usable, real, 0.0), jnp.where(usable, imag, 0.0)
    src_valid = jnp.where(usable[:, :LANES], 1.0, 0.0)
    for ref, value in ((src_re, real), (src_diff, imag - real), (src_sum, imag + real)):
        for block in range(nbins // LANES):
            ref[block] = value[:, block * LANES : (block + 1) * LANES]
    tile = keep if segments <= 2 else min(keep, 16)

    def spread(ref, block, row):
        return jnp.concatenate([ref[block, pl.ds(row, 8, stride=0), :]] * (tile // 8), axis=0)

    def multiply(block, carry):
        at = pl.ds(pl.multiple_of(block * LANES, LANES), LANES)
        for first in range(0, keep, tile):
            taken = [
                (receivers[which], slice(place * keep + first, place * keep + first + tile))
                for which, place in places
            ]
            r_re = [block_refs[0][row, at] for block_refs, row in taken]
            r_im = [block_refs[1][row, at] for block_refs, row in taken]
            r_both = [block_refs[2][row, at] for block_refs, row in taken]
            for source in range(count):
                p, q, w = [], [], []
                for t in range(segments):
                    row = t * count + source
                    p.append(spread(src_re, block, row) * r_both[t])
                    q.append(spread(src_diff, block, row) * r_im[t])
                    w.append(spread(src_sum, block, row) * r_re[t])
                p, q, w = (functools.reduce(jnp.add, part) for part in (p, q, w))
                to = slice(source * keep + first, source * keep + first + tile)
                cross[0, block, to] = (p + q).astype(cross.dtype)
                cross[1, block, to] = (w - p).astype(cross.dtype)
        return carry

    lax.fori_loop(0, nbins // LANES, multiply, 0)

    def project(place, part):
        value = [cross[place, block, part] for block in range(nbins // LANES)]
        return jnp.dot(
            jnp.concatenate(value, axis=1).astype(jnp.bfloat16),
            table_ref[place * nbins : (place + 1) * nbins],
            preferred_element_type=jnp.float32,
        )

    ends = []
    for first in (0, count // 2):
        at = slice(first * keep, (first + count // 2) * keep)
        sums = [project(place, at) for place in range(2)]
        if not first_stage:
            sums = [before[0][place, at] + sums[place] for place in range(2)]
        if stage == "sums":
            for place in range(2):
                after[0][place, at] = sums[place]
        ends.append(sums)

    lags = 2 * LAG + 1
    scale = 2.0 / math.sqrt(nbins)
    mirror = LAG - FIRST_LAG - iota((keep, LANES), 1)
    pieces = max(1, count // 4)
    for source in range(count):
        to = slice(source * keep, (source + 1) * keep)
        common = [
            src_valid[t * count + source : t * count + source + 1]
            * receivers[which][3][place * keep : (place + 1) * keep, :]
            for t, (which, place) in enumerate(places)
        ] + ([] if first_stage else [before[1][to]])
        common = functools.reduce(jnp.add, common)
        if stage == "sums":
            after[1][to] = common
            continue
        weight = scale / jnp.maximum(common, 1.0)
        inside = slice(source % (count // 2) * keep, (source % (count // 2) + 1) * keep)
        even, odd = (total[inside] for total in ends[source // (count // 2)])
        ahead = even + odd
        behind = even - odd
        low_part = jnp.take_along_axis(
            behind[:, :LANES], jnp.clip(mirror, 0, LANES - 1), axis=1
        )
        high_part = jnp.take_along_axis(
            behind[:, LANES:], jnp.clip(mirror - LANES, 0, LANES - 1), axis=1
        )
        result[to, :LANES] = jnp.where(mirror < LANES, low_part, high_part) * weight
        for first in range(0, lags - LANES, LANES):
            last = min(first + LANES, lags - LANES)
            value = ahead[:, first : first + LANES] * weight
            result[to, LANES + first : LANES + last] = value[:, : last - first]
        if stage == "store" and (source + 1) % pieces == 0:
            first, size = (source + 1 - pieces) * keep, pieces * keep
            at = pl.multiple_of((1 - part) * rows + first, size)
            copies.append(
                pltpu.make_async_copy(
                    result.at[pl.ds(first, size)],
                    after[0].at[pl.ds(at, size)],
                    written.at[source // pieces],
                )
            )
            copies[-1].start()
    for copy in copies:
        copy.wait()


def encode(segments, spectra, valid, sources):
    channels, width = spectra.shape
    keep = channels // segments
    slab = jax.ShapeDtypeStruct((sources.size, width // 2), jnp.bfloat16)
    block = jax.ShapeDtypeStruct((keep, width), jnp.bfloat16)
    padded = pltpu.VMEM((sources.size, width // 2 + 2 * LANES), jnp.bfloat16)
    pinned = [pltpu.with_memory_space_constraint(x, pltpu.HBM) for x in (spectra, valid, sources)]
    return pl.pallas_call(
        functools.partial(encode_kernel, segments),
        out_shape=(slab, slab) + (block,) * segments,
        in_specs=[HBM] * 3,
        out_specs=(VMEM,) * (2 + segments),
        scratch_shapes=[
            pltpu.VMEM((channels, width), kind_for(keep)),
            pltpu.VMEM((channels, width), jnp.bfloat16),
            pltpu.VMEM((1, channels), jnp.int32),
            pltpu.SMEM(sources.shape, jnp.int32),
            padded,
            padded,
            pltpu.VMEM((BLOCK + 2 * LANES, BLOCK), jnp.bfloat16),
            pltpu.SemaphoreType.DMA((3,)),
        ],
        compiler_params=pltpu.CompilerParams(vmem_limit_bytes=12 * MEBI),
        name="encode_and_pick",
    )(*pinned)


def whiten_blocks(blocks):
    segments, (keep, width) = len(blocks), blocks[0].shape
    count, nbins = segments * keep, width // 2
    padded = pltpu.VMEM((count, nbins + 2 * LANES), jnp.bfloat16)
    part = jax.ShapeDtypeStruct((count, nbins), jnp.float32)
    return pl.pallas_call(
        functools.partial(whiten_kernel, segments),
        out_shape=(part, part, part, jax.ShapeDtypeStruct((count, LANES), jnp.float32)),
        in_specs=[VMEM] * segments,
        out_specs=(VMEM,) * 4,
        scratch_shapes=[padded, padded],
        compiler_params=pltpu.CompilerParams(vmem_limit_bytes=20 * MEBI),
        cost_estimate=pl.CostEstimate(
            flops=count * width * 1024, bytes_accessed=count * width * 4, transcendentals=0
        ),
        name="whiten_receivers",
    )(*blocks)


def stack_stage(keep, slabs, places, receivers, table, stage, before=(), ready=()):
    count, nbins = slabs.shape[0] // (2 * len(places)), slabs.shape[1]
    rows, lags = count * keep, 2 * LAG + 1
    part = pltpu.VMEM((nbins // LANES, len(places) * count, LANES), jnp.float32)
    cross = pltpu.VMEM((2, nbins // LANES, rows, LANES), kind_for(keep))
    scratch = [part, part, part, cross]
    sums = (
        jax.ShapeDtypeStruct((2, rows, BLOCK), jnp.float32),
        jax.ShapeDtypeStruct((rows, LANES), jnp.float32),
    )
    if stage == "store":
        scratch += [pltpu.VMEM((rows, lags), jnp.float32), pltpu.SemaphoreType.DMA((count + 1,))]
    out_rows = 2 * rows if stage == "store" else rows
    result = jax.ShapeDtypeStruct((out_rows, lags), jnp.float32)
    inputs = [slabs, *sum(receivers, ()), table, *before, *ready]
    return pl.pallas_call(
        functools.partial(stack_kernel, places, (not before, stage)),
        out_shape=sums if stage == "sums" else result,
        in_specs=[VMEM] * len(inputs),
        out_specs=(VMEM, VMEM) if stage == "sums" else HBM if stage == "store" else VMEM,
        scratch_shapes=scratch,
        compiler_params=pltpu.CompilerParams(vmem_limit_bytes=20 * MEBI),
        cost_estimate=pl.CostEstimate(
            flops=4 * rows * nbins * 2 * LAG, bytes_accessed=nbins * 2048, transcendentals=0
        ),
        name="stack_" + stage,
    )(*inputs)


def swapped(value, axis, size, step):
    return lax.ppermute(value, axis, [(i, i ^ step) for i in range(size)])


def shards(rcv_size, tm_size, spectra, valid, sources):
    channels, _, width = spectra.shape
    keep = channels // tm_size
    rounds, per_round = sources.shape
    own, other, *receivers = encode(
        tm_size, spectra[:, 0, :], valid.reshape(1, channels), sources
    )
    receivers[-1] = swapped(receivers[-1], "tm", tm_size, tm_size - 1)
    own = own + swapped(other, "rcv", rcv_size, 1)
    own, later = lax.optimization_barrier((own, receivers[1:-1]))
    receivers[1:-1] = [
        swapped(block, "tm", tm_size, place) for place, block in enumerate(later, 1)
    ]
    step = 2
    while step < rcv_size:
        wide = min(4, rcv_size // step)
        parts = [swapped(own, "rcv", rcv_size, place * step) for place in range(1, wide)]
        if step == 2:
            parts[-1], receivers[-1] = lax.optimization_barrier((parts[-1], receivers[-1]))
        own = functools.reduce(jnp.add, parts, own)
        step *= wide
    own = [own] + [swapped(own, "tm", tm_size, place) for place in range(1, tm_size)]
    table = jnp.asarray(lag_table(width // 2))
    far = tm_size - 1
    early = tuple(whiten_blocks([receivers[0], receivers[far]]))
    late = tuple(whiten_blocks(receivers[1:far]))
    own[far], early, late = lax.optimization_barrier((own[far], early, late))
    sums = stack_stage(
        keep, jnp.concatenate([own[0], own[far]], axis=0), [(0, 0), (0, 1)], [early], table, "sums"
    )
    rest, sums, late = lax.optimization_barrier((own[1:far], sums, late))
    slabs = jnp.concatenate([own[0], own[far], *rest], axis=0)
    other = swapped(slabs, "rcv", rcv_size, 1)
    places = [(0, place) for place in range(far - 1)]
    first = stack_stage(
        keep, slabs[2 * own[0].shape[0] :], places, [late], table, "result", sums
    )
    places = [(0, 0), (0, 1)] + [(1, place) for place in range(far - 1)]
    stack = stack_stage(keep, other, places, [early, late], table, "store", (), (first,))
    return stack.reshape(rounds, per_round, keep, 2 * LAG + 1)


def solution(mesh):
    body = functools.partial(shards, mesh.shape["rcv"], mesh.shape["tm"])
    in_specs = (P("rcv", "tm", None), P("rcv", "tm"), P())
    out_specs = P(None, None, ("rcv", "tm"), None)
    return jax.shard_map(body, mesh=mesh, in_specs=in_specs, out_specs=out_specs, check_vma=False)
```

```python
import functools
import math

import jax
import jax.numpy as jnp
import numpy as np
from jax import lax
from jax.experimental import pallas as pl
from jax.experimental.pallas import tpu as pltpu
from jax.sharding import PartitionSpec as P

NT = 4096
LAG = 150
HALF_WIN = 64
EPSILON = 1e-06

UNUSABLE = 1024.0
USABLE_BELOW = 512.0

LANES = 128
BLOCK = 256
MEBI = 1 << 20
FIRST_LAG = LANES - LAG
VMEM = pl.BlockSpec(memory_space=pltpu.VMEM)
HBM = pl.BlockSpec(memory_space=pltpu.HBM)


def lag_table(nbins):
    winding = np.mod(
        np.arange(1, nbins + 1, dtype=np.int64)[:, None]
        * np.arange(FIRST_LAG, FIRST_LAG + BLOCK, dtype=np.int64)[None, :],
        NT,
    )
    theta = winding * (2.0 * math.pi / NT)
    return np.concatenate([np.cos(theta), -np.sin(theta)], axis=0).astype(jnp.bfloat16)


def kind_for(rows):
    return jnp.bfloat16 if rows % 16 == 0 else jnp.float32


def iota(shape, dim):
    return lax.broadcasted_iota(jnp.int32, shape, dim)


def band_matrix():
    shape = (BLOCK + 2 * LANES, BLOCK)
    near = jnp.abs(iota(shape, 0) - LANES - iota(shape, 1)) <= HALF_WIN
    return jnp.where(near, 1.0, 0.0).astype(jnp.bfloat16)


def whitening(real, imag, high, low, unusable=0.0, band=None):
    count, nbins = real.shape
    blocks = nbins // BLOCK
    span = BLOCK + 2 * LANES
    amplitude = jnp.sqrt(real * real + imag * imag)
    rounded = amplitude.astype(jnp.bfloat16)
    edge = jnp.zeros((count, LANES), jnp.bfloat16)
    for part, value in (
        (high, rounded),
        (low, (amplitude - rounded.astype(jnp.float32)).astype(jnp.bfloat16)),
    ):
        part[:, :LANES] = edge
        part[:, LANES : LANES + nbins] = value
        part[:, LANES + nbins :] = edge
    band = band_matrix() if band is None else band[...]
    pieces = [
        part[:, block * BLOCK : block * BLOCK + span] for block in range(blocks) for part in (high, low)
    ]
    windows = jnp.dot(
        jnp.concatenate(pieces, axis=0), band, preferred_element_type=jnp.float32
    )
    for block in range(blocks):
        first = block * BLOCK
        at = 2 * block * count
        window = windows[at : at + count] + windows[at + count : at + 2 * count]
        index = first + iota((1, BLOCK), 1)
        counted = jnp.minimum(index, HALF_WIN) + jnp.minimum(nbins - 1 - index, HALF_WIN) + 1
        factor = 1.0 / (window / counted.astype(jnp.float32) + EPSILON)
        re = real[:, first : first + BLOCK]
        im = imag[:, first : first + BLOCK]
        usable = re < USABLE_BELOW
        re = jnp.where(usable, re * factor, unusable).astype(jnp.bfloat16).astype(jnp.float32)
        im = jnp.where(usable, im * factor, unusable).astype(jnp.bfloat16).astype(jnp.float32)
        yield slice(first, first + BLOCK), re, im


def usable_rows(real):
    return jnp.where(real[:, :LANES] < USABLE_BELOW, 1.0, 0.0)


def encode_kernel(
    segments, spectra_ref, valid_ref, sources_ref, own_ref, other_ref, *refs
):
    blocks, refs = refs[:segments], refs[segments:]
    encoded_ref, spectra, valid, sources, high, low, band, arrived = refs
    copies = [
        pltpu.make_async_copy(spectra_ref, spectra, arrived.at[0]),
        pltpu.make_async_copy(sources_ref, sources, arrived.at[1]),
        pltpu.make_async_copy(valid_ref, valid, arrived.at[2]),
    ]
    for copy in copies:
        copy.start()
    channels, width = spectra_ref.shape
    nbins = width // 2
    rounds, per_round = sources.shape
    half = rounds * per_round // 2
    index = lax.axis_index("rcv")
    copies[1].wait()
    copies[2].wait()
    diagonal = iota((channels, channels), 0) == iota((channels, channels), 1)
    usable = jnp.sum(jnp.where(diagonal, valid[...], 0), axis=1, keepdims=True) != 0
    row = iota((2 * half, channels), 0)
    local = jnp.zeros((2 * half, channels), jnp.int32)
    for place in range(2 * half):
        number = (index % 2 if place < half else 1 - index % 2) * half + place % half
        here = sources[number // per_round, number % per_round] - index * channels
        local = jnp.where(row == place, here, local)
    onehot = jnp.where(local == iota((2 * half, channels), 1), 1.0, 0.0).astype(jnp.bfloat16)
    band[...] = band_matrix()
    copies[0].wait()
    encoded = jnp.where(usable, spectra[...].astype(jnp.float32), UNUSABLE).astype(jnp.bfloat16)
    picked = jnp.dot(onehot, encoded, preferred_element_type=jnp.float32)
    for at, re, im in whitening(picked[:, :nbins], picked[:, nbins:], high, low, UNUSABLE, band):
        for first, ref in ((0, own_ref), (half, other_ref)):
            rows = slice(first, first + half)
            ref[:, at] = jnp.concatenate([re[rows], im[rows]], axis=0).astype(ref.dtype)
    encoded_ref[...] = encoded.astype(encoded_ref.dtype)
    keep = channels // segments
    for step, block in enumerate(blocks):
        at = pl.multiple_of((lax.axis_index("tm") ^ step) * keep, keep)
        block[...] = encoded_ref[pl.ds(at, keep), :].astype(block.dtype)


def whiten_kernel(segments, *refs):
    blocks, refs = refs[:segments], refs[segments:]
    real_ref, imag_ref, both_ref, valid_ref, high, low = refs
    rows = jnp.concatenate([ref[...].astype(jnp.float32) for ref in blocks], axis=0)
    nbins = rows.shape[1] // 2
    real, imag = rows[:, :nbins], rows[:, nbins:]
    for at, re, im in whitening(real, imag, high, low):
        real_ref[:, at] = re
        imag_ref[:, at] = im
        both_ref[:, at] = re + im
    valid_ref[...] = usable_rows(real)


def stack_kernel(places, stage, *refs):
    segments, sets = len(places), 1 + max(which for which, _ in places)
    slabs, refs = refs[0], refs[1:]
    receivers = [refs[4 * which : 4 * which + 4] for which in range(sets)]
    table_ref, refs = refs[4 * sets], refs[4 * sets + 1 :]
    first_stage, stage = stage
    before, refs = ([], refs) if first_stage else (refs[:2], refs[2:])
    ready, refs = (refs[0], refs[1:]) if stage == "store" else (None, refs)
    after, refs = (refs[:2], refs[2:]) if stage == "sums" else (refs[:1], refs[1:])
    src_re, src_diff, src_sum, cross, *refs = refs
    nbins, rows = slabs.shape[1], cross.shape[2]
    count = slabs.shape[0] // (2 * segments)
    keep = rows // count
    copies = []
    if stage == "store":
        result, written = refs
        part = lax.axis_index("rcv") % 2
        at = pl.multiple_of(part * rows, rows)
        copies.append(
            pltpu.make_async_copy(ready, after[0].at[pl.ds(at, rows)], written.at[count])
        )
        copies[0].start()
    elif stage == "result":
        result = after[0]
    values = slabs[...].astype(jnp.float32)
    real = jnp.concatenate(
        [values[2 * count * t : 2 * count * t + count] for t in range(segments)], axis=0
    )
    imag = jnp.concatenate(
        [values[2 * count * t + count : 2 * count * (t + 1)] for t in range(segments)], axis=0
    )
    usable = real < USABLE_BELOW
    real, imag = jnp.where(usable, real, 0.0), jnp.where(usable, imag, 0.0)
    src_valid = jnp.where(usable[:, :LANES], 1.0, 0.0)
    for ref, value in ((src_re, real), (src_diff, imag - real), (src_sum, imag + real)):
        for block in range(nbins // LANES):
            ref[block] = value[:, block * LANES : (block + 1) * LANES]
    tile = keep if segments <= 2 else min(keep, 16)

    def spread(ref, block, row):
        return jnp.concatenate([ref[block, pl.ds(row, 8, stride=0), :]] * (tile // 8), axis=0)

    def multiply(block, carry):
        at = pl.ds(pl.multiple_of(block * LANES, LANES), LANES)
        for first in range(0, keep, tile):
            taken = [
                (receivers[which], slice(place * keep + first, place * keep + first + tile))
                for which, place in places
            ]
            r_re = [block_refs[0][row, at] for block_refs, row in taken]
            r_im = [block_refs[1][row, at] for block_refs, row in taken]
            r_both = [block_refs[2][row, at] for block_refs, row in taken]
            for source in range(count):
                p, q, w = [], [], []
                for t in range(segments):
                    row = t * count + source
                    p.append(spread(src_re, block, row) * r_both[t])
                    q.append(spread(src_diff, block, row) * r_im[t])
                    w.append(spread(src_sum, block, row) * r_re[t])
                p, q, w = (functools.reduce(jnp.add, part) for part in (p, q, w))
                to = slice(source * keep + first, source * keep + first + tile)
                cross[0, block, to] = (p + q).astype(cross.dtype)
                cross[1, block, to] = (w - p).astype(cross.dtype)
        return carry

    lax.fori_loop(0, nbins // LANES, multiply, 0)

    def project(place, part):
        value = [cross[place, block, part] for block in range(nbins // LANES)]
        return jnp.dot(
            jnp.concatenate(value, axis=1).astype(jnp.bfloat16),
            table_ref[place * nbins : (place + 1) * nbins],
            preferred_element_type=jnp.float32,
        )

    ends = []
    for first in (0, count // 2):
        at = slice(first * keep, (first + count // 2) * keep)
        sums = [project(place, at) for place in range(2)]
        if not first_stage:
            sums = [before[0][place, at] + sums[place] for place in range(2)]
        if stage == "sums":
            for place in range(2):
                after[0][place, at] = sums[place]
        ends.append(sums)

    lags = 2 * LAG + 1
    scale = 2.0 / math.sqrt(nbins)
    mirror = LAG - FIRST_LAG - iota((keep, LANES), 1)
    pieces = max(1, count // 4)
    for source in range(count):
        to = slice(source * keep, (source + 1) * keep)
        common = [
            src_valid[t * count + source : t * count + source + 1]
            * receivers[which][3][place * keep : (place + 1) * keep, :]
            for t, (which, place) in enumerate(places)
        ] + ([] if first_stage else [before[1][to]])
        common = functools.reduce(jnp.add, common)
        if stage == "sums":
            after[1][to] = common
            continue
        weight = scale / jnp.maximum(common, 1.0)
        inside = slice(source % (count // 2) * keep, (source % (count // 2) + 1) * keep)
        even, odd = (total[inside] for total in ends[source // (count // 2)])
        ahead = even + odd
        behind = even - odd
        low_part = jnp.take_along_axis(
            behind[:, :LANES], jnp.clip(mirror, 0, LANES - 1), axis=1
        )
        high_part = jnp.take_along_axis(
            behind[:, LANES:], jnp.clip(mirror - LANES, 0, LANES - 1), axis=1
        )
        result[to, :LANES] = jnp.where(mirror < LANES, low_part, high_part) * weight
        for first in range(0, lags - LANES, LANES):
            last = min(first + LANES, lags - LANES)
            value = ahead[:, first : first + LANES] * weight
            result[to, LANES + first : LANES + last] = value[:, : last - first]
        if stage == "store" and (source + 1) % pieces == 0:
            first, size = (source + 1 - pieces) * keep, pieces * keep
            at = pl.multiple_of((1 - part) * rows + first, size)
            copies.append(
                pltpu.make_async_copy(
                    result.at[pl.ds(first, size)],
                    after[0].at[pl.ds(at, size)],
                    written.at[source // pieces],
                )
            )
            copies[-1].start()
    for copy in copies:
        copy.wait()


def encode(segments, spectra, valid, sources):
    channels, width = spectra.shape
    keep = channels // segments
    slab = jax.ShapeDtypeStruct((sources.size, width // 2), jnp.bfloat16)
    block = jax.ShapeDtypeStruct((keep, width), jnp.bfloat16)
    padded = pltpu.VMEM((sources.size, width // 2 + 2 * LANES), jnp.bfloat16)
    pinned = [pltpu.with_memory_space_constraint(x, pltpu.HBM) for x in (spectra, valid, sources)]
    return pl.pallas_call(
        functools.partial(encode_kernel, segments),
        out_shape=(slab, slab) + (block,) * segments,
        in_specs=[HBM] * 3,
        out_specs=(VMEM,) * (2 + segments),
        scratch_shapes=[
            pltpu.VMEM((channels, width), kind_for(keep)),
            pltpu.VMEM((channels, width), jnp.bfloat16),
            pltpu.VMEM((1, channels), jnp.int32),
            pltpu.SMEM(sources.shape, jnp.int32),
            padded,
            padded,
            pltpu.VMEM((BLOCK + 2 * LANES, BLOCK), jnp.bfloat16),
            pltpu.SemaphoreType.DMA((3,)),
        ],
        compiler_params=pltpu.CompilerParams(vmem_limit_bytes=12 * MEBI),
        name="encode_and_pick",
    )(*pinned)


def whiten_blocks(blocks):
    segments, (keep, width) = len(blocks), blocks[0].shape
    count, nbins = segments * keep, width // 2
    padded = pltpu.VMEM((count, nbins + 2 * LANES), jnp.bfloat16)
    part = jax.ShapeDtypeStruct((count, nbins), jnp.float32)
    return pl.pallas_call(
        functools.partial(whiten_kernel, segments),
        out_shape=(part, part, part, jax.ShapeDtypeStruct((count, LANES), jnp.float32)),
        in_specs=[VMEM] * segments,
        out_specs=(VMEM,) * 4,
        scratch_shapes=[padded, padded],
        compiler_params=pltpu.CompilerParams(vmem_limit_bytes=20 * MEBI),
        cost_estimate=pl.CostEstimate(
            flops=count * width * 1024, bytes_accessed=count * width * 4, transcendentals=0
        ),
        name="whiten_receivers",
    )(*blocks)


def stack_stage(keep, slabs, places, receivers, table, stage, before=(), ready=()):
    count, nbins = slabs.shape[0] // (2 * len(places)), slabs.shape[1]
    rows, lags = count * keep, 2 * LAG + 1
    part = pltpu.VMEM((nbins // LANES, len(places) * count, LANES), jnp.float32)
    cross = pltpu.VMEM((2, nbins // LANES, rows, LANES), kind_for(keep))
    scratch = [part, part, part, cross]
    sums = (
        jax.ShapeDtypeStruct((2, rows, BLOCK), jnp.float32),
        jax.ShapeDtypeStruct((rows, LANES), jnp.float32),
    )
    if stage == "store":
        scratch += [pltpu.VMEM((rows, lags), jnp.float32), pltpu.SemaphoreType.DMA((count + 1,))]
    out_rows = 2 * rows if stage == "store" else rows
    result = jax.ShapeDtypeStruct((out_rows, lags), jnp.float32)
    inputs = [slabs, *sum(receivers, ()), table, *before, *ready]
    return pl.pallas_call(
        functools.partial(stack_kernel, places, (not before, stage)),
        out_shape=sums if stage == "sums" else result,
        in_specs=[VMEM] * len(inputs),
        out_specs=(VMEM, VMEM) if stage == "sums" else HBM if stage == "store" else VMEM,
        scratch_shapes=scratch,
        compiler_params=pltpu.CompilerParams(vmem_limit_bytes=20 * MEBI),
        cost_estimate=pl.CostEstimate(
            flops=4 * rows * nbins * 2 * LAG, bytes_accessed=nbins * 2048, transcendentals=0
        ),
        name="stack_" + stage,
    )(*inputs)


def swapped(value, axis, size, step):
    return lax.ppermute(value, axis, [(i, i ^ step) for i in range(size)])


def shards(rcv_size, tm_size, spectra, valid, sources):
    channels, _, width = spectra.shape
    keep = channels // tm_size
    rounds, per_round = sources.shape
    own, other, *receivers = encode(
        tm_size, spectra[:, 0, :], valid.reshape(1, channels), sources
    )
    receivers[-1] = swapped(receivers[-1], "tm", tm_size, tm_size - 1)
    own = own + swapped(other, "rcv", rcv_size, 1)
    own, later = lax.optimization_barrier((own, receivers[1:-1]))
    receivers[1:-1] = [
        swapped(block, "tm", tm_size, place) for place, block in enumerate(later, 1)
    ]
    step = 2
    while step < rcv_size:
        wide = min(4, rcv_size // step)
        parts = [swapped(own, "rcv", rcv_size, place * step) for place in range(1, wide)]
        if step == 2:
            parts[-1], receivers[-1] = lax.optimization_barrier((parts[-1], receivers[-1]))
            early = tuple(whiten_blocks([receivers[0], receivers[-1]]))
            parts[-2:-1], early = lax.optimization_barrier((parts[-2:-1], early))
        own = functools.reduce(jnp.add, parts, own)
        step *= wide
    own = [own] + [swapped(own, "tm", tm_size, place) for place in range(1, tm_size)]
    table = jnp.asarray(lag_table(width // 2))
    far = tm_size - 1
    late = tuple(whiten_blocks(receivers[1:far]))
    own[far], late = lax.optimization_barrier((own[far], late))
    sums = stack_stage(
        keep, jnp.concatenate([own[0], own[far]], axis=0), [(0, 0), (0, 1)], [early], table, "sums"
    )
    rest, sums, late = lax.optimization_barrier((own[1:far], sums, late))
    slabs = jnp.concatenate([own[0], own[far], *rest], axis=0)
    other = swapped(slabs, "rcv", rcv_size, 1)
    places = [(0, place) for place in range(far - 1)]
    first = stack_stage(
        keep, slabs[2 * own[0].shape[0] :], places, [late], table, "result", sums
    )
    places = [(0, 0), (0, 1)] + [(1, place) for place in range(far - 1)]
    stack = stack_stage(keep, other, places, [early, late], table, "store", (), (first,))
    return stack.reshape(rounds, per_round, keep, 2 * LAG + 1)


def solution(mesh):
    body = functools.partial(shards, mesh.shape["rcv"], mesh.shape["tm"])
    in_specs = (P("rcv", "tm", None), P("rcv", "tm"), P())
    out_specs = P(None, None, ("rcv", "tm"), None)
    return jax.shard_map(body, mesh=mesh, in_specs=in_specs, out_specs=out_specs, check_vma=False)
```

```python
import functools
import math

import jax
import jax.numpy as jnp
import numpy as np
from jax import lax
from jax.experimental import pallas as pl
from jax.experimental.pallas import tpu as pltpu
from jax.sharding import PartitionSpec as P

NT = 4096
LAG = 150
HALF_WIN = 64
EPSILON = 1e-06

UNUSABLE = 1024.0
USABLE_BELOW = 512.0

LANES = 128
BLOCK = 256
MEBI = 1 << 20
FIRST_LAG = LANES - LAG
VMEM = pl.BlockSpec(memory_space=pltpu.VMEM)
HBM = pl.BlockSpec(memory_space=pltpu.HBM)


def lag_table(nbins):
    winding = np.mod(
        np.arange(1, nbins + 1, dtype=np.int64)[:, None]
        * np.arange(FIRST_LAG, FIRST_LAG + BLOCK, dtype=np.int64)[None, :],
        NT,
    )
    theta = winding * (2.0 * math.pi / NT)
    return np.concatenate([np.cos(theta), -np.sin(theta)], axis=0).astype(jnp.bfloat16)


def kind_for(rows):
    return jnp.bfloat16 if rows % 16 == 0 else jnp.float32


def iota(shape, dim):
    return lax.broadcasted_iota(jnp.int32, shape, dim)


def band_matrix():
    shape = (BLOCK + 2 * LANES, BLOCK)
    near = jnp.abs(iota(shape, 0) - LANES - iota(shape, 1)) <= HALF_WIN
    return jnp.where(near, 1.0, 0.0).astype(jnp.bfloat16)


def whitening(real, imag, high, low, unusable=0.0, band=None):
    count, nbins = real.shape
    blocks = nbins // BLOCK
    span = BLOCK + 2 * LANES
    amplitude = jnp.sqrt(real * real + imag * imag)
    rounded = amplitude.astype(jnp.bfloat16)
    edge = jnp.zeros((count, LANES), jnp.bfloat16)
    for part, value in (
        (high, rounded),
        (low, (amplitude - rounded.astype(jnp.float32)).astype(jnp.bfloat16)),
    ):
        part[:, :LANES] = edge
        part[:, LANES : LANES + nbins] = value
        part[:, LANES + nbins :] = edge
    band = band_matrix() if band is None else band[...]
    pieces = [
        part[:, block * BLOCK : block * BLOCK + span] for block in range(blocks) for part in (high, low)
    ]
    windows = jnp.dot(
        jnp.concatenate(pieces, axis=0), band, preferred_element_type=jnp.float32
    )
    for block in range(blocks):
        first = block * BLOCK
        at = 2 * block * count
        window = windows[at : at + count] + windows[at + count : at + 2 * count]
        index = first + iota((1, BLOCK), 1)
        counted = jnp.minimum(index, HALF_WIN) + jnp.minimum(nbins - 1 - index, HALF_WIN) + 1
        factor = 1.0 / (window / counted.astype(jnp.float32) + EPSILON)
        re = real[:, first : first + BLOCK]
        im = imag[:, first : first + BLOCK]
        usable = re < USABLE_BELOW
        re = jnp.where(usable, re * factor, unusable).astype(jnp.bfloat16).astype(jnp.float32)
        im = jnp.where(usable, im * factor, unusable).astype(jnp.bfloat16).astype(jnp.float32)
        yield slice(first, first + BLOCK), re, im


def usable_rows(real):
    return jnp.where(real[:, :LANES] < USABLE_BELOW, 1.0, 0.0)


def encode_kernel(
    segments, spectra_ref, valid_ref, sources_ref, own_ref, other_ref, *refs
):
    blocks, refs = refs[:segments], refs[segments:]
    encoded_ref, spectra, valid, sources, high, low, band, arrived = refs
    copies = [
        pltpu.make_async_copy(spectra_ref, spectra, arrived.at[0]),
        pltpu.make_async_copy(sources_ref, sources, arrived.at[1]),
        pltpu.make_async_copy(valid_ref, valid, arrived.at[2]),
    ]
    for copy in copies:
        copy.start()
    channels, width = spectra_ref.shape
    nbins = width // 2
    rounds, per_round = sources.shape
    half = rounds * per_round // 2
    index = lax.axis_index("rcv")
    copies[1].wait()
    copies[2].wait()
    diagonal = iota((channels, channels), 0) == iota((channels, channels), 1)
    usable = jnp.sum(jnp.where(diagonal, valid[...], 0), axis=1, keepdims=True) != 0
    row = iota((2 * half, channels), 0)
    local = jnp.zeros((2 * half, channels), jnp.int32)
    for place in range(2 * half):
        number = (index % 2 if place < half else 1 - index % 2) * half + place % half
        here = sources[number // per_round, number % per_round] - index * channels
        local = jnp.where(row == place, here, local)
    onehot = jnp.where(local == iota((2 * half, channels), 1), 1.0, 0.0).astype(jnp.bfloat16)
    band[...] = band_matrix()
    copies[0].wait()
    encoded = jnp.where(usable, spectra[...].astype(jnp.float32), UNUSABLE).astype(jnp.bfloat16)
    picked = jnp.dot(onehot, encoded, preferred_element_type=jnp.float32)
    for at, re, im in whitening(picked[:, :nbins], picked[:, nbins:], high, low, UNUSABLE, band):
        for first, ref in ((0, own_ref), (half, other_ref)):
            rows = slice(first, first + half)
            ref[:, at] = jnp.concatenate([re[rows], im[rows]], axis=0).astype(ref.dtype)
    encoded_ref[...] = encoded.astype(encoded_ref.dtype)
    keep = channels // segments
    for step, block in enumerate(blocks):
        at = pl.multiple_of((lax.axis_index("tm") ^ step) * keep, keep)
        block[...] = encoded_ref[pl.ds(at, keep), :].astype(block.dtype)


def whiten_kernel(segments, *refs):
    blocks, refs = refs[:segments], refs[segments:]
    real_ref, imag_ref, both_ref, valid_ref, high, low = refs
    rows = jnp.concatenate([ref[...].astype(jnp.float32) for ref in blocks], axis=0)
    nbins = rows.shape[1] // 2
    real, imag = rows[:, :nbins], rows[:, nbins:]
    for at, re, im in whitening(real, imag, high, low):
        real_ref[:, at] = re
        imag_ref[:, at] = im
        both_ref[:, at] = re + im
    valid_ref[...] = usable_rows(real)


def stack_kernel(places, stage, *refs):
    segments, sets = len(places), 1 + max(which for which, _ in places)
    slabs, refs = refs[0], refs[1:]
    receivers = [refs[4 * which : 4 * which + 4] for which in range(sets)]
    table_ref, refs = refs[4 * sets], refs[4 * sets + 1 :]
    first_stage, stage = stage
    before, refs = ([], refs) if first_stage else (refs[:2], refs[2:])
    ready, refs = (refs[0], refs[1:]) if stage == "store" else (None, refs)
    after, refs = (refs[:2], refs[2:]) if stage == "sums" else (refs[:1], refs[1:])
    src_re, src_diff, src_sum, cross, *refs = refs
    nbins, rows = slabs.shape[1], cross.shape[2]
    count = slabs.shape[0] // (2 * segments)
    keep = rows // count
    copies = []
    if stage == "store":
        result, written = refs
        part = lax.axis_index("rcv") % 2
        at = pl.multiple_of(part * rows, rows)
        copies.append(
            pltpu.make_async_copy(ready, after[0].at[pl.ds(at, rows)], written.at[count])
        )
        copies[0].start()
    elif stage == "result":
        result = after[0]
    values = slabs[...].astype(jnp.float32)
    real = jnp.concatenate(
        [values[2 * count * t : 2 * count * t + count] for t in range(segments)], axis=0
    )
    imag = jnp.concatenate(
        [values[2 * count * t + count : 2 * count * (t + 1)] for t in range(segments)], axis=0
    )
    usable = real < USABLE_BELOW
    real, imag = jnp.where(usable, real, 0.0), jnp.where(usable, imag, 0.0)
    src_valid = jnp.where(usable[:, :LANES], 1.0, 0.0)
    for ref, value in ((src_re, real), (src_diff, imag - real), (src_sum, imag + real)):
        for block in range(nbins // LANES):
            ref[block] = value[:, block * LANES : (block + 1) * LANES]
    tile = keep if segments <= 2 else min(keep, 16)

    def spread(ref, block, row):
        return jnp.concatenate([ref[block, pl.ds(row, 8, stride=0), :]] * (tile // 8), axis=0)

    def multiply(block, carry):
        at = pl.ds(pl.multiple_of(block * LANES, LANES), LANES)
        for first in range(0, keep, tile):
            taken = [
                (receivers[which], slice(place * keep + first, place * keep + first + tile))
                for which, place in places
            ]
            r_re = [block_refs[0][row, at] for block_refs, row in taken]
            r_im = [block_refs[1][row, at] for block_refs, row in taken]
            r_both = [block_refs[2][row, at] for block_refs, row in taken]
            for source in range(count):
                p, q, w = [], [], []
                for t in range(segments):
                    row = t * count + source
                    p.append(spread(src_re, block, row) * r_both[t])
                    q.append(spread(src_diff, block, row) * r_im[t])
                    w.append(spread(src_sum, block, row) * r_re[t])
                p, q, w = (functools.reduce(jnp.add, part) for part in (p, q, w))
                to = slice(source * keep + first, source * keep + first + tile)
                cross[0, block, to] = (p + q).astype(cross.dtype)
                cross[1, block, to] = (w - p).astype(cross.dtype)
        return carry

    lax.fori_loop(0, nbins // LANES, multiply, 0)

    def project(place, part):
        value = [cross[place, block, part] for block in range(nbins // LANES)]
        return jnp.dot(
            jnp.concatenate(value, axis=1).astype(jnp.bfloat16),
            table_ref[place * nbins : (place + 1) * nbins],
            preferred_element_type=jnp.float32,
        )

    ends = []
    for first in (0, count // 2):
        at = slice(first * keep, (first + count // 2) * keep)
        sums = [project(place, at) for place in range(2)]
        if not first_stage:
            sums = [before[0][place, at] + sums[place] for place in range(2)]
        if stage == "sums":
            for place in range(2):
                after[0][place, at] = sums[place]
        ends.append(sums)

    lags = 2 * LAG + 1
    scale = 2.0 / math.sqrt(nbins)
    mirror = LAG - FIRST_LAG - iota((keep, LANES), 1)
    pieces = max(1, count // 4)
    for source in range(count):
        to = slice(source * keep, (source + 1) * keep)
        common = [
            src_valid[t * count + source : t * count + source + 1]
            * receivers[which][3][place * keep : (place + 1) * keep, :]
            for t, (which, place) in enumerate(places)
        ] + ([] if first_stage else [before[1][to]])
        common = functools.reduce(jnp.add, common)
        if stage == "sums":
            after[1][to] = common
            continue
        weight = scale / jnp.maximum(common, 1.0)
        inside = slice(source % (count // 2) * keep, (source % (count // 2) + 1) * keep)
        even, odd = (total[inside] for total in ends[source // (count // 2)])
        ahead = even + odd
        behind = even - odd
        low_part = jnp.take_along_axis(
            behind[:, :LANES], jnp.clip(mirror, 0, LANES - 1), axis=1
        )
        high_part = jnp.take_along_axis(
            behind[:, LANES:], jnp.clip(mirror - LANES, 0, LANES - 1), axis=1
        )
        result[to, :LANES] = jnp.where(mirror < LANES, low_part, high_part) * weight
        for first in range(0, lags - LANES, LANES):
            last = min(first + LANES, lags - LANES)
            value = ahead[:, first : first + LANES] * weight
            result[to, LANES + first : LANES + last] = value[:, : last - first]
        if stage == "store" and (source + 1) % pieces == 0:
            first, size = (source + 1 - pieces) * keep, pieces * keep
            at = pl.multiple_of((1 - part) * rows + first, size)
            copies.append(
                pltpu.make_async_copy(
                    result.at[pl.ds(first, size)],
                    after[0].at[pl.ds(at, size)],
                    written.at[source // pieces],
                )
            )
            copies[-1].start()
    for copy in copies:
        copy.wait()


def encode(segments, spectra, valid, sources):
    channels, width = spectra.shape
    keep = channels // segments
    slab = jax.ShapeDtypeStruct((sources.size, width // 2), jnp.bfloat16)
    block = jax.ShapeDtypeStruct((keep, width), jnp.bfloat16)
    padded = pltpu.VMEM((sources.size, width // 2 + 2 * LANES), jnp.bfloat16)
    pinned = [pltpu.with_memory_space_constraint(x, pltpu.HBM) for x in (spectra, valid, sources)]
    return pl.pallas_call(
        functools.partial(encode_kernel, segments),
        out_shape=(slab, slab) + (block,) * segments,
        in_specs=[HBM] * 3,
        out_specs=(VMEM,) * (2 + segments),
        scratch_shapes=[
            pltpu.VMEM((channels, width), kind_for(keep)),
            pltpu.VMEM((channels, width), jnp.bfloat16),
            pltpu.VMEM((1, channels), jnp.int32),
            pltpu.SMEM(sources.shape, jnp.int32),
            padded,
            padded,
            pltpu.VMEM((BLOCK + 2 * LANES, BLOCK), jnp.bfloat16),
            pltpu.SemaphoreType.DMA((3,)),
        ],
        compiler_params=pltpu.CompilerParams(vmem_limit_bytes=12 * MEBI),
        name="encode_and_pick",
    )(*pinned)


def whiten_blocks(blocks):
    segments, (keep, width) = len(blocks), blocks[0].shape
    count, nbins = segments * keep, width // 2
    padded = pltpu.VMEM((count, nbins + 2 * LANES), jnp.bfloat16)
    part = jax.ShapeDtypeStruct((count, nbins), jnp.float32)
    return pl.pallas_call(
        functools.partial(whiten_kernel, segments),
        out_shape=(part, part, part, jax.ShapeDtypeStruct((count, LANES), jnp.float32)),
        in_specs=[VMEM] * segments,
        out_specs=(VMEM,) * 4,
        scratch_shapes=[padded, padded],
        compiler_params=pltpu.CompilerParams(vmem_limit_bytes=20 * MEBI),
        cost_estimate=pl.CostEstimate(
            flops=count * width * 1024, bytes_accessed=count * width * 4, transcendentals=0
        ),
        name="whiten_receivers",
    )(*blocks)


def stack_stage(keep, slabs, places, receivers, table, stage, before=(), ready=()):
    count, nbins = slabs.shape[0] // (2 * len(places)), slabs.shape[1]
    rows, lags = count * keep, 2 * LAG + 1
    part = pltpu.VMEM((nbins // LANES, len(places) * count, LANES), jnp.float32)
    cross = pltpu.VMEM((2, nbins // LANES, rows, LANES), kind_for(keep))
    scratch = [part, part, part, cross]
    sums = (
        jax.ShapeDtypeStruct((2, rows, BLOCK), jnp.float32),
        jax.ShapeDtypeStruct((rows, LANES), jnp.float32),
    )
    if stage == "store":
        scratch += [pltpu.VMEM((rows, lags), jnp.float32), pltpu.SemaphoreType.DMA((count + 1,))]
    out_rows = 2 * rows if stage == "store" else rows
    result = jax.ShapeDtypeStruct((out_rows, lags), jnp.float32)
    inputs = [slabs, *sum(receivers, ()), table, *before, *ready]
    return pl.pallas_call(
        functools.partial(stack_kernel, places, (not before, stage)),
        out_shape=sums if stage == "sums" else result,
        in_specs=[VMEM] * len(inputs),
        out_specs=(VMEM, VMEM) if stage == "sums" else HBM if stage == "store" else VMEM,
        scratch_shapes=scratch,
        compiler_params=pltpu.CompilerParams(vmem_limit_bytes=20 * MEBI),
        cost_estimate=pl.CostEstimate(
            flops=4 * rows * nbins * 2 * LAG, bytes_accessed=nbins * 2048, transcendentals=0
        ),
        name="stack_" + stage,
    )(*inputs)


def swapped(value, axis, size, step):
    return lax.ppermute(value, axis, [(i, i ^ step) for i in range(size)])


def shards(rcv_size, tm_size, spectra, valid, sources):
    channels, _, width = spectra.shape
    keep = channels // tm_size
    rounds, per_round = sources.shape
    own, other, *receivers = encode(
        tm_size, spectra[:, 0, :], valid.reshape(1, channels), sources
    )
    receivers[-1] = swapped(receivers[-1], "tm", tm_size, tm_size - 1)
    receivers[-2] = swapped(receivers[-2], "tm", tm_size, tm_size - 2)
    own = own + swapped(other, "rcv", rcv_size, 1)
    own, later = lax.optimization_barrier((own, receivers[1:-2]))
    receivers[1:-2] = [
        swapped(block, "tm", tm_size, place) for place, block in enumerate(later, 1)
    ]
    step = 2
    while step < rcv_size:
        wide = min(4, rcv_size // step)
        parts = [swapped(own, "rcv", rcv_size, place * step) for place in range(1, wide)]
        if step == 2:
            parts[-1], receivers[-2:] = lax.optimization_barrier((parts[-1], receivers[-2:]))
            early = tuple(whiten_blocks([receivers[0], receivers[-1], receivers[-2]]))
            parts[-2:-1], early = lax.optimization_barrier((parts[-2:-1], early))
        own = functools.reduce(jnp.add, parts, own)
        step *= wide
    own = [own] + [swapped(own, "tm", tm_size, place) for place in range(1, tm_size)]
    table = jnp.asarray(lag_table(width // 2))
    far = tm_size - 1
    late = tuple(whiten_blocks(receivers[1:-2]))
    own[far], late = lax.optimization_barrier((own[far], late))
    sums = stack_stage(
        keep, jnp.concatenate([own[0], own[far]], axis=0), [(0, 0), (0, 1)], [early], table, "sums"
    )
    rest, sums, late = lax.optimization_barrier((own[1:far], sums, late))
    slabs = jnp.concatenate([own[0], own[far], *rest], axis=0)
    other = swapped(slabs, "rcv", rcv_size, 1)
    between = [(1, place) for place in range(far - 2)] + [(0, 2)]
    first = stack_stage(
        keep, slabs[2 * own[0].shape[0] :], between, [early, late], table, "result", sums
    )
    places = [(0, 0), (0, 1)] + between
    stack = stack_stage(keep, other, places, [early, late], table, "store", (), (first,))
    return stack.reshape(rounds, per_round, keep, 2 * LAG + 1)


def solution(mesh):
    body = functools.partial(shards, mesh.shape["rcv"], mesh.shape["tm"])
    in_specs = (P("rcv", "tm", None), P("rcv", "tm"), P())
    out_specs = P(None, None, ("rcv", "tm"), None)
    return jax.shard_map(body, mesh=mesh, in_specs=in_specs, out_specs=out_specs, check_vma=False)
```

```python
import functools
import math

import jax
import jax.numpy as jnp
import numpy as np
from jax import lax
from jax.experimental import pallas as pl
from jax.experimental.pallas import tpu as pltpu
from jax.sharding import PartitionSpec as P

NT = 4096
LAG = 150
HALF_WIN = 64
EPSILON = 1e-06

UNUSABLE = 1024.0
USABLE_BELOW = 512.0

LANES = 128
BLOCK = 256
MEBI = 1 << 20
FIRST_LAG = LANES - LAG
VMEM = pl.BlockSpec(memory_space=pltpu.VMEM)
HBM = pl.BlockSpec(memory_space=pltpu.HBM)


def lag_table(nbins):
    winding = np.mod(
        np.arange(1, nbins + 1, dtype=np.int64)[:, None]
        * np.arange(FIRST_LAG, FIRST_LAG + BLOCK, dtype=np.int64)[None, :],
        NT,
    )
    theta = winding * (2.0 * math.pi / NT)
    return np.concatenate([np.cos(theta), -np.sin(theta)], axis=0).astype(jnp.bfloat16)


def kind_for(rows):
    return jnp.bfloat16 if rows % 16 == 0 else jnp.float32


def iota(shape, dim):
    return lax.broadcasted_iota(jnp.int32, shape, dim)


def band_matrix():
    shape = (BLOCK + 2 * LANES, BLOCK)
    near = jnp.abs(iota(shape, 0) - LANES - iota(shape, 1)) <= HALF_WIN
    return jnp.where(near, 1.0, 0.0).astype(jnp.bfloat16)


def whitening(real, imag, high, low, unusable=0.0, band=None):
    count, nbins = real.shape
    blocks = nbins // BLOCK
    span = BLOCK + 2 * LANES
    amplitude = jnp.sqrt(real * real + imag * imag)
    rounded = amplitude.astype(jnp.bfloat16)
    edge = jnp.zeros((count, LANES), jnp.bfloat16)
    for part, value in (
        (high, rounded),
        (low, (amplitude - rounded.astype(jnp.float32)).astype(jnp.bfloat16)),
    ):
        part[:, :LANES] = edge
        part[:, LANES : LANES + nbins] = value
        part[:, LANES + nbins :] = edge
    band = band_matrix() if band is None else band[...]
    pieces = [
        part[:, block * BLOCK : block * BLOCK + span] for block in range(blocks) for part in (high, low)
    ]
    windows = jnp.dot(
        jnp.concatenate(pieces, axis=0), band, preferred_element_type=jnp.float32
    )
    for block in range(blocks):
        first = block * BLOCK
        at = 2 * block * count
        window = windows[at : at + count] + windows[at + count : at + 2 * count]
        index = first + iota((1, BLOCK), 1)
        counted = jnp.minimum(index, HALF_WIN) + jnp.minimum(nbins - 1 - index, HALF_WIN) + 1
        factor = 1.0 / (window / counted.astype(jnp.float32) + EPSILON)
        re = real[:, first : first + BLOCK]
        im = imag[:, first : first + BLOCK]
        usable = re < USABLE_BELOW
        re = jnp.where(usable, re * factor, unusable).astype(jnp.bfloat16).astype(jnp.float32)
        im = jnp.where(usable, im * factor, unusable).astype(jnp.bfloat16).astype(jnp.float32)
        yield slice(first, first + BLOCK), re, im


def usable_rows(real):
    return jnp.where(real[:, :LANES] < USABLE_BELOW, 1.0, 0.0)


def encode_kernel(
    segments, spectra_ref, valid_ref, sources_ref, own_ref, other_ref, *refs
):
    blocks, refs = refs[:segments], refs[segments:]
    encoded_ref, spectra, valid, sources, high, low, band, arrived = refs
    copies = [
        pltpu.make_async_copy(spectra_ref, spectra, arrived.at[0]),
        pltpu.make_async_copy(sources_ref, sources, arrived.at[1]),
        pltpu.make_async_copy(valid_ref, valid, arrived.at[2]),
    ]
    for copy in copies:
        copy.start()
    channels, width = spectra_ref.shape
    nbins = width // 2
    rounds, per_round = sources.shape
    half = rounds * per_round // 2
    index = lax.axis_index("rcv")
    copies[1].wait()
    copies[2].wait()
    diagonal = iota((channels, channels), 0) == iota((channels, channels), 1)
    usable = jnp.sum(jnp.where(diagonal, valid[...], 0), axis=1, keepdims=True) != 0
    row = iota((2 * half, channels), 0)
    local = jnp.zeros((2 * half, channels), jnp.int32)
    for place in range(2 * half):
        number = (index % 2 if place < half else 1 - index % 2) * half + place % half
        here = sources[number // per_round, number % per_round] - index * channels
        local = jnp.where(row == place, here, local)
    onehot = jnp.where(local == iota((2 * half, channels), 1), 1.0, 0.0).astype(jnp.bfloat16)
    band[...] = band_matrix()
    copies[0].wait()
    encoded = jnp.where(usable, spectra[...].astype(jnp.float32), UNUSABLE).astype(jnp.bfloat16)
    picked = jnp.dot(onehot, encoded, preferred_element_type=jnp.float32)
    for at, re, im in whitening(picked[:, :nbins], picked[:, nbins:], high, low, UNUSABLE, band):
        for first, ref in ((0, own_ref), (half, other_ref)):
            rows = slice(first, first + half)
            ref[:, at] = jnp.concatenate([re[rows], im[rows]], axis=0).astype(ref.dtype)
    encoded_ref[...] = encoded.astype(encoded_ref.dtype)
    keep = channels // segments
    for step, block in enumerate(blocks):
        at = pl.multiple_of((lax.axis_index("tm") ^ step) * keep, keep)
        block[...] = encoded_ref[pl.ds(at, keep), :].astype(block.dtype)


def whiten_kernel(segments, *refs):
    blocks, refs = refs[:segments], refs[segments:]
    real_ref, imag_ref, both_ref, valid_ref, high, low = refs
    rows = jnp.concatenate([ref[...].astype(jnp.float32) for ref in blocks], axis=0)
    nbins = rows.shape[1] // 2
    real, imag = rows[:, :nbins], rows[:, nbins:]
    for at, re, im in whitening(real, imag, high, low):
        real_ref[:, at] = re
        imag_ref[:, at] = im
        both_ref[:, at] = re + im
    valid_ref[...] = usable_rows(real)


def stack_kernel(places, stage, *refs):
    segments, sets = len(places), 1 + max(which for which, _ in places)
    slabs, refs = refs[0], refs[1:]
    receivers = [refs[4 * which : 4 * which + 4] for which in range(sets)]
    table_ref, refs = refs[4 * sets], refs[4 * sets + 1 :]
    first_stage, stage = stage
    before, refs = ([], refs) if first_stage else (refs[:2], refs[2:])
    ready, refs = (refs[0], refs[1:]) if stage == "store" else (None, refs)
    after, refs = (refs[:2], refs[2:]) if stage == "sums" else (refs[:1], refs[1:])
    src_re, src_diff, src_sum, cross, *refs = refs
    nbins, rows = slabs.shape[1], cross.shape[2]
    count = slabs.shape[0] // (2 * segments)
    keep = rows // count
    copies = []
    if stage == "store":
        result, written = refs
        part = lax.axis_index("rcv") % 2
        at = pl.multiple_of(part * rows, rows)
        copies.append(
            pltpu.make_async_copy(ready, after[0].at[pl.ds(at, rows)], written.at[count])
        )
        copies[0].start()
    elif stage == "result":
        result = after[0]
    values = slabs[...].astype(jnp.float32)
    real = jnp.concatenate(
        [values[2 * count * t : 2 * count * t + count] for t in range(segments)], axis=0
    )
    imag = jnp.concatenate(
        [values[2 * count * t + count : 2 * count * (t + 1)] for t in range(segments)], axis=0
    )
    usable = real < USABLE_BELOW
    real, imag = jnp.where(usable, real, 0.0), jnp.where(usable, imag, 0.0)
    src_valid = jnp.where(usable[:, :LANES], 1.0, 0.0)
    for ref, value in ((src_re, real), (src_diff, imag - real), (src_sum, imag + real)):
        for block in range(nbins // LANES):
            ref[block] = value[:, block * LANES : (block + 1) * LANES]
    tile = keep if segments <= 2 else min(keep, 16)

    def spread(ref, block, row):
        return jnp.concatenate([ref[block, pl.ds(row, 8, stride=0), :]] * (tile // 8), axis=0)

    def multiply(block, carry):
        at = pl.ds(pl.multiple_of(block * LANES, LANES), LANES)
        for first in range(0, keep, tile):
            taken = [
                (receivers[which], slice(place * keep + first, place * keep + first + tile))
                for which, place in places
            ]
            r_re = [block_refs[0][row, at] for block_refs, row in taken]
            r_im = [block_refs[1][row, at] for block_refs, row in taken]
            r_both = [block_refs[2][row, at] for block_refs, row in taken]
            for source in range(count):
                p, q, w = [], [], []
                for t in range(segments):
                    row = t * count + source
                    p.append(spread(src_re, block, row) * r_both[t])
                    q.append(spread(src_diff, block, row) * r_im[t])
                    w.append(spread(src_sum, block, row) * r_re[t])
                p, q, w = (functools.reduce(jnp.add, part) for part in (p, q, w))
                to = slice(source * keep + first, source * keep + first + tile)
                cross[0, block, to] = (p + q).astype(cross.dtype)
                cross[1, block, to] = (w - p).astype(cross.dtype)
        return carry

    lax.fori_loop(0, nbins // LANES, multiply, 0)

    def project(place, part):
        value = [cross[place, block, part] for block in range(nbins // LANES)]
        return jnp.dot(
            jnp.concatenate(value, axis=1).astype(jnp.bfloat16),
            table_ref[place * nbins : (place + 1) * nbins],
            preferred_element_type=jnp.float32,
        )

    ends = []
    for first in (0, count // 2):
        at = slice(first * keep, (first + count // 2) * keep)
        sums = [project(place, at) for place in range(2)]
        if not first_stage:
            sums = [before[0][place, at] + sums[place] for place in range(2)]
        if stage == "sums":
            for place in range(2):
                after[0][place, at] = sums[place]
        ends.append(sums)

    lags = 2 * LAG + 1
    scale = 2.0 / math.sqrt(nbins)
    mirror = LAG - FIRST_LAG - iota((keep, LANES), 1)
    pieces = max(1, count // 4)
    for source in range(count):
        to = slice(source * keep, (source + 1) * keep)
        common = [
            src_valid[t * count + source : t * count + source + 1]
            * receivers[which][3][place * keep : (place + 1) * keep, :]
            for t, (which, place) in enumerate(places)
        ] + ([] if first_stage else [before[1][to]])
        common = functools.reduce(jnp.add, common)
        if stage == "sums":
            after[1][to] = common
            continue
        weight = scale / jnp.maximum(common, 1.0)
        inside = slice(source % (count // 2) * keep, (source % (count // 2) + 1) * keep)
        even, odd = (total[inside] for total in ends[source // (count // 2)])
        ahead = even + odd
        behind = even - odd
        low_part = jnp.take_along_axis(
            behind[:, :LANES], jnp.clip(mirror, 0, LANES - 1), axis=1
        )
        high_part = jnp.take_along_axis(
            behind[:, LANES:], jnp.clip(mirror - LANES, 0, LANES - 1), axis=1
        )
        result[to, :LANES] = jnp.where(mirror < LANES, low_part, high_part) * weight
        for first in range(0, lags - LANES, LANES):
            last = min(first + LANES, lags - LANES)
            value = ahead[:, first : first + LANES] * weight
            result[to, LANES + first : LANES + last] = value[:, : last - first]
        if stage == "store" and (source + 1) % pieces == 0:
            first, size = (source + 1 - pieces) * keep, pieces * keep
            at = pl.multiple_of((1 - part) * rows + first, size)
            copies.append(
                pltpu.make_async_copy(
                    result.at[pl.ds(first, size)],
                    after[0].at[pl.ds(at, size)],
                    written.at[source // pieces],
                )
            )
            copies[-1].start()
    for copy in copies:
        copy.wait()


def encode(segments, spectra, valid, sources):
    channels, width = spectra.shape
    keep = channels // segments
    slab = jax.ShapeDtypeStruct((sources.size, width // 2), jnp.bfloat16)
    block = jax.ShapeDtypeStruct((keep, width), jnp.bfloat16)
    padded = pltpu.VMEM((sources.size, width // 2 + 2 * LANES), jnp.bfloat16)
    pinned = [pltpu.with_memory_space_constraint(x, pltpu.HBM) for x in (spectra, valid, sources)]
    return pl.pallas_call(
        functools.partial(encode_kernel, segments),
        out_shape=(slab, slab) + (block,) * segments,
        in_specs=[HBM] * 3,
        out_specs=(VMEM,) * (2 + segments),
        scratch_shapes=[
            pltpu.VMEM((channels, width), kind_for(keep)),
            pltpu.VMEM((channels, width), jnp.bfloat16),
            pltpu.VMEM((1, channels), jnp.int32),
            pltpu.SMEM(sources.shape, jnp.int32),
            padded,
            padded,
            pltpu.VMEM((BLOCK + 2 * LANES, BLOCK), jnp.bfloat16),
            pltpu.SemaphoreType.DMA((3,)),
        ],
        compiler_params=pltpu.CompilerParams(vmem_limit_bytes=12 * MEBI),
        name="encode_and_pick",
    )(*pinned)


def whiten_blocks(blocks):
    segments, (keep, width) = len(blocks), blocks[0].shape
    count, nbins = segments * keep, width // 2
    padded = pltpu.VMEM((count, nbins + 2 * LANES), jnp.bfloat16)
    part = jax.ShapeDtypeStruct((count, nbins), jnp.float32)
    return pl.pallas_call(
        functools.partial(whiten_kernel, segments),
        out_shape=(part, part, part, jax.ShapeDtypeStruct((count, LANES), jnp.float32)),
        in_specs=[VMEM] * segments,
        out_specs=(VMEM,) * 4,
        scratch_shapes=[padded, padded],
        compiler_params=pltpu.CompilerParams(vmem_limit_bytes=20 * MEBI),
        cost_estimate=pl.CostEstimate(
            flops=count * width * 1024, bytes_accessed=count * width * 4, transcendentals=0
        ),
        name="whiten_receivers",
    )(*blocks)


def stack_stage(keep, slabs, places, receivers, table, stage, before=(), ready=()):
    count, nbins = slabs.shape[0] // (2 * len(places)), slabs.shape[1]
    rows, lags = count * keep, 2 * LAG + 1
    part = pltpu.VMEM((nbins // LANES, len(places) * count, LANES), jnp.float32)
    cross = pltpu.VMEM((2, nbins // LANES, rows, LANES), kind_for(keep))
    scratch = [part, part, part, cross]
    sums = (
        jax.ShapeDtypeStruct((2, rows, BLOCK), jnp.float32),
        jax.ShapeDtypeStruct((rows, LANES), jnp.float32),
    )
    if stage == "store":
        scratch += [pltpu.VMEM((rows, lags), jnp.float32), pltpu.SemaphoreType.DMA((count + 1,))]
    out_rows = 2 * rows if stage == "store" else rows
    result = jax.ShapeDtypeStruct((out_rows, lags), jnp.float32)
    inputs = [slabs, *sum(receivers, ()), table, *before, *ready]
    return pl.pallas_call(
        functools.partial(stack_kernel, places, (not before, stage)),
        out_shape=sums if stage == "sums" else result,
        in_specs=[VMEM] * len(inputs),
        out_specs=(VMEM, VMEM) if stage == "sums" else HBM if stage == "store" else VMEM,
        scratch_shapes=scratch,
        compiler_params=pltpu.CompilerParams(vmem_limit_bytes=20 * MEBI),
        cost_estimate=pl.CostEstimate(
            flops=4 * rows * nbins * 2 * LAG, bytes_accessed=nbins * 2048, transcendentals=0
        ),
        name="stack_" + stage,
    )(*inputs)


def swapped(value, axis, size, step):
    return lax.ppermute(value, axis, [(i, i ^ step) for i in range(size)])


def shards(rcv_size, tm_size, spectra, valid, sources):
    channels, _, width = spectra.shape
    keep = channels // tm_size
    rounds, per_round = sources.shape
    own, other, *receivers = encode(
        tm_size, spectra[:, 0, :], valid.reshape(1, channels), sources
    )
    receivers[-1] = swapped(receivers[-1], "tm", tm_size, tm_size - 1)
    own = own + swapped(other, "rcv", rcv_size, 1)
    own, later = lax.optimization_barrier((own, receivers[1:-1]))
    last, receivers[-1] = lax.optimization_barrier((later[-1], receivers[-1]))
    receivers[1:-1] = [
        swapped(block, "tm", tm_size, place) for place, block in enumerate(later[:-1] + [last], 1)
    ]
    step = 2
    while step < rcv_size:
        wide = min(4, rcv_size // step)
        parts = [swapped(own, "rcv", rcv_size, place * step) for place in range(1, wide)]
        if step == 2:
            early = tuple(whiten_blocks([receivers[0], receivers[-1]]))
            parts[-2:-1], early = lax.optimization_barrier((parts[-2:-1], early))
        own = functools.reduce(jnp.add, parts, own)
        step *= wide
    own = [own] + [swapped(own, "tm", tm_size, place) for place in range(1, tm_size)]
    table = jnp.asarray(lag_table(width // 2))
    far = tm_size - 1
    late = tuple(whiten_blocks(receivers[1:far]))
    own[far], late = lax.optimization_barrier((own[far], late))
    sums = stack_stage(
        keep, jnp.concatenate([own[0], own[far]], axis=0), [(0, 0), (0, 1)], [early], table, "sums"
    )
    rest, sums, late = lax.optimization_barrier((own[1:far], sums, late))
    slabs = jnp.concatenate([own[0], own[far], *rest], axis=0)
    other = swapped(slabs, "rcv", rcv_size, 1)
    places = [(0, place) for place in range(far - 1)]
    first = stack_stage(
        keep, slabs[2 * own[0].shape[0] :], places, [late], table, "result", sums
    )
    places = [(0, 0), (0, 1)] + [(1, place) for place in range(far - 1)]
    stack = stack_stage(keep, other, places, [early, late], table, "store", (), (first,))
    return stack.reshape(rounds, per_round, keep, 2 * LAG + 1)


def solution(mesh):
    body = functools.partial(shards, mesh.shape["rcv"], mesh.shape["tm"])
    in_specs = (P("rcv", "tm", None), P("rcv", "tm"), P())
    out_specs = P(None, None, ("rcv", "tm"), None)
    return jax.shard_map(body, mesh=mesh, in_specs=in_specs, out_specs=out_specs, check_vma=False)
```

```python
import functools
import math

import jax
import jax.numpy as jnp
import numpy as np
from jax import lax
from jax.experimental import pallas as pl
from jax.experimental.pallas import tpu as pltpu
from jax.sharding import PartitionSpec as P

NT = 4096
LAG = 150
HALF_WIN = 64
EPSILON = 1e-06

UNUSABLE = 1024.0
USABLE_BELOW = 512.0

LANES = 128
BLOCK = 256
MEBI = 1 << 20
FIRST_LAG = LANES - LAG
VMEM = pl.BlockSpec(memory_space=pltpu.VMEM)
HBM = pl.BlockSpec(memory_space=pltpu.HBM)


def lag_table(nbins):
    winding = np.mod(
        np.arange(1, nbins + 1, dtype=np.int64)[:, None]
        * np.arange(FIRST_LAG, FIRST_LAG + BLOCK, dtype=np.int64)[None, :],
        NT,
    )
    theta = winding * (2.0 * math.pi / NT)
    return np.concatenate([np.cos(theta), -np.sin(theta)], axis=0).astype(jnp.bfloat16)


def kind_for(rows):
    return jnp.bfloat16 if rows % 16 == 0 else jnp.float32


def iota(shape, dim):
    return lax.broadcasted_iota(jnp.int32, shape, dim)


def band_matrix():
    shape = (BLOCK + 2 * LANES, BLOCK)
    near = jnp.abs(iota(shape, 0) - LANES - iota(shape, 1)) <= HALF_WIN
    return jnp.where(near, 1.0, 0.0).astype(jnp.bfloat16)


def whitening(real, imag, high, low, unusable=0.0, band=None):
    count, nbins = real.shape
    blocks = nbins // BLOCK
    span = BLOCK + 2 * LANES
    amplitude = jnp.sqrt(real * real + imag * imag)
    rounded = amplitude.astype(jnp.bfloat16)
    edge = jnp.zeros((count, LANES), jnp.bfloat16)
    for part, value in (
        (high, rounded),
        (low, (amplitude - rounded.astype(jnp.float32)).astype(jnp.bfloat16)),
    ):
        part[:, :LANES] = edge
        part[:, LANES : LANES + nbins] = value
        part[:, LANES + nbins :] = edge
    band = band_matrix() if band is None else band[...]
    pieces = [
        part[:, block * BLOCK : block * BLOCK + span] for block in range(blocks) for part in (high, low)
    ]
    windows = jnp.dot(
        jnp.concatenate(pieces, axis=0), band, preferred_element_type=jnp.float32
    )
    for block in range(blocks):
        first = block * BLOCK
        at = 2 * block * count
        window = windows[at : at + count] + windows[at + count : at + 2 * count]
        index = first + iota((1, BLOCK), 1)
        counted = jnp.minimum(index, HALF_WIN) + jnp.minimum(nbins - 1 - index, HALF_WIN) + 1
        factor = 1.0 / (window / counted.astype(jnp.float32) + EPSILON)
        re = real[:, first : first + BLOCK]
        im = imag[:, first : first + BLOCK]
        usable = re < USABLE_BELOW
        re = jnp.where(usable, re * factor, unusable).astype(jnp.bfloat16).astype(jnp.float32)
        im = jnp.where(usable, im * factor, unusable).astype(jnp.bfloat16).astype(jnp.float32)
        yield slice(first, first + BLOCK), re, im


def usable_rows(real):
    return jnp.where(real[:, :LANES] < USABLE_BELOW, 1.0, 0.0)


def encode_kernel(
    segments, spectra_ref, valid_ref, sources_ref, own_ref, other_ref, *refs
):
    blocks, refs = refs[:segments], refs[segments:]
    encoded_ref, spectra, valid, sources, high, low, band, arrived = refs
    copies = [
        pltpu.make_async_copy(spectra_ref, spectra, arrived.at[0]),
        pltpu.make_async_copy(sources_ref, sources, arrived.at[1]),
        pltpu.make_async_copy(valid_ref, valid, arrived.at[2]),
    ]
    for copy in copies:
        copy.start()
    channels, width = spectra_ref.shape
    nbins = width // 2
    rounds, per_round = sources.shape
    half = rounds * per_round // 2
    index = lax.axis_index("rcv")
    copies[1].wait()
    copies[2].wait()
    diagonal = iota((channels, channels), 0) == iota((channels, channels), 1)
    usable = jnp.sum(jnp.where(diagonal, valid[...], 0), axis=1, keepdims=True) != 0
    row = iota((2 * half, channels), 0)
    local = jnp.zeros((2 * half, channels), jnp.int32)
    for place in range(2 * half):
        number = (index % 2 if place < half else 1 - index % 2) * half + place % half
        here = sources[number // per_round, number % per_round] - index * channels
        local = jnp.where(row == place, here, local)
    onehot = jnp.where(local == iota((2 * half, channels), 1), 1.0, 0.0).astype(jnp.bfloat16)
    band[...] = band_matrix()
    copies[0].wait()
    encoded = jnp.where(usable, spectra[...].astype(jnp.float32), UNUSABLE).astype(jnp.bfloat16)
    picked = jnp.dot(onehot, encoded, preferred_element_type=jnp.float32)
    for at, re, im in whitening(picked[:, :nbins], picked[:, nbins:], high, low, UNUSABLE, band):
        own_rows, other_rows = (
            jnp.concatenate([re[first : first + half], im[first : first + half]], axis=0)
            for first in (0, half)
        )
        own_ref[:, at] = own_rows.astype(own_ref.dtype)
        other_ref[: 2 * half, at] = other_rows.astype(other_ref.dtype)
        other_ref[2 * half :, at] = own_rows.astype(other_ref.dtype)
    encoded_ref[...] = encoded.astype(encoded_ref.dtype)
    keep = channels // segments
    for step, block in enumerate(blocks):
        at = pl.multiple_of((lax.axis_index("tm") ^ step) * keep, keep)
        block[...] = encoded_ref[pl.ds(at, keep), :].astype(block.dtype)


def whiten_kernel(segments, *refs):
    blocks, refs = refs[:segments], refs[segments:]
    real_ref, imag_ref, both_ref, valid_ref, high, low = refs
    rows = jnp.concatenate([ref[...].astype(jnp.float32) for ref in blocks], axis=0)
    nbins = rows.shape[1] // 2
    real, imag = rows[:, :nbins], rows[:, nbins:]
    for at, re, im in whitening(real, imag, high, low):
        real_ref[:, at] = re
        imag_ref[:, at] = im
        both_ref[:, at] = re + im
    valid_ref[...] = usable_rows(real)


def stack_kernel(places, stage, *refs):
    segments, sets = len(places), 1 + max(which for which, _ in places)
    slabs, refs = refs[0], refs[1:]
    receivers = [refs[4 * which : 4 * which + 4] for which in range(sets)]
    table_ref, refs = refs[4 * sets], refs[4 * sets + 1 :]
    first_stage, stage = stage
    before, refs = ([], refs) if first_stage else (refs[:2], refs[2:])
    ready, refs = (refs[0], refs[1:]) if stage == "store" else (None, refs)
    after, refs = (refs[:2], refs[2:]) if stage == "sums" else (refs[:1], refs[1:])
    src_re, src_diff, src_sum, cross, *refs = refs
    nbins, rows = slabs.shape[1], cross.shape[2]
    count = slabs.shape[0] // (2 * segments)
    keep = rows // count
    copies = []
    if stage == "store":
        result, written = refs
        part = lax.axis_index("rcv") % 2
        at = pl.multiple_of(part * rows, rows)
        copies.append(
            pltpu.make_async_copy(ready, after[0].at[pl.ds(at, rows)], written.at[count])
        )
        copies[0].start()
    elif stage == "result":
        result = after[0]
    values = slabs[...].astype(jnp.float32)
    real = jnp.concatenate(
        [values[2 * count * t : 2 * count * t + count] for t in range(segments)], axis=0
    )
    imag = jnp.concatenate(
        [values[2 * count * t + count : 2 * count * (t + 1)] for t in range(segments)], axis=0
    )
    usable = real < USABLE_BELOW
    real, imag = jnp.where(usable, real, 0.0), jnp.where(usable, imag, 0.0)
    src_valid = jnp.where(usable[:, :LANES], 1.0, 0.0)
    for ref, value in ((src_re, real), (src_diff, imag - real), (src_sum, imag + real)):
        for block in range(nbins // LANES):
            ref[block] = value[:, block * LANES : (block + 1) * LANES]
    tile = keep if segments <= 2 else min(keep, 16)

    def spread(ref, block, row):
        return jnp.concatenate([ref[block, pl.ds(row, 8, stride=0), :]] * (tile // 8), axis=0)

    def multiply(block, carry):
        at = pl.ds(pl.multiple_of(block * LANES, LANES), LANES)
        for first in range(0, keep, tile):
            taken = [
                (receivers[which], slice(place * keep + first, place * keep + first + tile))
                for which, place in places
            ]
            r_re = [block_refs[0][row, at] for block_refs, row in taken]
            r_im = [block_refs[1][row, at] for block_refs, row in taken]
            r_both = [block_refs[2][row, at] for block_refs, row in taken]
            for source in range(count):
                p, q, w = [], [], []
                for t in range(segments):
                    row = t * count + source
                    p.append(spread(src_re, block, row) * r_both[t])
                    q.append(spread(src_diff, block, row) * r_im[t])
                    w.append(spread(src_sum, block, row) * r_re[t])
                p, q, w = (functools.reduce(jnp.add, part) for part in (p, q, w))
                to = slice(source * keep + first, source * keep + first + tile)
                cross[0, block, to] = (p + q).astype(cross.dtype)
                cross[1, block, to] = (w - p).astype(cross.dtype)
        return carry

    lax.fori_loop(0, nbins // LANES, multiply, 0)

    def project(place, part):
        value = [cross[place, block, part] for block in range(nbins // LANES)]
        return jnp.dot(
            jnp.concatenate(value, axis=1).astype(jnp.bfloat16),
            table_ref[place * nbins : (place + 1) * nbins],
            preferred_element_type=jnp.float32,
        )

    ends = []
    for first in (0, count // 2):
        at = slice(first * keep, (first + count // 2) * keep)
        sums = [project(place, at) for place in range(2)]
        if not first_stage:
            sums = [before[0][place, at] + sums[place] for place in range(2)]
        if stage == "sums":
            for place in range(2):
                after[0][place, at] = sums[place]
        ends.append(sums)

    lags = 2 * LAG + 1
    scale = 2.0 / math.sqrt(nbins)
    mirror = LAG - FIRST_LAG - iota((keep, LANES), 1)
    pieces = max(1, count // 4)
    for source in range(count):
        to = slice(source * keep, (source + 1) * keep)
        common = [
            src_valid[t * count + source : t * count + source + 1]
            * receivers[which][3][place * keep : (place + 1) * keep, :]
            for t, (which, place) in enumerate(places)
        ] + ([] if first_stage else [before[1][to]])
        common = functools.reduce(jnp.add, common)
        if stage == "sums":
            after[1][to] = common
            continue
        weight = scale / jnp.maximum(common, 1.0)
        inside = slice(source % (count // 2) * keep, (source % (count // 2) + 1) * keep)
        even, odd = (total[inside] for total in ends[source // (count // 2)])
        ahead = even + odd
        behind = even - odd
        low_part = jnp.take_along_axis(
            behind[:, :LANES], jnp.clip(mirror, 0, LANES - 1), axis=1
        )
        high_part = jnp.take_along_axis(
            behind[:, LANES:], jnp.clip(mirror - LANES, 0, LANES - 1), axis=1
        )
        result[to, :LANES] = jnp.where(mirror < LANES, low_part, high_part) * weight
        for first in range(0, lags - LANES, LANES):
            last = min(first + LANES, lags - LANES)
            value = ahead[:, first : first + LANES] * weight
            result[to, LANES + first : LANES + last] = value[:, : last - first]
        if stage == "store" and (source + 1) % pieces == 0:
            first, size = (source + 1 - pieces) * keep, pieces * keep
            at = pl.multiple_of((1 - part) * rows + first, size)
            copies.append(
                pltpu.make_async_copy(
                    result.at[pl.ds(first, size)],
                    after[0].at[pl.ds(at, size)],
                    written.at[source // pieces],
                )
            )
            copies[-1].start()
    for copy in copies:
        copy.wait()


def encode(segments, spectra, valid, sources):
    channels, width = spectra.shape
    keep = channels // segments
    slab = jax.ShapeDtypeStruct((sources.size, width // 2), jnp.bfloat16)
    slabs = jax.ShapeDtypeStruct((2 * sources.size, width // 2), jnp.bfloat16)
    block = jax.ShapeDtypeStruct((keep, width), jnp.bfloat16)
    padded = pltpu.VMEM((sources.size, width // 2 + 2 * LANES), jnp.bfloat16)
    pinned = [pltpu.with_memory_space_constraint(x, pltpu.HBM) for x in (spectra, valid, sources)]
    return pl.pallas_call(
        functools.partial(encode_kernel, segments),
        out_shape=(slab, slabs) + (block,) * segments,
        in_specs=[HBM] * 3,
        out_specs=(VMEM,) * (2 + segments),
        scratch_shapes=[
            pltpu.VMEM((channels, width), kind_for(keep)),
            pltpu.VMEM((channels, width), jnp.bfloat16),
            pltpu.VMEM((1, channels), jnp.int32),
            pltpu.SMEM(sources.shape, jnp.int32),
            padded,
            padded,
            pltpu.VMEM((BLOCK + 2 * LANES, BLOCK), jnp.bfloat16),
            pltpu.SemaphoreType.DMA((3,)),
        ],
        compiler_params=pltpu.CompilerParams(vmem_limit_bytes=12 * MEBI),
        name="encode_and_pick",
    )(*pinned)


def whiten_blocks(blocks):
    segments, (keep, width) = len(blocks), blocks[0].shape
    count, nbins = segments * keep, width // 2
    padded = pltpu.VMEM((count, nbins + 2 * LANES), jnp.bfloat16)
    part = jax.ShapeDtypeStruct((count, nbins), jnp.float32)
    return pl.pallas_call(
        functools.partial(whiten_kernel, segments),
        out_shape=(part, part, part, jax.ShapeDtypeStruct((count, LANES), jnp.float32)),
        in_specs=[VMEM] * segments,
        out_specs=(VMEM,) * 4,
        scratch_shapes=[padded, padded],
        compiler_params=pltpu.CompilerParams(vmem_limit_bytes=20 * MEBI),
        cost_estimate=pl.CostEstimate(
            flops=count * width * 1024, bytes_accessed=count * width * 4, transcendentals=0
        ),
        name="whiten_receivers",
    )(*blocks)


def stack_stage(keep, slabs, places, receivers, table, stage, before=(), ready=()):
    count, nbins = slabs.shape[0] // (2 * len(places)), slabs.shape[1]
    rows, lags = count * keep, 2 * LAG + 1
    part = pltpu.VMEM((nbins // LANES, len(places) * count, LANES), jnp.float32)
    cross = pltpu.VMEM((2, nbins // LANES, rows, LANES), kind_for(keep))
    scratch = [part, part, part, cross]
    sums = (
        jax.ShapeDtypeStruct((2, rows, BLOCK), jnp.float32),
        jax.ShapeDtypeStruct((rows, LANES), jnp.float32),
    )
    if stage == "store":
        scratch += [pltpu.VMEM((rows, lags), jnp.float32), pltpu.SemaphoreType.DMA((count + 1,))]
    out_rows = 2 * rows if stage == "store" else rows
    result = jax.ShapeDtypeStruct((out_rows, lags), jnp.float32)
    inputs = [slabs, *sum(receivers, ()), table, *before, *ready]
    return pl.pallas_call(
        functools.partial(stack_kernel, places, (not before, stage)),
        out_shape=sums if stage == "sums" else result,
        in_specs=[VMEM] * len(inputs),
        out_specs=(VMEM, VMEM) if stage == "sums" else HBM if stage == "store" else VMEM,
        scratch_shapes=scratch,
        compiler_params=pltpu.CompilerParams(vmem_limit_bytes=20 * MEBI),
        cost_estimate=pl.CostEstimate(
            flops=4 * rows * nbins * 2 * LAG, bytes_accessed=nbins * 2048, transcendentals=0
        ),
        name="stack_" + stage,
    )(*inputs)


def swapped(value, axis, size, step):
    return lax.ppermute(value, axis, [(i, i ^ step) for i in range(size)])


def shards(rcv_size, tm_size, spectra, valid, sources):
    channels, _, width = spectra.shape
    keep = channels // tm_size
    rounds, per_round = sources.shape
    own, other, *receivers = encode(
        tm_size, spectra[:, 0, :], valid.reshape(1, channels), sources
    )
    receivers[-1] = swapped(receivers[-1], "tm", tm_size, tm_size - 1)
    own = own + swapped(other, "rcv", rcv_size, 1)[: own.shape[0]]
    own, later = lax.optimization_barrier((own, receivers[1:-1]))
    last, receivers[-1] = lax.optimization_barrier((later[-1], receivers[-1]))
    receivers[1:-1] = [
        swapped(block, "tm", tm_size, place) for place, block in enumerate(later[:-1] + [last], 1)
    ]
    step = 2
    while step < rcv_size:
        wide = min(4, rcv_size // step)
        parts = [swapped(own, "rcv", rcv_size, place * step) for place in range(1, wide)]
        if step == 2:
            early = tuple(whiten_blocks([receivers[0], receivers[-1]]))
            parts[-2:-1], early = lax.optimization_barrier((parts[-2:-1], early))
        own = functools.reduce(jnp.add, parts, own)
        step *= wide
    own = [own] + [swapped(own, "tm", tm_size, place) for place in range(1, tm_size)]
    table = jnp.asarray(lag_table(width // 2))
    far = tm_size - 1
    late = tuple(whiten_blocks(receivers[1:far]))
    own[far], late = lax.optimization_barrier((own[far], late))
    sums = stack_stage(
        keep, jnp.concatenate([own[0], own[far]], axis=0), [(0, 0), (0, 1)], [early], table, "sums"
    )
    rest, sums, late = lax.optimization_barrier((own[1:far], sums, late))
    slabs = jnp.concatenate([own[0], own[far], *rest], axis=0)
    other = swapped(slabs, "rcv", rcv_size, 1)
    places = [(0, place) for place in range(far - 1)]
    first = stack_stage(
        keep, slabs[2 * own[0].shape[0] :], places, [late], table, "result", sums
    )
    places = [(0, 0), (0, 1)] + [(1, place) for place in range(far - 1)]
    stack = stack_stage(keep, other, places, [early, late], table, "store", (), (first,))
    return stack.reshape(rounds, per_round, keep, 2 * LAG + 1)


def solution(mesh):
    body = functools.partial(shards, mesh.shape["rcv"], mesh.shape["tm"])
    in_specs = (P("rcv", "tm", None), P("rcv", "tm"), P())
    out_specs = P(None, None, ("rcv", "tm"), None)
    return jax.shard_map(body, mesh=mesh, in_specs=in_specs, out_specs=out_specs, check_vma=False)
```

```python
import functools
import math

import jax
import jax.numpy as jnp
import numpy as np
from jax import lax
from jax.experimental import pallas as pl
from jax.experimental.pallas import tpu as pltpu
from jax.sharding import PartitionSpec as P

NT = 4096
LAG = 150
HALF_WIN = 64
EPSILON = 1e-06

UNUSABLE = 1024.0
USABLE_BELOW = 512.0

LANES = 128
BLOCK = 256
MEBI = 1 << 20
FIRST_LAG = LANES - LAG
VMEM = pl.BlockSpec(memory_space=pltpu.VMEM)
HBM = pl.BlockSpec(memory_space=pltpu.HBM)


def lag_table(nbins):
    winding = np.mod(
        np.arange(1, nbins + 1, dtype=np.int64)[:, None]
        * np.arange(FIRST_LAG, FIRST_LAG + BLOCK, dtype=np.int64)[None, :],
        NT,
    )
    theta = winding * (2.0 * math.pi / NT)
    return np.concatenate([np.cos(theta), -np.sin(theta)], axis=0).astype(jnp.bfloat16)


def kind_for(rows):
    return jnp.bfloat16 if rows % 16 == 0 else jnp.float32


def iota(shape, dim):
    return lax.broadcasted_iota(jnp.int32, shape, dim)


def band_matrix():
    shape = (BLOCK + 2 * LANES, BLOCK)
    near = jnp.abs(iota(shape, 0) - LANES - iota(shape, 1)) <= HALF_WIN
    return jnp.where(near, 1.0, 0.0).astype(jnp.bfloat16)


def whitening(real, imag, high, low, unusable=0.0, band=None):
    count, nbins = real.shape
    blocks = nbins // BLOCK
    span = BLOCK + 2 * LANES
    amplitude = jnp.sqrt(real * real + imag * imag)
    rounded = amplitude.astype(jnp.bfloat16)
    edge = jnp.zeros((count, LANES), jnp.bfloat16)
    for part, value in (
        (high, rounded),
        (low, (amplitude - rounded.astype(jnp.float32)).astype(jnp.bfloat16)),
    ):
        part[:, :LANES] = edge
        part[:, LANES : LANES + nbins] = value
        part[:, LANES + nbins :] = edge
    band = band_matrix() if band is None else band[...]
    pieces = [
        part[:, block * BLOCK : block * BLOCK + span] for block in range(blocks) for part in (high, low)
    ]
    windows = jnp.dot(
        jnp.concatenate(pieces, axis=0), band, preferred_element_type=jnp.float32
    )
    for block in range(blocks):
        first = block * BLOCK
        at = 2 * block * count
        window = windows[at : at + count] + windows[at + count : at + 2 * count]
        index = first + iota((1, BLOCK), 1)
        counted = jnp.minimum(index, HALF_WIN) + jnp.minimum(nbins - 1 - index, HALF_WIN) + 1
        factor = 1.0 / (window / counted.astype(jnp.float32) + EPSILON)
        re = real[:, first : first + BLOCK]
        im = imag[:, first : first + BLOCK]
        usable = re < USABLE_BELOW
        re = jnp.where(usable, re * factor, unusable).astype(jnp.bfloat16).astype(jnp.float32)
        im = jnp.where(usable, im * factor, unusable).astype(jnp.bfloat16).astype(jnp.float32)
        yield slice(first, first + BLOCK), re, im


def usable_rows(real):
    return jnp.where(real[:, :LANES] < USABLE_BELOW, 1.0, 0.0)


def encode_kernel(
    segments, spectra_ref, valid_ref, sources_ref, own_ref, other_ref, *refs
):
    blocks, refs = refs[:segments], refs[segments:]
    encoded_ref, spectra, valid, sources, high, low, band, arrived = refs
    copies = [
        pltpu.make_async_copy(spectra_ref, spectra, arrived.at[0]),
        pltpu.make_async_copy(sources_ref, sources, arrived.at[1]),
        pltpu.make_async_copy(valid_ref, valid, arrived.at[2]),
    ]
    for copy in copies:
        copy.start()
    channels, width = spectra_ref.shape
    nbins = width // 2
    rounds, per_round = sources.shape
    half = rounds * per_round // 2
    index = lax.axis_index("rcv")
    copies[1].wait()
    copies[2].wait()
    diagonal = iota((channels, channels), 0) == iota((channels, channels), 1)
    usable = jnp.sum(jnp.where(diagonal, valid[...], 0), axis=1, keepdims=True) != 0
    row = iota((2 * half, channels), 0)
    local = jnp.zeros((2 * half, channels), jnp.int32)
    for place in range(2 * half):
        number = (index % 2 if place < half else 1 - index % 2) * half + place % half
        here = sources[number // per_round, number % per_round] - index * channels
        local = jnp.where(row == place, here, local)
    onehot = jnp.where(local == iota((2 * half, channels), 1), 1.0, 0.0).astype(jnp.bfloat16)
    band[...] = band_matrix()
    copies[0].wait()
    encoded = jnp.where(usable, spectra[...].astype(jnp.float32), UNUSABLE).astype(jnp.bfloat16)
    picked = jnp.dot(onehot, encoded, preferred_element_type=jnp.float32)
    for at, re, im in whitening(picked[:, :nbins], picked[:, nbins:], high, low, UNUSABLE, band):
        own_rows, other_rows = (
            jnp.concatenate([re[first : first + half], im[first : first + half]], axis=0)
            for first in (0, half)
        )
        own_ref[:, at] = own_rows.astype(own_ref.dtype)
        other_ref[: 2 * half, at] = other_rows.astype(other_ref.dtype)
        other_ref[2 * half :, at] = own_rows.astype(other_ref.dtype)
    encoded_ref[...] = encoded.astype(encoded_ref.dtype)
    keep = channels // segments
    for step, block in enumerate(blocks):
        at = pl.multiple_of((lax.axis_index("tm") ^ step) * keep, keep)
        block[...] = encoded_ref[pl.ds(at, keep), :].astype(block.dtype)


def whiten_kernel(segments, *refs):
    blocks, refs = refs[:segments], refs[segments:]
    real_ref, imag_ref, both_ref, valid_ref, high, low = refs
    rows = jnp.concatenate([ref[...].astype(jnp.float32) for ref in blocks], axis=0)
    nbins = rows.shape[1] // 2
    real, imag = rows[:, :nbins], rows[:, nbins:]
    for at, re, im in whitening(real, imag, high, low):
        real_ref[:, at] = re
        imag_ref[:, at] = im
        both_ref[:, at] = re + im
    valid_ref[...] = usable_rows(real)


def stack_kernel(places, stage, *refs):
    segments, sets = len(places), 1 + max(which for which, _ in places)
    slabs, refs = refs[0], refs[1:]
    receivers = [refs[4 * which : 4 * which + 4] for which in range(sets)]
    table_ref, refs = refs[4 * sets], refs[4 * sets + 1 :]
    first_stage, stage = stage
    before, refs = ([], refs) if first_stage else (refs[:2], refs[2:])
    ready, refs = (refs[0], refs[1:]) if stage == "store" else (None, refs)
    after, refs = (refs[:2], refs[2:]) if stage == "sums" else (refs[:1], refs[1:])
    src_re, src_diff, src_sum, cross, *refs = refs
    nbins, rows = slabs.shape[1], cross.shape[2]
    count = slabs.shape[0] // (2 * segments)
    keep = rows // count
    copies = []
    if stage == "store":
        result, written = refs
        part = lax.axis_index("rcv") % 2
        at = pl.multiple_of(part * rows, rows)
        copies.append(
            pltpu.make_async_copy(ready, after[0].at[pl.ds(at, rows)], written.at[count])
        )
        copies[0].start()
    elif stage == "result":
        result = after[0]
    values = slabs[...].astype(jnp.float32)
    real = jnp.concatenate(
        [values[2 * count * t : 2 * count * t + count] for t in range(segments)], axis=0
    )
    imag = jnp.concatenate(
        [values[2 * count * t + count : 2 * count * (t + 1)] for t in range(segments)], axis=0
    )
    usable = real < USABLE_BELOW
    real, imag = jnp.where(usable, real, 0.0), jnp.where(usable, imag, 0.0)
    src_valid = jnp.where(usable[:, :LANES], 1.0, 0.0)
    for ref, value in ((src_re, real), (src_diff, imag - real), (src_sum, imag + real)):
        for block in range(nbins // LANES):
            ref[block] = value[:, block * LANES : (block + 1) * LANES]
    tile = keep if segments <= 2 else min(keep, 16)

    def spread(ref, block, row):
        return jnp.concatenate([ref[block, pl.ds(row, 8, stride=0), :]] * (tile // 8), axis=0)

    def multiply(block, carry):
        at = pl.ds(pl.multiple_of(block * LANES, LANES), LANES)
        for first in range(0, keep, tile):
            taken = [
                (receivers[which], slice(place * keep + first, place * keep + first + tile))
                for which, place in places
            ]
            r_re = [block_refs[0][row, at] for block_refs, row in taken]
            r_im = [block_refs[1][row, at] for block_refs, row in taken]
            r_both = [block_refs[2][row, at] for block_refs, row in taken]
            for source in range(count):
                p, q, w = [], [], []
                for t in range(segments):
                    row = t * count + source
                    p.append(spread(src_re, block, row) * r_both[t])
                    q.append(spread(src_diff, block, row) * r_im[t])
                    w.append(spread(src_sum, block, row) * r_re[t])
                p, q, w = (functools.reduce(jnp.add, part) for part in (p, q, w))
                to = slice(source * keep + first, source * keep + first + tile)
                cross[0, block, to] = (p + q).astype(cross.dtype)
                cross[1, block, to] = (w - p).astype(cross.dtype)
        return carry

    lax.fori_loop(0, nbins // LANES, multiply, 0)

    def project(place, part):
        value = [cross[place, block, part] for block in range(nbins // LANES)]
        return jnp.dot(
            jnp.concatenate(value, axis=1).astype(jnp.bfloat16),
            table_ref[place * nbins : (place + 1) * nbins],
            preferred_element_type=jnp.float32,
        )

    ends = []
    for first in (0, count // 2):
        at = slice(first * keep, (first + count // 2) * keep)
        sums = [project(place, at) for place in range(2)]
        if not first_stage:
            sums = [before[0][place, at] + sums[place] for place in range(2)]
        if stage == "sums":
            for place in range(2):
                after[0][place, at] = sums[place]
        ends.append(sums)

    lags = 2 * LAG + 1
    scale = 2.0 / math.sqrt(nbins)
    mirror = LAG - FIRST_LAG - iota((keep, LANES), 1)
    pieces = max(1, count // 4)
    for source in range(count):
        to = slice(source * keep, (source + 1) * keep)
        common = [
            src_valid[t * count + source : t * count + source + 1]
            * receivers[which][3][place * keep : (place + 1) * keep, :]
            for t, (which, place) in enumerate(places)
        ] + ([] if first_stage else [before[1][to]])
        common = functools.reduce(jnp.add, common)
        if stage == "sums":
            after[1][to] = common
            continue
        weight = scale / jnp.maximum(common, 1.0)
        inside = slice(source % (count // 2) * keep, (source % (count // 2) + 1) * keep)
        even, odd = (total[inside] for total in ends[source // (count // 2)])
        ahead = even + odd
        behind = even - odd
        low_part = jnp.take_along_axis(
            behind[:, :LANES], jnp.clip(mirror, 0, LANES - 1), axis=1
        )
        high_part = jnp.take_along_axis(
            behind[:, LANES:], jnp.clip(mirror - LANES, 0, LANES - 1), axis=1
        )
        result[to, :LANES] = jnp.where(mirror < LANES, low_part, high_part) * weight
        for first in range(0, lags - LANES, LANES):
            last = min(first + LANES, lags - LANES)
            value = ahead[:, first : first + LANES] * weight
            result[to, LANES + first : LANES + last] = value[:, : last - first]
        if stage == "store" and (source + 1) % pieces == 0:
            first, size = (source + 1 - pieces) * keep, pieces * keep
            at = pl.multiple_of((1 - part) * rows + first, size)
            copies.append(
                pltpu.make_async_copy(
                    result.at[pl.ds(first, size)],
                    after[0].at[pl.ds(at, size)],
                    written.at[source // pieces],
                )
            )
            copies[-1].start()
    for copy in copies:
        copy.wait()


def encode(segments, spectra, valid, sources):
    channels, width = spectra.shape
    keep = channels // segments
    slab = jax.ShapeDtypeStruct((sources.size, width // 2), jnp.bfloat16)
    slabs = jax.ShapeDtypeStruct((2 * sources.size, width // 2), jnp.bfloat16)
    block = jax.ShapeDtypeStruct((keep, width), jnp.bfloat16)
    padded = pltpu.VMEM((sources.size, width // 2 + 2 * LANES), jnp.bfloat16)
    pinned = [pltpu.with_memory_space_constraint(x, pltpu.HBM) for x in (spectra, valid, sources)]
    return pl.pallas_call(
        functools.partial(encode_kernel, segments),
        out_shape=(slab, slabs) + (block,) * segments,
        in_specs=[HBM] * 3,
        out_specs=(VMEM,) * (2 + segments),
        scratch_shapes=[
            pltpu.VMEM((channels, width), kind_for(keep)),
            pltpu.VMEM((channels, width), jnp.bfloat16),
            pltpu.VMEM((1, channels), jnp.int32),
            pltpu.SMEM(sources.shape, jnp.int32),
            padded,
            padded,
            pltpu.VMEM((BLOCK + 2 * LANES, BLOCK), jnp.bfloat16),
            pltpu.SemaphoreType.DMA((3,)),
        ],
        compiler_params=pltpu.CompilerParams(vmem_limit_bytes=12 * MEBI),
        name="encode_and_pick",
    )(*pinned)


def whiten_blocks(blocks):
    segments, (keep, width) = len(blocks), blocks[0].shape
    count, nbins = segments * keep, width // 2
    padded = pltpu.VMEM((count, nbins + 2 * LANES), jnp.bfloat16)
    part = jax.ShapeDtypeStruct((count, nbins), jnp.float32)
    return pl.pallas_call(
        functools.partial(whiten_kernel, segments),
        out_shape=(part, part, part, jax.ShapeDtypeStruct((count, LANES), jnp.float32)),
        in_specs=[VMEM] * segments,
        out_specs=(VMEM,) * 4,
        scratch_shapes=[padded, padded],
        compiler_params=pltpu.CompilerParams(vmem_limit_bytes=20 * MEBI),
        cost_estimate=pl.CostEstimate(
            flops=count * width * 1024, bytes_accessed=count * width * 4, transcendentals=0
        ),
        name="whiten_receivers",
    )(*blocks)


def stack_stage(keep, slabs, places, receivers, table, stage, before=(), ready=()):
    count, nbins = slabs.shape[0] // (2 * len(places)), slabs.shape[1]
    rows, lags = count * keep, 2 * LAG + 1
    part = pltpu.VMEM((nbins // LANES, len(places) * count, LANES), jnp.float32)
    cross = pltpu.VMEM((2, nbins // LANES, rows, LANES), kind_for(keep))
    scratch = [part, part, part, cross]
    sums = (
        jax.ShapeDtypeStruct((2, rows, BLOCK), jnp.float32),
        jax.ShapeDtypeStruct((rows, LANES), jnp.float32),
    )
    if stage == "store":
        scratch += [pltpu.VMEM((rows, lags), jnp.float32), pltpu.SemaphoreType.DMA((count + 1,))]
    out_rows = 2 * rows if stage == "store" else rows
    result = jax.ShapeDtypeStruct((out_rows, lags), jnp.float32)
    inputs = [slabs, *sum(receivers, ()), table, *before, *ready]
    return pl.pallas_call(
        functools.partial(stack_kernel, places, (not before, stage)),
        out_shape=sums if stage == "sums" else result,
        in_specs=[VMEM] * len(inputs),
        out_specs=(VMEM, VMEM) if stage == "sums" else HBM if stage == "store" else VMEM,
        scratch_shapes=scratch,
        compiler_params=pltpu.CompilerParams(vmem_limit_bytes=20 * MEBI),
        cost_estimate=pl.CostEstimate(
            flops=4 * rows * nbins * 2 * LAG, bytes_accessed=nbins * 2048, transcendentals=0
        ),
        name="stack_" + stage,
    )(*inputs)


def swapped(value, axis, size, step):
    return lax.ppermute(value, axis, [(i, i ^ step) for i in range(size)])


def shards(rcv_size, tm_size, spectra, valid, sources):
    channels, _, width = spectra.shape
    keep = channels // tm_size
    rounds, per_round = sources.shape
    own, other, *receivers = encode(
        tm_size, spectra[:, 0, :], valid.reshape(1, channels), sources
    )
    receivers[-1] = swapped(receivers[-1], "tm", tm_size, tm_size - 1)
    own = own + swapped(other, "rcv", rcv_size, 1)[: own.shape[0]]
    own, later = lax.optimization_barrier((own, receivers[1:-1]))
    receivers[1:-2] = [
        swapped(block, "tm", tm_size, place) for place, block in enumerate(later[:-1], 1)
    ]
    step = 2
    while step < rcv_size:
        wide = min(4, rcv_size // step)
        parts = [swapped(own, "rcv", rcv_size, place * step) for place in range(1, wide)]
        if step == 2:
            parts[0], last = lax.optimization_barrier((parts[0], later[-1]))
            receivers[-2] = swapped(last, "tm", tm_size, tm_size - 2)
            early = tuple(whiten_blocks([receivers[0], receivers[-1]]))
            parts[-2:-1], early = lax.optimization_barrier((parts[-2:-1], early))
        own = functools.reduce(jnp.add, parts, own)
        step *= wide
    own = [own] + [swapped(own, "tm", tm_size, place) for place in range(1, tm_size)]
    table = jnp.asarray(lag_table(width // 2))
    far = tm_size - 1
    late = tuple(whiten_blocks(receivers[1:far]))
    own[far], late = lax.optimization_barrier((own[far], late))
    sums = stack_stage(
        keep, jnp.concatenate([own[0], own[far]], axis=0), [(0, 0), (0, 1)], [early], table, "sums"
    )
    rest, sums, late = lax.optimization_barrier((own[1:far], sums, late))
    slabs = jnp.concatenate([own[0], own[far], *rest], axis=0)
    other = swapped(slabs, "rcv", rcv_size, 1)
    places = [(0, place) for place in range(far - 1)]
    first = stack_stage(
        keep, slabs[2 * own[0].shape[0] :], places, [late], table, "result", sums
    )
    places = [(0, 0), (0, 1)] + [(1, place) for place in range(far - 1)]
    stack = stack_stage(keep, other, places, [early, late], table, "store", (), (first,))
    return stack.reshape(rounds, per_round, keep, 2 * LAG + 1)


def solution(mesh):
    body = functools.partial(shards, mesh.shape["rcv"], mesh.shape["tm"])
    in_specs = (P("rcv", "tm", None), P("rcv", "tm"), P())
    out_specs = P(None, None, ("rcv", "tm"), None)
    return jax.shard_map(body, mesh=mesh, in_specs=in_specs, out_specs=out_specs, check_vma=False)
```

```python
import functools
import math

import jax
import jax.numpy as jnp
import numpy as np
from jax import lax
from jax.experimental import pallas as pl
from jax.experimental.pallas import tpu as pltpu
from jax.sharding import PartitionSpec as P

NT = 4096
LAG = 150
HALF_WIN = 64
EPSILON = 1e-06

UNUSABLE = 1024.0
USABLE_BELOW = 512.0

LANES = 128
BLOCK = 256
MEBI = 1 << 20
FIRST_LAG = LANES - LAG
VMEM = pl.BlockSpec(memory_space=pltpu.VMEM)
HBM = pl.BlockSpec(memory_space=pltpu.HBM)


def lag_table(nbins):
    winding = np.mod(
        np.arange(1, nbins + 1, dtype=np.int64)[:, None]
        * np.arange(FIRST_LAG, FIRST_LAG + BLOCK, dtype=np.int64)[None, :],
        NT,
    )
    theta = winding * (2.0 * math.pi / NT)
    return np.concatenate([np.cos(theta), -np.sin(theta)], axis=0).astype(jnp.bfloat16)


def kind_for(rows):
    return jnp.bfloat16 if rows % 16 == 0 else jnp.float32


def iota(shape, dim):
    return lax.broadcasted_iota(jnp.int32, shape, dim)


def band_matrix():
    shape = (BLOCK + 2 * LANES, BLOCK)
    near = jnp.abs(iota(shape, 0) - LANES - iota(shape, 1)) <= HALF_WIN
    return jnp.where(near, 1.0, 0.0).astype(jnp.bfloat16)


def whitening(real, imag, high, low, unusable=0.0, band=None):
    count, nbins = real.shape
    blocks = nbins // BLOCK
    span = BLOCK + 2 * LANES
    amplitude = jnp.sqrt(real * real + imag * imag)
    rounded = amplitude.astype(jnp.bfloat16)
    edge = jnp.zeros((count, LANES), jnp.bfloat16)
    for part, value in (
        (high, rounded),
        (low, (amplitude - rounded.astype(jnp.float32)).astype(jnp.bfloat16)),
    ):
        part[:, :LANES] = edge
        part[:, LANES : LANES + nbins] = value
        part[:, LANES + nbins :] = edge
    band = band_matrix() if band is None else band[...]
    pieces = [
        part[:, block * BLOCK : block * BLOCK + span] for block in range(blocks) for part in (high, low)
    ]
    windows = jnp.dot(
        jnp.concatenate(pieces, axis=0), band, preferred_element_type=jnp.float32
    )
    for block in range(blocks):
        first = block * BLOCK
        at = 2 * block * count
        window = windows[at : at + count] + windows[at + count : at + 2 * count]
        index = first + iota((1, BLOCK), 1)
        counted = jnp.minimum(index, HALF_WIN) + jnp.minimum(nbins - 1 - index, HALF_WIN) + 1
        factor = 1.0 / (window / counted.astype(jnp.float32) + EPSILON)
        re = real[:, first : first + BLOCK]
        im = imag[:, first : first + BLOCK]
        usable = re < USABLE_BELOW
        re = jnp.where(usable, re * factor, unusable).astype(jnp.bfloat16).astype(jnp.float32)
        im = jnp.where(usable, im * factor, unusable).astype(jnp.bfloat16).astype(jnp.float32)
        yield slice(first, first + BLOCK), re, im


def usable_rows(real):
    return jnp.where(real[:, :LANES] < USABLE_BELOW, 1.0, 0.0)


def encode_kernel(
    segments, spectra_ref, valid_ref, sources_ref, own_ref, other_ref, *refs
):
    blocks, refs = refs[:segments], refs[segments:]
    encoded_ref, spectra, valid, sources, high, low, band, arrived = refs
    copies = [
        pltpu.make_async_copy(spectra_ref, spectra, arrived.at[0]),
        pltpu.make_async_copy(sources_ref, sources, arrived.at[1]),
        pltpu.make_async_copy(valid_ref, valid, arrived.at[2]),
    ]
    for copy in copies:
        copy.start()
    channels, width = spectra_ref.shape
    nbins = width // 2
    rounds, per_round = sources.shape
    half = rounds * per_round // 2
    index = lax.axis_index("rcv")
    copies[1].wait()
    copies[2].wait()
    diagonal = iota((channels, channels), 0) == iota((channels, channels), 1)
    usable = jnp.sum(jnp.where(diagonal, valid[...], 0), axis=1, keepdims=True) != 0
    row = iota((2 * half, channels), 0)
    local = jnp.zeros((2 * half, channels), jnp.int32)
    for place in range(2 * half):
        number = (index % 2 if place < half else 1 - index % 2) * half + place % half
        here = sources[number // per_round, number % per_round] - index * channels
        local = jnp.where(row == place, here, local)
    onehot = jnp.where(local == iota((2 * half, channels), 1), 1.0, 0.0).astype(jnp.bfloat16)
    band[...] = band_matrix()
    copies[0].wait()
    encoded = jnp.where(usable, spectra[...].astype(jnp.float32), UNUSABLE).astype(jnp.bfloat16)
    picked = jnp.dot(onehot, encoded, preferred_element_type=jnp.float32)
    for at, re, im in whitening(picked[:, :nbins], picked[:, nbins:], high, low, UNUSABLE, band):
        own_rows, other_rows = (
            jnp.concatenate([re[first : first + half], im[first : first + half]], axis=0)
            for first in (0, half)
        )
        own_ref[:, at] = own_rows.astype(own_ref.dtype)
        other_ref[: 2 * half, at] = other_rows.astype(other_ref.dtype)
        other_ref[2 * half :, at] = own_rows.astype(other_ref.dtype)
    encoded_ref[...] = encoded.astype(encoded_ref.dtype)
    keep = channels // segments
    for step, block in enumerate(blocks):
        at = pl.multiple_of((lax.axis_index("tm") ^ step) * keep, keep)
        block[...] = encoded_ref[pl.ds(at, keep), :].astype(block.dtype)


def whiten_kernel(segments, *refs):
    blocks, refs = refs[:segments], refs[segments:]
    real_ref, imag_ref, both_ref, valid_ref, high, low = refs
    rows = jnp.concatenate([ref[...].astype(jnp.float32) for ref in blocks], axis=0)
    nbins = rows.shape[1] // 2
    real, imag = rows[:, :nbins], rows[:, nbins:]
    for at, re, im in whitening(real, imag, high, low):
        real_ref[:, at] = re
        imag_ref[:, at] = im
        both_ref[:, at] = re + im
    valid_ref[...] = usable_rows(real)


def stack_kernel(places, stage, *refs):
    segments, sets = len(places), 1 + max(which for which, _ in places)
    slabs, refs = refs[0], refs[1:]
    receivers = [refs[4 * which : 4 * which + 4] for which in range(sets)]
    table_ref, refs = refs[4 * sets], refs[4 * sets + 1 :]
    first_stage, stage = stage
    before, refs = ([], refs) if first_stage else (refs[:2], refs[2:])
    ready, refs = (refs[0], refs[1:]) if stage == "store" else (None, refs)
    after, refs = (refs[:2], refs[2:]) if stage == "sums" else (refs[:1], refs[1:])
    src_re, src_diff, src_sum, cross, *refs = refs
    nbins, rows = slabs.shape[1], cross.shape[2]
    count = slabs.shape[0] // (2 * segments)
    keep = rows // count
    copies = []
    if stage == "store":
        result, written = refs
        part = lax.axis_index("rcv") % 2
        at = pl.multiple_of(part * rows, rows)
        copies.append(
            pltpu.make_async_copy(ready, after[0].at[pl.ds(at, rows)], written.at[count])
        )
        copies[0].start()
    elif stage == "result":
        result = after[0]
    values = slabs[...].astype(jnp.float32)
    real = jnp.concatenate(
        [values[2 * count * t : 2 * count * t + count] for t in range(segments)], axis=0
    )
    imag = jnp.concatenate(
        [values[2 * count * t + count : 2 * count * (t + 1)] for t in range(segments)], axis=0
    )
    usable = real < USABLE_BELOW
    real, imag = jnp.where(usable, real, 0.0), jnp.where(usable, imag, 0.0)
    src_valid = jnp.where(usable[:, :LANES], 1.0, 0.0)
    for ref, value in ((src_re, real), (src_diff, imag - real), (src_sum, imag + real)):
        for block in range(nbins // LANES):
            ref[block, : segments * count] = value[:, block * LANES : (block + 1) * LANES]
    tile = keep if segments <= 2 else min(keep, 16)

    def spread(ref, block, row):
        return jnp.concatenate([ref[block, pl.ds(row, 8, stride=0), :]] * (tile // 8), axis=0)

    def multiply(block, carry):
        at = pl.ds(pl.multiple_of(block * LANES, LANES), LANES)
        for first in range(0, keep, tile):
            taken = [
                (receivers[which], slice(place * keep + first, place * keep + first + tile))
                for which, place in places
            ]
            r_re = [block_refs[0][row, at] for block_refs, row in taken]
            r_im = [block_refs[1][row, at] for block_refs, row in taken]
            r_both = [block_refs[2][row, at] for block_refs, row in taken]
            for source in range(count):
                p, q, w = [], [], []
                for t in range(segments):
                    row = t * count + source
                    p.append(spread(src_re, block, row) * r_both[t])
                    q.append(spread(src_diff, block, row) * r_im[t])
                    w.append(spread(src_sum, block, row) * r_re[t])
                p, q, w = (functools.reduce(jnp.add, part) for part in (p, q, w))
                to = slice(source * keep + first, source * keep + first + tile)
                cross[0, block, to] = (p + q).astype(cross.dtype)
                cross[1, block, to] = (w - p).astype(cross.dtype)
        return carry

    lax.fori_loop(0, nbins // LANES, multiply, 0)

    def project(place, part):
        value = [cross[place, block, part] for block in range(nbins // LANES)]
        return jnp.dot(
            jnp.concatenate(value, axis=1).astype(jnp.bfloat16),
            table_ref[place * nbins : (place + 1) * nbins],
            preferred_element_type=jnp.float32,
        )

    ends = []
    for first in (0, count // 2):
        at = slice(first * keep, (first + count // 2) * keep)
        sums = [project(place, at) for place in range(2)]
        if not first_stage:
            sums = [before[0][place, at] + sums[place] for place in range(2)]
        if stage == "sums":
            for place in range(2):
                after[0][place, at] = sums[place]
        ends.append(sums)

    lags = 2 * LAG + 1
    scale = 2.0 / math.sqrt(nbins)
    mirror = LAG - FIRST_LAG - iota((keep, LANES), 1)
    pieces = max(1, count // 4)
    for source in range(count):
        to = slice(source * keep, (source + 1) * keep)
        common = [
            src_valid[t * count + source : t * count + source + 1]
            * receivers[which][3][place * keep : (place + 1) * keep, :]
            for t, (which, place) in enumerate(places)
        ] + ([] if first_stage else [before[1][to]])
        common = functools.reduce(jnp.add, common)
        if stage == "sums":
            after[1][to] = common
            continue
        weight = scale / jnp.maximum(common, 1.0)
        inside = slice(source % (count // 2) * keep, (source % (count // 2) + 1) * keep)
        even, odd = (total[inside] for total in ends[source // (count // 2)])
        ahead = even + odd
        behind = even - odd
        low_part = jnp.take_along_axis(
            behind[:, :LANES], jnp.clip(mirror, 0, LANES - 1), axis=1
        )
        high_part = jnp.take_along_axis(
            behind[:, LANES:], jnp.clip(mirror - LANES, 0, LANES - 1), axis=1
        )
        result[to, :LANES] = jnp.where(mirror < LANES, low_part, high_part) * weight
        for first in range(0, lags - LANES, LANES):
            last = min(first + LANES, lags - LANES)
            value = ahead[:, first : first + LANES] * weight
            result[to, LANES + first : LANES + last] = value[:, : last - first]
        if stage == "store" and (source + 1) % pieces == 0:
            first, size = (source + 1 - pieces) * keep, pieces * keep
            at = pl.multiple_of((1 - part) * rows + first, size)
            copies.append(
                pltpu.make_async_copy(
                    result.at[pl.ds(first, size)],
                    after[0].at[pl.ds(at, size)],
                    written.at[source // pieces],
                )
            )
            copies[-1].start()
    for copy in copies:
        copy.wait()


def encode(segments, spectra, valid, sources):
    channels, width = spectra.shape
    keep = channels // segments
    slab = jax.ShapeDtypeStruct((sources.size, width // 2), jnp.bfloat16)
    slabs = jax.ShapeDtypeStruct((2 * sources.size, width // 2), jnp.bfloat16)
    block = jax.ShapeDtypeStruct((keep, width), jnp.bfloat16)
    padded = pltpu.VMEM((sources.size, width // 2 + 2 * LANES), jnp.bfloat16)
    pinned = [pltpu.with_memory_space_constraint(x, pltpu.HBM) for x in (spectra, valid, sources)]
    return pl.pallas_call(
        functools.partial(encode_kernel, segments),
        out_shape=(slab, slabs) + (block,) * segments,
        in_specs=[HBM] * 3,
        out_specs=(VMEM,) * (2 + segments),
        scratch_shapes=[
            pltpu.VMEM((channels, width), kind_for(keep)),
            pltpu.VMEM((channels, width), jnp.bfloat16),
            pltpu.VMEM((1, channels), jnp.int32),
            pltpu.SMEM(sources.shape, jnp.int32),
            padded,
            padded,
            pltpu.VMEM((BLOCK + 2 * LANES, BLOCK), jnp.bfloat16),
            pltpu.SemaphoreType.DMA((3,)),
        ],
        compiler_params=pltpu.CompilerParams(vmem_limit_bytes=12 * MEBI),
        name="encode_and_pick",
    )(*pinned)


def whiten_blocks(blocks):
    segments, (keep, width) = len(blocks), blocks[0].shape
    count, nbins = segments * keep, width // 2
    padded = pltpu.VMEM((count, nbins + 2 * LANES), jnp.bfloat16)
    part = jax.ShapeDtypeStruct((count, nbins), jnp.float32)
    return pl.pallas_call(
        functools.partial(whiten_kernel, segments),
        out_shape=(part, part, part, jax.ShapeDtypeStruct((count, LANES), jnp.float32)),
        in_specs=[VMEM] * segments,
        out_specs=(VMEM,) * 4,
        scratch_shapes=[padded, padded],
        compiler_params=pltpu.CompilerParams(vmem_limit_bytes=20 * MEBI),
        cost_estimate=pl.CostEstimate(
            flops=count * width * 1024, bytes_accessed=count * width * 4, transcendentals=0
        ),
        name="whiten_receivers",
    )(*blocks)


def stack_stage(keep, slabs, places, receivers, table, stage, before=(), ready=()):
    count, nbins = slabs.shape[0] // (2 * len(places)), slabs.shape[1]
    rows, lags = count * keep, 2 * LAG + 1
    part = pltpu.VMEM((nbins // LANES, len(places) * count + 8, LANES), jnp.float32)
    cross = pltpu.VMEM((2, nbins // LANES, rows, LANES), kind_for(keep))
    scratch = [part, part, part, cross]
    sums = (
        jax.ShapeDtypeStruct((2, rows, BLOCK), jnp.float32),
        jax.ShapeDtypeStruct((rows, LANES), jnp.float32),
    )
    if stage == "store":
        scratch += [pltpu.VMEM((rows, lags), jnp.float32), pltpu.SemaphoreType.DMA((count + 1,))]
    out_rows = 2 * rows if stage == "store" else rows
    result = jax.ShapeDtypeStruct((out_rows, lags), jnp.float32)
    inputs = [slabs, *sum(receivers, ()), table, *before, *ready]
    return pl.pallas_call(
        functools.partial(stack_kernel, places, (not before, stage)),
        out_shape=sums if stage == "sums" else result,
        in_specs=[VMEM] * len(inputs),
        out_specs=(VMEM, VMEM) if stage == "sums" else HBM if stage == "store" else VMEM,
        scratch_shapes=scratch,
        compiler_params=pltpu.CompilerParams(vmem_limit_bytes=20 * MEBI),
        cost_estimate=pl.CostEstimate(
            flops=4 * rows * nbins * 2 * LAG, bytes_accessed=nbins * 2048, transcendentals=0
        ),
        name="stack_" + stage,
    )(*inputs)


def swapped(value, axis, size, step):
    return lax.ppermute(value, axis, [(i, i ^ step) for i in range(size)])


def shards(rcv_size, tm_size, spectra, valid, sources):
    channels, _, width = spectra.shape
    keep = channels // tm_size
    rounds, per_round = sources.shape
    own, other, *receivers = encode(
        tm_size, spectra[:, 0, :], valid.reshape(1, channels), sources
    )
    receivers[-1] = swapped(receivers[-1], "tm", tm_size, tm_size - 1)
    own = own + swapped(other, "rcv", rcv_size, 1)[: own.shape[0]]
    own, later = lax.optimization_barrier((own, receivers[1:-1]))
    last, receivers[-1] = lax.optimization_barrier((later[-1], receivers[-1]))
    receivers[1:-1] = [
        swapped(block, "tm", tm_size, place) for place, block in enumerate(later[:-1] + [last], 1)
    ]
    step = 2
    while step < rcv_size:
        wide = min(4, rcv_size // step)
        parts = [swapped(own, "rcv", rcv_size, place * step) for place in range(1, wide)]
        if step == 2:
            early = tuple(whiten_blocks([receivers[0], receivers[-1]]))
            parts[-2:-1], early = lax.optimization_barrier((parts[-2:-1], early))
        own = functools.reduce(jnp.add, parts, own)
        step *= wide
    own = [own] + [swapped(own, "tm", tm_size, place) for place in range(1, tm_size)]
    table = jnp.asarray(lag_table(width // 2))
    far = tm_size - 1
    late = tuple(whiten_blocks(receivers[1:far]))
    own[far], late = lax.optimization_barrier((own[far], late))
    sums = stack_stage(
        keep, jnp.concatenate([own[0], own[far]], axis=0), [(0, 0), (0, 1)], [early], table, "sums"
    )
    rest, sums, late = lax.optimization_barrier((own[1:far], sums, late))
    slabs = jnp.concatenate([own[0], own[far], *rest], axis=0)
    other = swapped(slabs, "rcv", rcv_size, 1)
    places = [(0, place) for place in range(far - 1)]
    first = stack_stage(
        keep, slabs[2 * own[0].shape[0] :], places, [late], table, "result", sums
    )
    places = [(0, 0), (0, 1)] + [(1, place) for place in range(far - 1)]
    stack = stack_stage(keep, other, places, [early, late], table, "store", (), (first,))
    return stack.reshape(rounds, per_round, keep, 2 * LAG + 1)


def solution(mesh):
    body = functools.partial(shards, mesh.shape["rcv"], mesh.shape["tm"])
    in_specs = (P("rcv", "tm", None), P("rcv", "tm"), P())
    out_specs = P(None, None, ("rcv", "tm"), None)
    return jax.shard_map(body, mesh=mesh, in_specs=in_specs, out_specs=out_specs, check_vma=False)
```

```python
import functools
import math

import jax
import jax.numpy as jnp
import numpy as np
from jax import lax
from jax.experimental import pallas as pl
from jax.experimental.pallas import tpu as pltpu
from jax.sharding import PartitionSpec as P

NT = 4096
LAG = 150
HALF_WIN = 64
EPSILON = 1e-06

UNUSABLE = 1024.0
USABLE_BELOW = 512.0

LANES = 128
BLOCK = 256
MEBI = 1 << 20
FIRST_LAG = LANES - LAG
VMEM = pl.BlockSpec(memory_space=pltpu.VMEM)
HBM = pl.BlockSpec(memory_space=pltpu.HBM)


def lag_table(nbins):
    winding = np.mod(
        np.arange(1, nbins + 1, dtype=np.int64)[:, None]
        * np.arange(FIRST_LAG, FIRST_LAG + BLOCK, dtype=np.int64)[None, :],
        NT,
    )
    theta = winding * (2.0 * math.pi / NT)
    return np.concatenate([np.cos(theta), -np.sin(theta)], axis=0).astype(jnp.bfloat16)


def kind_for(rows):
    return jnp.bfloat16 if rows % 16 == 0 else jnp.float32


def iota(shape, dim):
    return lax.broadcasted_iota(jnp.int32, shape, dim)


def band_matrix():
    shape = (BLOCK + 2 * LANES, BLOCK)
    near = jnp.abs(iota(shape, 0) - LANES - iota(shape, 1)) <= HALF_WIN
    return jnp.where(near, 1.0, 0.0).astype(jnp.bfloat16)


def whitening(real, imag, high, low, unusable=0.0, band=None):
    count, nbins = real.shape
    blocks = nbins // BLOCK
    span = BLOCK + 2 * LANES
    amplitude = jnp.sqrt(real * real + imag * imag)
    rounded = amplitude.astype(jnp.bfloat16)
    edge = jnp.zeros((count, LANES), jnp.bfloat16)
    for part, value in (
        (high, rounded),
        (low, (amplitude - rounded.astype(jnp.float32)).astype(jnp.bfloat16)),
    ):
        part[:, :LANES] = edge
        part[:, LANES : LANES + nbins] = value
        part[:, LANES + nbins :] = edge
    band = band_matrix() if band is None else band[...]
    pieces = [
        part[:, block * BLOCK : block * BLOCK + span] for block in range(blocks) for part in (high, low)
    ]
    windows = jnp.dot(
        jnp.concatenate(pieces, axis=0), band, preferred_element_type=jnp.float32
    )
    for block in range(blocks):
        first = block * BLOCK
        at = 2 * block * count
        window = windows[at : at + count] + windows[at + count : at + 2 * count]
        index = first + iota((1, BLOCK), 1)
        counted = jnp.minimum(index, HALF_WIN) + jnp.minimum(nbins - 1 - index, HALF_WIN) + 1
        factor = 1.0 / (window / counted.astype(jnp.float32) + EPSILON)
        re = real[:, first : first + BLOCK]
        im = imag[:, first : first + BLOCK]
        usable = re < USABLE_BELOW
        re = jnp.where(usable, re * factor, unusable).astype(jnp.bfloat16).astype(jnp.float32)
        im = jnp.where(usable, im * factor, unusable).astype(jnp.bfloat16).astype(jnp.float32)
        yield slice(first, first + BLOCK), re, im


def usable_rows(real):
    return jnp.where(real[:, :LANES] < USABLE_BELOW, 1.0, 0.0)


def encode_kernel(
    segments, spectra_ref, valid_ref, sources_ref, own_ref, other_ref, *refs
):
    blocks, refs = refs[:segments], refs[segments:]
    encoded_ref, spectra, valid, sources, high, low, band, arrived = refs
    copies = [
        pltpu.make_async_copy(spectra_ref, spectra, arrived.at[0]),
        pltpu.make_async_copy(sources_ref, sources, arrived.at[1]),
        pltpu.make_async_copy(valid_ref, valid, arrived.at[2]),
    ]
    for copy in copies:
        copy.start()
    channels, width = spectra_ref.shape
    nbins = width // 2
    rounds, per_round = sources.shape
    half = rounds * per_round // 2
    index = lax.axis_index("rcv")
    copies[1].wait()
    copies[2].wait()
    diagonal = iota((channels, channels), 0) == iota((channels, channels), 1)
    usable = jnp.sum(jnp.where(diagonal, valid[...], 0), axis=1, keepdims=True) != 0
    row = iota((2 * half, channels), 0)
    local = jnp.zeros((2 * half, channels), jnp.int32)
    for place in range(2 * half):
        number = (index % 2 if place < half else 1 - index % 2) * half + place % half
        here = sources[number // per_round, number % per_round] - index * channels
        local = jnp.where(row == place, here, local)
    onehot = jnp.where(local == iota((2 * half, channels), 1), 1.0, 0.0).astype(jnp.bfloat16)
    band[...] = band_matrix()
    copies[0].wait()
    encoded = jnp.where(usable, spectra[...].astype(jnp.float32), UNUSABLE).astype(jnp.bfloat16)
    picked = jnp.dot(onehot, encoded, preferred_element_type=jnp.float32)
    for at, re, im in whitening(picked[:, :nbins], picked[:, nbins:], high, low, UNUSABLE, band):
        own_rows, other_rows = (
            jnp.concatenate([re[first : first + half], im[first : first + half]], axis=0)
            for first in (0, half)
        )
        own_ref[:, at] = own_rows.astype(own_ref.dtype)
        other_ref[: 2 * half, at] = other_rows.astype(other_ref.dtype)
        other_ref[2 * half :, at] = own_rows.astype(other_ref.dtype)
    encoded_ref[...] = encoded.astype(encoded_ref.dtype)
    keep = channels // segments
    for step, block in enumerate(blocks):
        at = pl.multiple_of((lax.axis_index("tm") ^ step) * keep, keep)
        block[...] = encoded_ref[pl.ds(at, keep), :].astype(block.dtype)


def whiten_kernel(segments, *refs):
    blocks, refs = refs[:segments], refs[segments:]
    real_ref, imag_ref, both_ref, valid_ref, high, low = refs
    rows = jnp.concatenate([ref[...].astype(jnp.float32) for ref in blocks], axis=0)
    nbins = rows.shape[1] // 2
    real, imag = rows[:, :nbins], rows[:, nbins:]
    for at, re, im in whitening(real, imag, high, low):
        real_ref[:, at] = re
        imag_ref[:, at] = im
        both_ref[:, at] = re + im
    valid_ref[...] = usable_rows(real)


def stack_kernel(places, stage, *refs):
    segments, sets = len(places), 1 + max(which for which, _ in places)
    slabs, refs = refs[0], refs[1:]
    receivers = [refs[4 * which : 4 * which + 4] for which in range(sets)]
    table_ref, refs = refs[4 * sets], refs[4 * sets + 1 :]
    first_stage, stage = stage
    before, refs = ([], refs) if first_stage else (refs[:2], refs[2:])
    ready, refs = (refs[0], refs[1:]) if stage == "store" else (None, refs)
    after, refs = (refs[:2], refs[2:]) if stage == "sums" else (refs[:1], refs[1:])
    src_re, src_diff, src_sum, cross, *refs = refs
    nbins, rows = slabs.shape[1], cross.shape[2]
    count = slabs.shape[0] // (2 * segments)
    keep = rows // count
    copies = []
    if stage == "store":
        result, written = refs
        part = lax.axis_index("rcv") % 2
        at = pl.multiple_of(part * rows, rows)
        copies.append(
            pltpu.make_async_copy(ready, after[0].at[pl.ds(at, rows)], written.at[count])
        )
        copies[0].start()
    elif stage == "result":
        result = after[0]
    values = slabs[...].astype(jnp.float32)
    real = jnp.concatenate(
        [values[2 * count * t : 2 * count * t + count] for t in range(segments)], axis=0
    )
    imag = jnp.concatenate(
        [values[2 * count * t + count : 2 * count * (t + 1)] for t in range(segments)], axis=0
    )
    usable = real < USABLE_BELOW
    real, imag = jnp.where(usable, real, 0.0), jnp.where(usable, imag, 0.0)
    src_valid = jnp.where(usable[:, :LANES], 1.0, 0.0)
    for ref, value in ((src_re, real), (src_diff, imag - real), (src_sum, imag + real)):
        for block in range(nbins // LANES):
            ref[block, : segments * count] = value[:, block * LANES : (block + 1) * LANES]
    tile = keep if segments <= 2 else min(keep, 16)

    def spread(ref, block, row):
        return jnp.concatenate([ref[block, pl.ds(row, 8, stride=0), :]] * (tile // 8), axis=0)

    def multiply(block, carry):
        at = pl.ds(pl.multiple_of(block * LANES, LANES), LANES)
        for first in range(0, keep, tile):
            taken = [
                (receivers[which], slice(place * keep + first, place * keep + first + tile))
                for which, place in places
            ]
            r_re = [block_refs[0][row, at] for block_refs, row in taken]
            r_im = [block_refs[1][row, at] for block_refs, row in taken]
            r_both = [block_refs[2][row, at] for block_refs, row in taken]
            for source in range(count):
                p, q, w = [], [], []
                for t in range(segments):
                    row = t * count + source
                    p.append(spread(src_re, block, row) * r_both[t])
                    q.append(spread(src_diff, block, row) * r_im[t])
                    w.append(spread(src_sum, block, row) * r_re[t])
                p, q, w = (functools.reduce(jnp.add, part) for part in (p, q, w))
                to = slice(source * keep + first, source * keep + first + tile)
                cross[0, block, to] = (p + q).astype(cross.dtype)
                cross[1, block, to] = (w - p).astype(cross.dtype)
        return carry

    lax.fori_loop(0, nbins // LANES, multiply, 0)

    def project(place, part):
        value = [cross[place, block, part] for block in range(nbins // LANES)]
        return jnp.dot(
            jnp.concatenate(value, axis=1).astype(jnp.bfloat16),
            table_ref[place * nbins : (place + 1) * nbins],
            preferred_element_type=jnp.float32,
        )

    ends = []
    for first in (0, count // 2):
        at = slice(first * keep, (first + count // 2) * keep)
        sums = [project(place, at) for place in range(2)]
        if not first_stage:
            sums = [before[0][place, at] + sums[place] for place in range(2)]
        if stage == "sums":
            for place in range(2):
                after[0][place, at] = sums[place]
        ends.append(sums)

    lags = 2 * LAG + 1
    scale = 2.0 / math.sqrt(nbins)
    mirror = LAG - FIRST_LAG - iota((keep, LANES), 1)
    pieces = max(1, count // 4)
    for source in range(count):
        to = slice(source * keep, (source + 1) * keep)
        common = [
            src_valid[t * count + source : t * count + source + 1]
            * receivers[which][3][place * keep : (place + 1) * keep, :]
            for t, (which, place) in enumerate(places)
        ] + ([] if first_stage else [before[1][to]])
        common = functools.reduce(jnp.add, common)
        if stage == "sums":
            after[1][to] = common
            continue
        weight = scale / jnp.maximum(common, 1.0)
        inside = slice(source % (count // 2) * keep, (source % (count // 2) + 1) * keep)
        even, odd = (total[inside] for total in ends[source // (count // 2)])
        ahead = even + odd
        behind = even - odd
        low_part = jnp.take_along_axis(
            behind[:, :LANES], jnp.clip(mirror, 0, LANES - 1), axis=1
        )
        high_part = jnp.take_along_axis(
            behind[:, LANES:], jnp.clip(mirror - LANES, 0, LANES - 1), axis=1
        )
        result[to, :LANES] = jnp.where(mirror < LANES, low_part, high_part) * weight
        for first in range(0, lags - LANES, LANES):
            last = min(first + LANES, lags - LANES)
            value = ahead[:, first : first + LANES] * weight
            result[to, LANES + first : LANES + last] = value[:, : last - first]
        if stage == "store" and (source + 1) % pieces == 0:
            first, size = (source + 1 - pieces) * keep, pieces * keep
            at = pl.multiple_of((1 - part) * rows + first, size)
            copies.append(
                pltpu.make_async_copy(
                    result.at[pl.ds(first, size)],
                    after[0].at[pl.ds(at, size)],
                    written.at[source // pieces],
                )
            )
            copies[-1].start()
    for copy in copies:
        copy.wait()


def encode(segments, spectra, valid, sources):
    channels, width = spectra.shape
    keep = channels // segments
    slab = jax.ShapeDtypeStruct((sources.size, width // 2), jnp.bfloat16)
    slabs = jax.ShapeDtypeStruct((2 * sources.size, width // 2), jnp.bfloat16)
    block = jax.ShapeDtypeStruct((keep, width), jnp.bfloat16)
    padded = pltpu.VMEM((sources.size, width // 2 + 2 * LANES), jnp.bfloat16)
    pinned = [pltpu.with_memory_space_constraint(x, pltpu.HBM) for x in (spectra, valid, sources)]
    return pl.pallas_call(
        functools.partial(encode_kernel, segments),
        out_shape=(slab, slabs) + (block,) * segments,
        in_specs=[HBM] * 3,
        out_specs=(VMEM,) * (2 + segments),
        scratch_shapes=[
            pltpu.VMEM((channels, width), kind_for(keep)),
            pltpu.VMEM((channels, width), jnp.bfloat16),
            pltpu.VMEM((1, channels), jnp.int32),
            pltpu.SMEM(sources.shape, jnp.int32),
            padded,
            padded,
            pltpu.VMEM((BLOCK + 2 * LANES, BLOCK), jnp.bfloat16),
            pltpu.SemaphoreType.DMA((3,)),
        ],
        compiler_params=pltpu.CompilerParams(vmem_limit_bytes=12 * MEBI),
        name="encode_and_pick",
    )(*pinned)


def whiten_blocks(blocks):
    segments, (keep, width) = len(blocks), blocks[0].shape
    count, nbins = segments * keep, width // 2
    padded = pltpu.VMEM((count, nbins + 2 * LANES), jnp.bfloat16)
    part = jax.ShapeDtypeStruct((count, nbins), jnp.float32)
    return pl.pallas_call(
        functools.partial(whiten_kernel, segments),
        out_shape=(part, part, part, jax.ShapeDtypeStruct((count, LANES), jnp.float32)),
        in_specs=[VMEM] * segments,
        out_specs=(VMEM,) * 4,
        scratch_shapes=[padded, padded],
        compiler_params=pltpu.CompilerParams(vmem_limit_bytes=20 * MEBI),
        cost_estimate=pl.CostEstimate(
            flops=count * width * 1024, bytes_accessed=count * width * 4, transcendentals=0
        ),
        name="whiten_receivers",
    )(*blocks)


def stack_stage(keep, slabs, places, receivers, table, stage, before=(), ready=()):
    count, nbins = slabs.shape[0] // (2 * len(places)), slabs.shape[1]
    rows, lags = count * keep, 2 * LAG + 1
    part = pltpu.VMEM((nbins // LANES, len(places) * count + 8, LANES), jnp.float32)
    cross = pltpu.VMEM((2, nbins // LANES, rows, LANES), kind_for(keep))
    scratch = [part, part, part, cross]
    sums = (
        jax.ShapeDtypeStruct((2, rows, BLOCK), jnp.float32),
        jax.ShapeDtypeStruct((rows, LANES), jnp.float32),
    )
    if stage == "store":
        scratch += [pltpu.VMEM((rows, lags), jnp.float32), pltpu.SemaphoreType.DMA((count + 1,))]
    out_rows = 2 * rows if stage == "store" else rows
    result = jax.ShapeDtypeStruct((out_rows, lags), jnp.float32)
    inputs = [slabs, *sum(receivers, ()), table, *before, *ready]
    return pl.pallas_call(
        functools.partial(stack_kernel, places, (not before, stage)),
        out_shape=sums if stage == "sums" else result,
        in_specs=[VMEM] * len(inputs),
        out_specs=(VMEM, VMEM) if stage == "sums" else HBM if stage == "store" else VMEM,
        scratch_shapes=scratch,
        compiler_params=pltpu.CompilerParams(vmem_limit_bytes=20 * MEBI),
        cost_estimate=pl.CostEstimate(
            flops=4 * rows * nbins * 2 * LAG, bytes_accessed=nbins * 2048, transcendentals=0
        ),
        name="stack_" + stage,
    )(*inputs)


def swapped(value, axis, size, step):
    return lax.ppermute(value, axis, [(i, i ^ step) for i in range(size)])


def shards(rcv_size, tm_size, spectra, valid, sources):
    channels, _, width = spectra.shape
    keep = channels // tm_size
    rounds, per_round = sources.shape
    own, other, *receivers = encode(
        tm_size, spectra[:, 0, :], valid.reshape(1, channels), sources
    )
    receivers[-1] = swapped(receivers[-1], "tm", tm_size, tm_size - 1)
    own = own + swapped(other, "rcv", rcv_size, 1)[: own.shape[0]]
    own, later = lax.optimization_barrier((own, receivers[1:-1]))
    last, receivers[-1] = lax.optimization_barrier((later[0], receivers[-1]))
    receivers[1:-1] = [
        swapped(block, "tm", tm_size, place) for place, block in enumerate([last] + later[1:], 1)
    ]
    step = 2
    while step < rcv_size:
        wide = min(4, rcv_size // step)
        parts = [swapped(own, "rcv", rcv_size, place * step) for place in range(1, wide)]
        if step == 2:
            early = tuple(whiten_blocks([receivers[0], receivers[-1]]))
            parts[-2:-1], early = lax.optimization_barrier((parts[-2:-1], early))
        own = functools.reduce(jnp.add, parts, own)
        step *= wide
    own = [own] + [swapped(own, "tm", tm_size, place) for place in range(1, tm_size)]
    table = jnp.asarray(lag_table(width // 2))
    far = tm_size - 1
    late = tuple(whiten_blocks(receivers[1:far]))
    own[far], late = lax.optimization_barrier((own[far], late))
    sums = stack_stage(
        keep, jnp.concatenate([own[0], own[far]], axis=0), [(0, 0), (0, 1)], [early], table, "sums"
    )
    rest, sums, late = lax.optimization_barrier((own[1:far], sums, late))
    slabs = jnp.concatenate([own[0], own[far], *rest], axis=0)
    other = swapped(slabs, "rcv", rcv_size, 1)
    places = [(0, place) for place in range(far - 1)]
    first = stack_stage(
        keep, slabs[2 * own[0].shape[0] :], places, [late], table, "result", sums
    )
    places = [(0, 0), (0, 1)] + [(1, place) for place in range(far - 1)]
    stack = stack_stage(keep, other, places, [early, late], table, "store", (), (first,))
    return stack.reshape(rounds, per_round, keep, 2 * LAG + 1)


def solution(mesh):
    body = functools.partial(shards, mesh.shape["rcv"], mesh.shape["tm"])
    in_specs = (P("rcv", "tm", None), P("rcv", "tm"), P())
    out_specs = P(None, None, ("rcv", "tm"), None)
    return jax.shard_map(body, mesh=mesh, in_specs=in_specs, out_specs=out_specs, check_vma=False)
```

```python
import functools
import math

import jax
import jax.numpy as jnp
import numpy as np
from jax import lax
from jax.experimental import pallas as pl
from jax.experimental.pallas import tpu as pltpu
from jax.sharding import PartitionSpec as P

NT = 4096
LAG = 150
HALF_WIN = 64
EPSILON = 1e-06

UNUSABLE = 1024.0
USABLE_BELOW = 512.0

LANES = 128
BLOCK = 256
MEBI = 1 << 20
FIRST_LAG = LANES - LAG
VMEM = pl.BlockSpec(memory_space=pltpu.VMEM)
HBM = pl.BlockSpec(memory_space=pltpu.HBM)


def lag_table(nbins):
    winding = np.mod(
        np.arange(1, nbins + 1, dtype=np.int64)[:, None]
        * np.arange(FIRST_LAG, FIRST_LAG + BLOCK, dtype=np.int64)[None, :],
        NT,
    )
    theta = winding * (2.0 * math.pi / NT)
    return np.concatenate([np.cos(theta), -np.sin(theta)], axis=0).astype(jnp.bfloat16)


def kind_for(rows):
    return jnp.bfloat16 if rows % 16 == 0 else jnp.float32


def iota(shape, dim):
    return lax.broadcasted_iota(jnp.int32, shape, dim)


def band_matrix():
    shape = (BLOCK + 2 * LANES, BLOCK)
    near = jnp.abs(iota(shape, 0) - LANES - iota(shape, 1)) <= HALF_WIN
    return jnp.where(near, 1.0, 0.0).astype(jnp.bfloat16)


def whitening(real, imag, high, low, unusable=0.0, band=None):
    count, nbins = real.shape
    blocks = nbins // BLOCK
    span = BLOCK + 2 * LANES
    amplitude = jnp.sqrt(real * real + imag * imag)
    rounded = amplitude.astype(jnp.bfloat16)
    edge = jnp.zeros((count, LANES), jnp.bfloat16)
    for part, value in (
        (high, rounded),
        (low, (amplitude - rounded.astype(jnp.float32)).astype(jnp.bfloat16)),
    ):
        part[:, :LANES] = edge
        part[:, LANES : LANES + nbins] = value
        part[:, LANES + nbins :] = edge
    band = band_matrix() if band is None else band[...]
    pieces = [
        part[:, block * BLOCK : block * BLOCK + span] for block in range(blocks) for part in (high, low)
    ]
    windows = jnp.dot(
        jnp.concatenate(pieces, axis=0), band, preferred_element_type=jnp.float32
    )
    for block in range(blocks):
        first = block * BLOCK
        at = 2 * block * count
        window = windows[at : at + count] + windows[at + count : at + 2 * count]
        index = first + iota((1, BLOCK), 1)
        counted = jnp.minimum(index, HALF_WIN) + jnp.minimum(nbins - 1 - index, HALF_WIN) + 1
        factor = 1.0 / (window / counted.astype(jnp.float32) + EPSILON)
        re = real[:, first : first + BLOCK]
        im = imag[:, first : first + BLOCK]
        usable = re < USABLE_BELOW
        re = jnp.where(usable, re * factor, unusable).astype(jnp.bfloat16).astype(jnp.float32)
        im = jnp.where(usable, im * factor, unusable).astype(jnp.bfloat16).astype(jnp.float32)
        yield slice(first, first + BLOCK), re, im


def usable_rows(real):
    return jnp.where(real[:, :LANES] < USABLE_BELOW, 1.0, 0.0)


def encode_kernel(
    segments, spectra_ref, valid_ref, sources_ref, own_ref, other_ref, *refs
):
    blocks, refs = refs[:segments], refs[segments:]
    encoded_ref, spectra, valid, sources, high, low, band, arrived = refs
    copies = [
        pltpu.make_async_copy(spectra_ref, spectra, arrived.at[0]),
        pltpu.make_async_copy(sources_ref, sources, arrived.at[1]),
        pltpu.make_async_copy(valid_ref, valid, arrived.at[2]),
    ]
    for copy in copies:
        copy.start()
    channels, width = spectra_ref.shape
    nbins = width // 2
    rounds, per_round = sources.shape
    half = rounds * per_round // 2
    index = lax.axis_index("rcv")
    copies[1].wait()
    copies[2].wait()
    diagonal = iota((channels, channels), 0) == iota((channels, channels), 1)
    usable = jnp.sum(jnp.where(diagonal, valid[...], 0), axis=1, keepdims=True) != 0
    row = iota((2 * half, channels), 0)
    local = jnp.zeros((2 * half, channels), jnp.int32)
    for place in range(2 * half):
        number = (index % 2 if place < half else 1 - index % 2) * half + place % half
        here = sources[number // per_round, number % per_round] - index * channels
        local = jnp.where(row == place, here, local)
    onehot = jnp.where(local == iota((2 * half, channels), 1), 1.0, 0.0).astype(jnp.bfloat16)
    band[...] = band_matrix()
    copies[0].wait()
    encoded = jnp.where(usable, spectra[...].astype(jnp.float32), UNUSABLE).astype(jnp.bfloat16)
    picked = jnp.dot(onehot, encoded, preferred_element_type=jnp.float32)
    for at, re, im in whitening(picked[:, :nbins], picked[:, nbins:], high, low, UNUSABLE, band):
        own_rows, other_rows = (
            jnp.concatenate([re[first : first + half], im[first : first + half]], axis=0)
            for first in (0, half)
        )
        own_ref[:, at] = own_rows.astype(own_ref.dtype)
        other_ref[: 2 * half, at] = other_rows.astype(other_ref.dtype)
        other_ref[2 * half :, at] = own_rows.astype(other_ref.dtype)
    encoded_ref[...] = encoded.astype(encoded_ref.dtype)
    keep = channels // segments
    for step, block in enumerate(blocks):
        at = pl.multiple_of((lax.axis_index("tm") ^ step) * keep, keep)
        block[...] = encoded_ref[pl.ds(at, keep), :].astype(block.dtype)


def whiten_kernel(segments, *refs):
    blocks, refs = refs[:segments], refs[segments:]
    real_ref, imag_ref, both_ref, valid_ref, high, low = refs
    rows = jnp.concatenate([ref[...].astype(jnp.float32) for ref in blocks], axis=0)
    nbins = rows.shape[1] // 2
    real, imag = rows[:, :nbins], rows[:, nbins:]
    for at, re, im in whitening(real, imag, high, low):
        real_ref[:, at] = re
        imag_ref[:, at] = im
        both_ref[:, at] = re + im
    valid_ref[...] = usable_rows(real)


def stack_kernel(places, stage, *refs):
    segments, sets = len(places), 1 + max(which for which, _ in places)
    slabs, refs = refs[0], refs[1:]
    receivers = [refs[4 * which : 4 * which + 4] for which in range(sets)]
    table_ref, refs = refs[4 * sets], refs[4 * sets + 1 :]
    first_stage, stage = stage
    before, refs = ([], refs) if first_stage else (refs[:2], refs[2:])
    ready, refs = (refs[0], refs[1:]) if stage == "store" else (None, refs)
    after, refs = (refs[:2], refs[2:]) if stage == "sums" else (refs[:1], refs[1:])
    src_re, src_diff, src_sum, cross, *refs = refs
    nbins, rows = slabs.shape[1], cross.shape[2]
    count = slabs.shape[0] // (2 * segments)
    keep = rows // count
    copies = []
    if stage == "store":
        result, written = refs
        part = lax.axis_index("rcv") % 2
        at = pl.multiple_of(part * rows, rows)
        copies.append(
            pltpu.make_async_copy(ready, after[0].at[pl.ds(at, rows)], written.at[count])
        )
        copies[0].start()
    elif stage == "result":
        result = after[0]
    values = slabs[...].astype(jnp.float32)
    real = jnp.concatenate(
        [values[2 * count * t : 2 * count * t + count] for t in range(segments)], axis=0
    )
    imag = jnp.concatenate(
        [values[2 * count * t + count : 2 * count * (t + 1)] for t in range(segments)], axis=0
    )
    usable = real < USABLE_BELOW
    real, imag = jnp.where(usable, real, 0.0), jnp.where(usable, imag, 0.0)
    src_valid = jnp.where(usable[:, :LANES], 1.0, 0.0)
    for ref, value in ((src_re, real), (src_diff, imag - real), (src_sum, imag + real)):
        for block in range(nbins // LANES):
            ref[block, : segments * count] = value[:, block * LANES : (block + 1) * LANES]
    tile = keep if segments <= 2 else min(keep, 16)

    def spread(ref, block, row):
        return jnp.concatenate([ref[block, pl.ds(row, 8, stride=0), :]] * (tile // 8), axis=0)

    def multiply(sources, block, carry):
        at = pl.ds(pl.multiple_of(block * LANES, LANES), LANES)
        for first in range(0, keep, tile):
            taken = [
                (receivers[which], slice(place * keep + first, place * keep + first + tile))
                for which, place in places
            ]
            r_re = [block_refs[0][row, at] for block_refs, row in taken]
            r_im = [block_refs[1][row, at] for block_refs, row in taken]
            r_both = [block_refs[2][row, at] for block_refs, row in taken]
            for source in sources:
                p, q, w = [], [], []
                for t in range(segments):
                    row = t * count + source
                    p.append(spread(src_re, block, row) * r_both[t])
                    q.append(spread(src_diff, block, row) * r_im[t])
                    w.append(spread(src_sum, block, row) * r_re[t])
                p, q, w = (functools.reduce(jnp.add, part) for part in (p, q, w))
                to = slice(source * keep + first, source * keep + first + tile)
                cross[0, block, to] = (p + q).astype(cross.dtype)
                cross[1, block, to] = (w - p).astype(cross.dtype)
        return carry

    def project(place, part):
        value = [cross[place, block, part] for block in range(nbins // LANES)]
        return jnp.dot(
            jnp.concatenate(value, axis=1).astype(jnp.bfloat16),
            table_ref[place * nbins : (place + 1) * nbins],
            preferred_element_type=jnp.float32,
        )

    lags = 2 * LAG + 1
    scale = 2.0 / math.sqrt(nbins)
    mirror = LAG - FIRST_LAG - iota((keep, LANES), 1)
    pieces = max(1, count // 4)
    ends = []
    for first in (0, count // 2):
        sources = range(first, first + count // 2)
        lax.fori_loop(0, nbins // LANES, functools.partial(multiply, sources), 0)
        at = slice(first * keep, (first + count // 2) * keep)
        sums = [project(place, at) for place in range(2)]
        if not first_stage:
            sums = [before[0][place, at] + sums[place] for place in range(2)]
        if stage == "sums":
            for place in range(2):
                after[0][place, at] = sums[place]
        ends.append(sums)
        for source in sources:
            to = slice(source * keep, (source + 1) * keep)
            common = [
                src_valid[t * count + source : t * count + source + 1]
                * receivers[which][3][place * keep : (place + 1) * keep, :]
                for t, (which, place) in enumerate(places)
            ] + ([] if first_stage else [before[1][to]])
            common = functools.reduce(jnp.add, common)
            if stage == "sums":
                after[1][to] = common
                continue
            weight = scale / jnp.maximum(common, 1.0)
            inside = slice(source % (count // 2) * keep, (source % (count // 2) + 1) * keep)
            even, odd = (total[inside] for total in ends[source // (count // 2)])
            ahead = even + odd
            behind = even - odd
            low_part = jnp.take_along_axis(
                behind[:, :LANES], jnp.clip(mirror, 0, LANES - 1), axis=1
            )
            high_part = jnp.take_along_axis(
                behind[:, LANES:], jnp.clip(mirror - LANES, 0, LANES - 1), axis=1
            )
            result[to, :LANES] = jnp.where(mirror < LANES, low_part, high_part) * weight
            for first in range(0, lags - LANES, LANES):
                last = min(first + LANES, lags - LANES)
                value = ahead[:, first : first + LANES] * weight
                result[to, LANES + first : LANES + last] = value[:, : last - first]
            if stage == "store" and (source + 1) % pieces == 0:
                first, size = (source + 1 - pieces) * keep, pieces * keep
                at = pl.multiple_of((1 - part) * rows + first, size)
                copies.append(
                    pltpu.make_async_copy(
                        result.at[pl.ds(first, size)],
                        after[0].at[pl.ds(at, size)],
                        written.at[source // pieces],
                    )
                )
                copies[-1].start()
    for copy in copies:
        copy.wait()


def encode(segments, spectra, valid, sources):
    channels, width = spectra.shape
    keep = channels // segments
    slab = jax.ShapeDtypeStruct((sources.size, width // 2), jnp.bfloat16)
    slabs = jax.ShapeDtypeStruct((2 * sources.size, width // 2), jnp.bfloat16)
    block = jax.ShapeDtypeStruct((keep, width), jnp.bfloat16)
    padded = pltpu.VMEM((sources.size, width // 2 + 2 * LANES), jnp.bfloat16)
    pinned = [pltpu.with_memory_space_constraint(x, pltpu.HBM) for x in (spectra, valid, sources)]
    return pl.pallas_call(
        functools.partial(encode_kernel, segments),
        out_shape=(slab, slabs) + (block,) * segments,
        in_specs=[HBM] * 3,
        out_specs=(VMEM,) * (2 + segments),
        scratch_shapes=[
            pltpu.VMEM((channels, width), kind_for(keep)),
            pltpu.VMEM((channels, width), jnp.bfloat16),
            pltpu.VMEM((1, channels), jnp.int32),
            pltpu.SMEM(sources.shape, jnp.int32),
            padded,
            padded,
            pltpu.VMEM((BLOCK + 2 * LANES, BLOCK), jnp.bfloat16),
            pltpu.SemaphoreType.DMA((3,)),
        ],
        compiler_params=pltpu.CompilerParams(vmem_limit_bytes=12 * MEBI),
        name="encode_and_pick",
    )(*pinned)


def whiten_blocks(blocks):
    segments, (keep, width) = len(blocks), blocks[0].shape
    count, nbins = segments * keep, width // 2
    padded = pltpu.VMEM((count, nbins + 2 * LANES), jnp.bfloat16)
    part = jax.ShapeDtypeStruct((count, nbins), jnp.float32)
    return pl.pallas_call(
        functools.partial(whiten_kernel, segments),
        out_shape=(part, part, part, jax.ShapeDtypeStruct((count, LANES), jnp.float32)),
        in_specs=[VMEM] * segments,
        out_specs=(VMEM,) * 4,
        scratch_shapes=[padded, padded],
        compiler_params=pltpu.CompilerParams(vmem_limit_bytes=20 * MEBI),
        cost_estimate=pl.CostEstimate(
            flops=count * width * 1024, bytes_accessed=count * width * 4, transcendentals=0
        ),
        name="whiten_receivers",
    )(*blocks)


def stack_stage(keep, slabs, places, receivers, table, stage, before=(), ready=()):
    count, nbins = slabs.shape[0] // (2 * len(places)), slabs.shape[1]
    rows, lags = count * keep, 2 * LAG + 1
    part = pltpu.VMEM((nbins // LANES, len(places) * count + 8, LANES), jnp.float32)
    cross = pltpu.VMEM((2, nbins // LANES, rows, LANES), kind_for(keep))
    scratch = [part, part, part, cross]
    sums = (
        jax.ShapeDtypeStruct((2, rows, BLOCK), jnp.float32),
        jax.ShapeDtypeStruct((rows, LANES), jnp.float32),
    )
    if stage == "store":
        scratch += [pltpu.VMEM((rows, lags), jnp.float32), pltpu.SemaphoreType.DMA((count + 1,))]
    out_rows = 2 * rows if stage == "store" else rows
    result = jax.ShapeDtypeStruct((out_rows, lags), jnp.float32)
    inputs = [slabs, *sum(receivers, ()), table, *before, *ready]
    return pl.pallas_call(
        functools.partial(stack_kernel, places, (not before, stage)),
        out_shape=sums if stage == "sums" else result,
        in_specs=[VMEM] * len(inputs),
        out_specs=(VMEM, VMEM) if stage == "sums" else HBM if stage == "store" else VMEM,
        scratch_shapes=scratch,
        compiler_params=pltpu.CompilerParams(vmem_limit_bytes=20 * MEBI),
        cost_estimate=pl.CostEstimate(
            flops=4 * rows * nbins * 2 * LAG, bytes_accessed=nbins * 2048, transcendentals=0
        ),
        name="stack_" + stage,
    )(*inputs)


def swapped(value, axis, size, step):
    return lax.ppermute(value, axis, [(i, i ^ step) for i in range(size)])


def shards(rcv_size, tm_size, spectra, valid, sources):
    channels, _, width = spectra.shape
    keep = channels // tm_size
    rounds, per_round = sources.shape
    own, other, *receivers = encode(
        tm_size, spectra[:, 0, :], valid.reshape(1, channels), sources
    )
    receivers[-1] = swapped(receivers[-1], "tm", tm_size, tm_size - 1)
    own = own + swapped(other, "rcv", rcv_size, 1)[: own.shape[0]]
    own, later = lax.optimization_barrier((own, receivers[1:-1]))
    last, receivers[-1] = lax.optimization_barrier((later[-1], receivers[-1]))
    receivers[1:-1] = [
        swapped(block, "tm", tm_size, place) for place, block in enumerate(later[:-1] + [last], 1)
    ]
    step = 2
    while step < rcv_size:
        wide = min(4, rcv_size // step)
        parts = [swapped(own, "rcv", rcv_size, place * step) for place in range(1, wide)]
        if step == 2:
            early = tuple(whiten_blocks([receivers[0], receivers[-1]]))
            parts[-2:-1], early = lax.optimization_barrier((parts[-2:-1], early))
        own = functools.reduce(jnp.add, parts, own)
        step *= wide
    own = [own] + [swapped(own, "tm", tm_size, place) for place in range(1, tm_size)]
    table = jnp.asarray(lag_table(width // 2))
    far = tm_size - 1
    late = tuple(whiten_blocks(receivers[1:far]))
    own[far], late = lax.optimization_barrier((own[far], late))
    sums = stack_stage(
        keep, jnp.concatenate([own[0], own[far]], axis=0), [(0, 0), (0, 1)], [early], table, "sums"
    )
    rest, sums, late = lax.optimization_barrier((own[1:far], sums, late))
    slabs = jnp.concatenate([own[0], own[far], *rest], axis=0)
    other = swapped(slabs, "rcv", rcv_size, 1)
    places = [(0, place) for place in range(far - 1)]
    first = stack_stage(
        keep, slabs[2 * own[0].shape[0] :], places, [late], table, "result", sums
    )
    places = [(0, 0), (0, 1)] + [(1, place) for place in range(far - 1)]
    stack = stack_stage(keep, other, places, [early, late], table, "store", (), (first,))
    return stack.reshape(rounds, per_round, keep, 2 * LAG + 1)


def solution(mesh):
    body = functools.partial(shards, mesh.shape["rcv"], mesh.shape["tm"])
    in_specs = (P("rcv", "tm", None), P("rcv", "tm"), P())
    out_specs = P(None, None, ("rcv", "tm"), None)
    return jax.shard_map(body, mesh=mesh, in_specs=in_specs, out_specs=out_specs, check_vma=False)
```
